32 devices in a mesh: dp: 16 (over z, y, x), tensor: 2 (over core).
Axes of the slice: x: 2, y: 2, z: 4, core: 2. Of those that a mesh axis runs over, the one named last changes fastest.
Arguments:
- tokens: bfloat16 [32768, 512], P(('dp', 'tensor')), may hold values from -6 to 6
- segment_ids: int32 [32, 1024], P('dp'), may hold values from 0 to 15, never falling along the last dimension, each value on 1 to 512 neighbouring positions
- padding: int32 [32, 1024], P('dp'), may hold values from 0 to 1, as said below
- mixer_gain: float32 [512], replicated, may hold values from 0.25 to 1.75
- query_weight: float32 [512, 512], P('dp', 'tensor'), may hold values from -0.75 to 0.75
- key_weight: float32 [512, 512], P('dp', 'tensor'), may hold values from -0.75 to 0.75
- value_weight: float32 [512, 512], P('dp', 'tensor'), may hold values from -0.25 to 0.25
- slot_weight: float32 [512, 512], P('dp', 'tensor'), may hold values from -0.5 to 0.5
- out_weight: float32 [512, 512], P('tensor', 'dp'), may hold values from -0.5 to 0.5
- feed_gain: float32 [512], replicated, may hold values from 0.25 to 1.75
- up_weight: float32 [512, 2048], P('dp', 'tensor'), may hold values from -0.25 to 0.25
- up_bias: float32 [2048], replicated, may hold values from -3 to 3
- down_weight: float32 [2048, 512], P('tensor', 'dp'), may hold values from -0.1875 to 0.1875
- down_bias: float32 [512], replicated, may hold values from -2 to 2
- cotangent: bfloat16 [32768, 512], P(('dp', 'tensor')), may hold values from -6 to 6
Outputs:
- layer_output: bfloat16 [32768, 512], P(('dp', 'tensor'))
- input_grad: bfloat16 [32768, 512], P(('dp', 'tensor'))
- mixer_gain_grad: float32 [512], replicated
- query_grad: float32 [512, 512], P('dp', 'tensor')
- key_grad: float32 [512, 512], P('dp', 'tensor')
- value_grad: float32 [512, 512], P('dp', 'tensor')
- slot_grad: float32 [512, 512], P('dp', 'tensor')
- out_grad: float32 [512, 512], P('tensor', 'dp')
- feed_gain_grad: float32 [512], replicated
- up_grad: float32 [512, 2048], P('dp', 'tensor')
- up_bias_grad: float32 [2048], replicated
- down_grad: float32 [2048, 512], P('tensor', 'dp')
- down_bias_grad: float32 [512], replicated
The draws below stay inside these ranges and needn't reach their ends.
Inputs may be any that keep to these rules, and one draw needn't show every extreme that they name: `segment_ids`: within each sequence the ids never fall; each document holds 1 to 512 positions, one of them exactly that many. `padding`: in each sequence the ones form a tail, possibly empty.
All inputs are finite; a program needn't handle non-finite values.
Results may differ from the reference program's by a relative error of at most 0.04.
The reference program's roundings to bfloat16 on the way count: a program that leaves them out, or rounds other values in their place, can miss the bound.
Values may be sent and summed in bfloat16 or wider, within the bound.
A program may use at most 128 MiB of HBM per device.

```python
import math
import jax
import jax.numpy as jnp
import numpy as np
from jax import lax

D = 512
HEADS = 8
HEAD_DIM = 64
SLOTS = 64
FF = 2048
SEQ_LEN = 1024
SEQUENCES = 32
TOKENS = 32768


def draw_padding(key, part):
    tail_length = jax.random.randint(key, (SEQUENCES, 1), 0, SEQ_LEN // 4 + 1)
    places = jnp.arange(SEQ_LEN)[None, :]
    return (places >= SEQ_LEN - tail_length).astype(jnp.int32)


def level_of(rng, extent, pieces, smallest, largest):
    def one(dim, shards_of):
        heights = jax.random.uniform(jax.random.fold_in(jax.random.fold_in(rng, 6), dim), (shards_of,), jnp.float32, smallest / len(pieces), largest / len(pieces))
        return jnp.repeat(jnp.exp(heights), extent[dim] // shards_of).reshape((-1,) + (1,) * (len(extent) - dim - 1))

    factor_of = one(*pieces[0])
    for cut in pieces[1:]:
        factor_of = factor_of * one(*cut)
    return factor_of


def split_up(number_of, total, reach, slope):
    weights = [(1 << 20) // math.isqrt(rank ** slope) + 1 for rank in range(2, number_of + 1)]
    rest, counts = total - reach - (number_of - 1), [1] * (number_of - 1)
    while rest > 0:
        free = [i for i in range(number_of - 1) if counts[i] < reach]
        whole, remaining = sum([weights[i] for i in free]), rest
        for i in free:
            more = min(reach - counts[i], max(1, remaining * weights[i] // whole), rest)
            counts[i] = counts[i] + more
            rest = rest - more
    return np.array([reach] + counts)


def uneven_parts(key, amount, total, reach, slope):
    if amount == 2:
        one = jax.random.randint(key, (), max(1, total - reach), min(reach, total - 1) + 1)
        return jnp.stack([one, total - one])
    sizes = jnp.asarray(split_up(amount, total, reach, slope), jnp.int32)
    pairs = (amount - 1) // 2
    giver, sink = sizes[1:1 + 2 * pairs:2], sizes[2:2 + 2 * pairs:2]
    margin = jnp.minimum(giver - 1, reach - sink)
    passed = jax.random.randint(jax.random.fold_in(key, 1), (pairs,), 0, 1 << 20) % (margin + 1)
    sizes = sizes.at[1:1 + 2 * pairs:2].set(giver - passed).at[2:2 + 2 * pairs:2].set(sink + passed)
    return sizes[jax.random.permutation(jax.random.fold_in(key, 2), amount)]


def scatter_about(key, dims, spread, most, shards=(), dtype=jnp.bfloat16):
    values = spread * jax.random.normal(key, dims, jnp.float32)
    if shards:
        values = values * level_of(key, dims, shards, -0.22, 0.18)
    return jnp.clip(values, -most, most).astype(dtype)


def setup_inputs(seed: int = 0) -> dict:
    seeds = jax.random.split(jax.random.key(seed), 16)
    return {
        "tokens": scatter_about(seeds[0], (TOKENS, D), 1.0, 6.0, ((0, 32),)),
        "segment_ids": jax.vmap(lambda own: jnp.searchsorted(jnp.cumsum(uneven_parts(own, max(4, SEQ_LEN // 64), SEQ_LEN, SEQ_LEN // 2, 2)), jnp.arange(SEQ_LEN), side="right"))(jax.random.split(seeds[1], SEQUENCES)).reshape((SEQUENCES, SEQ_LEN)).astype(jnp.int32),
        "padding": draw_padding(jax.random.fold_in(seeds[15], 71), 0),
        "mixer_gain": jnp.clip(1.0 + 0.15 * jax.random.normal(seeds[3], (D,), jnp.float32), 0.25, 1.75),
        "query_weight": scatter_about(seeds[4], (D, D), (D // 8) ** -0.5, 0.75, ((0, 16), (1, 2)), jnp.float32),
        "key_weight": scatter_about(seeds[5], (D, D), (D // 8) ** -0.5, 0.75, ((0, 16), (1, 2)), jnp.float32),
        "value_weight": scatter_about(seeds[6], (D, D), D ** -0.5, 0.25, ((0, 16), (1, 2)), jnp.float32),
        "slot_weight": scatter_about(seeds[7], (D, HEADS * SLOTS), (D // 4) ** -0.5, 0.5, ((0, 16), (1, 2)), jnp.float32),
        "out_weight": scatter_about(seeds[8], (D, D), (D // 4) ** -0.5, 0.5, ((0, 2), (1, 16)), jnp.float32),
        "feed_gain": jnp.clip(1.0 + 0.15 * jax.random.normal(seeds[9], (D,), jnp.float32), 0.25, 1.75),
        "up_weight": scatter_about(seeds[10], (D, FF), D ** -0.5, 0.25, ((0, 16), (1, 2)), jnp.float32),
        "up_bias": scatter_about(seeds[11], (FF,), 0.5, 3.0, (), jnp.float32),
        "down_weight": scatter_about(seeds[12], (FF, D), (FF // 2) ** -0.5, 0.1875, ((0, 2), (1, 16)), jnp.float32),
        "down_bias": scatter_about(seeds[13], (D,), 0.3, 2.0, (), jnp.float32),
        "cotangent": scatter_about(seeds[14], (TOKENS, D), 1.0, 6.0, ((0, 32),)),
    }


highest = lax.Precision.HIGHEST

@jax.custom_vjp
def low(v):
    return lax.optimization_barrier(v.astype(jnp.bfloat16)).astype(jnp.float32)

@jax.custom_vjp
def low_back(v):
    return v

def low_keep(v):
    return (low(v), None)

def low_pass(kept, grad):
    return (grad,)

def back_keep(v):
    return (v, None)

def back_low(kept, grad):
    return (low(grad),)
low.defvjp(low_keep, low_pass)
low_back.defvjp(back_keep, back_low)

def matmul(left, right):
    return jnp.dot(left, right, precision=highest, preferred_element_type=jnp.float32)

def smooth_unit(linear):
    return 0.5 * linear * (1.0 + jnp.tanh(0.7978845608 * (linear + 0.044715 * linear * linear * linear)))

def layer_norm(token_rows, gain_vec):
    row_mean = lax.optimization_barrier(jnp.mean(token_rows, axis=-1, keepdims=True))
    centred = token_rows - row_mean
    variance = lax.optimization_barrier(jnp.mean(centred * centred, axis=-1, keepdims=True))
    return centred * lax.rsqrt(variance + 1e-05) * gain_vec

def mixer_head(queries, key_rows, values, logits, segment, padding):
    length = queries.shape[0]
    places = jnp.arange(length)
    allowed = jnp.logical_and(places[None, :] <= places[:, None], segment[None, :] == segment[:, None]).astype(jnp.float32)
    keep_mask = 1.0 - padding.astype(jnp.float32)
    writes = jnp.exp(logits) * keep_mask[:, None]
    pairs = jnp.dot(queries, key_rows.T, precision=highest) * allowed
    totals = jnp.dot(allowed, writes, precision=highest) + (1.0 - keep_mask)[:, None]
    scores = jnp.dot(pairs, writes, precision=highest) / (totals * math.sqrt(queries.shape[1]))
    shifted = scores - lax.optimization_barrier(jnp.max(scores, axis=1, keepdims=True))
    powers = jnp.exp(shifted)
    chances = powers / lax.optimization_barrier(jnp.sum(powers, axis=1, keepdims=True))
    mixing = jnp.dot(chances / totals, writes.T, precision=highest) * allowed
    return jnp.dot(mixing, values, precision=highest) * keep_mask[:, None]

def heads_first(matrix, groups, width):
    length = matrix.shape[0] // groups
    return matrix.reshape(groups, length, -1, width).transpose(0, 2, 1, 3).reshape(-1, length, width)

def mixer_all(queries, key_rows, values, logits, segment_ids, padding):
    groups = segment_ids.shape[0]
    length = segment_ids.shape[1]
    head_count = queries.shape[1] // HEAD_DIM
    stacked = (heads_first(queries, groups, HEAD_DIM), heads_first(key_rows, groups, HEAD_DIM), heads_first(values, groups, HEAD_DIM), heads_first(logits, groups, SLOTS), jnp.repeat(segment_ids, head_count, axis=0), jnp.repeat(padding, head_count, axis=0))

    def per_head(member):
        return jax.checkpoint(mixer_head)(member[0], member[1], member[2], member[3], member[4], member[5])
    result = lax.map(per_head, stacked)
    return result.reshape(groups, head_count, length, HEAD_DIM).transpose(0, 2, 1, 3).reshape(groups * length, head_count * HEAD_DIM)

def sequence_layer(weights, token_rows, segment, padding):
    mixer_gain, query_weight, key_weight, value_weight, slot_weight, out_weight, feed_gain, up_weight, up_bias, down_weight, down_bias = weights
    normed = low(layer_norm(token_rows, mixer_gain))
    queries = low_back(low(matmul(normed, query_weight)))
    key_rows = low_back(low(matmul(normed, key_weight)))
    values = low_back(low(matmul(normed, value_weight)))
    logits = low_back(matmul(normed, slot_weight))
    mixed = low(mixer_all(queries, key_rows, values, logits, segment[None, :], padding[None, :]))
    branch = low_back(matmul(mixed, out_weight))
    hidden = token_rows + branch
    normed_feed = low(layer_norm(hidden, feed_gain))
    linear = low_back(matmul(normed_feed, up_weight) + up_bias)
    active = low(smooth_unit(linear))
    return hidden + matmul(active, down_weight) + down_bias

def reference(tokens, segment_ids, padding, mixer_gain, query_weight, key_weight, value_weight, slot_weight, out_weight, feed_gain, up_weight, up_bias, down_weight, down_bias, cotangent):
    token_rows = tokens.astype(jnp.float32).reshape(SEQUENCES, SEQ_LEN, D)
    params = (mixer_gain, query_weight, key_weight, value_weight, slot_weight, out_weight, feed_gain, up_weight, up_bias, down_weight, down_bias)

    def whole_layer(rows_in, params_in):
        gain_one, query_in, key_in, value_in, slot_in, out_in, gain_two, up_in, bias_one, down_in, bias_two = params_in
        rounded = (gain_one, low(query_in), low(key_in), low(value_in), low(slot_in), low(out_in), gain_two, low(up_in), bias_one, low(down_in), bias_two)

        def per_sequence(member):
            return jax.checkpoint(sequence_layer)(rounded, member[0], member[1], member[2])
        return lax.map(per_sequence, (rows_in, segment_ids, padding))
    output, pullback = jax.vjp(whole_layer, token_rows, params)
    rows_grad, params_grad = pullback(cotangent.astype(jnp.float32).reshape(SEQUENCES, SEQ_LEN, D))
    return (output.reshape(TOKENS, D).astype(jnp.bfloat16), rows_grad.reshape(TOKENS, D).astype(jnp.bfloat16), params_grad[0], params_grad[1], params_grad[2], params_grad[3], params_grad[4], params_grad[5], params_grad[6], params_grad[7], params_grad[8], params_grad[9], params_grad[10])
```

```python
import functools
import math

import jax
import jax.numpy as jnp
from jax import lax
from jax.experimental import pallas as pl
from jax.experimental.pallas import tpu as pltpu
from jax.sharding import PartitionSpec as P

HEAD_DIM = 64
SLOTS = 64
CHUNK = 128
GROUP = 256
TILE = 256

F32 = jnp.float32
BF16 = jnp.bfloat16
MESH = pl.DeviceIdType.MESH


def dot(left, right):
    return lax.dot_general(left, right, (((1,), (0,)), ((), ())), preferred_element_type=F32)


def dot_rt(left, right):
    return lax.dot_general(left, right, (((1,), (1,)), ((), ())), preferred_element_type=F32)


def dot_lt(left, right):
    return lax.dot_general(left, right, (((0,), (0,)), ((), ())), preferred_element_type=F32)


def twice(block):
    return jnp.concatenate([block, block], axis=1)


def four(block):
    return jnp.concatenate([block, block, block, block], axis=1)


def standardise(rows):
    centred = rows - jnp.mean(rows, axis=-1, keepdims=True)
    scale = lax.rsqrt(jnp.mean(centred * centred, axis=-1, keepdims=True) + 1e-05)
    return centred * scale, scale


def head_stack(block):
    lane = lax.broadcasted_iota(jnp.int32, block.shape, 1) // HEAD_DIM
    zero = jnp.zeros_like(block)
    return jnp.concatenate([jnp.where(lane == h, block, zero) for h in range(4)], axis=0)


def head_blocks():
    row = lax.broadcasted_iota(jnp.int32, (GROUP, GROUP), 0) // HEAD_DIM
    column = lax.broadcasted_iota(jnp.int32, (GROUP, GROUP), 1) // HEAD_DIM
    return row == column


def head_sum(block, ones):
    high = block.astype(BF16)
    low = (block - high.astype(F32)).astype(BF16)
    return dot(high, ones) + dot(low, ones)


def head_max(block):
    halves = []
    lane = lax.broadcasted_iota(jnp.int32, (block.shape[0], 128), 1) < HEAD_DIM
    for j in range(block.shape[1] // 128):
        part = block[:, j * 128 : (j + 1) * 128]
        first = jnp.max(jnp.where(lane, part, -jnp.inf), axis=1, keepdims=True)
        second = jnp.max(jnp.where(lane, -jnp.inf, part), axis=1, keepdims=True)
        halves.append(jnp.where(lane, first, second))
    return jnp.concatenate(halves, axis=1)


def rows_to_columns(seg_row, pad_row, segc, keepc, length):
    segc[pl.ds(0, 8), :] = jnp.full((8, 128), -1.0, F32)
    segc[pl.ds(8 + length, 8), :] = jnp.full((8, 128), -2.0, F32)
    for c in range(length // CHUNK):
        here = slice(c * CHUNK, (c + 1) * CHUNK)
        seg = jnp.broadcast_to(seg_row[:, here].astype(F32), (CHUNK, CHUNK))
        pad = jnp.broadcast_to(pad_row[:, here].astype(F32), (CHUNK, CHUNK))
        segc[pl.ds(8 + c * CHUNK, CHUNK), :] = seg.T
        keepc[pl.ds(c * CHUNK, CHUNK), :] = 1.0 - pad.T


def project(r, tok, gain, wa, keepc, n1, q, k, v, w):
    rows = pl.ds(pl.multiple_of(r * TILE, TILE), TILE)
    xhat, _ = standardise(tok[rows, :].astype(F32))
    normed = (xhat * gain[...]).astype(BF16)
    n1[rows, :] = normed
    keep = twice(keepc[rows, :])
    for g in range(2):
        out = dot(normed, wa[g])
        q[g, rows, :] = out[:, 0:256].astype(BF16)
        k[g, rows, :] = out[:, 256:512].astype(BF16)
        v[g, rows, :] = out[:, 512:768].astype(BF16)
        w[g, rows, :] = (jnp.exp(out[:, 768:1024]) * keep).astype(BF16)


def chunk_masks(c, segc):
    base = pl.multiple_of(c * CHUNK, CHUNK)
    seg = segc[pl.ds(base + 8, CHUNK), :]
    across = seg.T
    row = lax.broadcasted_iota(jnp.int32, (CHUNK, CHUNK), 0)
    column = lax.broadcasted_iota(jnp.int32, (CHUNK, CHUNK), 1)
    same = seg == across
    causal = jnp.where(same & (column <= row), 1.0, 0.0)
    anti = jnp.where(same & (row <= column), 1.0, 0.0)
    before = segc[pl.ds(base + 7, 1), :]
    first = segc[pl.ds(base + 8, 1), :]
    last = segc[pl.ds(base + 7 + CHUNK, 1), :]
    after = segc[pl.ds(base + 8 + CHUNK, 1), :]
    one = lambda test: jnp.where(test, 1.0, 0.0)
    return causal, anti, dict(
        from_before=one(seg == before),
        to_after=one(seg == last),
        from_after=one(seg == after),
        to_before=one(seg == first),
        carry_on=one(before == last),
        carry_back=one(after == first),
    )


def mix_forward(c, segc, keepc, q, k, v, w, probs, inv, score, mixed, kw, wv, zsum, kw_all, wv_all):
    rows = pl.ds(pl.multiple_of(c * CHUNK, CHUNK), CHUNK)
    causal, _, edge = chunk_masks(c, segc)
    causal4 = four(causal)
    causal_low = causal.astype(BF16)
    blocks = head_blocks()
    ones = jnp.where(blocks, 1.0, 0.0).astype(BF16)
    keep = twice(keepc[rows, :])
    come = twice(edge["from_before"])
    come_low = come.astype(BF16)
    go_low = twice(edge["to_after"]).astype(BF16)
    carry = twice(edge["carry_on"])
    for g in range(2):
        qc, kc, vc, wc = q[g, rows, :], k[g, rows, :], v[g, rows, :], w[g, rows, :]
        kw_low, wv_low = kw[g].astype(BF16), wv[g].astype(BF16)
        kw_all[c, g] = kw_low
        wv_all[c, g] = wv_low
        ws = head_stack(wc)
        pairs = (dot_rt(qc, head_stack(kc)) * causal4).astype(BF16)
        total = dot(causal_low, wc) + come * zsum[g, 0:1, :] + (1.0 - keep)
        inverse = 1.0 / total
        scores = (dot(pairs, ws) + dot(qc * come_low, kw_low)) * (inverse * (HEAD_DIM**-0.5))
        powers = jnp.exp(scores - head_max(scores))
        chances = powers / head_sum(powers, ones)
        ratio = (chances * inverse).astype(BF16)
        probs[g, rows, :] = chances
        inv[g, rows, :] = inverse
        score[g, rows, :] = scores
        mixing = (dot_rt(ratio, ws) * causal4).astype(BF16)
        out = dot(mixing, head_stack(vc)) + dot(ratio * come_low, wv_low)
        mixed[rows, g * GROUP : (g + 1) * GROUP] = (out * keep).astype(BF16)
        wg = wc * go_low
        kw[g] = kw[g] * carry[0:1, :] + jnp.where(blocks, dot_lt(kc, wg), 0.0)
        wv[g] = wv[g] * carry[0:1, :] + jnp.where(blocks, dot_lt(wg, vc), 0.0)
        added = jnp.sum(wg.astype(F32), axis=0, keepdims=True)
        zsum[g] = zsum[g] * carry[0:1, :] + added


def mix_backward(
    c, segc, keepc, q, k, v, w, probs, inv, score, gm, kw_all, wv_all, rg, uq, zgrad, gy
):
    rows = pl.ds(pl.multiple_of(c * CHUNK, CHUNK), CHUNK)
    causal, anti, edge = chunk_masks(c, segc)
    causal4, anti4 = four(causal), four(anti)
    anti_low = anti.astype(BF16)
    blocks = head_blocks()
    ones = jnp.where(blocks, 1.0, 0.0).astype(BF16)
    come_low = twice(edge["from_before"]).astype(BF16)
    late = twice(edge["from_after"])
    late_low = late.astype(BF16)
    back = twice(edge["to_before"])
    back_low = back.astype(BF16)
    carry = twice(edge["carry_back"])
    for g in range(2):
        qc, kc, vc, wc = q[g, rows, :], k[g, rows, :], v[g, rows, :], w[g, rows, :]
        grad = gm[g, rows, :]
        chances, inverse, scores = probs[g, rows, :], inv[g, rows, :], score[g, rows, :]
        ratio = (chances * inverse).astype(BF16)
        ws, grads, ratios = head_stack(wc), head_stack(grad), head_stack(ratio)
        d_mixing = (dot_rt(grad, head_stack(vc)) * causal4).astype(BF16)
        d_ratio = dot(d_mixing, ws) + dot_rt(grad * come_low, wv_all[c, g])
        d_chance = d_ratio * inverse
        weighted = d_chance * chances
        d_score = chances * d_chance - chances * head_sum(weighted, ones)
        d_pw = (d_score * inverse * (HEAD_DIM**-0.5)).astype(BF16)
        d_total = (weighted + d_score * scores) * inverse
        d_pairs = (dot_rt(d_pw, ws) * causal4).astype(BF16)
        gq = dot(d_pairs, head_stack(kc)) + dot_rt(d_pw * come_low, kw_all[c, g])
        rg_low, uq_low = rg[g].astype(BF16), uq[g].astype(BF16)
        d_pws = head_stack(d_pw)
        mixing_t = (dot_rt(wc, ratios) * anti4).astype(BF16)
        w_late = wc * late_low
        gv = dot(mixing_t, grads) + dot(w_late, rg_low)
        d_pairs_t = (dot_rt(wc, d_pws) * anti4).astype(BF16)
        gk = dot(d_pairs_t, head_stack(qc)) + dot(w_late, uq_low)
        d_mixing_t = (dot_rt(vc, grads) * anti4).astype(BF16)
        pairs_t = (dot_rt(kc, head_stack(qc)) * anti4).astype(BF16)
        z_high = d_total.astype(BF16)
        z_low = (d_total - z_high.astype(F32)).astype(BF16)
        dw = dot(d_mixing_t, ratios) + dot(pairs_t, d_pws)
        dw += dot_rt(vc * late_low, rg_low) + dot_rt(kc * late_low, uq_low)
        dw -= dot(anti_low, z_high) + dot(anti_low, z_low) + late * zgrad[g, 0:1, :]
        gy[g, rows, 0:256] = gq.astype(BF16)
        gy[g, rows, 256:512] = gk.astype(BF16)
        gy[g, rows, 512:768] = gv.astype(BF16)
        gy[g, rows, 768:1024] = (dw * wc.astype(F32)).astype(BF16)
        rg[g] = rg[g] * carry[0:1, :] + jnp.where(blocks, dot_lt(ratio * back_low, grad), 0.0)
        uq[g] = uq[g] * carry[0:1, :] + jnp.where(blocks, dot_lt(d_pw * back_low, qc), 0.0)
        zgrad[g] = zgrad[g] * carry[0:1, :] + jnp.sum(d_total * back, axis=0, keepdims=True)


def feed(
    r, tok, cot, gain, up_bias, down_bias, wb, keepc, mixed, n2, act, lin, xhat, gh, gb, gm, small, out
):
    rows = pl.ds(pl.multiple_of(r * TILE, TILE), TILE)
    hidden = tok[rows, :].astype(F32)
    for g in range(2):
        hidden += dot_rt(mixed[rows, g * GROUP : (g + 1) * GROUP], wb[g, :, 0:256])
    hat, scale = standardise(hidden)
    xhat[...] = hat
    normed = (hat * gain[...]).astype(BF16)
    n2[rows, :] = normed
    grad = cot[rows, :]
    k0 = 0.7978845608
    k1 = k0 * 0.044715
    total = hidden + down_bias[...]
    back = jnp.zeros((TILE, 512), F32)
    for g in range(2):
        for j in range(4):
            here = slice(j * 256, (j + 1) * 256)
            unit = g * 1024 + j * 256
            up = wb[g, :, 256 + j * 256 : 512 + j * 256]
            down = wb[g, :, 1280 + j * 256 : 1536 + j * 256]
            linear = dot(normed, up) + up_bias[:, unit : unit + 256]
            square = linear * linear
            gate = 0.5 * jnp.tanh(linear * (square * k1 + k0)) + 0.5
            active = linear * gate
            slope = gate + active * (1.0 - gate) * (square * (6.0 * k1) + 2.0 * k0)
            active_low = active.astype(BF16)
            grad_low = (dot(grad, down) * slope).astype(BF16)
            act[g, rows, here] = active_low
            lin[g, rows, here] = grad_low
            small[4:5, unit : unit + 256] += jnp.sum(grad_low.astype(F32), axis=0, keepdims=True)
    for g in range(2):
        total += dot_rt(act[g, rows, :], wb[g, :, 1280:2304])
        back += dot_rt(lin[g, rows, :], wb[g, :, 256:1280])
    out[rows, :] = total.astype(BF16)
    hat = xhat[...]
    scaled = back * gain[...]
    inner = scaled - jnp.mean(scaled, axis=-1, keepdims=True)
    inner -= hat * jnp.mean(scaled * hat, axis=-1, keepdims=True)
    grad_f32 = grad.astype(F32)
    grad_hidden = grad_f32 + scale * inner
    gh[rows, :] = grad_hidden
    low = grad_hidden.astype(BF16)
    gb[rows, :] = low
    small[0:1, 0:512] += jnp.sum(back * hat, axis=0, keepdims=True)
    small[2:3, 0:512] += jnp.sum(grad_f32, axis=0, keepdims=True)
    keep = twice(keepc[rows, :])
    for g in range(2):
        gm[g, rows, :] = (dot(low, wb[g, :, 0:256]) * keep).astype(BF16)


def transpose_into(source, target, length):
    for r in range(length // TILE):
        target[:, r * TILE : (r + 1) * TILE] = source[r * TILE : (r + 1) * TILE, :].T


def weight_grad(left_t, right, target, target_column, columns):
    def step(j, carry):
        here = pl.ds(pl.multiple_of(j * 256, 256), 256)
        there = pl.ds(pl.multiple_of(target_column + j * 256, 256), 256)
        target[:, there] = dot(left_t[...], right[:, here]).astype(BF16)
        return carry

    lax.fori_loop(0, columns // 256, step, 0)


def finish(r, tok, gain, wa, gy, gh, small, grad_out):
    rows = pl.ds(pl.multiple_of(r * TILE, TILE), TILE)
    hat, scale = standardise(tok[rows, :].astype(F32))
    back = dot_rt(gy[0, rows, :], wa[0]) + dot_rt(gy[1, rows, :], wa[1])
    scaled = back * gain[...]
    inner = scaled - jnp.mean(scaled, axis=-1, keepdims=True)
    inner -= hat * jnp.mean(scaled * hat, axis=-1, keepdims=True)
    grad_out[rows, :] = (gh[rows, :] + scale * inner).astype(BF16)
    small[1:2, 0:512] += jnp.sum(back * hat, axis=0, keepdims=True)


def layer_kernel(
    length,
    tok,
    cot,
    seg_row,
    pad_row,
    gain_one,
    gain_two,
    up_bias,
    down_bias,
    wa,
    wb,
    out,
    grad_out,
    ga,
    gw,
    small,
    segc,
    keepc,
    n1,
    q,
    k,
    v,
    w,
    probs,
    inv,
    score,
    mixed,
    kw,
    wv,
    zsum,
    kw_all,
    wv_all,
    n2,
    act,
    lin,
    xhat,
    gh,
    gb,
    gm,
    flip,
):
    chunks, tiles = length // CHUNK, length // TILE
    small[...] = jnp.zeros_like(small)
    rows_to_columns(seg_row, pad_row, segc, keepc, length)

    @pl.loop(0, tiles)
    def _(r):
        project(r, tok, gain_one, wa, keepc, n1, q, k, v, w)

    kw[...] = jnp.zeros_like(kw)
    wv[...] = jnp.zeros_like(wv)
    zsum[...] = jnp.zeros_like(zsum)

    @pl.loop(0, chunks)
    def _(c):
        mix_forward(
            c, segc, keepc, q, k, v, w, probs, inv, score, mixed, kw, wv, zsum, kw_all, wv_all
        )

    @pl.loop(0, tiles)
    def _(r):
        feed(
            r, tok, cot, gain_two, up_bias, down_bias, wb, keepc, mixed, n2, act, lin, xhat, gh, gb,
            gm, small, out,
        )

    transpose_into(cot, flip, length)
    for g in range(2):
        weight_grad(flip, act.at[g], gw.at[g], 1280, 1024)
    transpose_into(n2, flip, length)
    for g in range(2):
        weight_grad(flip, lin.at[g], gw.at[g], 256, 1024)
    transpose_into(gb, flip, length)
    for g in range(2):
        gw[g, :, 0:256] = dot(flip[...], mixed[:, g * GROUP : (g + 1) * GROUP]).astype(BF16)

    kw[...] = jnp.zeros_like(kw)
    wv[...] = jnp.zeros_like(wv)
    zsum[...] = jnp.zeros_like(zsum)

    @pl.loop(0, chunks)
    def _(i):
        mix_backward(
            chunks - 1 - i, segc, keepc, q, k, v, w, probs, inv, score, gm, kw_all, wv_all, kw, wv,
            zsum, act,
        )

    transpose_into(n1, flip, length)
    for g in range(2):
        weight_grad(flip, act.at[g], ga.at[g], 0, 1024)

    @pl.loop(0, tiles)
    def _(r):
        finish(r, tok, gain_one, wa, act, gh, small, grad_out)


def layer(tokens, cotangent, seg_row, pad_row, gain_one, gain_two, up_bias, down_bias, wa, wb):
    length, width = tokens.shape
    chunks = length // CHUNK
    shape = jax.ShapeDtypeStruct
    vmem = pltpu.VMEM
    return pl.pallas_call(
        functools.partial(layer_kernel, length),
        out_shape=(
            shape((length, width), BF16),
            shape((length, width), BF16),
            shape(wa.shape, BF16),
            shape(wb.shape, BF16),
            shape((8, 2048), F32),
        ),
        in_specs=[pl.BlockSpec(memory_space=pltpu.VMEM)] * 10,
        out_specs=tuple([pl.BlockSpec(memory_space=pltpu.VMEM)] * 5),
        scratch_shapes=[
            vmem((length + 16, 128), F32),
            vmem((length, 128), F32),
            vmem((length, width), BF16),
            vmem((2, length, GROUP), BF16),
            vmem((2, length, GROUP), BF16),
            vmem((2, length, GROUP), BF16),
            vmem((2, length, GROUP), BF16),
            vmem((2, length, GROUP), F32),
            vmem((2, length, GROUP), F32),
            vmem((2, length, GROUP), F32),
            vmem((length, width), BF16),
            vmem((2, GROUP, GROUP), F32),
            vmem((2, GROUP, GROUP), F32),
            vmem((2, 8, GROUP), F32),
            vmem((chunks, 2, GROUP, GROUP), BF16),
            vmem((chunks, 2, GROUP, GROUP), BF16),
            vmem((length, width), BF16),
            vmem((2, length, 1024), BF16),
            vmem((2, length, 1024), BF16),
            vmem((TILE, width), F32),
            vmem((length, width), F32),
            vmem((length, width), BF16),
            vmem((2, length, GROUP), BF16),
            vmem((width, length), BF16),
        ],
        compiler_params=pltpu.CompilerParams(vmem_limit_bytes=60 * 1024 * 1024),
        name="layer",
    )(tokens, cotangent, seg_row, pad_row, gain_one, gain_two, up_bias, down_bias, wa, wb)


class Place:
    def __init__(self, depth):
        index = lax.axis_index("dp")
        self.depth = depth
        self.x = lax.rem(index, 2)
        self.y = lax.rem(index // 2, 2)
        self.z = index // 4
        self.t = lax.axis_index("tensor")

    def chip(self, z, y, x):
        return {"dp": (z * 2 + y) * 2 + x}

    def above(self, step):
        return lax.rem(self.z + step, self.depth)

    def x_side(self):
        return self.chip(self.z, self.y, 1 - self.x)

    def y_side(self):
        return self.chip(self.z, 1 - self.y, self.x)

    def core(self):
        return {"tensor": 1 - self.t}

    def friends(self):
        others = [self.chip(self.above(s), self.y, self.x) for s in range(1, self.depth)]
        return [self.core(), self.x_side(), self.y_side()] + others

    def greet(self):
        barrier = pltpu.get_barrier_semaphore()
        friends = self.friends()
        for friend in friends:
            pl.semaphore_signal(barrier, inc=1, device_id=friend, device_id_type=MESH)
        pl.semaphore_wait(barrier, len(friends))


def send(source, target, sems, number, device):
    copy = pltpu.make_async_remote_copy(
        src_ref=source,
        dst_ref=target,
        send_sem=sems.at[0, number],
        recv_sem=sems.at[1, number],
        device_id=device,
        device_id_type=MESH,
    )
    copy.start()
    return copy


class Gather:
    COPIES = 16

    def __init__(self, place, full, sems):
        self.p, self.full, self.sems = place, full, sems
        self.copies = []
        self.count = 0

    def push(self, index, device):
        part = self.full.at[index]
        copy = send(part, part, self.sems, self.count, device)
        self.count += 1
        self.copies.append(copy)
        return copy

    def first(self):
        p = self.p
        own = (p.t, p.z, p.y, p.x)
        self.along_z = [self.push(own, p.chip(p.above(s), p.y, p.x)) for s in range(1, p.depth)]

    def second(self):
        p = self.p
        for copy in self.along_z:
            copy.wait_recv()
        every = slice(None)
        self.one = [
            self.push((p.t, every, p.y, p.x, 0), p.x_side()),
            self.push((p.t, every, p.y, p.x, 1), p.y_side()),
        ]
        self.pair = [self.push((p.t, every, p.y, p.x), p.core())]

    def third(self):
        p = self.p
        every = slice(None)
        self.one[0].wait_recv()
        self.two = [self.push((p.t, every, p.y, every, 0), p.y_side())]
        self.one[1].wait_recv()
        self.two += [self.push((p.t, every, every, p.x, 1), p.x_side())]
        self.pair += [
            self.push((p.t, every, p.y, 1 - p.x, 0), p.core()),
            self.push((p.t, every, 1 - p.y, p.x, 1), p.core()),
        ]

    def fourth(self):
        p = self.p
        every = slice(None)
        self.two[0].wait_recv()
        self.pair += [self.push((p.t, every, 1 - p.y, every, 0), p.core())]
        self.two[1].wait_recv()
        self.pair += [self.push((p.t, every, every, 1 - p.x, 1), p.core())]

    def last(self):
        for copy in self.pair:
            copy.wait_recv()
        for copy in self.copies:
            copy.wait_send()


def gather_kernel(depth, own_a, own_b, full_a, full_b, sems_a, sems_b):
    place = Place(depth)
    mine = (place.t, place.z, place.y, place.x)
    full_a[mine] = own_a[...]
    full_b[mine] = own_b[...]
    place.greet()
    one, two = Gather(place, full_a, sems_a), Gather(place, full_b, sems_b)
    one.first()
    two.first()
    one.second()
    two.second()
    one.third()
    two.third()
    one.fourth()
    two.fourth()
    one.last()
    two.last()


def gather(depth, own_a, own_b):
    shape = jax.ShapeDtypeStruct
    halves = lambda own: own.reshape(2, 16, own.shape[1])
    full = lambda own: shape((2, depth, 2, 2, 2, 16, own.shape[1]), BF16)
    full_a, full_b = pl.pallas_call(
        functools.partial(gather_kernel, depth),
        out_shape=(full(own_a), full(own_b)),
        in_specs=[pl.BlockSpec(memory_space=pltpu.VMEM)] * 2,
        out_specs=tuple([pl.BlockSpec(memory_space=pltpu.VMEM)] * 2),
        scratch_shapes=[pltpu.SemaphoreType.DMA((2, Gather.COPIES))] * 2,
        compiler_params=pltpu.CompilerParams(
            collective_id=0, has_side_effects=True, vmem_limit_bytes=32 * 1024 * 1024
        ),
        name="gather",
    )(halves(own_a), halves(own_b))
    flat = lambda full: full.reshape(2, -1, full.shape[-1])
    return flat(full_a), flat(full_b)


class Scatter:
    COPIES = 16

    def __init__(self, place, part, pair_in, one_in, two_in, last_in, sems):
        self.p, self.part, self.sems = place, part, sems
        self.pair_in, self.one_in, self.two_in, self.last_in = pair_in, one_in, two_in, last_in
        self.count = 0
        self.copies = []

    def push(self, source, target, device):
        copy = send(source, target, self.sems, self.count, device)
        self.count += 1
        self.copies.append(copy)
        return copy

    def add(self, index, landed):
        mine = self.part[index].astype(F32)
        self.part[index] = (mine + landed.astype(F32)).astype(BF16)

    def first(self):
        p = self.p
        self.pair = self.push(self.part.at[1 - p.t], self.pair_in, p.core())

    def second(self):
        p = self.p
        self.pair.wait_recv()
        every = slice(None)
        for z in range(p.depth):
            for y in range(2):
                for x in range(2):
                    self.add((p.t, z, y, x), self.pair_in[z, y, x])
        self.one = [
            self.push(self.part.at[p.t, every, 1 - p.y, every, 0], self.one_in.at[0], p.y_side()),
            self.push(self.part.at[p.t, every, every, 1 - p.x, 1], self.one_in.at[1], p.x_side()),
        ]

    def third(self):
        p = self.p
        every = slice(None)
        self.one[0].wait_recv()
        for z in range(p.depth):
            for x in range(2):
                self.add((p.t, z, p.y, x, 0), self.one_in[0, z, x])
        self.one[1].wait_recv()
        for z in range(p.depth):
            for y in range(2):
                self.add((p.t, z, y, p.x, 1), self.one_in[1, z, y])
        self.two = [
            self.push(self.part.at[p.t, every, p.y, 1 - p.x, 0], self.two_in.at[0], p.x_side()),
            self.push(self.part.at[p.t, every, 1 - p.y, p.x, 1], self.two_in.at[1], p.y_side()),
        ]

    def fourth(self):
        p = self.p
        for half in range(2):
            self.two[half].wait_recv()
            for z in range(p.depth):
                self.add((p.t, z, p.y, p.x, half), self.two_in[half, z])
        self.along_z = []
        for s in range(1, p.depth):
            z = p.above(s)
            self.along_z.append(
                self.push(
                    self.part.at[p.t, z, p.y, p.x], self.last_in.at[s - 1], p.chip(z, p.y, p.x)
                )
            )

    def last(self):
        p = self.p
        for copy in self.along_z:
            copy.wait_recv()
        total = self.part[p.t, p.z, p.y, p.x].astype(F32)
        for s in range(1, p.depth):
            total += self.last_in[s - 1].astype(F32)
        for copy in self.copies:
            copy.wait_send()
        return total


def scatter_buffers(depth, columns):
    vmem = pltpu.VMEM
    return [
        vmem((depth, 2, 2, 2, 16, columns), BF16),
        vmem((2, depth, 2, 16, columns), BF16),
        vmem((2, depth, 16, columns), BF16),
        vmem((depth - 1, 2, 16, columns), BF16),
        pltpu.SemaphoreType.DMA((2, Scatter.COPIES)),
    ]


class Reduce:
    COPIES = 8

    def __init__(self, place, total, landing, sems):
        self.p, self.total, self.landing, self.sems = place, total, landing, sems
        self.count = 0

    def swap(self, devices):
        copies = []
        for device in devices:
            n = self.count
            copies.append(send(self.total, self.landing.at[n], self.sems, n, device))
            self.count += 1
        return copies

    def step(self, device):
        n = self.count
        (copy,) = self.swap([device])
        copy.wait()
        self.total[...] += self.landing[n]

    def along_z(self):
        p = self.p
        first = self.count
        copies = self.swap([p.chip(p.above(s), p.y, p.x) for s in range(1, p.depth)])
        for copy in copies:
            copy.wait()
        own = self.total[...]
        total = jnp.zeros_like(own)
        for z in range(p.depth):
            part = jnp.where(p.z == z, own, 0.0)
            for s in range(1, p.depth):
                came = lax.rem(p.z + p.depth - s, p.depth)
                part = jnp.where(came == z, self.landing[first + s - 1], part)
            total += part
        self.total[...] = total


def scatter_kernel(depth, ga, gw, small_in, da, dw, small, *scratch):
    place = Place(depth)
    part_a, part_w = scratch[0], scratch[1]
    one = Scatter(place, part_a, *scratch[2:7])
    two = Scatter(place, part_w, *scratch[7:12])
    landing, sems = scratch[12], scratch[13]
    part_w[...] = gw[...]
    part_a[...] = ga[...]
    small[...] = small_in[...]
    place.greet()
    gains = Reduce(place, small, landing, sems)
    two.first()
    one.first()
    gains.step(place.core())
    two.second()
    one.second()
    gains.step(place.x_side())
    two.third()
    one.third()
    gains.step(place.y_side())
    two.fourth()
    one.fourth()
    gains.along_z()
    dw[...] = two.last()
    da[...] = one.last()


def scatter(depth, ga, gw, small):
    shape = jax.ShapeDtypeStruct
    full = lambda part: part.reshape(2, depth, 2, 2, 2, 16, part.shape[-1])
    columns_a, columns_w = ga.shape[-1], gw.shape[-1]
    da, dw, small = pl.pallas_call(
        functools.partial(scatter_kernel, depth),
        out_shape=(
            shape((2, 16, columns_a), F32),
            shape((2, 16, columns_w), F32),
            shape(small.shape, F32),
        ),
        in_specs=[pl.BlockSpec(memory_space=pltpu.VMEM)] * 3,
        out_specs=tuple([pl.BlockSpec(memory_space=pltpu.VMEM)] * 3),
        scratch_shapes=[
            pltpu.VMEM((2, depth, 2, 2, 2, 16, columns_a), BF16),
            pltpu.VMEM((2, depth, 2, 2, 2, 16, columns_w), BF16),
        ]
        + scatter_buffers(depth, columns_a)
        + scatter_buffers(depth, columns_w)
        + [
            pltpu.VMEM((Reduce.COPIES,) + small.shape, F32),
            pltpu.SemaphoreType.DMA((2, Reduce.COPIES)),
        ],
        compiler_params=pltpu.CompilerParams(
            collective_id=1, has_side_effects=True, vmem_limit_bytes=60 * 1024 * 1024
        ),
        name="scatter",
    )(full(ga), full(gw), small)
    return da.reshape(32, columns_a), dw.reshape(32, columns_w), small


def per_device(
    direct,
    tokens,
    segment_ids,
    padding,
    mixer_gain,
    query_weight,
    key_weight,
    value_weight,
    slot_weight,
    out_weight,
    feed_gain,
    up_weight,
    up_bias,
    down_weight,
    down_bias,
    cotangent,
):
    own_a = jnp.concatenate([query_weight, key_weight, value_weight, slot_weight], 1).astype(BF16)
    own_b = jnp.concatenate([out_weight.T, up_weight, down_weight.T], 1).astype(BF16)
    depth = lax.axis_size("dp") // 4
    if direct:
        wa, wb = gather(depth, own_a, own_b)
    else:
        wa, wb = (
            lax.all_gather(lax.all_gather(own, "dp", axis=0, tiled=True), "tensor")
            for own in (own_a, own_b)
        )
    half = lax.axis_index("tensor")
    pick = lambda rows: lax.dynamic_slice_in_dim(rows, half, 1, 0)
    out, grad_out, ga, gw, small = layer(
        tokens,
        cotangent,
        pick(segment_ids),
        pick(padding),
        mixer_gain[None],
        feed_gain[None],
        up_bias[None],
        down_bias[None],
        wa,
        wb,
    )
    if direct:
        da, dw, small = scatter(depth, ga, gw, small)
    else:
        da, dw = (
            lax.psum_scatter(
                lax.psum_scatter(part.astype(F32), "tensor", scatter_dimension=0),
                "dp",
                scatter_dimension=0,
                tiled=True,
            )
            for part in (ga, gw)
        )
        small = lax.psum(small, ("dp", "tensor"))
    width = mixer_gain.shape[0]
    return (
        out,
        grad_out,
        small[1, :width],
        da[:, 0:256],
        da[:, 256:512],
        da[:, 512:768],
        da[:, 768:1024],
        dw[:, 0:256].T,
        small[0, :width],
        dw[:, 256:1280],
        small[4],
        dw[:, 1280:2304].T,
        small[2, :width],
    )


def solution(mesh):
    in_specs = (
        P(("dp", "tensor"), None),
        P("dp", None),
        P("dp", None),
        P(),
        P("dp", "tensor"),
        P("dp", "tensor"),
        P("dp", "tensor"),
        P("dp", "tensor"),
        P("tensor", "dp"),
        P(),
        P("dp", "tensor"),
        P(),
        P("tensor", "dp"),
        P(),
        P(("dp", "tensor"), None),
    )
    out_specs = (
        P(("dp", "tensor"), None),
        P(("dp", "tensor"), None),
        P(),
        P("dp", "tensor"),
        P("dp", "tensor"),
        P("dp", "tensor"),
        P("dp", "tensor"),
        P("tensor", "dp"),
        P(),
        P("dp", "tensor"),
        P(),
        P("tensor", "dp"),
        P(),
    )
    direct = mesh.shape["dp"] == 16 and mesh.shape["tensor"] == 2
    return jax.shard_map(
        functools.partial(per_device, direct),
        mesh=mesh,
        in_specs=in_specs,
        out_specs=out_specs,
        check_vma=False,
    )
```

```python
import functools
import math

import jax
import jax.numpy as jnp
from jax import lax
from jax.experimental import pallas as pl
from jax.experimental.pallas import tpu as pltpu
from jax.sharding import PartitionSpec as P

HEAD_DIM = 64
SLOTS = 64
CHUNK = 128
GROUP = 256
TILE = 256

F32 = jnp.float32
BF16 = jnp.bfloat16
MESH = pl.DeviceIdType.MESH


def dot(left, right):
    return lax.dot_general(left, right, (((1,), (0,)), ((), ())), preferred_element_type=F32)


def dot_rt(left, right):
    return lax.dot_general(left, right, (((1,), (1,)), ((), ())), preferred_element_type=F32)


def dot_lt(left, right):
    return lax.dot_general(left, right, (((0,), (0,)), ((), ())), preferred_element_type=F32)


def twice(block):
    return jnp.concatenate([block, block], axis=1)


def four(block):
    return jnp.concatenate([block, block, block, block], axis=1)


def standardise(rows):
    centred = rows - jnp.mean(rows, axis=-1, keepdims=True)
    scale = lax.rsqrt(jnp.mean(centred * centred, axis=-1, keepdims=True) + 1e-05)
    return centred * scale, scale


def head_stack(block):
    lane = lax.broadcasted_iota(jnp.int32, block.shape, 1) // HEAD_DIM
    zero = jnp.zeros_like(block)
    return jnp.concatenate([jnp.where(lane == h, block, zero) for h in range(4)], axis=0)


def head_blocks():
    row = lax.broadcasted_iota(jnp.int32, (GROUP, GROUP), 0) // HEAD_DIM
    column = lax.broadcasted_iota(jnp.int32, (GROUP, GROUP), 1) // HEAD_DIM
    return row == column


def head_sum(block, ones):
    high = block.astype(BF16)
    low = (block - high.astype(F32)).astype(BF16)
    return dot(high, ones) + dot(low, ones)


def head_max(block):
    halves = []
    lane = lax.broadcasted_iota(jnp.int32, (block.shape[0], 128), 1) < HEAD_DIM
    for j in range(block.shape[1] // 128):
        part = block[:, j * 128 : (j + 1) * 128]
        first = jnp.max(jnp.where(lane, part, -jnp.inf), axis=1, keepdims=True)
        second = jnp.max(jnp.where(lane, -jnp.inf, part), axis=1, keepdims=True)
        halves.append(jnp.where(lane, first, second))
    return jnp.concatenate(halves, axis=1)


def flat(block):
    return block.reshape(-1, block.shape[-1])


def rows_to_columns(seg_row, pad_row, segc, keepc, length):
    segc[pl.ds(0, 8), :] = jnp.full((8, 128), -1.0, F32)
    segc[pl.ds(8 + length, 8), :] = jnp.full((8, 128), -2.0, F32)
    for c in range(length // CHUNK):
        here = slice(c * CHUNK, (c + 1) * CHUNK)
        seg = jnp.broadcast_to(seg_row[:, here].astype(F32), (CHUNK, CHUNK))
        pad = jnp.broadcast_to(pad_row[:, here].astype(F32), (CHUNK, CHUNK))
        segc[pl.ds(8 + c * CHUNK, CHUNK), :] = seg.T
        keepc[pl.ds(c * CHUNK, CHUNK), :] = 1.0 - pad.T


def normalise(r, tok, gain, n1):
    rows = pl.ds(pl.multiple_of(r * TILE, TILE), TILE)
    xhat, _ = standardise(tok[rows, :].astype(F32))
    n1[rows, :] = (xhat * gain[...]).astype(BF16)


def project(r, wa, keepc, n1, q, k, v, w):
    rows = pl.ds(pl.multiple_of(r * TILE, TILE), TILE)
    normed = n1[rows, :]
    keep = twice(keepc[rows, :])
    for g in range(2):
        out = dot(normed, flat(wa[g]))
        q[g, rows, :] = out[:, 0:256].astype(BF16)
        k[g, rows, :] = out[:, 256:512].astype(BF16)
        v[g, rows, :] = out[:, 512:768].astype(BF16)
        w[g, rows, :] = (jnp.exp(out[:, 768:1024]) * keep).astype(BF16)


def chunk_masks(c, segc):
    base = pl.multiple_of(c * CHUNK, CHUNK)
    seg = segc[pl.ds(base + 8, CHUNK), :]
    across = seg.T
    row = lax.broadcasted_iota(jnp.int32, (CHUNK, CHUNK), 0)
    column = lax.broadcasted_iota(jnp.int32, (CHUNK, CHUNK), 1)
    same = seg == across
    causal = jnp.where(same & (column <= row), 1.0, 0.0)
    anti = jnp.where(same & (row <= column), 1.0, 0.0)
    before = segc[pl.ds(base + 7, 1), :]
    first = segc[pl.ds(base + 8, 1), :]
    last = segc[pl.ds(base + 7 + CHUNK, 1), :]
    after = segc[pl.ds(base + 8 + CHUNK, 1), :]
    one = lambda test: jnp.where(test, 1.0, 0.0)
    return causal, anti, dict(
        from_before=one(seg == before),
        to_after=one(seg == last),
        from_after=one(seg == after),
        to_before=one(seg == first),
        carry_on=one(before == last),
        carry_back=one(after == first),
    )


def mix_forward(c, segc, keepc, q, k, v, w, probs, inv, score, mixed, kw, wv, zsum, kw_all, wv_all):
    rows = pl.ds(pl.multiple_of(c * CHUNK, CHUNK), CHUNK)
    causal, _, edge = chunk_masks(c, segc)
    causal4 = four(causal)
    causal_low = causal.astype(BF16)
    blocks = head_blocks()
    ones = jnp.where(blocks, 1.0, 0.0).astype(BF16)
    keep = twice(keepc[rows, :])
    come = twice(edge["from_before"])
    come_low = come.astype(BF16)
    go_low = twice(edge["to_after"]).astype(BF16)
    carry = twice(edge["carry_on"])
    for g in range(2):
        qc, kc, vc, wc = q[g, rows, :], k[g, rows, :], v[g, rows, :], w[g, rows, :]
        kw_low, wv_low = kw[g].astype(BF16), wv[g].astype(BF16)
        kw_all[c, g] = kw_low
        wv_all[c, g] = wv_low
        ws = head_stack(wc)
        pairs = (dot_rt(qc, head_stack(kc)) * causal4).astype(BF16)
        total = dot(causal_low, wc) + come * zsum[g, 0:1, :] + (1.0 - keep)
        inverse = 1.0 / total
        scores = (dot(pairs, ws) + dot(qc * come_low, kw_low)) * (inverse * (HEAD_DIM**-0.5))
        powers = jnp.exp(scores - head_max(scores))
        chances = powers / head_sum(powers, ones)
        ratio = (chances * inverse).astype(BF16)
        probs[g, rows, :] = chances
        inv[g, rows, :] = inverse
        score[g, rows, :] = scores
        mixing = (dot_rt(ratio, ws) * causal4).astype(BF16)
        out = dot(mixing, head_stack(vc)) + dot(ratio * come_low, wv_low)
        mixed[rows, g * GROUP : (g + 1) * GROUP] = (out * keep).astype(BF16)
        wg = wc * go_low
        kw[g] = kw[g] * carry[0:1, :] + jnp.where(blocks, dot_lt(kc, wg), 0.0)
        wv[g] = wv[g] * carry[0:1, :] + jnp.where(blocks, dot_lt(wg, vc), 0.0)
        added = jnp.sum(wg.astype(F32), axis=0, keepdims=True)
        zsum[g] = zsum[g] * carry[0:1, :] + added


def mix_backward(
    c, segc, keepc, q, k, v, w, probs, inv, score, gm, kw_all, wv_all, rg, uq, zgrad, gy
):
    rows = pl.ds(pl.multiple_of(c * CHUNK, CHUNK), CHUNK)
    causal, anti, edge = chunk_masks(c, segc)
    causal4, anti4 = four(causal), four(anti)
    anti_low = anti.astype(BF16)
    blocks = head_blocks()
    ones = jnp.where(blocks, 1.0, 0.0).astype(BF16)
    come_low = twice(edge["from_before"]).astype(BF16)
    late = twice(edge["from_after"])
    late_low = late.astype(BF16)
    back = twice(edge["to_before"])
    back_low = back.astype(BF16)
    carry = twice(edge["carry_back"])
    for g in range(2):
        qc, kc, vc, wc = q[g, rows, :], k[g, rows, :], v[g, rows, :], w[g, rows, :]
        grad = gm[g, rows, :]
        chances, inverse, scores = probs[g, rows, :], inv[g, rows, :], score[g, rows, :]
        ratio = (chances * inverse).astype(BF16)
        ws, grads, ratios = head_stack(wc), head_stack(grad), head_stack(ratio)
        d_mixing = (dot_rt(grad, head_stack(vc)) * causal4).astype(BF16)
        d_ratio = dot(d_mixing, ws) + dot_rt(grad * come_low, wv_all[c, g])
        d_chance = d_ratio * inverse
        weighted = d_chance * chances
        d_score = chances * d_chance - chances * head_sum(weighted, ones)
        d_pw = (d_score * inverse * (HEAD_DIM**-0.5)).astype(BF16)
        d_total = (weighted + d_score * scores) * inverse
        d_pairs = (dot_rt(d_pw, ws) * causal4).astype(BF16)
        gq = dot(d_pairs, head_stack(kc)) + dot_rt(d_pw * come_low, kw_all[c, g])
        rg_low, uq_low = rg[g].astype(BF16), uq[g].astype(BF16)
        d_pws = head_stack(d_pw)
        mixing_t = (dot_rt(wc, ratios) * anti4).astype(BF16)
        w_late = wc * late_low
        gv = dot(mixing_t, grads) + dot(w_late, rg_low)
        d_pairs_t = (dot_rt(wc, d_pws) * anti4).astype(BF16)
        gk = dot(d_pairs_t, head_stack(qc)) + dot(w_late, uq_low)
        d_mixing_t = (dot_rt(vc, grads) * anti4).astype(BF16)
        pairs_t = (dot_rt(kc, head_stack(qc)) * anti4).astype(BF16)
        z_high = d_total.astype(BF16)
        z_low = (d_total - z_high.astype(F32)).astype(BF16)
        dw = dot(d_mixing_t, ratios) + dot(pairs_t, d_pws)
        dw += dot_rt(vc * late_low, rg_low) + dot_rt(kc * late_low, uq_low)
        dw -= dot(anti_low, z_high) + dot(anti_low, z_low) + late * zgrad[g, 0:1, :]
        gy[g, rows, 0:256] = gq.astype(BF16)
        gy[g, rows, 256:512] = gk.astype(BF16)
        gy[g, rows, 512:768] = gv.astype(BF16)
        gy[g, rows, 768:1024] = (dw * wc.astype(F32)).astype(BF16)
        rg[g] = rg[g] * carry[0:1, :] + jnp.where(blocks, dot_lt(ratio * back_low, grad), 0.0)
        uq[g] = uq[g] * carry[0:1, :] + jnp.where(blocks, dot_lt(d_pw * back_low, qc), 0.0)
        zgrad[g] = zgrad[g] * carry[0:1, :] + jnp.sum(d_total * back, axis=0, keepdims=True)


def feed(
    r, tok, cot, gain, up_bias, down_bias, wb, keepc, mixed, n2, act, lin, xhat, gh, gb, gm, small, out
):
    rows = pl.ds(pl.multiple_of(r * TILE, TILE), TILE)
    hidden = tok[rows, :].astype(F32)
    for g in range(2):
        hidden += dot_rt(mixed[rows, g * GROUP : (g + 1) * GROUP], flat(wb[g, ..., 0:256]))
    hat, scale = standardise(hidden)
    xhat[...] = hat
    normed = (hat * gain[...]).astype(BF16)
    n2[rows, :] = normed
    grad = cot[rows, :]
    k0 = 0.7978845608
    k1 = k0 * 0.044715
    total = hidden + down_bias[...]
    back = jnp.zeros((TILE, 512), F32)
    for g in range(2):
        for j in range(4):
            here = slice(j * 256, (j + 1) * 256)
            unit = g * 1024 + j * 256
            up = flat(wb[g, ..., 256 + j * 256 : 512 + j * 256])
            down = flat(wb[g, ..., 1280 + j * 256 : 1536 + j * 256])
            linear = dot(normed, up) + up_bias[:, unit : unit + 256]
            square = linear * linear
            gate = 0.5 * jnp.tanh(linear * (square * k1 + k0)) + 0.5
            active = linear * gate
            slope = gate + active * (1.0 - gate) * (square * (6.0 * k1) + 2.0 * k0)
            active_low = active.astype(BF16)
            grad_low = (dot(grad, down) * slope).astype(BF16)
            act[g, rows, here] = active_low
            lin[g, rows, here] = grad_low
            row, column = 4 + unit // 512, unit % 512
            small[row : row + 1, column : column + 256] += jnp.sum(
                grad_low.astype(F32), axis=0, keepdims=True
            )
    for g in range(2):
        total += dot_rt(act[g, rows, :], flat(wb[g, ..., 1280:2304]))
        back += dot_rt(lin[g, rows, :], flat(wb[g, ..., 256:1280]))
    out[rows, :] = total.astype(BF16)
    hat = xhat[...]
    scaled = back * gain[...]
    inner = scaled - jnp.mean(scaled, axis=-1, keepdims=True)
    inner -= hat * jnp.mean(scaled * hat, axis=-1, keepdims=True)
    grad_f32 = grad.astype(F32)
    grad_hidden = grad_f32 + scale * inner
    gh[rows, :] = grad_hidden
    low = grad_hidden.astype(BF16)
    gb[rows, :] = low
    small[0:1, :] += jnp.sum(back * hat, axis=0, keepdims=True)
    small[2:3, :] += jnp.sum(grad_f32, axis=0, keepdims=True)
    keep = twice(keepc[rows, :])
    for g in range(2):
        gm[g, rows, :] = (dot(low, flat(wb[g, ..., 0:256])) * keep).astype(BF16)


def transpose_into(source, target, length):
    for r in range(length // TILE):
        target[:, r * TILE : (r + 1) * TILE] = source[r * TILE : (r + 1) * TILE, :].T


def weight_grad(left_t, right, target, g, target_column, columns):
    shape = target.shape[1:-1] + (256,)

    def step(j, carry):
        here = pl.ds(pl.multiple_of(j * 256, 256), 256)
        there = pl.ds(pl.multiple_of(target_column + j * 256, 256), 256)
        target[g, ..., there] = dot(left_t[...], right[:, here]).astype(BF16).reshape(shape)
        return carry

    lax.fori_loop(0, columns // 256, step, 0)


def finish(r, tok, gain, wa, gy, gh, small, grad_out):
    rows = pl.ds(pl.multiple_of(r * TILE, TILE), TILE)
    hat, scale = standardise(tok[rows, :].astype(F32))
    back = dot_rt(gy[0, rows, :], flat(wa[0])) + dot_rt(gy[1, rows, :], flat(wa[1]))
    scaled = back * gain[...]
    inner = scaled - jnp.mean(scaled, axis=-1, keepdims=True)
    inner -= hat * jnp.mean(scaled * hat, axis=-1, keepdims=True)
    grad_out[rows, :] = (gh[rows, :] + scale * inner).astype(BF16)
    small[1:2, :] += jnp.sum(back * hat, axis=0, keepdims=True)


class Quiet:
    def before(self):
        pass

    def weights_a(self):
        pass

    def mixing(self, c):
        pass

    def weights_b(self):
        pass

    def grads_w(self, which):
        pass

    def mixing_back(self, i):
        pass

    def grads_a(self):
        pass

    def after(self):
        pass


LAYER_INPUTS = 8
LAYER_SCRATCH = 24


def layer_body(
    length,
    comm,
    tok,
    cot,
    seg_row,
    pad_row,
    gain_one,
    gain_two,
    up_bias,
    down_bias,
    wa,
    wb,
    out,
    grad_out,
    ga,
    gw,
    small,
    segc,
    keepc,
    n1,
    q,
    k,
    v,
    w,
    probs,
    inv,
    score,
    mixed,
    kw,
    wv,
    zsum,
    kw_all,
    wv_all,
    n2,
    act,
    lin,
    xhat,
    gh,
    gb,
    gm,
    flip,
):
    chunks, tiles = length // CHUNK, length // TILE
    comm.before()
    small[...] = jnp.zeros_like(small)
    rows_to_columns(seg_row, pad_row, segc, keepc, length)

    @pl.loop(0, tiles)
    def _(r):
        normalise(r, tok, gain_one, n1)

    kw[...] = jnp.zeros_like(kw)
    wv[...] = jnp.zeros_like(wv)
    zsum[...] = jnp.zeros_like(zsum)
    comm.weights_a()

    @pl.loop(0, tiles)
    def _(r):
        project(r, wa, keepc, n1, q, k, v, w)

    @pl.loop(0, chunks)
    def _(c):
        comm.mixing(c)
        mix_forward(
            c, segc, keepc, q, k, v, w, probs, inv, score, mixed, kw, wv, zsum, kw_all, wv_all
        )

    comm.weights_b()

    @pl.loop(0, tiles)
    def _(r):
        feed(
            r, tok, cot, gain_two, up_bias, down_bias, wb, keepc, mixed, n2, act, lin, xhat, gh, gb,
            gm, small, out,
        )

    transpose_into(cot, flip, length)
    for g in range(2):
        weight_grad(flip, act.at[g], gw, g, 1280, 1024)
    comm.grads_w(0)
    transpose_into(n2, flip, length)
    for g in range(2):
        weight_grad(flip, lin.at[g], gw, g, 256, 1024)
    transpose_into(gb, flip, length)
    for g in range(2):
        weight_grad(flip, mixed.at[:, g * GROUP : (g + 1) * GROUP], gw, g, 0, GROUP)
    comm.grads_w(1)

    kw[...] = jnp.zeros_like(kw)
    wv[...] = jnp.zeros_like(wv)
    zsum[...] = jnp.zeros_like(zsum)

    @pl.loop(0, chunks)
    def _(i):
        comm.mixing_back(i)
        mix_backward(
            chunks - 1 - i, segc, keepc, q, k, v, w, probs, inv, score, gm, kw_all, wv_all, kw, wv,
            zsum, act,
        )

    transpose_into(n1, flip, length)
    for g in range(2):
        weight_grad(flip, act.at[g], ga, g, 0, 1024)
    comm.grads_a()

    @pl.loop(0, tiles)
    def _(r):
        finish(r, tok, gain_one, wa, act, gh, small, grad_out)

    comm.after()


def layer_scratch(length, width):
    vmem = pltpu.VMEM
    chunks = length // CHUNK
    return [
        vmem((length + 16, 128), F32),
        vmem((length, 128), F32),
        vmem((length, width), BF16),
        vmem((2, length, GROUP), BF16),
        vmem((2, length, GROUP), BF16),
        vmem((2, length, GROUP), BF16),
        vmem((2, length, GROUP), BF16),
        vmem((2, length, GROUP), F32),
        vmem((2, length, GROUP), F32),
        vmem((2, length, GROUP), F32),
        vmem((length, width), BF16),
        vmem((2, GROUP, GROUP), F32),
        vmem((2, GROUP, GROUP), F32),
        vmem((2, 8, GROUP), F32),
        vmem((chunks, 2, GROUP, GROUP), BF16),
        vmem((chunks, 2, GROUP, GROUP), BF16),
        vmem((length, width), BF16),
        vmem((2, length, 1024), BF16),
        vmem((2, length, 1024), BF16),
        vmem((TILE, width), F32),
        vmem((length, width), F32),
        vmem((length, width), BF16),
        vmem((2, length, GROUP), BF16),
        vmem((width, length), BF16),
    ]


def layer_kernel(length, *refs):
    layer_body(length, Quiet(), *refs)


def layer(tokens, cotangent, seg_row, pad_row, gain_one, gain_two, up_bias, down_bias, wa, wb):
    length, width = tokens.shape
    shape = jax.ShapeDtypeStruct
    cut = lambda full: full.reshape(2, -1, 2, 2, 2, 16, full.shape[-1])
    wa, wb = cut(wa), cut(wb)
    space = pl.BlockSpec(memory_space=pltpu.VMEM)
    out, grad_out, ga, gw, small = pl.pallas_call(
        functools.partial(layer_kernel, length),
        out_shape=(
            shape((length, width), BF16),
            shape((length, width), BF16),
            shape(wa.shape, BF16),
            shape(wb.shape, BF16),
            shape((8, width), F32),
        ),
        in_specs=[space] * 10,
        out_specs=tuple([space] * 5),
        scratch_shapes=layer_scratch(length, width),
        compiler_params=pltpu.CompilerParams(vmem_limit_bytes=60 * 1024 * 1024),
        name="layer",
    )(tokens, cotangent, seg_row, pad_row, gain_one, gain_two, up_bias, down_bias, wa, wb)
    whole = lambda full: full.reshape(2, width, full.shape[-1])
    return out, grad_out, whole(ga), whole(gw), small


class Place:
    def __init__(self, depth):
        index = lax.axis_index("dp")
        t = lax.axis_index("tensor")
        x, y, z = lax.rem(index, 2), lax.rem(index // 2, 2), index // 4
        self.depth = depth
        self.x, self.y, self.z, self.t, self.other = x, y, z, t, 1 - t
        self.near = (y + t * (1 - 2 * y), x + (1 - t) * (1 - 2 * x))
        self.next = (y + (1 - t) * (1 - 2 * y), x + t * (1 - 2 * x))
        self.far = (1 - y, 1 - x)
        chip = lambda z, y, x: (z * 2 + y) * 2 + x
        self.levels = [lax.rem(z + s, depth) for s in range(depth)]
        self.chips_z = [chip(level, y, x) for level in self.levels]
        self.to_near = {"dp": chip(z, *self.near)}
        self.to_next = {"dp": chip(z, *self.next)}
        self.to_pair = {"tensor": self.other}
        self.to_x = {"dp": chip(z, y, 1 - x)}
        self.to_y = {"dp": chip(z, 1 - y, x)}

    def along_z(self, step, core):
        return {"dp": self.chips_z[step], "tensor": core}

    def greet(self):
        barrier = pltpu.get_barrier_semaphore()
        friends = [self.to_pair, self.to_x, self.to_y]
        friends += [self.along_z(s, core) for s in range(1, self.depth) for core in range(2)]
        for friend in friends:
            pl.semaphore_signal(barrier, inc=1, device_id=friend, device_id_type=MESH)
        pl.semaphore_wait(barrier, len(friends))


class Copies:
    def __init__(self, sems):
        self.sems = sems
        self.started = []

    def build(self, source, target, device, out_sem, in_sem):
        return pltpu.make_async_remote_copy(
            src_ref=source,
            dst_ref=target,
            send_sem=self.sems.at[0, out_sem],
            recv_sem=self.sems.at[1, in_sem],
            device_id=device,
            device_id_type=MESH,
        )

    def start(self, source, target, device, number, in_sem=None):
        copy = self.build(source(), target, device, number, number if in_sem is None else in_sem)
        copy.start()
        self.started.append((source, number))

    def landed(self, target, number):
        self.build(target, target, {"tensor": 0}, number, number).wait_recv()

    def left(self):
        for source, number in self.started:
            part = source()
            self.build(part, part, {"tensor": 0}, number, number).wait_send()


class Gather(Copies):
    COPIES = 14

    def __init__(self, place, own, full, columns, sems):
        super().__init__(sems)
        self.p, self.own, self.full, self.columns = place, own, full, columns

    def at(self, g, z, spot, half):
        return self.full.at[g, z, spot[0], spot[1], half, :, self.columns]

    def block(self, spot, half):
        return self.at(slice(None), slice(None), spot, half)

    def forward(self, spot, device, number):
        block = lambda: self.block(spot, self.p.t)
        self.start(block, block(), device, number)

    def first(self):
        p = self.p
        here = (p.y, p.x)
        for s in range(1, p.depth):
            for core in range(2):
                self.start(
                    lambda core=core: self.own.at[core, :, self.columns],
                    self.at(p.t, p.z, here, core),
                    p.along_z(s, core),
                    2 * (s - 1) + core,
                    2 * (s - 1) + p.t,
                )
        self.start(
            lambda: self.own.at[p.other, :, self.columns],
            self.at(p.t, p.z, here, p.other),
            p.to_pair,
            6,
        )
        self.full[p.t, p.z, p.y, p.x, p.t, :, self.columns] = self.own[p.t, :, self.columns]

    def second(self):
        p = self.p
        here = (p.y, p.x)
        for n in range(7):
            self.landed(self.at(p.t, p.z, here, p.t), n)
        self.forward(here, p.to_near, 7)
        self.forward(here, p.to_next, 8)
        self.forward(here, p.to_pair, 9)

    def third(self):
        p = self.p
        self.landed(self.block(p.near, p.t), 7)
        self.forward(p.near, p.to_next, 10)
        self.forward(p.near, p.to_pair, 11)
        self.landed(self.block(p.next, p.t), 8)
        self.forward(p.next, p.to_pair, 12)

    def fourth(self):
        p = self.p
        self.landed(self.block(p.far, p.t), 10)
        self.forward(p.far, p.to_pair, 13)

    def last(self):
        p = self.p
        for n in (9, 11, 12, 13):
            self.landed(self.block((p.y, p.x), p.other), n)


class Scatter(Copies):
    COPIES = 11

    def __init__(self, place, part, columns, pair_in, near_in, next_in, last_in, sems):
        super().__init__(sems)
        self.p, self.part, self.columns = place, part, columns
        self.pair_in, self.near_in, self.next_in, self.last_in = pair_in, near_in, next_in, last_in

    def at(self, g, z, spot, half):
        return self.part.at[g, z, spot[0], spot[1], half, :, self.columns]

    def block(self, spot, half):
        return self.at(slice(None), slice(None), spot, half)

    def add(self, spot, landed):
        p = self.p
        here = (slice(None), slice(None), spot[0], spot[1], p.t, slice(None), self.columns)
        self.part[here] = (self.part[here].astype(F32) + landed.astype(F32)).astype(BF16)

    def first(self):
        p = self.p
        self.start(
            lambda: self.part.at[:, :, :, :, p.other, :, self.columns], self.pair_in, p.to_pair, 0
        )

    def second(self):
        p = self.p
        self.landed(self.pair_in, 0)
        for spot, number in ((p.far, 1), (p.near, 2)):
            self.add(spot, self.pair_in[:, :, spot[0], spot[1]])
            self.start(
                lambda spot=spot: self.block(spot, p.t),
                self.near_in.at[number - 1],
                p.to_near,
                number,
            )
        for spot in (p.next, (p.y, p.x)):
            self.add(spot, self.pair_in[:, :, spot[0], spot[1]])

    def third(self):
        p = self.p
        self.landed(self.near_in.at[0], 1)
        self.add(p.next, self.near_in[0])
        self.start(lambda: self.block(p.next, p.t), self.next_in, p.to_next, 3)
        self.landed(self.near_in.at[1], 2)
        self.add((p.y, p.x), self.near_in[1])

    def fourth(self):
        p = self.p
        here = (p.y, p.x)
        self.landed(self.next_in, 3)
        self.add(here, self.next_in[...])
        for s in range(1, p.depth):
            for core in range(2):
                self.start(
                    lambda s=s, core=core: self.at(core, p.levels[s], here, p.t),
                    self.last_in.at[2 * (s - 1) + p.t],
                    p.along_z(s, core),
                    4 + 2 * (s - 1) + core,
                    4 + 2 * (s - 1) + p.t,
                )
        self.start(
            lambda: self.at(p.other, p.z, here, p.t),
            self.last_in.at[2 * (p.depth - 1)],
            p.to_pair,
            10,
        )

    def last(self, target):
        p = self.p
        for n in range(7):
            self.landed(self.last_in.at[n], 4 + n)
        mine = self.part[p.t, p.z, p.y, p.x, p.t, :, self.columns].astype(F32)
        rest = self.last_in[2 * (p.depth - 1)].astype(F32)
        for s in range(1, p.depth):
            mine += self.last_in[2 * (s - 1) + p.t].astype(F32)
            rest += self.last_in[2 * (s - 1) + p.other].astype(F32)
        target[p.t] = mine
        target[p.other] = rest


def scatter_scratch(depth, columns):
    vmem = pltpu.VMEM
    return [
        vmem((2, depth, 2, 2, 16, columns), BF16),
        vmem((2, 2, depth, 16, columns), BF16),
        vmem((2, depth, 16, columns), BF16),
        vmem((2 * depth - 1, 16, columns), BF16),
        pltpu.SemaphoreType.DMA((2, Scatter.COPIES)),
    ]


class Reduce(Copies):
    COPIES = 6

    def __init__(self, place, total, landing, sems):
        super().__init__(sems)
        self.p, self.total, self.landing = place, total, landing

    def swap(self, number, device):
        self.start(lambda: self.total.at[number], self.landing.at[number], device, number)
        self.landed(self.landing.at[number], number)
        self.total[number + 1] = self.total[number] + self.landing[number]

    def finish(self):
        p = self.p
        for s in range(1, p.depth):
            self.start(
                lambda: self.total.at[3], self.landing.at[2 + s], {"dp": p.chips_z[s]}, 2 + s
            )
        for s in range(1, p.depth):
            self.landed(self.landing.at[2 + s], 2 + s)
        own = self.total[3]
        total = jnp.zeros_like(own)
        for z in range(p.depth):
            part = jnp.where(p.z == z, own, 0.0)
            for s in range(1, p.depth):
                came = lax.rem(p.z + p.depth - s, p.depth)
                part = jnp.where(came == z, self.landing[2 + s], part)
            total += part
        return total


class Woven:
    def __init__(self, place, owns, own_a, own_b, wa, wb, ga, gw, gains, gathers, scatters, targets):
        self.p = place
        self.owns, self.own_a, self.own_b = owns, own_a, own_b
        self.a = [
            Gather(place, own_a, wa, slice(0, 512), gathers[0]),
            Gather(place, own_a, wa, slice(512, 1024), gathers[1]),
        ]
        self.b = [
            Gather(place, own_b, wb, slice(0, 1280), gathers[2]),
            Gather(place, own_b, wb, slice(1280, 2304), gathers[3]),
        ]
        self.w = [
            Scatter(place, gw, slice(1280, 2304), *scatters[0]),
            Scatter(place, gw, slice(0, 1280), *scatters[1]),
        ]
        self.g = [
            Scatter(place, ga, slice(0, 512), *scatters[2]),
            Scatter(place, ga, slice(512, 1024), *scatters[3]),
        ]
        self.gains = gains
        self.da, self.dw = targets

    def before(self):
        p = self.p
        query, key, value, slot, out_t, up, down_t = self.owns
        halves = lambda ref: ref[...].astype(BF16).reshape(2, 16, ref.shape[1])
        self.own_a[:, :, 0:256] = halves(query)
        self.own_a[:, :, 256:512] = halves(key)
        self.own_a[:, :, 512:768] = halves(value)
        self.own_a[:, :, 768:1024] = halves(slot)
        self.own_b[:, :, 0:256] = halves(out_t)
        self.own_b[:, :, 256:1280] = halves(up)
        self.own_b[:, :, 1280:2304] = halves(down_t)
        p.greet()
        self.a[0].first()
        self.a[1].first()

    def weights_a(self):
        one, two = self.a
        one.second()
        two.second()
        self.b[0].first()
        one.third()
        two.third()
        one.fourth()
        two.fourth()
        self.b[1].first()
        one.last()
        two.last()

    def mixing(self, c):
        one, two = self.b
        for i, step in enumerate((one.second, one.third, one.fourth, two.second, two.third)):
            pl.when(c == i + 1)(step)

    def weights_b(self):
        one, two = self.b
        two.fourth()
        one.last()
        two.last()

    def grads_w(self, which):
        self.w[which].first()
        if which == 1:
            self.w[0].second()

    def mixing_back(self, i):
        one, two = self.w
        steps = (one.third, two.second, one.fourth, two.third, None, two.fourth)
        for n, step in enumerate(steps):
            if step is not None:
                pl.when(i == n + 1)(step)

    def grads_a(self):
        self.g[0].first()
        self.g[1].first()
        self.w[0].last(self.dw.at[:, :, 1280:2304])
        self.w[1].last(self.dw.at[:, :, 0:1280])
        self.g[0].second()
        self.g[1].second()

    def after(self):
        p = self.p
        one, two = self.g
        self.gains.swap(0, p.to_pair)
        one.third()
        two.third()
        self.gains.swap(1, p.to_x)
        one.fourth()
        two.fourth()
        self.gains.swap(2, p.to_y)
        one.last(self.da.at[:, :, 0:512])
        two.last(self.da.at[:, :, 512:1024])
        self.total = self.gains.finish()
        for copies in self.a + self.b + self.w + self.g + [self.gains]:
            copies.left()


def woven_kernel(length, depth, *refs):
    refs = list(refs)
    take = lambda n: [refs.pop(0) for _ in range(n)]
    tok, cot, seg_rows, pad_rows, gain_one, gain_two, up_bias, down_bias = take(LAYER_INPUTS)
    owns = take(7)
    out, grad_out, da, dw, small_out = take(5)
    own_a, own_b, wa, wb, ga, gw, seg_row, pad_row = take(8)
    small, landing, gain_sems = take(3)
    gathers = take(4)
    scatters = [take(5) for _ in range(4)]
    place = Place(depth)
    gains = Reduce(place, small, landing, gain_sems)
    comm = Woven(place, owns, own_a, own_b, wa, wb, ga, gw, gains, gathers, scatters, (da, dw))
    first = (lax.axis_index("tensor") == 0)
    for rows, row in ((seg_rows, seg_row), (pad_rows, pad_row)):
        row[...] = jnp.where(first, rows[0:1, :], rows[1:2, :])
    layer_body(
        length, comm, tok, cot, seg_row, pad_row, gain_one, gain_two, up_bias, down_bias, wa, wb,
        out, grad_out, ga, gw, small.at[0], *refs,
    )
    small_out[...] = comm.total


def woven(depth, tokens, cotangent, segments, padding, gains, biases, owns):
    length, width = tokens.shape
    shape = jax.ShapeDtypeStruct
    space = pl.BlockSpec(memory_space=pltpu.VMEM)
    vmem = pltpu.VMEM
    dma = pltpu.SemaphoreType.DMA
    full = lambda columns: vmem((2, depth, 2, 2, 2, 16, columns), BF16)
    out, grad_out, da, dw, small = pl.pallas_call(
        functools.partial(woven_kernel, length, depth),
        out_shape=(
            shape((length, width), BF16),
            shape((length, width), BF16),
            shape((2, 16, 1024), F32),
            shape((2, 16, 2304), F32),
            shape((8, width), F32),
        ),
        in_specs=[space] * (LAYER_INPUTS + 7),
        out_specs=tuple([space] * 5),
        scratch_shapes=[
            vmem((2, 16, 1024), BF16),
            vmem((2, 16, 2304), BF16),
            full(1024),
            full(2304),
            full(1024),
            full(2304),
            vmem((1, length), jnp.int32),
            vmem((1, length), jnp.int32),
            vmem((4, 8, width), F32),
            vmem((Reduce.COPIES, 8, width), F32),
            dma((2, Reduce.COPIES)),
        ]
        + [dma((2, Gather.COPIES))] * 4
        + scatter_scratch(depth, 1024)
        + scatter_scratch(depth, 1280)
        + scatter_scratch(depth, 512)
        + scatter_scratch(depth, 512)
        + layer_scratch(length, width),
        compiler_params=pltpu.CompilerParams(
            collective_id=0, has_side_effects=True, vmem_limit_bytes=62 * 1024 * 1024
        ),
        name="woven",
    )(tokens, cotangent, segments, padding, *gains, *biases, *owns)
    return out, grad_out, da.reshape(32, 1024), dw.reshape(32, 2304), small


def per_device(
    direct,
    tokens,
    segment_ids,
    padding,
    mixer_gain,
    query_weight,
    key_weight,
    value_weight,
    slot_weight,
    out_weight,
    feed_gain,
    up_weight,
    up_bias,
    down_weight,
    down_bias,
    cotangent,
):
    gains = (mixer_gain[None], feed_gain[None])
    biases = (up_bias[None], down_bias[None])
    if direct:
        owns = (
            query_weight, key_weight, value_weight, slot_weight, out_weight.T, up_weight,
            down_weight.T,
        )
        depth = lax.axis_size("dp") // 4
        out, grad_out, da, dw, small = woven(
            depth, tokens, cotangent, segment_ids, padding, gains, biases, owns
        )
    else:
        own_a = jnp.concatenate([query_weight, key_weight, value_weight, slot_weight], 1)
        own_b = jnp.concatenate([out_weight.T, up_weight, down_weight.T], 1)
        wa, wb = (
            lax.all_gather(
                lax.all_gather(own.astype(BF16), "dp", axis=0, tiled=True), "tensor"
            )
            for own in (own_a, own_b)
        )
        half = lax.axis_index("tensor")
        pick = lambda rows: lax.dynamic_slice_in_dim(rows, half, 1, 0)
        out, grad_out, ga, gw, small = layer(
            tokens, cotangent, pick(segment_ids), pick(padding), *gains, *biases, wa, wb
        )
        da, dw = (
            lax.psum_scatter(
                lax.psum_scatter(part.astype(F32), "tensor", scatter_dimension=0),
                "dp",
                scatter_dimension=0,
                tiled=True,
            )
            for part in (ga, gw)
        )
        small = lax.psum(small, ("dp", "tensor"))
    return (
        out,
        grad_out,
        small[1],
        da[:, 0:256],
        da[:, 256:512],
        da[:, 512:768],
        da[:, 768:1024],
        dw[:, 0:256].T,
        small[0],
        dw[:, 256:1280],
        small[4:8].reshape(-1),
        dw[:, 1280:2304].T,
        small[2],
    )


def solution(mesh):
    in_specs = (
        P(("dp", "tensor"), None),
        P("dp", None),
        P("dp", None),
        P(),
        P("dp", "tensor"),
        P("dp", "tensor"),
        P("dp", "tensor"),
        P("dp", "tensor"),
        P("tensor", "dp"),
        P(),
        P("dp", "tensor"),
        P(),
        P("tensor", "dp"),
        P(),
        P(("dp", "tensor"), None),
    )
    out_specs = (
        P(("dp", "tensor"), None),
        P(("dp", "tensor"), None),
        P(),
        P("dp", "tensor"),
        P("dp", "tensor"),
        P("dp", "tensor"),
        P("dp", "tensor"),
        P("tensor", "dp"),
        P(),
        P("dp", "tensor"),
        P(),
        P("tensor", "dp"),
        P(),
    )
    direct = mesh.shape["dp"] == 16 and mesh.shape["tensor"] == 2
    return jax.shard_map(
        functools.partial(per_device, direct),
        mesh=mesh,
        in_specs=in_specs,
        out_specs=out_specs,
        check_vma=False,
    )
```

```python
import functools
import math

import jax
import jax.numpy as jnp
from jax import lax
from jax.experimental import pallas as pl
from jax.experimental.pallas import tpu as pltpu
from jax.sharding import PartitionSpec as P

HEAD_DIM = 64
SLOTS = 64
CHUNK = 128
GROUP = 256
TILE = 256

F32 = jnp.float32
BF16 = jnp.bfloat16
MESH = pl.DeviceIdType.MESH


def dot(left, right):
    return lax.dot_general(left, right, (((1,), (0,)), ((), ())), preferred_element_type=F32)


def dot_rt(left, right):
    return lax.dot_general(left, right, (((1,), (1,)), ((), ())), preferred_element_type=F32)


def dot_lt(left, right):
    return lax.dot_general(left, right, (((0,), (0,)), ((), ())), preferred_element_type=F32)


def twice(block):
    return jnp.concatenate([block, block], axis=1)


def four(block):
    return jnp.concatenate([block, block, block, block], axis=1)


def standardise(rows):
    centred = rows - jnp.mean(rows, axis=-1, keepdims=True)
    scale = lax.rsqrt(jnp.mean(centred * centred, axis=-1, keepdims=True) + 1e-05)
    return centred * scale, scale


def head_stack(block):
    lane = lax.broadcasted_iota(jnp.int32, block.shape, 1) // HEAD_DIM
    zero = jnp.zeros_like(block)
    return jnp.concatenate([jnp.where(lane == h, block, zero) for h in range(4)], axis=0)


def head_blocks():
    row = lax.broadcasted_iota(jnp.int32, (GROUP, GROUP), 0) // HEAD_DIM
    column = lax.broadcasted_iota(jnp.int32, (GROUP, GROUP), 1) // HEAD_DIM
    return row == column


def head_sum(block, ones):
    high = block.astype(BF16)
    low = (block - high.astype(F32)).astype(BF16)
    return dot(high, ones) + dot(low, ones)


def head_max(block):
    halves = []
    lane = lax.broadcasted_iota(jnp.int32, (block.shape[0], 128), 1) < HEAD_DIM
    for j in range(block.shape[1] // 128):
        part = block[:, j * 128 : (j + 1) * 128]
        first = jnp.max(jnp.where(lane, part, -jnp.inf), axis=1, keepdims=True)
        second = jnp.max(jnp.where(lane, -jnp.inf, part), axis=1, keepdims=True)
        halves.append(jnp.where(lane, first, second))
    return jnp.concatenate(halves, axis=1)


def flat(block):
    return block.reshape(-1, block.shape[-1])


def rows_to_columns(seg_row, pad_row, segc, keepc, length):
    segc[pl.ds(0, 8), :] = jnp.full((8, 128), -1.0, F32)
    segc[pl.ds(8 + length, 8), :] = jnp.full((8, 128), -2.0, F32)
    for c in range(length // CHUNK):
        here = slice(c * CHUNK, (c + 1) * CHUNK)
        seg = jnp.broadcast_to(seg_row[:, here].astype(F32), (CHUNK, CHUNK))
        pad = jnp.broadcast_to(pad_row[:, here].astype(F32), (CHUNK, CHUNK))
        segc[pl.ds(8 + c * CHUNK, CHUNK), :] = seg.T
        keepc[pl.ds(c * CHUNK, CHUNK), :] = 1.0 - pad.T


def normalise(r, tok, gain, n1):
    rows = pl.ds(pl.multiple_of(r * TILE, TILE), TILE)
    xhat, _ = standardise(tok[rows, :].astype(F32))
    n1[rows, :] = (xhat * gain[...]).astype(BF16)


def project(g, r, wa, keepc, n1, q, k, v, w):
    rows = pl.ds(pl.multiple_of(r * TILE, TILE), TILE)
    out = dot(n1[rows, :], flat(wa[g]))
    q[g, rows, :] = out[:, 0:256].astype(BF16)
    k[g, rows, :] = out[:, 256:512].astype(BF16)
    v[g, rows, :] = out[:, 512:768].astype(BF16)
    w[g, rows, :] = (jnp.exp(out[:, 768:1024]) * twice(keepc[rows, :])).astype(BF16)


def chunk_masks(c, segc):
    base = pl.multiple_of(c * CHUNK, CHUNK)
    seg = segc[pl.ds(base + 8, CHUNK), :]
    across = seg.T
    row = lax.broadcasted_iota(jnp.int32, (CHUNK, CHUNK), 0)
    column = lax.broadcasted_iota(jnp.int32, (CHUNK, CHUNK), 1)
    same = seg == across
    causal = jnp.where(same & (column <= row), 1.0, 0.0)
    anti = jnp.where(same & (row <= column), 1.0, 0.0)
    before = segc[pl.ds(base + 7, 1), :]
    first = segc[pl.ds(base + 8, 1), :]
    last = segc[pl.ds(base + 7 + CHUNK, 1), :]
    after = segc[pl.ds(base + 8 + CHUNK, 1), :]
    one = lambda test: jnp.where(test, 1.0, 0.0)
    return causal, anti, dict(
        from_before=one(seg == before),
        to_after=one(seg == last),
        from_after=one(seg == after),
        to_before=one(seg == first),
        carry_on=one(before == last),
        carry_back=one(after == first),
    )


def mix_forward(
    g, i, segc, keepc, q, k, v, w, probs, inv, score, mixed, kw, wv, zsum, kw_all, wv_all
):
    blocks = head_blocks()
    ones = jnp.where(blocks, 1.0, 0.0).astype(BF16)
    state_k, state_v, state_z = kw[...], wv[...], zsum[0:1, :]
    for n in range(2):
        c = 2 * i + n
        rows = pl.ds(pl.multiple_of(c * CHUNK, CHUNK), CHUNK)
        causal, _, edge = chunk_masks(c, segc)
        causal4 = four(causal)
        keep = twice(keepc[rows, :])
        come = twice(edge["from_before"])
        come_low = come.astype(BF16)
        carry = twice(edge["carry_on"])
        qc, kc, vc, wc = q[g, rows, :], k[g, rows, :], v[g, rows, :], w[g, rows, :]
        kw_low, wv_low = state_k.astype(BF16), state_v.astype(BF16)
        kw_all[g, c] = kw_low
        wv_all[g, c] = wv_low
        ws = head_stack(wc)
        pairs = (dot_rt(qc, head_stack(kc)) * causal4).astype(BF16)
        total = dot(causal.astype(BF16), wc) + come * state_z + (1.0 - keep)
        inverse = 1.0 / total
        scores = (dot(pairs, ws) + dot(qc * come_low, kw_low)) * (inverse * (HEAD_DIM**-0.5))
        powers = jnp.exp(scores - head_max(scores))
        chances = powers / head_sum(powers, ones)
        ratio = (chances * inverse).astype(BF16)
        probs[g, rows, :] = chances
        inv[g, rows, :] = inverse
        score[g, rows, :] = scores
        mixing = (dot_rt(ratio, ws) * causal4).astype(BF16)
        out = dot(mixing, head_stack(vc)) + dot(ratio * come_low, wv_low)
        mixed[g, rows, :] = (out * keep).astype(BF16)
        wg = wc * twice(edge["to_after"]).astype(BF16)
        state_k = state_k * carry + jnp.where(blocks, dot_lt(kc, wg), 0.0)
        state_v = state_v * carry + jnp.where(blocks, dot_lt(wg, vc), 0.0)
        state_z = state_z * carry + jnp.sum(wg.astype(F32), axis=0, keepdims=True)
    kw[...] = state_k
    wv[...] = state_v
    zsum[...] = jnp.broadcast_to(state_z, zsum.shape)


def mix_backward(
    g, i, segc, keepc, q, k, v, w, probs, inv, score, gm, rg, uq, zgrad, kw_all, wv_all, gy
):
    blocks = head_blocks()
    ones = jnp.where(blocks, 1.0, 0.0).astype(BF16)
    state_v, state_k, state_z = rg[...], uq[...], zgrad[0:1, :]
    for n in range(2):
        c = 2 * i + 1 - n
        rows = pl.ds(pl.multiple_of(c * CHUNK, CHUNK), CHUNK)
        causal, anti, edge = chunk_masks(c, segc)
        causal4, anti4 = four(causal), four(anti)
        anti_low = anti.astype(BF16)
        come_low = twice(edge["from_before"]).astype(BF16)
        late = twice(edge["from_after"])
        late_low = late.astype(BF16)
        back = twice(edge["to_before"])
        back_low = back.astype(BF16)
        carry = twice(edge["carry_back"])
        qc, kc, vc, wc = q[g, rows, :], k[g, rows, :], v[g, rows, :], w[g, rows, :]
        grad = gm[g, rows, :]
        chances, inverse, scores = probs[g, rows, :], inv[g, rows, :], score[g, rows, :]
        ratio = (chances * inverse).astype(BF16)
        ws, grads, ratios = head_stack(wc), head_stack(grad), head_stack(ratio)
        d_mixing = (dot_rt(grad, head_stack(vc)) * causal4).astype(BF16)
        d_ratio = dot(d_mixing, ws) + dot_rt(grad * come_low, wv_all[g, c])
        d_chance = d_ratio * inverse
        weighted = d_chance * chances
        d_score = weighted - chances * head_sum(weighted, ones)
        d_pw = (d_score * inverse * (HEAD_DIM**-0.5)).astype(BF16)
        d_total = (weighted + d_score * scores) * inverse
        d_pairs = (dot_rt(d_pw, ws) * causal4).astype(BF16)
        gq = dot(d_pairs, head_stack(kc)) + dot_rt(d_pw * come_low, kw_all[g, c])
        rg_low, uq_low = state_v.astype(BF16), state_k.astype(BF16)
        d_pws, queries = head_stack(d_pw), head_stack(qc)
        mixing_t = (dot_rt(wc, ratios) * anti4).astype(BF16)
        w_late = wc * late_low
        gv = dot(mixing_t, grads) + dot(w_late, rg_low)
        d_pairs_t = (dot_rt(wc, d_pws) * anti4).astype(BF16)
        gk = dot(d_pairs_t, queries) + dot(w_late, uq_low)
        d_mixing_t = (dot_rt(vc, grads) * anti4).astype(BF16)
        pairs_t = (dot_rt(kc, queries) * anti4).astype(BF16)
        z_high = d_total.astype(BF16)
        z_low = (d_total - z_high.astype(F32)).astype(BF16)
        dw = dot(d_mixing_t, ratios) + dot(pairs_t, d_pws)
        dw += dot_rt(vc * late_low, rg_low) + dot_rt(kc * late_low, uq_low)
        dw -= dot(anti_low, z_high) + dot(anti_low, z_low) + late * state_z
        gy[g, rows, 0:256] = gq.astype(BF16)
        gy[g, rows, 256:512] = gk.astype(BF16)
        gy[g, rows, 512:768] = gv.astype(BF16)
        gy[g, rows, 768:1024] = (dw * wc.astype(F32)).astype(BF16)
        state_v = state_v * carry + jnp.where(blocks, dot_lt(ratio * back_low, grad), 0.0)
        state_k = state_k * carry + jnp.where(blocks, dot_lt(d_pw * back_low, qc), 0.0)
        state_z = state_z * carry + jnp.sum(d_total * back, axis=0, keepdims=True)
    rg[...] = state_v
    uq[...] = state_k
    zgrad[...] = jnp.broadcast_to(state_z, zgrad.shape)


def feed_up(r, tok, gain, up_bias, wb, mixed, n2, act, lin, gh):
    rows = pl.ds(pl.multiple_of(r * TILE, TILE), TILE)
    hidden = tok[rows, :].astype(F32)
    for g in range(2):
        hidden += dot_rt(mixed[g, rows, :], flat(wb[g, ..., 0:256]))
    gh[rows, :] = hidden
    hat, _ = standardise(hidden)
    normed = (hat * gain[...]).astype(BF16)
    n2[rows, :] = normed
    k0 = 0.7978845608
    k1 = k0 * 0.044715
    for g in range(2):
        for j in range(4):
            here = slice(j * 256, (j + 1) * 256)
            unit = g * 1024 + j * 256
            up = flat(wb[g, ..., 256 + j * 256 : 512 + j * 256])
            linear = dot(normed, up) + up_bias[:, unit : unit + 256]
            square = linear * linear
            gate = 0.5 * jnp.tanh(linear * (square * k1 + k0)) + 0.5
            active = linear * gate
            slope = gate + active * (1.0 - gate) * (square * (6.0 * k1) + 2.0 * k0)
            act[g, rows, here] = active.astype(BF16)
            lin[g, rows, here] = slope.astype(BF16)


def feed_down(r, cot, gain, down_bias, wb, keepc, act, lin, gh, gb, gm, small, out):
    rows = pl.ds(pl.multiple_of(r * TILE, TILE), TILE)
    grad = cot[rows, :]
    hidden = gh[rows, :]
    total = hidden + down_bias[...]
    back = jnp.zeros((TILE, 512), F32)
    for g in range(2):
        for j in range(4):
            here = slice(j * 256, (j + 1) * 256)
            unit = g * 1024 + j * 256
            down = flat(wb[g, ..., 1280 + j * 256 : 1536 + j * 256])
            grad_low = (dot(grad, down) * lin[g, rows, here].astype(F32)).astype(BF16)
            lin[g, rows, here] = grad_low
            row, column = 4 + unit // 512, unit % 512
            small[row : row + 1, column : column + 256] += jnp.sum(
                grad_low.astype(F32), axis=0, keepdims=True
            )
    for g in range(2):
        total += dot_rt(act[g, rows, :], flat(wb[g, ..., 1280:2304]))
        back += dot_rt(lin[g, rows, :], flat(wb[g, ..., 256:1280]))
    out[rows, :] = total.astype(BF16)
    hat, scale = standardise(hidden)
    scaled = back * gain[...]
    inner = scaled - jnp.mean(scaled, axis=-1, keepdims=True)
    inner -= hat * jnp.mean(scaled * hat, axis=-1, keepdims=True)
    grad_f32 = grad.astype(F32)
    grad_hidden = grad_f32 + scale * inner
    gh[rows, :] = grad_hidden
    low = grad_hidden.astype(BF16)
    gb[rows, :] = low
    small[0:1, :] += jnp.sum(back * hat, axis=0, keepdims=True)
    small[2:3, :] += jnp.sum(grad_f32, axis=0, keepdims=True)
    keep = twice(keepc[rows, :])
    for g in range(2):
        gm[g, rows, :] = (dot(low, flat(wb[g, ..., 0:256])) * keep).astype(BF16)


def transpose_into(source, target, length):
    for r in range(length // TILE):
        target[:, r * TILE : (r + 1) * TILE] = source[r * TILE : (r + 1) * TILE, :].T


def weight_grad(left_t, right, target, g, target_column, columns):
    shape = target.shape[1:-1] + (256,)

    def step(j, carry):
        here = pl.ds(pl.multiple_of(j * 256, 256), 256)
        there = pl.ds(pl.multiple_of(target_column + j * 256, 256), 256)
        target[g, ..., there] = dot(left_t[...], right[:, here]).astype(BF16).reshape(shape)
        return carry

    lax.fori_loop(0, columns // 256, step, 0)


def finish(r, tok, gain, wa, gy, gh, small, grad_out):
    rows = pl.ds(pl.multiple_of(r * TILE, TILE), TILE)
    hat, scale = standardise(tok[rows, :].astype(F32))
    back = dot_rt(gy[0, rows, :], flat(wa[0])) + dot_rt(gy[1, rows, :], flat(wa[1]))
    scaled = back * gain[...]
    inner = scaled - jnp.mean(scaled, axis=-1, keepdims=True)
    inner -= hat * jnp.mean(scaled * hat, axis=-1, keepdims=True)
    grad_out[rows, :] = (gh[rows, :] + scale * inner).astype(BF16)
    small[1:2, :] += jnp.sum(back * hat, axis=0, keepdims=True)


class Quiet:
    def nothing(self, *at):
        pass

    before = weights_a = mixing = weights_up = feeding = weights_down = nothing
    grads_down = grads_up = mixing_back = grads_a = finishing = after = nothing


LAYER_INPUTS = 8


def layer_body(
    length,
    comm,
    tok,
    cot,
    seg_row,
    pad_row,
    gain_one,
    gain_two,
    up_bias,
    down_bias,
    wa,
    wb,
    out,
    grad_out,
    ga,
    gw,
    small,
    segc,
    keepc,
    n1,
    q,
    k,
    v,
    w,
    probs,
    inv,
    score,
    mixed,
    state_k,
    state_v,
    state_z,
    kw_all,
    wv_all,
    n2,
    act,
    lin,
    gh,
    gb,
    gm,
    flip,
):
    pairs, tiles = length // (2 * CHUNK), length // TILE

    def clear():
        state_k[...] = jnp.zeros_like(state_k)
        state_v[...] = jnp.zeros_like(state_v)
        state_z[...] = jnp.zeros_like(state_z)

    comm.before()
    small[...] = jnp.zeros_like(small)
    rows_to_columns(seg_row, pad_row, segc, keepc, length)

    @pl.loop(0, tiles)
    def _(r):
        normalise(r, tok, gain_one, n1)

    @pl.loop(0, 2)
    def _(g):
        comm.weights_a(g)
        clear()

        @pl.loop(0, tiles)
        def _(r):
            project(g, r, wa, keepc, n1, q, k, v, w)

        @pl.loop(0, pairs)
        def _(i):
            comm.mixing(g, i)
            mix_forward(
                g, i, segc, keepc, q, k, v, w, probs, inv, score, mixed, state_k, state_v, state_z,
                kw_all, wv_all,
            )

    comm.weights_up()

    @pl.loop(0, tiles)
    def _(r):
        comm.feeding(r)
        feed_up(r, tok, gain_two, up_bias, wb, mixed, n2, act, lin, gh)

    comm.weights_down()

    @pl.loop(0, tiles)
    def _(r):
        feed_down(r, cot, gain_two, down_bias, wb, keepc, act, lin, gh, gb, gm, small, out)

    transpose_into(cot, flip, length)
    for g in range(2):
        weight_grad(flip, act.at[g], gw, g, 1280, 1024)
    comm.grads_down()
    transpose_into(n2, flip, length)
    for g in range(2):
        weight_grad(flip, lin.at[g], gw, g, 256, 1024)
    transpose_into(gb, flip, length)
    for g in range(2):
        weight_grad(flip, mixed.at[g], gw, g, 0, GROUP)
    comm.grads_up()
    transpose_into(n1, flip, length)

    @pl.loop(0, 2)
    def _(g):
        clear()

        @pl.loop(0, pairs)
        def _(i):
            comm.mixing_back(g, i)
            mix_backward(
                g, pairs - 1 - i, segc, keepc, q, k, v, w, probs, inv, score, gm, state_v, state_k,
                state_z, kw_all, wv_all, act,
            )

        weight_grad(flip, act.at[g], ga, g, 0, 1024)
        comm.grads_a(g)

    @pl.loop(0, tiles)
    def _(r):
        comm.finishing(r)
        finish(r, tok, gain_one, wa, act, gh, small, grad_out)

    comm.after()


def layer_scratch(length, width):
    vmem = pltpu.VMEM
    chunks = length // CHUNK
    return [
        vmem((length + 16, 128), F32),
        vmem((length, 128), F32),
        vmem((length, width), BF16),
        vmem((2, length, GROUP), BF16),
        vmem((2, length, GROUP), BF16),
        vmem((2, length, GROUP), BF16),
        vmem((2, length, GROUP), BF16),
        vmem((2, length, GROUP), F32),
        vmem((2, length, GROUP), F32),
        vmem((2, length, GROUP), F32),
        vmem((2, length, GROUP), BF16),
        vmem((GROUP, GROUP), F32),
        vmem((GROUP, GROUP), F32),
        vmem((8, GROUP), F32),
        vmem((2, chunks, GROUP, GROUP), BF16),
        vmem((2, chunks, GROUP, GROUP), BF16),
        vmem((length, width), BF16),
        vmem((2, length, 1024), BF16),
        vmem((2, length, 1024), BF16),
        vmem((length, width), F32),
        vmem((length, width), BF16),
        vmem((2, length, GROUP), BF16),
        vmem((width, length), BF16),
    ]


def layer_kernel(length, *refs):
    layer_body(length, Quiet(), *refs)


def layer(tokens, cotangent, seg_row, pad_row, gain_one, gain_two, up_bias, down_bias, wa, wb):
    length, width = tokens.shape
    shape = jax.ShapeDtypeStruct
    cut = lambda full: full.reshape(2, -1, 2, 2, 2, 16, full.shape[-1])
    wa, wb = cut(wa), cut(wb)
    space = pl.BlockSpec(memory_space=pltpu.VMEM)
    out, grad_out, ga, gw, small = pl.pallas_call(
        functools.partial(layer_kernel, length),
        out_shape=(
            shape((length, width), BF16),
            shape((length, width), BF16),
            shape(wa.shape, BF16),
            shape(wb.shape, BF16),
            shape((8, width), F32),
        ),
        in_specs=[space] * 10,
        out_specs=tuple([space] * 5),
        scratch_shapes=layer_scratch(length, width),
        compiler_params=pltpu.CompilerParams(vmem_limit_bytes=60 * 1024 * 1024),
        name="layer",
    )(tokens, cotangent, seg_row, pad_row, gain_one, gain_two, up_bias, down_bias, wa, wb)
    whole = lambda full: full.reshape(2, width, full.shape[-1])
    return out, grad_out, whole(ga), whole(gw), small


class Place:
    def __init__(self, depth):
        index = lax.axis_index("dp")
        t = lax.axis_index("tensor")
        x, y, z = lax.rem(index, 2), lax.rem(index // 2, 2), index // 4
        self.depth = depth
        self.x, self.y, self.z, self.t, self.other = x, y, z, t, 1 - t
        self.near = (y + t * (1 - 2 * y), x + (1 - t) * (1 - 2 * x))
        self.next = (y + (1 - t) * (1 - 2 * y), x + t * (1 - 2 * x))
        self.far = (1 - y, 1 - x)
        chip = lambda z, y, x: (z * 2 + y) * 2 + x
        self.levels = [lax.rem(z + s, depth) for s in range(depth)]
        self.chips_z = [chip(level, y, x) for level in self.levels]
        self.to_near = {"dp": chip(z, *self.near)}
        self.to_next = {"dp": chip(z, *self.next)}
        self.to_pair = {"tensor": self.other}
        self.spot = (y * 2 + x) * 2 + t
        flip = lambda value, bit: value + bit * (1 - 2 * value)
        self.level = [
            {
                "dp": chip(z, flip(y, offset // 4), flip(x, offset // 2 % 2)),
                "tensor": flip(t, offset % 2),
            }
            for offset in range(8)
        ]

    def along_z(self, step, core):
        return {"dp": self.chips_z[step], "tensor": core}

    def greet(self):
        barrier = pltpu.get_barrier_semaphore()
        friends = self.level[1:]
        friends += [self.along_z(s, core) for s in range(1, self.depth) for core in range(2)]
        for friend in friends:
            pl.semaphore_signal(barrier, inc=1, device_id=friend, device_id_type=MESH)
        pl.semaphore_wait(barrier, len(friends))


class Copies:
    def __init__(self, sems):
        self.sems = sems
        self.started = []

    def build(self, source, target, device, out_sem, in_sem):
        return pltpu.make_async_remote_copy(
            src_ref=source,
            dst_ref=target,
            send_sem=self.sems.at[0, out_sem],
            recv_sem=self.sems.at[1, in_sem],
            device_id=device,
            device_id_type=MESH,
        )

    def start(self, source, target, device, number, in_sem=None, only=None):
        def begin():
            landing = number if in_sem is None else in_sem
            self.build(source(), target, device, number, landing).start()

        begin() if only is None else pl.when(only)(begin)
        self.started.append((source, number, only))

    def landed(self, target, number, only=None):
        def wait():
            self.build(target, target, {"tensor": 0}, number, number).wait_recv()

        wait() if only is None else pl.when(only)(wait)

    def left(self):
        for source, number, only in self.started:

            def wait(source=source, number=number):
                part = source()
                self.build(part, part, {"tensor": 0}, number, number).wait_send()

            wait() if only is None else pl.when(only)(wait)


class Gather(Copies):
    COPIES = 14

    def __init__(self, place, own, full, group, columns, sems):
        super().__init__(sems)
        self.p, self.own, self.full, self.columns = place, own, full, columns
        self.group = group
        self.groups = slice(None) if group is None else slice(group, group + 1)
        self.mine = None if group is None else place.t == group
        self.pairs = None if group is None else place.t != group

    def at(self, g, z, spot, half):
        return self.full.at[g, z, spot[0], spot[1], half, :, self.columns]

    def block(self, spot, half):
        return self.at(self.groups, slice(None), spot, half)

    def forward(self, spot, device, number):
        block = lambda: self.block(spot, self.p.t)
        self.start(block, block(), device, number)

    def first(self):
        p = self.p
        here = (p.y, p.x)
        for s in range(1, p.depth):
            for core in range(2):
                self.start(
                    lambda core=core: self.own.at[core, :, self.columns],
                    self.at(p.t, p.z, here, core),
                    p.along_z(s, core),
                    2 * (s - 1) + core,
                    2 * (s - 1) + p.t,
                    only=self.mine,
                )
        self.start(
            lambda: self.own.at[p.other, :, self.columns],
            self.at(p.t, p.z, here, p.other),
            p.to_pair,
            6,
            only=self.mine,
        )

        def keep():
            self.full[p.t, p.z, p.y, p.x, p.t, :, self.columns] = self.own[p.t, :, self.columns]

        keep() if self.mine is None else pl.when(self.mine)(keep)

    def second(self):
        p = self.p
        here = (p.y, p.x)
        for n in range(6):
            if self.group is None or n % 2 == self.group:
                self.landed(self.at(p.t, p.z, here, p.t), n)
        self.landed(self.at(p.t, p.z, here, p.t), 6, only=self.pairs)
        self.forward(here, p.to_near, 7)
        self.forward(here, p.to_next, 8)
        self.forward(here, p.to_pair, 9)

    def third(self):
        p = self.p
        self.landed(self.block(p.near, p.t), 7)
        self.forward(p.near, p.to_next, 10)
        self.forward(p.near, p.to_pair, 11)
        self.landed(self.block(p.next, p.t), 8)
        self.forward(p.next, p.to_pair, 12)

    def fourth(self):
        p = self.p
        self.landed(self.block(p.far, p.t), 10)
        self.forward(p.far, p.to_pair, 13)

    def last(self):
        p = self.p
        for n in (9, 11, 12, 13):
            self.landed(self.block((p.y, p.x), p.other), n)


class Scatter(Copies):
    COPIES = 11

    def __init__(self, place, part, group, columns, pair_in, near_in, next_in, last_in, sems):
        super().__init__(sems)
        self.p, self.part, self.columns = place, part, columns
        self.pair_in, self.near_in, self.next_in, self.last_in = pair_in, near_in, next_in, last_in
        self.group = group
        self.groups = slice(None) if group is None else slice(group, group + 1)
        self.mine = None if group is None else place.t == group
        self.pairs = None if group is None else place.t != group

    def at(self, g, z, spot, half):
        return self.part.at[g, z, spot[0], spot[1], half, :, self.columns]

    def block(self, spot, half):
        return self.at(self.groups, slice(None), spot, half)

    def add(self, spot, landed):
        p = self.p
        here = (self.groups, slice(None), spot[0], spot[1], p.t, slice(None), self.columns)
        self.part[here] = (self.part[here].astype(F32) + landed.astype(F32)).astype(BF16)

    def first(self):
        p = self.p
        self.start(
            lambda: self.part.at[self.groups, :, :, :, p.other, :, self.columns],
            self.pair_in,
            p.to_pair,
            0,
        )

    def second(self):
        p = self.p
        self.landed(self.pair_in, 0)
        for spot, number in ((p.far, 1), (p.near, 2)):
            self.add(spot, self.pair_in[:, :, spot[0], spot[1]])
            self.start(
                lambda spot=spot: self.block(spot, p.t),
                self.near_in.at[number - 1],
                p.to_near,
                number,
            )
        for spot in (p.next, (p.y, p.x)):
            self.add(spot, self.pair_in[:, :, spot[0], spot[1]])

    def third(self):
        p = self.p
        self.landed(self.near_in.at[0], 1)
        self.add(p.next, self.near_in[0])
        self.start(lambda: self.block(p.next, p.t), self.next_in, p.to_next, 3)
        self.landed(self.near_in.at[1], 2)
        self.add((p.y, p.x), self.near_in[1])

    def fourth(self):
        p = self.p
        here = (p.y, p.x)
        self.landed(self.next_in, 3)
        self.add(here, self.next_in[...])
        for s in range(1, p.depth):
            for core in range(2) if self.group is None else (self.group,):
                self.start(
                    lambda s=s, core=core: self.at(core, p.levels[s], here, p.t),
                    self.last_in.at[2 * (s - 1) + p.t],
                    p.along_z(s, core),
                    4 + 2 * (s - 1) + core,
                    4 + 2 * (s - 1) + p.t,
                )
        self.start(
            lambda: self.at(p.other, p.z, here, p.t),
            self.last_in.at[2 * (p.depth - 1)],
            p.to_pair,
            10,
            only=self.pairs,
        )

    def last(self, target):
        p = self.p

        def write():
            for n in range(7):
                self.landed(self.last_in.at[n], 4 + n)
            mine = self.part[p.t, p.z, p.y, p.x, p.t, :, self.columns].astype(F32)
            rest = self.last_in[2 * (p.depth - 1)].astype(F32)
            for s in range(1, p.depth):
                mine += self.last_in[2 * (s - 1) + p.t].astype(F32)
                rest += self.last_in[2 * (s - 1) + p.other].astype(F32)
            target[p.t] = mine
            target[p.other] = rest

        write() if self.mine is None else pl.when(self.mine)(write)


def scatter_scratch(groups, depth, columns):
    vmem = pltpu.VMEM
    return [
        vmem((groups, depth, 2, 2, 16, columns), BF16),
        vmem((2, groups, depth, 16, columns), BF16),
        vmem((groups, depth, 16, columns), BF16),
        vmem((2 * depth - 1, 16, columns), BF16),
        pltpu.SemaphoreType.DMA((2, Scatter.COPIES)),
    ]


class Reduce(Copies):
    COPIES = 12

    def __init__(self, place, own, parts, sums, sems):
        super().__init__(sems)
        self.p, self.own, self.parts, self.sums = place, own, parts, sums

    def first(self):
        p = self.p
        self.parts[p.spot] = self.own[...]
        for offset in range(1, 8):
            self.start(
                lambda: self.own, self.parts.at[p.spot], p.level[offset], offset - 1
            )

    def second(self):
        p = self.p
        for n in range(7):
            self.landed(self.own, n)
        total = self.parts[0]
        for spot in range(1, 8):
            total += self.parts[spot]
        self.sums[p.z] = total
        for s in range(1, p.depth):
            self.start(
                lambda: self.sums.at[p.z], self.sums.at[p.z], {"dp": p.chips_z[s]}, 6 + s
            )

    def last(self):
        p = self.p
        for s in range(1, p.depth):
            self.landed(self.own, 6 + s)
        total = self.sums[0]
        for z in range(1, p.depth):
            total += self.sums[z]
        return total


class Woven:
    def __init__(self, place, owns, own_a, own_b, wa, wb, ga, gw, gains, gathers, scatters, targets):
        self.p = place
        self.owns, self.own_a, self.own_b = owns, own_a, own_b
        every, up, down = slice(0, 1024), slice(0, 1280), slice(1280, 2304)
        self.a = [Gather(place, own_a, wa, g, every, gathers[g]) for g in range(2)]
        self.up = Gather(place, own_b, wb, None, up, gathers[2])
        self.down = Gather(place, own_b, wb, None, down, gathers[3])
        self.down_grad = Scatter(place, gw, None, down, *scatters[0])
        self.up_grad = Scatter(place, gw, None, up, *scatters[1])
        self.a_grad = [Scatter(place, ga, g, every, *scatters[2 + g]) for g in range(2)]
        self.gains = gains
        self.da, self.dw = targets

    def before(self):
        query, key, value, slot, out_t, up, down_t = self.owns
        halves = lambda ref: ref[...].astype(BF16).reshape(2, 16, ref.shape[1])
        self.own_a[:, :, 0:256] = halves(query)
        self.own_a[:, :, 256:512] = halves(key)
        self.own_a[:, :, 512:768] = halves(value)
        self.own_a[:, :, 768:1024] = halves(slot)
        self.p.greet()
        self.a[0].first()
        self.a[1].first()
        self.own_b[:, :, 0:256] = halves(out_t)
        self.own_b[:, :, 256:1280] = halves(up)
        self.own_b[:, :, 1280:2304] = halves(down_t)

    def weights_a(self, g):
        one, two = self.a

        @pl.when(g == 0)
        def _():
            one.second()
            two.second()
            self.up.first()
            one.third()
            one.fourth()
            one.last()
            two.third()

        @pl.when(g == 1)
        def _():
            two.last()

    def mixing(self, g, i):
        steps = {
            (0, 0): (self.a[1].fourth, self.up.second, self.down.first),
            (1, 0): (self.up.third, self.down.second),
            (1, 2): (self.up.fourth,),
            (1, 3): (self.down.third,),
        }
        for (group, pair), calls in steps.items():

            @pl.when((g == group) & (i == pair))
            def _(calls=calls):
                for call in calls:
                    call()

    def weights_up(self):
        self.up.last()

    def feeding(self, r):
        pl.when(r == 1)(self.down.fourth)

    def weights_down(self):
        self.down.last()

    def grads_down(self):
        self.down_grad.first()

    def grads_up(self):
        self.up_grad.first()
        self.down_grad.second()

    def mixing_back(self, g, i):
        steps = {
            (0, 1): (self.up_grad.second,),
            (0, 2): (self.down_grad.third,),
            (0, 3): (self.up_grad.third,),
            (1, 0): (self.down_grad.fourth,),
            (1, 1): (self.up_grad.fourth, self.a_grad[0].second),
            (1, 3): (self.a_grad[0].third,),
        }
        for (group, pair), calls in steps.items():

            @pl.when((g == group) & (i == pair))
            def _(calls=calls):
                for call in calls:
                    call()

    def grads_a(self, g):
        for group in range(2):
            pl.when(g == group)(self.a_grad[group].first)

        @pl.when(g == 1)
        def _():
            self.a_grad[0].fourth()
            self.down_grad.last(self.dw.at[:, :, 1280:2304])
            self.up_grad.last(self.dw.at[:, :, 0:1280])

    def finishing(self, r):
        pl.when(r == 1)(self.a_grad[1].second)

    def after(self):
        self.gains.first()
        self.a_grad[1].third()
        self.gains.second()
        self.a_grad[0].last(self.da)
        self.a_grad[1].fourth()
        self.total = self.gains.last()
        self.a_grad[1].last(self.da)
        for copies in (
            *self.a, self.up, self.down, self.down_grad, self.up_grad, *self.a_grad, self.gains
        ):
            copies.left()


def woven_kernel(length, depth, *refs):
    refs = list(refs)
    take = lambda n: [refs.pop(0) for _ in range(n)]
    tok, cot, seg_rows, pad_rows, gain_one, gain_two, up_bias, down_bias = take(LAYER_INPUTS)
    owns = take(7)
    out, grad_out, da, dw, small_out = take(5)
    own_a, own_b, wa, wb, ga, gw, seg_row, pad_row = take(8)
    small, parts, sums, gain_sems = take(4)
    gathers = take(4)
    scatters = [take(5) for _ in range(4)]
    place = Place(depth)
    gains = Reduce(place, small, parts, sums, gain_sems)
    comm = Woven(place, owns, own_a, own_b, wa, wb, ga, gw, gains, gathers, scatters, (da, dw))
    first = lax.axis_index("tensor") == 0
    for rows, row in ((seg_rows, seg_row), (pad_rows, pad_row)):
        row[...] = jnp.where(first, rows[0:1, :], rows[1:2, :])
    layer_body(
        length, comm, tok, cot, seg_row, pad_row, gain_one, gain_two, up_bias, down_bias, wa, wb,
        out, grad_out, ga, gw, small, *refs,
    )
    small_out[...] = comm.total


def write_kernel(out_in, grad_in, da, dw, small, *refs):
    (
        out, grad_out, mixer_gain, query, key, value, slot, out_t, feed_gain, up, up_bias, down_t,
        down_bias, sems,
    ) = refs
    one = pltpu.make_async_copy(out_in, out, sems.at[0])
    two = pltpu.make_async_copy(grad_in, grad_out, sems.at[1])
    one.start()
    two.start()
    rows = lambda part: part.reshape(-1, part.shape[-1])
    query[...] = rows(da[:, :, 0:256])
    key[...] = rows(da[:, :, 256:512])
    value[...] = rows(da[:, :, 512:768])
    slot[...] = rows(da[:, :, 768:1024])
    out_t[...] = rows(dw[:, :, 0:256])
    up[...] = rows(dw[:, :, 256:1280])
    down_t[...] = rows(dw[:, :, 1280:2304])
    feed_gain[...] = small[0:1, :]
    mixer_gain[...] = small[1:2, :]
    down_bias[...] = small[2:3, :]
    for row in range(4):
        up_bias[:, row * 512 : (row + 1) * 512] = small[4 + row : 5 + row, :]
    one.wait()
    two.wait()


def write(out, grad_out, da, dw, small):
    shape = jax.ShapeDtypeStruct
    space = pl.BlockSpec(memory_space=pltpu.VMEM)
    far = pl.BlockSpec(memory_space=pl.ANY)
    width = out.shape[1]
    square, wide = shape((32, 256), F32), shape((32, 1024), F32)
    row = shape((1, width), F32)
    return pl.pallas_call(
        write_kernel,
        out_shape=(
            shape(out.shape, BF16),
            shape(out.shape, BF16),
            row,
            square,
            square,
            square,
            square,
            square,
            row,
            wide,
            shape((1, 4 * width), F32),
            wide,
            row,
        ),
        in_specs=[far, far, space, space, space],
        out_specs=(far, far) + (space,) * 11,
        scratch_shapes=[pltpu.SemaphoreType.DMA((2,))],
        name="write",
    )(out, grad_out, da, dw, small)


def woven(depth, tokens, cotangent, segments, padding, gains, biases, owns):
    length, width = tokens.shape
    shape = jax.ShapeDtypeStruct
    space = pl.BlockSpec(memory_space=pltpu.VMEM)
    vmem = pltpu.VMEM
    dma = pltpu.SemaphoreType.DMA
    full = lambda columns: vmem((2, depth, 2, 2, 2, 16, columns), BF16)
    return pl.pallas_call(
        functools.partial(woven_kernel, length, depth),
        out_shape=(
            shape((length, width), BF16),
            shape((length, width), BF16),
            shape((2, 16, 1024), F32),
            shape((2, 16, 2304), F32),
            shape((8, width), F32),
        ),
        in_specs=[space] * (LAYER_INPUTS + 7),
        out_specs=tuple([space] * 5),
        scratch_shapes=[
            vmem((2, 16, 1024), BF16),
            vmem((2, 16, 2304), BF16),
            full(1024),
            full(2304),
            full(1024),
            full(2304),
            vmem((1, length), jnp.int32),
            vmem((1, length), jnp.int32),
            vmem((8, width), F32),
            vmem((8, 8, width), F32),
            vmem((depth, 8, width), F32),
            dma((2, Reduce.COPIES)),
        ]
        + [dma((2, Gather.COPIES))] * 4
        + scatter_scratch(2, depth, 1024)
        + scatter_scratch(2, depth, 1280)
        + scatter_scratch(1, depth, 1024)
        + scatter_scratch(1, depth, 1024)
        + layer_scratch(length, width),
        compiler_params=pltpu.CompilerParams(
            collective_id=0, has_side_effects=True, vmem_limit_bytes=62 * 1024 * 1024
        ),
        name="woven",
    )(tokens, cotangent, segments, padding, *gains, *biases, *owns)


def per_device(
    direct,
    tokens,
    segment_ids,
    padding,
    mixer_gain,
    query_weight,
    key_weight,
    value_weight,
    slot_weight,
    out_weight,
    feed_gain,
    up_weight,
    up_bias,
    down_weight,
    down_bias,
    cotangent,
):
    gains = (mixer_gain[None], feed_gain[None])
    biases = (up_bias[None], down_bias[None])
    if direct:
        owns = (
            query_weight, key_weight, value_weight, slot_weight, out_weight.T, up_weight,
            down_weight.T,
        )
        depth = lax.axis_size("dp") // 4
        results = write(
            *woven(depth, tokens, cotangent, segment_ids, padding, gains, biases, owns)
        )
        (
            out, grad_out, gain_one, query, key, value, slot, out_t, gain_two, up, bias_one, down_t,
            bias_two,
        ) = results
        return (
            out, grad_out, gain_one[0], query, key, value, slot, out_t.T, gain_two[0], up,
            bias_one[0], down_t.T, bias_two[0],
        )
    own_a = jnp.concatenate([query_weight, key_weight, value_weight, slot_weight], 1)
    own_b = jnp.concatenate([out_weight.T, up_weight, down_weight.T], 1)
    wa, wb = (
        lax.all_gather(lax.all_gather(own.astype(BF16), "dp", axis=0, tiled=True), "tensor")
        for own in (own_a, own_b)
    )
    half = lax.axis_index("tensor")
    pick = lambda rows: lax.dynamic_slice_in_dim(rows, half, 1, 0)
    out, grad_out, ga, gw, small = layer(
        tokens, cotangent, pick(segment_ids), pick(padding), *gains, *biases, wa, wb
    )
    da, dw = (
        lax.psum_scatter(
            lax.psum_scatter(part.astype(F32), "tensor", scatter_dimension=0),
            "dp",
            scatter_dimension=0,
            tiled=True,
        )
        for part in (ga, gw)
    )
    small = lax.psum(small, ("dp", "tensor"))
    return (
        out,
        grad_out,
        small[1],
        da[:, 0:256],
        da[:, 256:512],
        da[:, 512:768],
        da[:, 768:1024],
        dw[:, 0:256].T,
        small[0],
        dw[:, 256:1280],
        small[4:8].reshape(-1),
        dw[:, 1280:2304].T,
        small[2],
    )


def solution(mesh):
    in_specs = (
        P(("dp", "tensor"), None),
        P("dp", None),
        P("dp", None),
        P(),
        P("dp", "tensor"),
        P("dp", "tensor"),
        P("dp", "tensor"),
        P("dp", "tensor"),
        P("tensor", "dp"),
        P(),
        P("dp", "tensor"),
        P(),
        P("tensor", "dp"),
        P(),
        P(("dp", "tensor"), None),
    )
    out_specs = (
        P(("dp", "tensor"), None),
        P(("dp", "tensor"), None),
        P(),
        P("dp", "tensor"),
        P("dp", "tensor"),
        P("dp", "tensor"),
        P("dp", "tensor"),
        P("tensor", "dp"),
        P(),
        P("dp", "tensor"),
        P(),
        P("tensor", "dp"),
        P(),
    )
    direct = mesh.shape["dp"] == 16 and mesh.shape["tensor"] == 2
    return jax.shard_map(
        functools.partial(per_device, direct),
        mesh=mesh,
        in_specs=in_specs,
        out_specs=out_specs,
        check_vma=False,
    )
```

```python
import functools
import math

import jax
import jax.numpy as jnp
from jax import lax
from jax.experimental import pallas as pl
from jax.experimental.pallas import tpu as pltpu
from jax.sharding import PartitionSpec as P

HEAD_DIM = 64
SLOTS = 64
CHUNK = 128
UNROLL = 4
GROUP = 256
TILE = 512
WIDE = 512

F32 = jnp.float32
BF16 = jnp.bfloat16
MESH = pl.DeviceIdType.MESH


def dot(left, right):
    return lax.dot_general(left, right, (((1,), (0,)), ((), ())), preferred_element_type=F32)


def dot_rt(left, right):
    return lax.dot_general(left, right, (((1,), (1,)), ((), ())), preferred_element_type=F32)


def dot_lt(left, right):
    return lax.dot_general(left, right, (((0,), (0,)), ((), ())), preferred_element_type=F32)


def twice(block):
    return jnp.concatenate([block, block], axis=1)


def standardise(rows):
    centred = rows - jnp.mean(rows, axis=-1, keepdims=True)
    scale = lax.rsqrt(jnp.mean(centred * centred, axis=-1, keepdims=True) + 1e-05)
    return centred * scale, scale


def head_stack(block):
    lane = lax.broadcasted_iota(jnp.int32, block.shape, 1) // HEAD_DIM
    zero = jnp.zeros_like(block)
    return jnp.concatenate([jnp.where(lane == h, block, zero) for h in range(4)], axis=0)


def diagonal(product):
    parts = [product[h * HEAD_DIM : (h + 1) * HEAD_DIM, :] for h in range(4)]
    lane = lax.broadcasted_iota(jnp.int32, parts[0].shape, 1) // HEAD_DIM
    kept = parts[3]
    for h in range(3):
        kept = jnp.where(lane == h, parts[h], kept)
    return kept


def over_heads(block, reduce, rest):
    halves = []
    lane = lax.broadcasted_iota(jnp.int32, (block.shape[0], 128), 1) < HEAD_DIM
    for j in range(block.shape[1] // 128):
        part = block[:, j * 128 : (j + 1) * 128]
        first = reduce(jnp.where(lane, part, rest), axis=1, keepdims=True)
        second = reduce(jnp.where(lane, rest, part), axis=1, keepdims=True)
        halves.append(jnp.where(lane, first, second))
    return jnp.concatenate(halves, axis=1)


def head_max(block):
    return over_heads(block, jnp.max, -jnp.inf)


def head_sum(block):
    return over_heads(block, jnp.sum, 0.0)


def head_pairs(product, allowed):
    parts = [product[h * CHUNK : (h + 1) * CHUNK, :] * allowed for h in range(4)]
    return jnp.concatenate(parts, axis=1).astype(BF16)


def flip_pairs(pairs):
    parts = [pairs[:, h * CHUNK : (h + 1) * CHUNK].T for h in range(4)]
    return jnp.concatenate(parts, axis=1)


def beside(*blocks):
    return jnp.concatenate(blocks, axis=1)


def above(*blocks):
    return jnp.concatenate(blocks, axis=0)


def flat(block):
    return block.reshape(-1, block.shape[-1])


def rows_to_columns(seg_row, pad_row, segc, keepc, length):
    segc[pl.ds(0, 8), :] = jnp.full((8, 128), -1.0, F32)
    segc[pl.ds(8 + length, 8), :] = jnp.full((8, 128), -2.0, F32)
    for c in range(length // CHUNK):
        here = slice(c * CHUNK, (c + 1) * CHUNK)
        seg = jnp.broadcast_to(seg_row[:, here].astype(F32), (CHUNK, CHUNK))
        pad = jnp.broadcast_to(pad_row[:, here].astype(F32), (CHUNK, CHUNK))
        segc[pl.ds(8 + c * CHUNK, CHUNK), :] = seg.T
        keepc[pl.ds(c * CHUNK, CHUNK), :] = 1.0 - pad.T


def normalise(r, tok, gain, n1):
    rows = pl.ds(pl.multiple_of(r * TILE, TILE), TILE)
    xhat, _ = standardise(tok[rows, :].astype(F32))
    n1[rows, :] = (xhat * gain[...]).astype(BF16)


def project(g, r, wa, keepc, n1, q, k, v, w):
    rows = pl.ds(pl.multiple_of(r * WIDE, WIDE), WIDE)
    out = dot(n1[rows, :], flat(wa[g]))
    q[g, rows, :] = out[:, 0:256].astype(BF16)
    k[g, rows, :] = out[:, 256:512].astype(BF16)
    v[g, rows, :] = out[:, 512:768].astype(BF16)
    w[g, rows, :] = (jnp.exp(out[:, 768:1024]) * twice(keepc[rows, :])).astype(BF16)


def chunk_masks(c, segc):
    base = pl.multiple_of(c * CHUNK, CHUNK)
    seg = segc[pl.ds(base + 8, CHUNK), :]
    across = seg.T
    row = lax.broadcasted_iota(jnp.int32, (CHUNK, CHUNK), 0)
    column = lax.broadcasted_iota(jnp.int32, (CHUNK, CHUNK), 1)
    same = seg == across
    causal = jnp.where(same & (column <= row), 1.0, 0.0)
    before = segc[pl.ds(base + 7, 1), :]
    first = segc[pl.ds(base + 8, 1), :]
    last = segc[pl.ds(base + 7 + CHUNK, 1), :]
    after = segc[pl.ds(base + 8 + CHUNK, 1), :]
    one = lambda test: jnp.where(test, 1.0, 0.0)
    return causal, dict(
        from_before=one(seg == before),
        to_after=one(seg == last),
        from_after=one(seg == after),
        to_before=one(seg == first),
        carry_on=one(before == last),
        carry_back=one(after == first),
    )


def mix_forward(
    g, i, segc, keepc, q, k, v, w, probs, inv, score, mixed, kw, wv, zsum, kw_all, wv_all, pt_all,
    mt_all,
):
    run = range(UNROLL)
    chunks = [UNROLL * i + n for n in run]
    rows = [pl.ds(pl.multiple_of(c * CHUNK, CHUNK), CHUNK) for c in chunks]
    masks = [chunk_masks(c, segc) for c in chunks]
    keep = [twice(keepc[r, :]) for r in rows]
    qc, kc, vc, wc = ([ref[g, r, :] for r in rows] for ref in (q, k, v, w))
    state_k, state_v, state_z = [kw[...]], [wv[...]], [zsum[0:1, :]]
    causal = [mask for mask, _ in masks]
    edge = [edges for _, edges in masks]
    come = [twice(edge[n]["from_before"]) for n in run]
    come_low = [come[n].astype(BF16) for n in run]
    pairs = [head_pairs(dot_rt(head_stack(qc[n]), kc[n]), causal[n]) for n in run]
    for n in run:
        carry = twice(edge[n]["carry_on"])
        wg = wc[n] * twice(edge[n]["to_after"]).astype(BF16)
        state_k.append(state_k[n] * carry + diagonal(dot_lt(kc[n], wg)))
        state_v.append(state_v[n] * carry + diagonal(dot_lt(wg, vc[n])))
        state_z.append(state_z[n] * carry + jnp.sum(wg.astype(F32), axis=0, keepdims=True))
    kw_low = [head_stack(state_k[n].astype(BF16)) for n in run]
    wv_low = [head_stack(state_v[n].astype(BF16)) for n in run]
    inverse = [
        1.0 / (dot(causal[n].astype(BF16), wc[n]) + come[n] * state_z[n] + (1.0 - keep[n]))
        for n in run
    ]
    scores = [
        dot(beside(pairs[n], qc[n] * come_low[n]), above(head_stack(wc[n]), kw_low[n]))
        * (inverse[n] * (HEAD_DIM**-0.5))
        for n in run
    ]
    powers = [jnp.exp(scores[n] - head_max(scores[n])) for n in run]
    chances = [powers[n] / head_sum(powers[n]) for n in run]
    ratio = [(chances[n] * inverse[n]).astype(BF16) for n in run]
    mixing = [head_pairs(dot_rt(head_stack(ratio[n]), wc[n]), causal[n]) for n in run]
    out = [
        dot(beside(mixing[n], ratio[n] * come_low[n]), above(head_stack(vc[n]), wv_low[n]))
        for n in run
    ]
    for n in run:
        r = rows[n]
        kw_all[g, chunks[n]] = diagonal(kw_low[n].T)
        wv_all[g, chunks[n]] = diagonal(wv_low[n].T)
        pt_all[g, r, :] = flip_pairs(pairs[n])
        mt_all[g, r, :] = flip_pairs(mixing[n])
        inv[g, r, :] = inverse[n]
        score[g, r, :] = scores[n]
        probs[g, r, :] = chances[n]
        mixed[g, r, :] = (out[n] * keep[n]).astype(BF16)
    kw[...] = state_k[-1]
    wv[...] = state_v[-1]
    zsum[...] = jnp.broadcast_to(state_z[-1], zsum.shape)


def mix_backward(
    g, i, segc, keepc, q, k, v, w, probs, inv, score, gm, rg, uq, zgrad, kw_all, wv_all, pt_all,
    mt_all, gy,
):
    run = range(UNROLL)
    chunks = [UNROLL * i + UNROLL - 1 - n for n in run]
    rows = [pl.ds(pl.multiple_of(c * CHUNK, CHUNK), CHUNK) for c in chunks]
    masks = [chunk_masks(c, segc) for c in chunks]
    qc, kc, vc, wc, grad, chances, inverse, scores, pairs_t, mixing_t = (
        [ref[g, r, :] for r in rows]
        for ref in (q, k, v, w, gm, probs, inv, score, pt_all, mt_all)
    )
    kw_t, wv_t = ([head_stack(ref[g, c]) for c in chunks] for ref in (kw_all, wv_all))
    state_v, state_k, state_z = [rg[...]], [uq[...]], [zgrad[0:1, :]]
    causal = [mask for mask, _ in masks]
    edge = [edges for _, edges in masks]
    come_low = [twice(edge[n]["from_before"]).astype(BF16) for n in run]
    late = [twice(edge[n]["from_after"]) for n in run]
    late_low = [late[n].astype(BF16) for n in run]
    back = [twice(edge[n]["to_before"]) for n in run]
    back_low = [back[n].astype(BF16) for n in run]
    carry = [twice(edge[n]["carry_back"]) for n in run]
    grads = [head_stack(grad[n]) for n in run]
    d_mixing = [head_pairs(dot_rt(grads[n], vc[n]), causal[n]) for n in run]
    d_chance = [
        dot(beside(d_mixing[n], grad[n] * come_low[n]), above(head_stack(wc[n]), wv_t[n]))
        * inverse[n]
        for n in run
    ]
    ratio = [(chances[n] * inverse[n]).astype(BF16) for n in run]
    ratios = [head_stack(ratio[n]) for n in run]
    for n in run:
        added = diagonal(dot_lt(ratio[n] * back_low[n], grad[n]))
        state_v.append(state_v[n] * carry[n] + added)
    rg_low = [head_stack(state_v[n].astype(BF16)) for n in run]
    w_late = [wc[n] * late_low[n] for n in run]
    gv = [dot(beside(mixing_t[n], w_late[n]), above(grads[n], rg_low[n])) for n in run]
    weighted = [d_chance[n] * chances[n] for n in run]
    d_score = [weighted[n] - chances[n] * head_sum(weighted[n]) for n in run]
    d_pw = [(d_score[n] * inverse[n] * (HEAD_DIM**-0.5)).astype(BF16) for n in run]
    d_total = [(weighted[n] + d_score[n] * scores[n]) * inverse[n] for n in run]
    d_pws = [head_stack(d_pw[n]) for n in run]
    d_pairs = [head_pairs(dot_rt(d_pws[n], wc[n]), causal[n]) for n in run]
    for n in run:
        added = diagonal(dot_lt(d_pw[n] * back_low[n], qc[n]))
        state_k.append(state_k[n] * carry[n] + added)
        added = jnp.sum(d_total[n] * back[n], axis=0, keepdims=True)
        state_z.append(state_z[n] * carry[n] + added)
    uq_low = [head_stack(state_k[n].astype(BF16)) for n in run]
    dw = []
    for n in run:
        z_high = d_total[n].astype(BF16)
        z_low = (d_total[n] - z_high.astype(F32)).astype(BF16)
        anti = -causal[n].T.astype(BF16)
        left = beside(
            flip_pairs(d_mixing[n]), pairs_t[n], vc[n] * late_low[n], kc[n] * late_low[n], anti, anti
        )
        right = above(ratios[n], d_pws[n], rg_low[n].T, uq_low[n].T, z_high, z_low)
        dw.append(dot(left, right) - late[n] * state_z[n])
    gq = [
        dot(beside(d_pairs[n], d_pw[n] * come_low[n]), above(head_stack(kc[n]), kw_t[n]))
        for n in run
    ]
    gk = [
        dot(beside(flip_pairs(d_pairs[n]), w_late[n]), above(head_stack(qc[n]), uq_low[n]))
        for n in run
    ]
    for n in run:
        gy[g, rows[n], 512:768] = gv[n].astype(BF16)
        gy[g, rows[n], 768:1024] = (dw[n] * wc[n].astype(F32)).astype(BF16)
        gy[g, rows[n], 0:256] = gq[n].astype(BF16)
        gy[g, rows[n], 256:512] = gk[n].astype(BF16)
    rg[...] = state_v[-1]
    uq[...] = state_k[-1]
    zgrad[...] = jnp.broadcast_to(state_z[-1], zgrad.shape)


def units(j):
    return j // 2 % 2, (j // 4 * 2 + j % 2) * 256


def feed_in(r, tok, gain, wb, mixed, n2, gh):
    rows = pl.ds(pl.multiple_of(r * TILE, TILE), TILE)
    hidden = tok[rows, :].astype(F32)
    for g in range(2):
        hidden += dot_rt(mixed[g, rows, :], flat(wb[g, ..., 0:256]))
    gh[rows, :] = hidden
    hat, _ = standardise(hidden)
    n2[rows, :] = (hat * gain[...]).astype(BF16)


def feed_up(part, r, up_bias, wb, n2, act, lin):
    rows = pl.ds(pl.multiple_of(r * TILE, TILE), TILE)
    normed = n2[rows, :]
    k0 = 0.7978845608
    k1 = k0 * 0.044715

    def linear_of(j):
        g, column = units(j)
        up = flat(wb[g, ..., 256 + column : 512 + column])
        bias = up_bias[:, g * 1024 + column : g * 1024 + column + 256]
        return dot(normed, up) + bias

    after = linear_of(4 * part)
    for j in range(4 * part, 4 * part + 4):
        linear = after
        if j < 4 * part + 3:
            after = linear_of(j + 1)
        square = linear * linear
        gate = 0.5 * jnp.tanh(linear * (square * k1 + k0)) + 0.5
        active = linear * gate
        slope = gate + active * (1.0 - gate) * (square * (6.0 * k1) + 2.0 * k0)
        g, column = units(j)
        act[g, rows, column : column + 256] = active.astype(BF16)
        lin[g, rows, column : column + 256] = slope.astype(BF16)


def feed_down(r, cot, gain, down_bias, wb, keepc, act, lin, gh, gm, small):
    rows = pl.ds(pl.multiple_of(r * TILE, TILE), TILE)
    grad = cot[rows, :]
    hidden = gh[rows, :]
    total = hidden + down_bias[...]
    back = jnp.zeros((TILE, 512), F32)

    def grad_of(j):
        g, column = divmod(j * 256, 1024)
        down = flat(wb[g, ..., 1280 + column : 1536 + column])
        return dot(grad, down) * lin[g, rows, column : column + 256].astype(F32)

    after = grad_of(0)
    for j in range(8):
        grad_low = after.astype(BF16)
        if j < 7:
            after = grad_of(j + 1)
        g, column = divmod(j * 256, 1024)
        lin[g, rows, column : column + 256] = grad_low
        row, column = 4 + j // 2, j % 2 * 256
        small[row : row + 1, column : column + 256] += jnp.sum(
            grad_low.astype(F32), axis=0, keepdims=True
        )
    for g in range(2):
        total += dot_rt(act[g, rows, :], flat(wb[g, ..., 1280:2304]))
        back += dot_rt(lin[g, rows, :], flat(wb[g, ..., 256:1280]))
    cot[rows, :] = total.astype(BF16)
    hat, scale = standardise(hidden)
    scaled = back * gain[...]
    inner = scaled - jnp.mean(scaled, axis=-1, keepdims=True)
    inner -= hat * jnp.mean(scaled * hat, axis=-1, keepdims=True)
    grad_f32 = grad.astype(F32)
    grad_hidden = grad_f32 + scale * inner
    gh[rows, :] = grad_hidden
    low = grad_hidden.astype(BF16)
    small[0:1, :] += jnp.sum(back * hat, axis=0, keepdims=True)
    small[2:3, :] += jnp.sum(grad_f32, axis=0, keepdims=True)
    keep = twice(keepc[rows, :])
    for g in range(2):
        gm[g, rows, :] = (dot(low, flat(wb[g, ..., 0:256])) * keep).astype(BF16)


def transpose_into(source, target, length):
    for r in range(length // 256):
        here = slice(r * 256, (r + 1) * 256)
        target[:, here] = source[here, :].astype(BF16).T


def weight_grad(left_t, right, target, g, target_column, columns):
    shape = target.shape[1:-1]
    block = min(columns, 512)

    def product(j):
        return dot(left_t[...], right[:, j * block : (j + 1) * block]).astype(BF16)

    after = product(0)
    for j in range(columns // block):
        here = after
        if (j + 1) * block < columns:
            after = product(j + 1)
        there = slice(target_column + j * block, target_column + (j + 1) * block)
        target[g, ..., there] = here.reshape(shape + (block,))


def finish(r, tok, gain, wa, gy, gh, small):
    rows = pl.ds(pl.multiple_of(r * WIDE, WIDE), WIDE)
    hat, scale = standardise(tok[rows, :].astype(F32))
    back = dot_rt(gy[0, rows, :], flat(wa[0])) + dot_rt(gy[1, rows, :], flat(wa[1]))
    scaled = back * gain[...]
    inner = scaled - jnp.mean(scaled, axis=-1, keepdims=True)
    inner -= hat * jnp.mean(scaled * hat, axis=-1, keepdims=True)
    tok[rows, :] = (gh[rows, :] + scale * inner).astype(BF16)
    small[1:2, :] += jnp.sum(back * hat, axis=0, keepdims=True)


class Quiet:
    def nothing(self, *at):
        pass

    before = enter = weights_a = projected = mixing = weights_up = feeding = weights_down = nothing
    grads_down = feeding_down = layer_out = grads_mid = grads_up = nothing
    mixing_back = mixed_back = grads_a = finishing = finished = after = nothing


LAYER_INPUTS = 6


def layer_body(
    length,
    comm,
    seg_row,
    pad_row,
    gain_one,
    gain_two,
    up_bias,
    down_bias,
    wa,
    wb,
    ga,
    gw,
    small,
    tok,
    cot,
    segc,
    keepc,
    n1,
    q,
    k,
    v,
    w,
    probs,
    inv,
    score,
    mixed,
    state_k,
    state_v,
    state_z,
    kw_all,
    wv_all,
    pt_all,
    mt_all,
    n2,
    act,
    lin,
    gh,
    gm,
    flip,
):
    runs, tiles = length // (UNROLL * CHUNK), length // TILE

    def clear():
        state_k[...] = jnp.zeros_like(state_k)
        state_v[...] = jnp.zeros_like(state_v)
        state_z[...] = jnp.zeros_like(state_z)

    comm.before()
    small[...] = jnp.zeros_like(small)
    rows_to_columns(seg_row, pad_row, segc, keepc, length)
    comm.enter()

    @pl.loop(0, tiles)
    def _(r):
        normalise(r, tok, gain_one, n1)

    transpose_into(cot, flip, length)

    @pl.loop(0, 2)
    def _(g):
        comm.weights_a(g)
        clear()

        @pl.loop(0, length // WIDE)
        def _(r):
            project(g, r, wa, keepc, n1, q, k, v, w)

        comm.projected(g)

        @pl.loop(0, runs)
        def _(i):
            comm.mixing(g, i)
            mix_forward(
                g, i, segc, keepc, q, k, v, w, probs, inv, score, mixed, state_k, state_v, state_z,
                kw_all, wv_all, pt_all, mt_all,
            )

    comm.weights_up(0)

    @pl.loop(0, tiles)
    def _(r):
        feed_in(r, tok, gain_two, wb, mixed, n2, gh)
        feed_up(0, r, up_bias, wb, n2, act, lin)

    comm.weights_up(1)

    @pl.loop(0, tiles)
    def _(r):
        comm.feeding(r)
        feed_up(1, r, up_bias, wb, n2, act, lin)

    for g in range(2):
        weight_grad(flip, act.at[g], gw, g, 1280, 1024)
    comm.grads_down()
    comm.weights_down()

    @pl.loop(0, tiles)
    def _(r):
        comm.feeding_down(r)
        feed_down(r, cot, gain_two, down_bias, wb, keepc, act, lin, gh, gm, small)

    comm.layer_out()
    transpose_into(n2, flip, length)
    weight_grad(flip, lin.at[0], gw, 0, 256, 1024)
    comm.grads_mid()
    weight_grad(flip, lin.at[1], gw, 1, 256, 1024)
    transpose_into(gh, flip, length)
    for g in range(2):
        weight_grad(flip, mixed.at[g], gw, g, 0, GROUP)
    comm.grads_up()
    transpose_into(n1, flip, length)

    @pl.loop(0, 2)
    def _(g):
        clear()

        @pl.loop(0, runs)
        def _(i):
            comm.mixing_back(g, i)
            mix_backward(
                g, runs - 1 - i, segc, keepc, q, k, v, w, probs, inv, score, gm, state_v, state_k,
                state_z, kw_all, wv_all, pt_all, mt_all, act,
            )

        comm.mixed_back(g)
        weight_grad(flip, act.at[g], ga, g, 0, 1024)
        comm.grads_a(g)

    @pl.loop(0, length // WIDE)
    def _(r):
        comm.finishing(r)
        finish(r, tok, gain_one, wa, act, gh, small)
        comm.finished(r)

    comm.after()


def layer_scratch(length, width):
    vmem = pltpu.VMEM
    chunks = length // CHUNK
    return [
        vmem((length + 16, 128), F32),
        vmem((length, 128), F32),
        vmem((length, width), BF16),
        vmem((2, length, GROUP), BF16),
        vmem((2, length, GROUP), BF16),
        vmem((2, length, GROUP), BF16),
        vmem((2, length, GROUP), BF16),
        vmem((2, length, GROUP), F32),
        vmem((2, length, GROUP), F32),
        vmem((2, length, GROUP), F32),
        vmem((2, length, GROUP), BF16),
        vmem((HEAD_DIM, GROUP), F32),
        vmem((HEAD_DIM, GROUP), F32),
        vmem((8, GROUP), F32),
        vmem((2, chunks, HEAD_DIM, GROUP), BF16),
        vmem((2, chunks, HEAD_DIM, GROUP), BF16),
        vmem((2, length, 4 * CHUNK), BF16),
        vmem((2, length, 4 * CHUNK), BF16),
        vmem((length, width), BF16),
        vmem((2, length, 1024), BF16),
        vmem((2, length, 1024), BF16),
        vmem((length, width), F32),
        vmem((2, length, GROUP), BF16),
        vmem((width, length), BF16),
    ]


def layer_kernel(length, tokens, cotangent, *refs):
    inputs, (out, grad_out), rest = refs[: LAYER_INPUTS + 2], refs[8:10], refs[10:]
    grad_out[...] = tokens[...]
    out[...] = cotangent[...]
    ga, gw, small = rest[:3]
    layer_body(length, Quiet(), *inputs, ga, gw, small, grad_out, out, *rest[3:])


def layer(tokens, cotangent, seg_row, pad_row, gain_one, gain_two, up_bias, down_bias, wa, wb):
    length, width = tokens.shape
    shape = jax.ShapeDtypeStruct
    cut = lambda full: full.reshape(2, -1, 2, 2, 2, 16, full.shape[-1])
    wa, wb = cut(wa), cut(wb)
    space = pl.BlockSpec(memory_space=pltpu.VMEM)
    out, grad_out, ga, gw, small = pl.pallas_call(
        functools.partial(layer_kernel, length),
        out_shape=(
            shape((length, width), BF16),
            shape((length, width), BF16),
            shape(wa.shape, BF16),
            shape(wb.shape, BF16),
            shape((8, width), F32),
        ),
        in_specs=[space] * 10,
        out_specs=tuple([space] * 5),
        scratch_shapes=layer_scratch(length, width),
        compiler_params=pltpu.CompilerParams(vmem_limit_bytes=62 * 1024 * 1024),
        name="layer",
    )(tokens, cotangent, seg_row, pad_row, gain_one, gain_two, up_bias, down_bias, wa, wb)
    whole = lambda full: full.reshape(2, width, full.shape[-1])
    return out, grad_out, whole(ga), whole(gw), small


class Place:
    def __init__(self, depth):
        index = lax.axis_index("dp")
        t = lax.axis_index("tensor")
        x, y, z = lax.rem(index, 2), lax.rem(index // 2, 2), index // 4
        self.depth = depth
        self.x, self.y, self.z, self.t, self.other = x, y, z, t, 1 - t
        self.near = (y + t * (1 - 2 * y), x + (1 - t) * (1 - 2 * x))
        self.next = (y + (1 - t) * (1 - 2 * y), x + t * (1 - 2 * x))
        self.far = (1 - y, 1 - x)
        chip = lambda z, y, x: (z * 2 + y) * 2 + x
        self.levels = [lax.rem(z + s, depth) for s in range(depth)]
        self.chips_z = [chip(level, y, x) for level in self.levels]
        self.to_near = {"dp": chip(z, *self.near)}
        self.to_next = {"dp": chip(z, *self.next)}
        self.to_pair = {"tensor": self.other}
        self.spot = (y * 2 + x) * 2 + t
        flip = lambda value, bit: value + bit * (1 - 2 * value)
        self.level = [
            {
                "dp": chip(z, flip(y, offset // 4), flip(x, offset // 2 % 2)),
                "tensor": flip(t, offset % 2),
            }
            for offset in range(8)
        ]

    def along_z(self, step, core):
        return {"dp": self.chips_z[step], "tensor": core}

    def friends(self):
        along = [self.along_z(s, core) for s in range(1, self.depth) for core in range(2)]
        return self.level[1:] + along

    def knock(self):
        barrier = pltpu.get_barrier_semaphore()
        for friend in self.friends():
            pl.semaphore_signal(barrier, inc=1, device_id=friend, device_id_type=MESH)

    def enter(self):
        pl.semaphore_wait(pltpu.get_barrier_semaphore(), len(self.friends()))


class Copies:
    def __init__(self, sems):
        self.sems = sems
        self.started = []

    def build(self, source, target, device, out_sem, in_sem):
        return pltpu.make_async_remote_copy(
            src_ref=source,
            dst_ref=target,
            send_sem=self.sems.at[0, out_sem],
            recv_sem=self.sems.at[1, in_sem],
            device_id=device,
            device_id_type=MESH,
        )

    def start(self, source, target, device, number, in_sem=None, only=None):
        def begin():
            landing = number if in_sem is None else in_sem
            self.build(source(), target, device, number, landing).start()

        begin() if only is None else pl.when(only)(begin)
        self.started.append((source, number, only))

    def landed(self, target, number, only=None):
        def wait():
            self.build(target, target, {"tensor": 0}, number, number).wait_recv()

        wait() if only is None else pl.when(only)(wait)

    def left(self):
        for source, number, only in self.started:

            def wait(source=source, number=number):
                part = source()
                self.build(part, part, {"tensor": 0}, number, number).wait_send()

            wait() if only is None else pl.when(only)(wait)


class Gather(Copies):
    COPIES = 14

    def __init__(self, place, own, full, group, columns, sems):
        super().__init__(sems)
        self.p, self.own, self.full, self.columns = place, own, full, columns
        self.group = group
        self.groups = slice(None) if group is None else slice(group, group + 1)
        self.mine = None if group is None else place.t == group
        self.pairs = None if group is None else place.t != group

    def at(self, g, z, spot, half):
        return self.full.at[g, z, spot[0], spot[1], half, :, self.columns]

    def block(self, spot, half):
        return self.at(self.groups, slice(None), spot, half)

    def forward(self, spot, device, number):
        block = lambda: self.block(spot, self.p.t)
        self.start(block, block(), device, number)

    def first(self):
        p = self.p
        here = (p.y, p.x)
        for s in range(1, p.depth):
            for core in range(2):
                self.start(
                    lambda core=core: self.own.at[core, :, self.columns],
                    self.at(p.t, p.z, here, core),
                    p.along_z(s, core),
                    2 * (s - 1) + core,
                    2 * (s - 1) + p.t,
                    only=self.mine,
                )
        self.start(
            lambda: self.own.at[p.other, :, self.columns],
            self.at(p.t, p.z, here, p.other),
            p.to_pair,
            6,
            only=self.mine,
        )

        def keep():
            self.full[p.t, p.z, p.y, p.x, p.t, :, self.columns] = self.own[p.t, :, self.columns]

        keep() if self.mine is None else pl.when(self.mine)(keep)

    def second(self):
        p = self.p
        here = (p.y, p.x)
        for n in range(6):
            if self.group is None or n % 2 == self.group:
                self.landed(self.at(p.t, p.z, here, p.t), n)
        self.landed(self.at(p.t, p.z, here, p.t), 6, only=self.pairs)
        self.forward(here, p.to_near, 7)
        self.forward(here, p.to_next, 8)
        self.forward(here, p.to_pair, 9)

    def third(self):
        p = self.p
        self.landed(self.block(p.near, p.t), 7)
        self.forward(p.near, p.to_next, 10)
        self.forward(p.near, p.to_pair, 11)
        self.landed(self.block(p.next, p.t), 8)
        self.forward(p.next, p.to_pair, 12)

    def fourth(self):
        p = self.p
        self.landed(self.block(p.far, p.t), 10)
        self.forward(p.far, p.to_pair, 13)

    def last(self):
        p = self.p
        for n in (9, 11, 12, 13):
            self.landed(self.block((p.y, p.x), p.other), n)


class Scatter(Copies):
    COPIES = 11

    def __init__(self, place, part, group, columns, pair_in, near_in, next_in, last_in, sems):
        super().__init__(sems)
        self.p, self.part, self.columns = place, part, columns
        self.pair_in, self.near_in, self.next_in, self.last_in = pair_in, near_in, next_in, last_in
        self.group = group
        self.groups = slice(None) if group is None else slice(group, group + 1)
        self.mine = None if group is None else place.t == group
        self.pairs = None if group is None else place.t != group

    def at(self, g, z, spot, half):
        return self.part.at[g, z, spot[0], spot[1], half, :, self.columns]

    def block(self, spot, half):
        return self.at(self.groups, slice(None), spot, half)

    def add(self, spot, landed):
        p = self.p
        here = (self.groups, slice(None), spot[0], spot[1], p.t, slice(None), self.columns)
        self.part[here] = (self.part[here].astype(F32) + landed.astype(F32)).astype(BF16)

    def first(self):
        p = self.p
        self.start(
            lambda: self.part.at[self.groups, :, :, :, p.other, :, self.columns],
            self.pair_in,
            p.to_pair,
            0,
        )

    def second(self):
        p = self.p
        self.landed(self.pair_in, 0)
        for spot, number in ((p.far, 1), (p.near, 2)):
            self.add(spot, self.pair_in[:, :, spot[0], spot[1]])
            self.start(
                lambda spot=spot: self.block(spot, p.t),
                self.near_in.at[number - 1],
                p.to_near,
                number,
            )
        for spot in (p.next, (p.y, p.x)):
            self.add(spot, self.pair_in[:, :, spot[0], spot[1]])

    def third(self):
        p = self.p
        self.landed(self.near_in.at[0], 1)
        self.add(p.next, self.near_in[0])
        self.start(lambda: self.block(p.next, p.t), self.next_in, p.to_next, 3)
        self.landed(self.near_in.at[1], 2)
        self.add((p.y, p.x), self.near_in[1])

    def fourth(self):
        p = self.p
        here = (p.y, p.x)
        self.landed(self.next_in, 3)
        self.add(here, self.next_in[...])
        for s in range(1, p.depth):
            for core in range(2) if self.group is None else (self.group,):
                self.start(
                    lambda s=s, core=core: self.at(core, p.levels[s], here, p.t),
                    self.last_in.at[2 * (s - 1) + p.t],
                    p.along_z(s, core),
                    4 + 2 * (s - 1) + core,
                    4 + 2 * (s - 1) + p.t,
                )
        self.start(
            lambda: self.at(p.other, p.z, here, p.t),
            self.last_in.at[2 * (p.depth - 1)],
            p.to_pair,
            10,
            only=self.pairs,
        )

    def last(self, target):
        p = self.p

        def write():
            for n in range(7):
                self.landed(self.last_in.at[n], 4 + n)
            mine = self.part[p.t, p.z, p.y, p.x, p.t, :, self.columns].astype(F32)
            rest = self.last_in[2 * (p.depth - 1)].astype(F32)
            for s in range(1, p.depth):
                mine += self.last_in[2 * (s - 1) + p.t].astype(F32)
                rest += self.last_in[2 * (s - 1) + p.other].astype(F32)
            target[p.t] = mine
            target[p.other] = rest

        write() if self.mine is None else pl.when(self.mine)(write)


def scatter_scratch(groups, depth, columns):
    vmem = pltpu.VMEM
    return [
        vmem((groups, depth, 2, 2, 16, columns), BF16),
        vmem((2, groups, depth, 16, columns), BF16),
        vmem((groups, depth, 16, columns), BF16),
        vmem((2 * depth - 1, 16, columns), BF16),
        pltpu.SemaphoreType.DMA((2, Scatter.COPIES)),
    ]


class Reduce(Copies):
    COPIES = 12

    def __init__(self, place, own, parts, sums, sems):
        super().__init__(sems)
        self.p, self.own, self.parts, self.sums = place, own, parts, sums

    def first(self):
        p = self.p
        self.parts[p.spot] = self.own[...]
        for offset in range(1, 8):
            self.start(
                lambda: self.own, self.parts.at[p.spot], p.level[offset], offset - 1
            )

    def second(self):
        p = self.p
        for n in range(7):
            self.landed(self.own, n)
        total = self.parts[0]
        for spot in range(1, 8):
            total += self.parts[spot]
        self.sums[p.z] = total
        for s in range(1, p.depth):
            self.start(
                lambda: self.sums.at[p.z], self.sums.at[p.z], {"dp": p.chips_z[s]}, 6 + s
            )

    def last(self):
        p = self.p
        for s in range(1, p.depth):
            self.landed(self.own, 6 + s)
        total = self.sums[0]
        for z in range(1, p.depth):
            total += self.sums[z]
        return total


class Woven:
    def __init__(
        self, place, owns, ends, own_a, own_b, wa, wb, ga, gw, gains, gathers, scatters, targets
    ):
        self.p = place
        self.owns, self.own_a, self.own_b = owns, own_a, own_b
        self.tokens, self.cotangent, self.out, self.grad_out, self.tok, self.cot, self.io = ends
        every = slice(0, 1024)
        self.a = [Gather(place, own_a, wa, g, every, gathers[g]) for g in range(2)]
        self.b = [
            Gather(place, own_b, wb, None, slice(768 * n, 768 * n + 768), gathers[2 + n])
            for n in range(3)
        ]
        self.down_grad = Scatter(place, gw, None, slice(1280, 2304), *scatters[0])
        self.up_grad = Scatter(place, gw, None, slice(0, 1280), *scatters[1])
        self.a_grad = [Scatter(place, ga, 0, every, *scatters[2])]
        self.a_grad += [
            Scatter(place, ga, 1, slice(512 * n, 512 * n + 512), *scatters[3 + n])
            for n in range(2)
        ]
        self.gains = gains
        self.da, self.dw = targets

    def table(self, at, steps):
        for place, calls in steps.items():
            here = None
            for value, wanted in zip(at, place):
                here = (value == wanted) if here is None else here & (value == wanted)

            @pl.when(here)
            def _(calls=calls):
                for call in calls:
                    call()

    def copy(self, n):
        here, there = (
            (self.tokens, self.tok),
            (self.cotangent, self.cot),
            (self.cot, self.out),
        )[n]
        return pltpu.make_async_copy(here, there, self.io.at[n])

    def copy_grad(self, r):
        rows = pl.ds(pl.multiple_of(r * WIDE, WIDE), WIDE)
        return pltpu.make_async_copy(self.tok.at[rows], self.grad_out.at[rows], self.io.at[3 + r])

    def before(self):
        self.p.knock()
        self.copy(0).start()
        self.copy(1).start()
        query, key, value, slot, out_t, up, down_t = self.owns
        halves = lambda ref: ref[...].astype(BF16).reshape(2, 16, ref.shape[1])
        self.own_a[:, :, 0:256] = halves(query)
        self.own_a[:, :, 256:512] = halves(key)
        self.own_a[:, :, 512:768] = halves(value)
        self.own_a[:, :, 768:1024] = halves(slot)
        self.own_b[:, :, 0:256] = halves(out_t)
        self.own_b[:, :, 256:1280] = halves(up)
        self.own_b[:, :, 1280:2304] = halves(down_t)

    def enter(self):
        self.p.enter()
        self.a[0].first()
        self.a[1].first()
        self.copy(0).wait()
        self.copy(1).wait()

    def weights_a(self, g):
        one, two = self.a
        b = self.b
        self.table(
            (g,),
            {
                (0,): (
                    one.second, b[0].first, two.second, one.third, b[1].first, two.third,
                    one.fourth, b[0].second, one.last,
                ),
                (1,): (two.last, b[0].third),
            },
        )

    def projected(self, g):
        self.table((g,), {(0,): (self.a[1].fourth,)})

    def mixing(self, g, i):
        b = self.b
        self.table((g, i), {(0, 1): (b[1].second, b[2].first), (1, 1): (b[0].fourth, b[2].second)})

    def weights_up(self, part):
        b = self.b
        if part == 0:
            b[1].third()
            b[0].last()
        else:
            b[1].fourth()
            b[1].last()

    def feeding(self, r):
        self.table((r,), {(0,): (self.b[2].third,)})

    def grads_down(self):
        self.down_grad.first()
        self.b[2].fourth()

    def weights_down(self):
        self.b[2].last()

    def feeding_down(self, r):
        self.table((r,), {(1,): (self.down_grad.second,)})

    def layer_out(self):
        self.copy(2).start()

    def grads_mid(self):
        pass

    def grads_up(self):
        self.up_grad.first()
        self.down_grad.third()

    def mixing_back(self, g, i):
        self.table(
            (g, i),
            {(0, 1): (self.up_grad.second,), (1, 1): (self.a_grad[0].second,)},
        )

    def mixed_back(self, g):
        self.table((g,), {(0,): (self.down_grad.fourth,), (1,): (self.up_grad.third,)})

    def grads_a(self, g):
        one, two, three = self.a_grad
        self.table((g,), {(0,): (one.first,), (1,): (two.first, three.first)})

    def finishing(self, r):
        one, two, three = self.a_grad
        self.table((r,), {(1,): (two.second, one.third)})

    def finished(self, r):
        self.copy_grad(r).start()

    def after(self):
        one, two, three = self.a_grad
        three.second()
        self.gains.first()
        self.down_grad.last(self.dw.at[:, :, 1280:2304])
        self.up_grad.fourth()
        two.third()
        one.fourth()
        self.gains.second()
        three.third()
        two.fourth()
        three.fourth()
        self.up_grad.last(self.dw.at[:, :, 0:1280])
        one.last(self.da)
        self.total = self.gains.last()
        two.last(self.da.at[:, :, 0:512])
        three.last(self.da.at[:, :, 512:1024])
        for copies in (*self.a, *self.b, self.down_grad, self.up_grad, *self.a_grad, self.gains):
            copies.left()
        self.copy(2).wait()
        for r in range(2):
            self.copy_grad(r).wait()


def woven_kernel(length, depth, *refs):
    refs = list(refs)
    take = lambda n: [refs.pop(0) for _ in range(n)]
    tokens, cotangent, seg_rows, pad_rows = take(4)
    layer_inputs = take(4)
    owns = take(7)
    out, grad_out, da, dw, small_out = take(5)
    tok, cot, io, own_a, own_b, wa, wb, ga, gw, seg_row, pad_row = take(11)
    small, parts, sums, gain_sems = take(4)
    gathers = take(5)
    scatters = [take(5) for _ in range(5)]
    place = Place(depth)
    gains = Reduce(place, small, parts, sums, gain_sems)
    ends = (tokens, cotangent, out, grad_out, tok, cot, io)
    comm = Woven(
        place, owns, ends, own_a, own_b, wa, wb, ga, gw, gains, gathers, scatters, (da, dw)
    )
    first = lax.axis_index("tensor") == 0
    for rows, row in ((seg_rows, seg_row), (pad_rows, pad_row)):
        row[...] = jnp.where(first, rows[0:1, :], rows[1:2, :])
    layer_body(
        length, comm, seg_row, pad_row, *layer_inputs, wa, wb, ga, gw, small, tok, cot, *refs
    )
    small_out[...] = comm.total


def write_kernel(out_in, grad_in, da, dw, small, *refs):
    (
        out, grad_out, mixer_gain, query, key, value, slot, out_t, feed_gain, up, up_bias, down_t,
        down_bias,
    ) = refs
    out[...] = out_in[...]
    grad_out[...] = grad_in[...]
    rows = lambda part: part.reshape(-1, part.shape[-1])
    query[...] = rows(da[:, :, 0:256])
    key[...] = rows(da[:, :, 256:512])
    value[...] = rows(da[:, :, 512:768])
    slot[...] = rows(da[:, :, 768:1024])
    out_t[...] = rows(dw[:, :, 0:256])
    up[...] = rows(dw[:, :, 256:1280])
    down_t[...] = rows(dw[:, :, 1280:2304])
    feed_gain[...] = small[0:1, :]
    mixer_gain[...] = small[1:2, :]
    down_bias[...] = small[2:3, :]
    for row in range(4):
        up_bias[:, row * 512 : (row + 1) * 512] = small[4 + row : 5 + row, :]


def write(out, grad_out, da, dw, small):
    shape = jax.ShapeDtypeStruct
    space = pl.BlockSpec(memory_space=pltpu.VMEM)
    width = out.shape[1]
    square, wide = shape((32, 256), F32), shape((32, 1024), F32)
    row = shape((1, width), F32)
    return pl.pallas_call(
        write_kernel,
        out_shape=(
            shape(out.shape, BF16),
            shape(out.shape, BF16),
            row,
            square,
            square,
            square,
            square,
            square,
            row,
            wide,
            shape((1, 4 * width), F32),
            wide,
            row,
        ),
        in_specs=[space] * 5,
        out_specs=(space,) * 13,
        name="write",
    )(out, grad_out, da, dw, small)


def woven(depth, tokens, cotangent, segments, padding, gains, biases, owns):
    length, width = tokens.shape
    shape = jax.ShapeDtypeStruct
    space = pl.BlockSpec(memory_space=pltpu.VMEM)
    far = pl.BlockSpec(memory_space=pl.ANY)
    vmem = pltpu.VMEM
    dma = pltpu.SemaphoreType.DMA
    full = lambda columns: vmem((2, depth, 2, 2, 2, 16, columns), BF16)
    return pl.pallas_call(
        functools.partial(woven_kernel, length, depth),
        out_shape=(
            shape((length, width), BF16),
            shape((length, width), BF16),
            shape((2, 16, 1024), F32),
            shape((2, 16, 2304), F32),
            shape((8, width), F32),
        ),
        in_specs=[far, far] + [space] * 13,
        out_specs=(far, far, space, space, space),
        scratch_shapes=[
            vmem((length, width), BF16),
            vmem((length, width), BF16),
            dma((5,)),
            vmem((2, 16, 1024), BF16),
            vmem((2, 16, 2304), BF16),
            full(1024),
            full(2304),
            full(1024),
            full(2304),
            vmem((1, length), jnp.int32),
            vmem((1, length), jnp.int32),
            vmem((8, width), F32),
            vmem((8, 8, width), F32),
            vmem((depth, 8, width), F32),
            dma((2, Reduce.COPIES)),
        ]
        + [dma((2, Gather.COPIES))] * 5
        + scatter_scratch(2, depth, 1024)
        + scatter_scratch(2, depth, 1280)
        + scatter_scratch(1, depth, 1024)
        + scatter_scratch(1, depth, 512)
        + scatter_scratch(1, depth, 512)
        + layer_scratch(length, width),
        compiler_params=pltpu.CompilerParams(
            collective_id=0, has_side_effects=True, vmem_limit_bytes=63 * 1024 * 1024
        ),
        name="woven",
    )(tokens, cotangent, segments, padding, *gains, *biases, *owns)


def per_device(
    direct,
    tokens,
    segment_ids,
    padding,
    mixer_gain,
    query_weight,
    key_weight,
    value_weight,
    slot_weight,
    out_weight,
    feed_gain,
    up_weight,
    up_bias,
    down_weight,
    down_bias,
    cotangent,
):
    gains = (mixer_gain[None], feed_gain[None])
    biases = (up_bias[None], down_bias[None])
    if direct:
        owns = (
            query_weight, key_weight, value_weight, slot_weight, out_weight.T, up_weight,
            down_weight.T,
        )
        depth = lax.axis_size("dp") // 4
        results = write(
            *woven(depth, tokens, cotangent, segment_ids, padding, gains, biases, owns)
        )
        (
            out, grad_out, gain_one, query, key, value, slot, out_t, gain_two, up, bias_one, down_t,
            bias_two,
        ) = results
        return (
            out, grad_out, gain_one[0], query, key, value, slot, out_t.T, gain_two[0], up,
            bias_one[0], down_t.T, bias_two[0],
        )
    own_a = jnp.concatenate([query_weight, key_weight, value_weight, slot_weight], 1)
    own_b = jnp.concatenate([out_weight.T, up_weight, down_weight.T], 1)
    wa, wb = (
        lax.all_gather(lax.all_gather(own.astype(BF16), "dp", axis=0, tiled=True), "tensor")
        for own in (own_a, own_b)
    )
    half = lax.axis_index("tensor")
    pick = lambda rows: lax.dynamic_slice_in_dim(rows, half, 1, 0)
    out, grad_out, ga, gw, small = layer(
        tokens, cotangent, pick(segment_ids), pick(padding), *gains, *biases, wa, wb
    )
    da, dw = (
        lax.psum_scatter(
            lax.psum_scatter(part.astype(F32), "tensor", scatter_dimension=0),
            "dp",
            scatter_dimension=0,
            tiled=True,
        )
        for part in (ga, gw)
    )
    small = lax.psum(small, ("dp", "tensor"))
    return (
        out,
        grad_out,
        small[1],
        da[:, 0:256],
        da[:, 256:512],
        da[:, 512:768],
        da[:, 768:1024],
        dw[:, 0:256].T,
        small[0],
        dw[:, 256:1280],
        small[4:8].reshape(-1),
        dw[:, 1280:2304].T,
        small[2],
    )


def solution(mesh):
    in_specs = (
        P(("dp", "tensor"), None),
        P("dp", None),
        P("dp", None),
        P(),
        P("dp", "tensor"),
        P("dp", "tensor"),
        P("dp", "tensor"),
        P("dp", "tensor"),
        P("tensor", "dp"),
        P(),
        P("dp", "tensor"),
        P(),
        P("tensor", "dp"),
        P(),
        P(("dp", "tensor"), None),
    )
    out_specs = (
        P(("dp", "tensor"), None),
        P(("dp", "tensor"), None),
        P(),
        P("dp", "tensor"),
        P("dp", "tensor"),
        P("dp", "tensor"),
        P("dp", "tensor"),
        P("tensor", "dp"),
        P(),
        P("dp", "tensor"),
        P(),
        P("tensor", "dp"),
        P(),
    )
    direct = mesh.shape["dp"] == 16 and mesh.shape["tensor"] == 2
    return jax.shard_map(
        functools.partial(per_device, direct),
        mesh=mesh,
        in_specs=in_specs,
        out_specs=out_specs,
        check_vma=False,
    )
```

```python
import functools
import math

import jax
import jax.numpy as jnp
from jax import lax
from jax.experimental import pallas as pl
from jax.experimental.pallas import tpu as pltpu
from jax.sharding import PartitionSpec as P

HEAD_DIM = 64
SLOTS = 64
CHUNK = 128
UNROLL = 4
GROUP = 256
TILE = 512
WIDE = 512
LAST = 256

F32 = jnp.float32
BF16 = jnp.bfloat16
MESH = pl.DeviceIdType.MESH


def dot(left, right):
    return lax.dot_general(left, right, (((1,), (0,)), ((), ())), preferred_element_type=F32)


def dot_rt(left, right):
    return lax.dot_general(left, right, (((1,), (1,)), ((), ())), preferred_element_type=F32)


def dot_lt(left, right):
    return lax.dot_general(left, right, (((0,), (0,)), ((), ())), preferred_element_type=F32)


def twice(block):
    return jnp.concatenate([block, block], axis=1)


def standardise(rows):
    centred = rows - jnp.mean(rows, axis=-1, keepdims=True)
    scale = lax.rsqrt(jnp.mean(centred * centred, axis=-1, keepdims=True) + 1e-05)
    return centred * scale, scale


def head_stack(block):
    lane = lax.broadcasted_iota(jnp.int32, block.shape, 1) // HEAD_DIM
    zero = jnp.zeros_like(block)
    return jnp.concatenate([jnp.where(lane == h, block, zero) for h in range(4)], axis=0)


def diagonal(product):
    parts = [product[h * HEAD_DIM : (h + 1) * HEAD_DIM, :] for h in range(4)]
    lane = lax.broadcasted_iota(jnp.int32, parts[0].shape, 1) // HEAD_DIM
    kept = parts[3]
    for h in range(3):
        kept = jnp.where(lane == h, parts[h], kept)
    return kept


def over_heads(block, reduce, rest):
    halves = []
    lane = lax.broadcasted_iota(jnp.int32, (block.shape[0], 128), 1) < HEAD_DIM
    for j in range(block.shape[1] // 128):
        part = block[:, j * 128 : (j + 1) * 128]
        first = reduce(jnp.where(lane, part, rest), axis=1, keepdims=True)
        second = reduce(jnp.where(lane, rest, part), axis=1, keepdims=True)
        halves.append(jnp.where(lane, first, second))
    return jnp.concatenate(halves, axis=1)


def head_max(block):
    return over_heads(block, jnp.max, -jnp.inf)


def head_sum(block):
    return over_heads(block, jnp.sum, 0.0)


def head_pairs(product, allowed):
    parts = [product[h * CHUNK : (h + 1) * CHUNK, :] * allowed for h in range(4)]
    return jnp.concatenate(parts, axis=1).astype(BF16)


def flip_pairs(pairs):
    parts = [pairs[:, h * CHUNK : (h + 1) * CHUNK].T for h in range(4)]
    return jnp.concatenate(parts, axis=1)


def beside(*blocks):
    return jnp.concatenate(blocks, axis=1)


def above(*blocks):
    return jnp.concatenate(blocks, axis=0)


def flat(block):
    return block.reshape(-1, block.shape[-1])


def rows_to_columns(seg_row, pad_row, segc, keepc, length):
    segc[pl.ds(0, 8), :] = jnp.full((8, 128), -1.0, F32)
    segc[pl.ds(8 + length, 8), :] = jnp.full((8, 128), -2.0, F32)
    for c in range(length // CHUNK):
        here = slice(c * CHUNK, (c + 1) * CHUNK)
        seg = jnp.broadcast_to(seg_row[:, here].astype(F32), (CHUNK, CHUNK))
        pad = jnp.broadcast_to(pad_row[:, here].astype(F32), (CHUNK, CHUNK))
        segc[pl.ds(8 + c * CHUNK, CHUNK), :] = seg.T
        keepc[pl.ds(c * CHUNK, CHUNK), :] = 1.0 - pad.T


def normalise(r, tok, gain, n1):
    rows = pl.ds(pl.multiple_of(r * TILE, TILE), TILE)
    xhat, _ = standardise(tok[rows, :].astype(F32))
    n1[rows, :] = (xhat * gain[...]).astype(BF16)


def project_qk(g, r, wa, n1, q, k):
    rows = pl.ds(pl.multiple_of(r * WIDE, WIDE), WIDE)
    out = dot(n1[rows, :], flat(wa[g, ..., 0:512]))
    q[g, rows, :] = out[:, 0:256].astype(BF16)
    k[g, rows, :] = out[:, 256:512].astype(BF16)


def project_vw(g, r, wa, keepc, n1, v, w):
    rows = pl.ds(pl.multiple_of(r * WIDE, WIDE), WIDE)
    out = dot(n1[rows, :], flat(wa[g, ..., 512:1024]))
    v[g, rows, :] = out[:, 0:256].astype(BF16)
    w[g, rows, :] = (jnp.exp(out[:, 256:512]) * twice(keepc[rows, :])).astype(BF16)


def chunk_masks(c, segc):
    base = pl.multiple_of(c * CHUNK, CHUNK)
    seg = segc[pl.ds(base + 8, CHUNK), :]
    across = seg.T
    row = lax.broadcasted_iota(jnp.int32, (CHUNK, CHUNK), 0)
    column = lax.broadcasted_iota(jnp.int32, (CHUNK, CHUNK), 1)
    same = seg == across
    causal = jnp.where(same & (column <= row), 1.0, 0.0)
    before = segc[pl.ds(base + 7, 1), :]
    first = segc[pl.ds(base + 8, 1), :]
    last = segc[pl.ds(base + 7 + CHUNK, 1), :]
    after = segc[pl.ds(base + 8 + CHUNK, 1), :]
    one = lambda test: jnp.where(test, 1.0, 0.0)
    return causal, dict(
        from_before=one(seg == before),
        to_after=one(seg == last),
        from_after=one(seg == after),
        to_before=one(seg == first),
        carry_on=one(before == last),
        carry_back=one(after == first),
    )


def mix_forward(
    g, i, segc, keepc, q, k, v, w, probs, inv, score, mixed, kw, wv, zsum, kw_all, wv_all, pt_all,
    mt_all,
):
    run = range(UNROLL)
    chunks = [UNROLL * i + n for n in run]
    rows = [pl.ds(pl.multiple_of(c * CHUNK, CHUNK), CHUNK) for c in chunks]
    masks = [chunk_masks(c, segc) for c in chunks]
    keep = [twice(keepc[r, :]) for r in rows]
    qc, kc, vc, wc = ([ref[g, r, :] for r in rows] for ref in (q, k, v, w))
    state_k, state_v, state_z = [kw[...]], [wv[...]], [zsum[0:1, :]]
    causal = [mask for mask, _ in masks]
    edge = [edges for _, edges in masks]
    come = [twice(edge[n]["from_before"]) for n in run]
    come_low = [come[n].astype(BF16) for n in run]
    pairs = [head_pairs(dot_rt(head_stack(qc[n]), kc[n]), causal[n]) for n in run]
    for n in run:
        carry = twice(edge[n]["carry_on"])
        wg = wc[n] * twice(edge[n]["to_after"]).astype(BF16)
        state_k.append(state_k[n] * carry + diagonal(dot_lt(kc[n], wg)))
        state_v.append(state_v[n] * carry + diagonal(dot_lt(wg, vc[n])))
        state_z.append(state_z[n] * carry + jnp.sum(wg.astype(F32), axis=0, keepdims=True))
    kw_low = [head_stack(state_k[n].astype(BF16)) for n in run]
    wv_low = [head_stack(state_v[n].astype(BF16)) for n in run]
    inverse = [
        1.0 / (dot(causal[n].astype(BF16), wc[n]) + come[n] * state_z[n] + (1.0 - keep[n]))
        for n in run
    ]
    scores = [
        dot(beside(pairs[n], qc[n] * come_low[n]), above(head_stack(wc[n]), kw_low[n]))
        * (inverse[n] * (HEAD_DIM**-0.5))
        for n in run
    ]
    powers = [jnp.exp(scores[n] - head_max(scores[n])) for n in run]
    chances = [powers[n] / head_sum(powers[n]) for n in run]
    ratio = [(chances[n] * inverse[n]).astype(BF16) for n in run]
    mixing = [head_pairs(dot_rt(head_stack(ratio[n]), wc[n]), causal[n]) for n in run]
    out = [
        dot(beside(mixing[n], ratio[n] * come_low[n]), above(head_stack(vc[n]), wv_low[n]))
        for n in run
    ]
    for n in run:
        r = rows[n]
        kw_all[g, chunks[n]] = diagonal(kw_low[n].T)
        wv_all[g, chunks[n]] = diagonal(wv_low[n].T)
        pt_all[g, r, :] = flip_pairs(pairs[n])
        mt_all[g, r, :] = flip_pairs(mixing[n])
        inv[g, r, :] = inverse[n]
        score[g, r, :] = scores[n]
        probs[g, r, :] = chances[n]
        mixed[g, r, :] = (out[n] * keep[n]).astype(BF16)
    kw[...] = state_k[-1]
    wv[...] = state_v[-1]
    zsum[...] = jnp.broadcast_to(state_z[-1], zsum.shape)


def mix_backward(
    g, i, segc, keepc, q, k, v, w, probs, inv, score, gm, rg, uq, zgrad, kw_all, wv_all, pt_all,
    mt_all, gy, between,
):
    run = range(UNROLL)
    chunks = [UNROLL * i + UNROLL - 1 - n for n in run]
    rows = [pl.ds(pl.multiple_of(c * CHUNK, CHUNK), CHUNK) for c in chunks]
    masks = [chunk_masks(c, segc) for c in chunks]
    qc, kc, vc, wc, grad, chances, inverse, scores, pairs_t, mixing_t = (
        [ref[g, r, :] for r in rows]
        for ref in (q, k, v, w, gm, probs, inv, score, pt_all, mt_all)
    )
    kw_t, wv_t = ([head_stack(ref[g, c]) for c in chunks] for ref in (kw_all, wv_all))
    state_v, state_k, state_z = [rg[...]], [uq[...]], [zgrad[0:1, :]]
    causal = [mask for mask, _ in masks]
    edge = [edges for _, edges in masks]
    come_low = [twice(edge[n]["from_before"]).astype(BF16) for n in run]
    late = [twice(edge[n]["from_after"]) for n in run]
    late_low = [late[n].astype(BF16) for n in run]
    back = [twice(edge[n]["to_before"]) for n in run]
    back_low = [back[n].astype(BF16) for n in run]
    carry = [twice(edge[n]["carry_back"]) for n in run]
    grads = [head_stack(grad[n]) for n in run]
    d_mixing = [head_pairs(dot_rt(grads[n], vc[n]), causal[n]) for n in run]
    d_chance = [
        dot(beside(d_mixing[n], grad[n] * come_low[n]), above(head_stack(wc[n]), wv_t[n]))
        * inverse[n]
        for n in run
    ]
    ratio = [(chances[n] * inverse[n]).astype(BF16) for n in run]
    ratios = [head_stack(ratio[n]) for n in run]
    for n in run:
        added = diagonal(dot_lt(ratio[n] * back_low[n], grad[n]))
        state_v.append(state_v[n] * carry[n] + added)
    rg_low = [head_stack(state_v[n].astype(BF16)) for n in run]
    w_late = [wc[n] * late_low[n] for n in run]
    gv = [dot(beside(mixing_t[n], w_late[n]), above(grads[n], rg_low[n])) for n in run]
    weighted = [d_chance[n] * chances[n] for n in run]
    d_score = [weighted[n] - chances[n] * head_sum(weighted[n]) for n in run]
    d_pw = [(d_score[n] * inverse[n] * (HEAD_DIM**-0.5)).astype(BF16) for n in run]
    d_total = [(weighted[n] + d_score[n] * scores[n]) * inverse[n] for n in run]
    d_pws = [head_stack(d_pw[n]) for n in run]
    d_pairs = [head_pairs(dot_rt(d_pws[n], wc[n]), causal[n]) for n in run]
    for n in run:
        added = diagonal(dot_lt(d_pw[n] * back_low[n], qc[n]))
        state_k.append(state_k[n] * carry[n] + added)
        added = jnp.sum(d_total[n] * back[n], axis=0, keepdims=True)
        state_z.append(state_z[n] * carry[n] + added)
    uq_low = [head_stack(state_k[n].astype(BF16)) for n in run]
    between()
    dw = []
    for n in run:
        z_high = d_total[n].astype(BF16)
        z_low = (d_total[n] - z_high.astype(F32)).astype(BF16)
        anti = -causal[n].T.astype(BF16)
        left = beside(
            flip_pairs(d_mixing[n]), pairs_t[n], vc[n] * late_low[n], kc[n] * late_low[n], anti, anti
        )
        right = above(ratios[n], d_pws[n], rg_low[n].T, uq_low[n].T, z_high, z_low)
        dw.append(dot(left, right) - late[n] * state_z[n])
    gq = [
        dot(beside(d_pairs[n], d_pw[n] * come_low[n]), above(head_stack(kc[n]), kw_t[n]))
        for n in run
    ]
    gk = [
        dot(beside(flip_pairs(d_pairs[n]), w_late[n]), above(head_stack(qc[n]), uq_low[n]))
        for n in run
    ]
    for n in run:
        gy[g, rows[n], 512:768] = gv[n].astype(BF16)
        gy[g, rows[n], 768:1024] = (dw[n] * wc[n].astype(F32)).astype(BF16)
        gy[g, rows[n], 0:256] = gq[n].astype(BF16)
        gy[g, rows[n], 256:512] = gk[n].astype(BF16)
    rg[...] = state_v[-1]
    uq[...] = state_k[-1]
    zgrad[...] = jnp.broadcast_to(state_z[-1], zgrad.shape)


def units(j):
    return j // 2 % 2, (j // 4 * 2 + j % 2) * 256


def feed_in(r, tok, gain, wb, mixed, n2, gh):
    rows = pl.ds(pl.multiple_of(r * TILE, TILE), TILE)
    hidden = tok[rows, :].astype(F32)
    for g in range(2):
        hidden += dot_rt(mixed[g, rows, :], flat(wb[g, ..., 0:256]))
    gh[rows, :] = hidden
    hat, _ = standardise(hidden)
    n2[rows, :] = (hat * gain[...]).astype(BF16)


def feed_up(part, r, up_bias, wb, n2, act, lin):
    rows = pl.ds(pl.multiple_of(r * TILE, TILE), TILE)
    normed = n2[rows, :]
    k0 = 0.7978845608
    k1 = k0 * 0.044715

    def linear_of(j):
        g, column = units(j)
        up = flat(wb[g, ..., 256 + column : 512 + column])
        bias = up_bias[:, g * 1024 + column : g * 1024 + column + 256]
        return dot(normed, up) + bias

    after = linear_of(4 * part)
    for j in range(4 * part, 4 * part + 4):
        linear = after
        if j < 4 * part + 3:
            after = linear_of(j + 1)
        square = linear * linear
        gate = 0.5 * jnp.tanh(linear * (square * k1 + k0)) + 0.5
        active = linear * gate
        slope = gate + active * (1.0 - gate) * (square * (6.0 * k1) + 2.0 * k0)
        g, column = units(j)
        act[g, rows, column : column + 256] = active.astype(BF16)
        lin[g, rows, column : column + 256] = slope.astype(BF16)


def feed_down(r, cot, gain, wb, keepc, lin, gh, gm, small, between):
    rows = pl.ds(pl.multiple_of(r * TILE, TILE), TILE)
    grad = cot[rows, :]
    hidden = gh[rows, :]
    back = jnp.zeros((TILE, 512), F32)

    def grad_of(j):
        g, column = divmod(j * 256, 1024)
        down = flat(wb[g, ..., 1280 + column : 1536 + column])
        return dot(grad, down) * lin[g, rows, column : column + 256].astype(F32)

    after = grad_of(0)
    for j in range(8):
        grad_low = after.astype(BF16)
        if j < 7:
            after = grad_of(j + 1)
        g, column = divmod(j * 256, 1024)
        lin[g, rows, column : column + 256] = grad_low
        row, column = 4 + j // 2, j % 2 * 256
        small[row : row + 1, column : column + 256] += jnp.sum(
            grad_low.astype(F32), axis=0, keepdims=True
        )
    between()
    for g in range(2):
        back += dot_rt(lin[g, rows, :], flat(wb[g, ..., 256:1280]))
    hat, scale = standardise(hidden)
    scaled = back * gain[...]
    inner = scaled - jnp.mean(scaled, axis=-1, keepdims=True)
    inner -= hat * jnp.mean(scaled * hat, axis=-1, keepdims=True)
    grad_f32 = grad.astype(F32)
    grad_hidden = grad_f32 + scale * inner
    gh[rows, :] = grad_hidden
    low = grad_hidden.astype(BF16)
    small[0:1, :] += jnp.sum(back * hat, axis=0, keepdims=True)
    small[2:3, :] += jnp.sum(grad_f32, axis=0, keepdims=True)
    keep = twice(keepc[rows, :])
    for g in range(2):
        gm[g, rows, :] = (dot(low, flat(wb[g, ..., 0:256])) * keep).astype(BF16)


def emit(r, tok, down_bias, wb, mixed, act):
    rows = pl.ds(pl.multiple_of(r * LAST, LAST), LAST)
    total = tok[rows, :].astype(F32)
    for g in range(2):
        total += dot_rt(mixed[g, rows, :], flat(wb[g, ..., 0:256]))
    total += down_bias[...]
    for g in range(2):
        total += dot_rt(act[g, rows, :], flat(wb[g, ..., 1280:2304]))
    tok[rows, :] = total.astype(BF16)


def transpose_into(source, target, length):
    for r in range(length // 256):
        here = slice(r * 256, (r + 1) * 256)
        target[:, here] = source[here, :].astype(BF16).T


def weight_grads(left_t, target, jobs):
    shape = target.shape[1:-1]

    def product(job):
        _, right, at, _, columns = job
        return dot(left_t[...], right[:, at : at + columns]).astype(BF16)

    after = product(jobs[0])
    for n, (g, _, _, to, columns) in enumerate(jobs):
        here = after
        if n + 1 < len(jobs):
            after = product(jobs[n + 1])
        target[g, ..., to : to + columns] = here.reshape(shape + (columns,))


def finish(r, tok, cot, gain, wa, gy, gh, small):
    rows = pl.ds(pl.multiple_of(r * LAST, LAST), LAST)
    hat, scale = standardise(tok[rows, :].astype(F32))
    back = dot_rt(gy[0, rows, :], flat(wa[0])) + dot_rt(gy[1, rows, :], flat(wa[1]))
    scaled = back * gain[...]
    inner = scaled - jnp.mean(scaled, axis=-1, keepdims=True)
    inner -= hat * jnp.mean(scaled * hat, axis=-1, keepdims=True)
    cot[rows, :] = (gh[rows, :] + scale * inner).astype(BF16)
    small[1:2, :] += jnp.sum(back * hat, axis=0, keepdims=True)


class Quiet:
    def nothing(self, *at):
        pass

    before = enter = normalised = weights_a = projected = mixing = nothing
    weights_up = feeding = weights_down = grads_down = feeding_down = fed = grads_up = nothing
    mixing_back = mixed_back = grads_a = finishing = finished = gained = after = nothing


LAYER_INPUTS = 6


def layer_body(
    length,
    comm,
    seg_row,
    pad_row,
    gain_one,
    gain_two,
    up_bias,
    down_bias,
    wa,
    wb,
    ga,
    gw,
    small,
    tok,
    cot,
    segc,
    keepc,
    n1,
    q,
    k,
    v,
    w,
    probs,
    inv,
    score,
    mixed,
    state_k,
    state_v,
    state_z,
    kw_all,
    wv_all,
    pt_all,
    mt_all,
    n2,
    act,
    lin,
    gh,
    gm,
    flip,
):
    runs, tiles = length // (UNROLL * CHUNK), length // TILE

    def clear():
        state_k[...] = jnp.zeros_like(state_k)
        state_v[...] = jnp.zeros_like(state_v)
        state_z[...] = jnp.zeros_like(state_z)

    comm.before()
    small[...] = jnp.zeros_like(small)
    rows_to_columns(seg_row, pad_row, segc, keepc, length)
    comm.enter()

    @pl.loop(0, tiles)
    def _(r):
        normalise(r, tok, gain_one, n1)

    comm.normalised()
    transpose_into(cot, flip, length)

    @pl.loop(0, 2)
    def _(g):
        comm.weights_a(g, 0)
        clear()

        @pl.loop(0, length // WIDE)
        def _(r):
            project_qk(g, r, wa, n1, q, k)

        comm.weights_a(g, 1)

        @pl.loop(0, length // WIDE)
        def _(r):
            project_vw(g, r, wa, keepc, n1, v, w)

        comm.projected(g)

        @pl.loop(0, runs)
        def _(i):
            comm.mixing(g, i)
            mix_forward(
                g, i, segc, keepc, q, k, v, w, probs, inv, score, mixed, state_k, state_v, state_z,
                kw_all, wv_all, pt_all, mt_all,
            )

    comm.weights_up(0)

    @pl.loop(0, tiles)
    def _(r):
        comm.feeding(0, r)
        feed_in(r, tok, gain_two, wb, mixed, n2, gh)
        feed_up(0, r, up_bias, wb, n2, act, lin)

    comm.weights_up(1)

    @pl.loop(0, tiles)
    def _(r):
        comm.feeding(1, r)
        feed_up(1, r, up_bias, wb, n2, act, lin)

    for part in range(2):
        at = part * 512
        weight_grads(flip, gw, [(g, act.at[g], at, 1280 + at, 512) for g in range(2)])
        comm.grads_down(part)
    comm.weights_down()

    @pl.loop(0, tiles)
    def _(r):
        comm.feeding_down(r, 0)
        feed_down(
            r, cot, gain_two, wb, keepc, lin, gh, gm, small,
            functools.partial(comm.feeding_down, r, 1),
        )

    comm.fed()
    transpose_into(n2, flip, length)
    weight_grads(flip, gw, [(g, lin.at[g], 512, 768, 512) for g in range(2)])
    comm.grads_up(0)
    weight_grads(flip, gw, [(g, lin.at[g], 0, 256, 512) for g in range(2)])
    transpose_into(gh, flip, length)
    weight_grads(flip, gw, [(g, mixed.at[g], 0, 0, GROUP) for g in range(2)])
    comm.grads_up(1)
    transpose_into(n1, flip, length)

    @pl.loop(0, 2)
    def _(g):
        clear()

        @pl.loop(0, runs)
        def _(i):
            comm.mixing_back(g, i, 0)
            mix_backward(
                g, runs - 1 - i, segc, keepc, q, k, v, w, probs, inv, score, gm, state_v, state_k,
                state_z, kw_all, wv_all, pt_all, mt_all, lin,
                functools.partial(comm.mixing_back, g, i, 1),
            )

        comm.mixed_back(g)
        for part in range(2):
            weight_grads(flip, ga, [(g, lin.at[g], part * 512, part * 512, 512)])
            comm.grads_a(g, part)

    @pl.loop(0, length // LAST)
    def _(r):
        comm.finishing(0, r)
        finish(r, tok, cot, gain_one, wa, lin, gh, small)
        comm.finished(0, r)

    comm.gained()

    @pl.loop(0, length // LAST)
    def _(r):
        comm.finishing(1, r)
        emit(r, tok, down_bias, wb, mixed, act)
        comm.finished(1, r)

    comm.after()


def layer_scratch(length, width):
    vmem = pltpu.VMEM
    chunks = length // CHUNK
    return [
        vmem((length + 16, 128), F32),
        vmem((length, 128), F32),
        vmem((length, width), BF16),
        vmem((2, length, GROUP), BF16),
        vmem((2, length, GROUP), BF16),
        vmem((2, length, GROUP), BF16),
        vmem((2, length, GROUP), BF16),
        vmem((2, length, GROUP), F32),
        vmem((2, length, GROUP), F32),
        vmem((2, length, GROUP), F32),
        vmem((2, length, GROUP), BF16),
        vmem((HEAD_DIM, GROUP), F32),
        vmem((HEAD_DIM, GROUP), F32),
        vmem((8, GROUP), F32),
        vmem((2, chunks, HEAD_DIM, GROUP), BF16),
        vmem((2, chunks, HEAD_DIM, GROUP), BF16),
        vmem((2, length, 4 * CHUNK), BF16),
        vmem((2, length, 4 * CHUNK), BF16),
        vmem((length, width), BF16),
        vmem((2, length, 1024), BF16),
        vmem((2, length, 1024), BF16),
        vmem((length, width), F32),
        vmem((2, length, GROUP), BF16),
        vmem((width, length), BF16),
    ]


def layer_kernel(length, tokens, cotangent, *refs):
    inputs, (out, grad_out), rest = refs[: LAYER_INPUTS + 2], refs[8:10], refs[10:]
    out[...] = tokens[...]
    grad_out[...] = cotangent[...]
    ga, gw, small = rest[:3]
    layer_body(length, Quiet(), *inputs, ga, gw, small, out, grad_out, *rest[3:])


def layer(tokens, cotangent, seg_row, pad_row, gain_one, gain_two, up_bias, down_bias, wa, wb):
    length, width = tokens.shape
    shape = jax.ShapeDtypeStruct
    cut = lambda full: full.reshape(2, -1, 2, 2, 2, 16, full.shape[-1])
    wa, wb = cut(wa), cut(wb)
    space = pl.BlockSpec(memory_space=pltpu.VMEM)
    out, grad_out, ga, gw, small = pl.pallas_call(
        functools.partial(layer_kernel, length),
        out_shape=(
            shape((length, width), BF16),
            shape((length, width), BF16),
            shape(wa.shape, BF16),
            shape(wb.shape, BF16),
            shape((8, width), F32),
        ),
        in_specs=[space] * 10,
        out_specs=tuple([space] * 5),
        scratch_shapes=layer_scratch(length, width),
        compiler_params=pltpu.CompilerParams(vmem_limit_bytes=62 * 1024 * 1024),
        name="layer",
    )(tokens, cotangent, seg_row, pad_row, gain_one, gain_two, up_bias, down_bias, wa, wb)
    whole = lambda full: full.reshape(2, width, full.shape[-1])
    return out, grad_out, whole(ga), whole(gw), small


class Place:
    def __init__(self, depth):
        index = lax.axis_index("dp")
        t = lax.axis_index("tensor")
        x, y, z = lax.rem(index, 2), lax.rem(index // 2, 2), index // 4
        self.depth = depth
        self.x, self.y, self.z, self.t, self.other = x, y, z, t, 1 - t
        self.near = (y + t * (1 - 2 * y), x + (1 - t) * (1 - 2 * x))
        self.next = (y + (1 - t) * (1 - 2 * y), x + t * (1 - 2 * x))
        self.far = (1 - y, 1 - x)
        chip = lambda z, y, x: (z * 2 + y) * 2 + x
        self.levels = [lax.rem(z + s, depth) for s in range(depth)]
        self.chips_z = [chip(level, y, x) for level in self.levels]
        self.to_near = {"dp": chip(z, *self.near)}
        self.to_next = {"dp": chip(z, *self.next)}
        self.to_pair = {"tensor": self.other}
        self.spot = (y * 2 + x) * 2 + t
        flip = lambda value, bit: value + bit * (1 - 2 * value)
        self.level = [
            {
                "dp": chip(z, flip(y, offset // 4), flip(x, offset // 2 % 2)),
                "tensor": flip(t, offset % 2),
            }
            for offset in range(8)
        ]

    def along_z(self, step, core):
        return {"dp": self.chips_z[step], "tensor": core}

    def friends(self):
        along = [self.along_z(s, core) for s in range(1, self.depth) for core in range(2)]
        return self.level[1:] + along

    def knock(self):
        barrier = pltpu.get_barrier_semaphore()
        for friend in self.friends():
            pl.semaphore_signal(barrier, inc=1, device_id=friend, device_id_type=MESH)

    def enter(self):
        pl.semaphore_wait(pltpu.get_barrier_semaphore(), len(self.friends()))


class Copies:
    def __init__(self, sems):
        self.sems = sems

    def build(self, source, target, device, out_sem, in_sem):
        return pltpu.make_async_remote_copy(
            src_ref=source,
            dst_ref=target,
            send_sem=self.sems.at[0, out_sem],
            recv_sem=self.sems.at[1, in_sem],
            device_id=device,
            device_id_type=MESH,
        )

    def start(self, source, target, device, number, in_sem=None, only=None):
        def begin():
            landing = number if in_sem is None else in_sem
            self.build(source(), target, device, number, landing).start()

        begin() if only is None else pl.when(only)(begin)

    def landed(self, target, number, only=None):
        def wait():
            self.build(target, target, {"tensor": 0}, number, number).wait_recv()

        wait() if only is None else pl.when(only)(wait)

    def sent(self, source, numbers, only=None):
        def wait():
            for number in numbers:
                self.build(source, source, {"tensor": 0}, number, number).wait_send()

        wait() if only is None else pl.when(only)(wait)


class Gather(Copies):
    COPIES = 14

    def __init__(self, place, own, full, group, columns, sems):
        super().__init__(sems)
        self.p, self.own, self.full, self.columns = place, own, full, columns
        self.group = group
        self.groups = slice(None) if group is None else slice(group, group + 1)
        self.mine = None if group is None else place.t == group
        self.pairs = None if group is None else place.t != group

    def at(self, g, z, spot, half):
        return self.full.at[g, z, spot[0], spot[1], half, :, self.columns]

    def block(self, spot, half):
        return self.at(self.groups, slice(None), spot, half)

    def forward(self, spot, device, number):
        block = lambda: self.block(spot, self.p.t)
        self.start(block, block(), device, number)

    def first(self):
        p = self.p
        here = (p.y, p.x)
        for s in range(1, p.depth):
            for core in range(2):
                self.start(
                    lambda core=core: self.own.at[core, :, self.columns],
                    self.at(p.t, p.z, here, core),
                    p.along_z(s, core),
                    2 * (s - 1) + core,
                    2 * (s - 1) + p.t,
                    only=self.mine,
                )
        self.start(
            lambda: self.own.at[p.other, :, self.columns],
            self.at(p.t, p.z, here, p.other),
            p.to_pair,
            6,
            only=self.mine,
        )

        def keep():
            self.full[p.t, p.z, p.y, p.x, p.t, :, self.columns] = self.own[p.t, :, self.columns]

        keep() if self.mine is None else pl.when(self.mine)(keep)

    def second(self):
        p = self.p
        here = (p.y, p.x)
        for n in range(6):
            if self.group is None or n % 2 == self.group:
                self.landed(self.at(p.t, p.z, here, p.t), n)
        self.landed(self.at(p.t, p.z, here, p.t), 6, only=self.pairs)
        self.forward(here, p.to_near, 7)
        self.forward(here, p.to_next, 8)
        self.forward(here, p.to_pair, 9)

    def third(self):
        p = self.p
        self.landed(self.block(p.near, p.t), 7)
        self.forward(p.near, p.to_next, 10)
        self.forward(p.near, p.to_pair, 11)
        self.landed(self.block(p.next, p.t), 8)
        self.forward(p.next, p.to_pair, 12)

    def fourth(self):
        p = self.p
        self.landed(self.block(p.far, p.t), 10)
        self.forward(p.far, p.to_pair, 13)

    def last(self):
        p = self.p
        for n in (9, 11, 12, 13):
            self.landed(self.block((p.y, p.x), p.other), n)

    def left(self):
        p = self.p
        self.sent(self.own.at[0, :, self.columns], range(7), self.mine)
        self.sent(self.block((p.y, p.x), p.t), range(7, 14))


class Scatter(Copies):
    COPIES = 11

    def __init__(self, place, part, group, columns, pair_in, near_in, next_in, last_in, sems):
        super().__init__(sems)
        self.p, self.part, self.columns = place, part, columns
        self.pair_in, self.near_in, self.next_in, self.last_in = pair_in, near_in, next_in, last_in
        self.group = group
        self.groups = slice(None) if group is None else slice(group, group + 1)
        self.mine = None if group is None else place.t == group
        self.pairs = None if group is None else place.t != group

    def at(self, g, z, spot, half):
        return self.part.at[g, z, spot[0], spot[1], half, :, self.columns]

    def block(self, spot, half):
        return self.at(self.groups, slice(None), spot, half)

    def add(self, spot, landed):
        p = self.p
        here = (self.groups, slice(None), spot[0], spot[1], p.t, slice(None), self.columns)
        self.part[here] = (self.part[here].astype(F32) + landed.astype(F32)).astype(BF16)

    def first(self):
        p = self.p
        self.start(
            lambda: self.part.at[self.groups, :, :, :, p.other, :, self.columns],
            self.pair_in,
            p.to_pair,
            0,
        )

    def second(self):
        p = self.p
        self.landed(self.pair_in, 0)
        for spot, number in ((p.far, 1), (p.near, 2)):
            self.add(spot, self.pair_in[:, :, spot[0], spot[1]])
            self.start(
                lambda spot=spot: self.block(spot, p.t),
                self.near_in.at[number - 1],
                p.to_near,
                number,
            )
        for spot in (p.next, (p.y, p.x)):
            self.add(spot, self.pair_in[:, :, spot[0], spot[1]])

    def third(self):
        p = self.p
        self.landed(self.near_in.at[0], 1)
        self.add(p.next, self.near_in[0])
        self.start(lambda: self.block(p.next, p.t), self.next_in, p.to_next, 3)
        self.landed(self.near_in.at[1], 2)
        self.add((p.y, p.x), self.near_in[1])

    def fourth(self):
        p = self.p
        here = (p.y, p.x)
        self.landed(self.next_in, 3)
        self.add(here, self.next_in[...])
        for s in range(1, p.depth):
            for core in range(2) if self.group is None else (self.group,):
                self.start(
                    lambda s=s, core=core: self.at(core, p.levels[s], here, p.t),
                    self.last_in.at[2 * (s - 1) + p.t],
                    p.along_z(s, core),
                    4 + 2 * (s - 1) + core,
                    4 + 2 * (s - 1) + p.t,
                )
        self.start(
            lambda: self.at(p.other, p.z, here, p.t),
            self.last_in.at[2 * (p.depth - 1)],
            p.to_pair,
            10,
            only=self.pairs,
        )

    def last(self, target):
        p = self.p

        def write():
            for n in range(7):
                self.landed(self.last_in.at[n], 4 + n)
            mine = self.part[p.t, p.z, p.y, p.x, p.t, :, self.columns].astype(F32)
            rest = self.last_in[2 * (p.depth - 1)].astype(F32)
            for s in range(1, p.depth):
                mine += self.last_in[2 * (s - 1) + p.t].astype(F32)
                rest += self.last_in[2 * (s - 1) + p.other].astype(F32)
            target[p.t] = mine
            target[p.other] = rest

        write() if self.mine is None else pl.when(self.mine)(write)

    def left(self):
        p = self.p
        self.sent(self.pair_in, (0,))
        self.sent(self.next_in, (1, 2, 3))
        for core in range(2) if self.group is None else (self.group,):
            self.sent(self.last_in.at[0], [4 + 2 * s + core for s in range(p.depth - 1)])
        self.sent(self.last_in.at[0], (10,), self.pairs)


def scatter_scratch(groups, depth, columns):
    vmem = pltpu.VMEM
    return [
        vmem((groups, depth, 2, 2, 16, columns), BF16),
        vmem((2, groups, depth, 16, columns), BF16),
        vmem((groups, depth, 16, columns), BF16),
        vmem((2 * depth - 1, 16, columns), BF16),
    ]


class Reduce(Copies):
    COPIES = 12

    def __init__(self, place, own, parts, sums, sems):
        super().__init__(sems)
        self.p, self.own, self.parts, self.sums = place, own, parts, sums

    def first(self):
        p = self.p
        self.parts[p.spot] = self.own[...]
        for offset in range(1, 8):
            self.start(
                lambda: self.own, self.parts.at[p.spot], p.level[offset], offset - 1
            )

    def second(self):
        p = self.p
        for n in range(7):
            self.landed(self.own, n)
        total = self.parts[0]
        for spot in range(1, 8):
            total += self.parts[spot]
        self.sums[p.z] = total
        for s in range(1, p.depth):
            self.start(
                lambda: self.sums.at[p.z], self.sums.at[p.z], {"dp": p.chips_z[s]}, 6 + s
            )

    def last(self):
        p = self.p
        for s in range(1, p.depth):
            self.landed(self.own, 6 + s)
        total = self.sums[0]
        for z in range(1, p.depth):
            total += self.sums[z]
        return total

    def left(self):
        self.sent(self.own, range(6 + self.p.depth))


class Woven:
    def __init__(self, place, far, near, own, full, gathers, scatters, gains):
        self.p, self.far, self.near, self.own = place, far, near, own
        wa, wb, ga, gw = full
        own_a, own_b = own
        ranges = [(own_a, wa, 0, 0, 512), (own_a, wa, 0, 512, 1024), (own_a, wa, 1, 0, 1024)]
        ranges += [(own_b, wb, None, 768 * n, 768 * n + 768) for n in range(3)]
        gather = [
            Gather(place, part, whole, g, slice(first, last), sems)
            for (part, whole, g, first, last), sems in zip(ranges, gathers)
        ]
        self.a0, self.a1, self.b = gather[:2], gather[2], gather[3:]
        ranges = [(gw, None, 1280, 1792), (gw, None, 1792, 2304)]
        ranges += [(gw, None, 768, 1280), (gw, None, 0, 768)]
        ranges += [(ga, 0, 0, 1024), (ga, 1, 0, 512), (ga, 1, 512, 1024)]
        scatter = [
            Scatter(place, part, g, slice(first, last), *buffers)
            for (part, g, first, last), buffers in zip(ranges, scatters)
        ]
        self.down_grad, self.up_grad = scatter[:2], scatter[2:4]
        self.a0_grad, self.a1_grad = scatter[4], scatter[5:]
        self.gains = gains
        self.everything = scatter + [gains]

    def table(self, at, steps):
        for place, calls in steps.items():
            here = None
            for value, wanted in zip(at, place):
                here = (value == wanted) if here is None else here & (value == wanted)

            @pl.when(here)
            def _(calls=calls):
                for call in calls:
                    call()

    def fetch(self, n):
        return pltpu.make_async_copy(self.far[n], self.near[n], self.near["sems"].at[n])

    def put(self, name, n):
        return pltpu.make_async_copy(self.near[name], self.far[name], self.near["sems"].at[n])

    def put_rows(self, which, r):
        rows = pl.ds(pl.multiple_of(r * LAST, LAST), LAST)
        source, target = ((1, "grad_out"), (0, "out"))[which]
        return pltpu.make_async_copy(
            self.near[source].at[rows],
            self.far[target].at[rows],
            self.near["sems"].at[18 + 4 * which + r],
        )

    def before(self):
        self.p.knock()
        for n in range(14, -1, -1):
            self.fetch(n).start()
        for n in range(2, 15):
            self.fetch(n).wait()
        first = self.p.t == 0
        for rows, row in ((2, "seg_row"), (3, "pad_row")):
            rows = self.near[rows]
            self.near[row][...] = jnp.where(first, rows[0:1, :], rows[1:2, :])
        own_a, own_b = self.own
        halves = lambda n: self.near[n][...].astype(BF16).reshape(2, 16, -1)
        for n in range(4):
            own_a[:, :, 256 * n : 256 * n + 256] = halves(8 + n)
        own_b[:, :, 0:256] = halves(12)
        own_b[:, :, 256:1280] = halves(13)
        own_b[:, :, 1280:2304] = halves(14)

    def enter(self):
        self.p.enter()
        self.a0[0].first()
        self.a0[1].first()
        self.fetch(0).wait()
        self.fetch(1).wait()

    def normalised(self):
        pass

    def weights_a(self, g, part):
        one, two = self.a0
        a1, b = self.a1, self.b
        self.table(
            (g,),
            (
                {
                    (0,): (
                        one.second, a1.first, two.second, b[0].first, one.third, two.third,
                        one.fourth, a1.second, one.last,
                    ),
                    (1,): (a1.fourth, a1.last),
                },
                {
                    (0,): (b[1].first, two.fourth, two.last),
                    (1,): (b[0].third,),
                },
            )[part],
        )

    def projected(self, g):
        self.table((g,), {(0,): (self.a1.third, self.b[0].second)})

    def mixing(self, g, i):
        one, two, three = self.b
        steps = {
            (0, 1): (two.second, self.a0[0].left, self.a0[1].left, three.first),
            (1, 1): (three.second, one.fourth, two.third),
        }
        self.table((g, i), steps)

    def weights_up(self, part):
        one, two, three = self.b
        if part == 0:
            one.last()
        else:
            three.third()
            two.fourth()
            two.last()

    def feeding(self, part, r):
        pass

    def grads_down(self, part):
        if part == 0:
            self.b[2].fourth()
            self.a1.left()
            self.b[0].left()
            self.b[1].left()
        self.down_grad[part].first()

    def weights_down(self):
        self.b[2].last()
        self.b[2].left()

    def feeding_down(self, r, part):
        one, two = self.down_grad
        if part == 0:
            self.table((r,), {(1,): (two.second,)})
        else:
            self.table((r,), {(0,): (one.second,)})

    def fed(self):
        pass

    def grads_up(self, part):
        one, two = self.down_grad
        self.up_grad[part].first()
        if part == 0:
            one.third()
        else:
            two.third()
            self.up_grad[0].second()

    def mixing_back(self, g, i, part):
        up, rest = self.up_grad
        one, two = self.down_grad
        steps = {
            (0, 0, 1): (one.fourth,),
            (0, 1, 0): (rest.second,),
            (0, 1, 1): (two.fourth, up.third),
            (1, 0, 1): (rest.third,),
            (1, 1, 0): (self.a0_grad.second, self.down_last, up.fourth),
        }
        self.table((g, i, part), steps)

    def mixed_back(self, g):
        self.table((g,), {(1,): (self.up_grad[1].fourth,)})

    def grads_a(self, g, part):
        one, two = self.a1_grad
        if part == 0:
            self.table((g,), {(1,): (one.first,)})
        else:
            self.table((g,), {(0,): (self.a0_grad.first,), (1,): (two.first, self.a0_grad.third)})

    def finishing(self, which, r):
        one, two = self.a1_grad
        steps = {
            (0, 1): (one.second,),
            (0, 2): (two.second,),
            (0, 3): (self.a0_grad.fourth,),
            (1, 1): (one.third,),
            (1, 2): (two.third,),
            (1, 3): (one.fourth,),
        }
        self.table((which, r), steps)

    def down_last(self):
        dw = self.near["dw"]
        self.down_grad[0].last(dw.at[:, :, 1280:1792])
        self.down_grad[1].last(dw.at[:, :, 1792:2304])

    def finished(self, which, r):
        self.put_rows(which, r).start()

    def gained(self):
        self.gains.first()

    def after(self):
        one, two = self.a1_grad
        up, rest = self.up_grad
        da, dw = self.near["da"], self.near["dw"]
        self.gains.second()
        two.fourth()
        up.last(dw.at[:, :, 768:1280])
        rest.last(dw.at[:, :, 0:768])
        self.put("dw", 15).start()
        self.near["total"][...] = self.gains.last()
        self.put("total", 16).start()
        self.a0_grad.last(da)
        one.last(da.at[:, :, 0:512])
        two.last(da.at[:, :, 512:1024])
        self.put("da", 17).start()
        self.everything_left()

    def everything_left(self):
        for copies in self.everything:
            copies.left()
        for r in range(4):
            self.put_rows(0, r).wait()
            self.put_rows(1, r).wait()
        self.put("dw", 15).wait()
        self.put("total", 16).wait()
        self.put("da", 17).wait()


def woven_kernel(length, depth, *refs):
    refs = list(refs)
    take = lambda n: [refs.pop(0) for _ in range(n)]
    far = dict(enumerate(take(15)))
    far.update(zip(("out", "grad_out", "da", "dw", "total"), take(5)))
    near = dict(enumerate(take(15)))
    near.update(zip(("da", "dw", "total", "seg_row", "pad_row", "sems"), take(6)))
    own, full = take(2), take(4)
    small, parts, sums, gain_sems = take(4)
    gathers = take(6)
    scatters = [take(4) for _ in range(7)]
    scatter_sems = gathers[:5] + take(2)
    scatters = [buffers + [sems] for buffers, sems in zip(scatters, scatter_sems)]
    place = Place(depth)
    gains = Reduce(place, small, parts, sums, gain_sems)
    comm = Woven(place, far, near, own, full, gathers, scatters, gains)
    layer_body(
        length, comm, near["seg_row"], near["pad_row"], *[near[n] for n in range(4, 8)], *full,
        small, near[0], near[1], *refs,
    )


def write_kernel(out_in, grad_in, da, dw, small, *refs):
    (
        out, grad_out, mixer_gain, query, key, value, slot, out_t, feed_gain, up, up_bias, down_t,
        down_bias,
    ) = refs
    out[...] = out_in[...]
    grad_out[...] = grad_in[...]
    rows = lambda part: part.reshape(-1, part.shape[-1])
    query[...] = rows(da[:, :, 0:256])
    key[...] = rows(da[:, :, 256:512])
    value[...] = rows(da[:, :, 512:768])
    slot[...] = rows(da[:, :, 768:1024])
    out_t[...] = rows(dw[:, :, 0:256])
    up[...] = rows(dw[:, :, 256:1280])
    down_t[...] = rows(dw[:, :, 1280:2304])
    feed_gain[...] = small[0:1, :]
    mixer_gain[...] = small[1:2, :]
    down_bias[...] = small[2:3, :]
    for row in range(4):
        up_bias[:, row * 512 : (row + 1) * 512] = small[4 + row : 5 + row, :]


def write(out, grad_out, da, dw, small):
    shape = jax.ShapeDtypeStruct
    space = pl.BlockSpec(memory_space=pltpu.VMEM)
    width = out.shape[1]
    square, wide = shape((32, 256), F32), shape((32, 1024), F32)
    row = shape((1, width), F32)
    return pl.pallas_call(
        write_kernel,
        out_shape=(
            shape(out.shape, BF16),
            shape(out.shape, BF16),
            row,
            square,
            square,
            square,
            square,
            square,
            row,
            wide,
            shape((1, 4 * width), F32),
            wide,
            row,
        ),
        in_specs=[space] * 5,
        out_specs=(space,) * 13,
        name="write",
    )(out, grad_out, da, dw, small)


def woven(depth, *inputs):
    length, width = inputs[0].shape
    shape = jax.ShapeDtypeStruct
    far = pl.BlockSpec(memory_space=pl.ANY)
    vmem = pltpu.VMEM
    dma = pltpu.SemaphoreType.DMA
    full = lambda columns: vmem((2, depth, 2, 2, 2, 16, columns), BF16)
    da, dw, total = shape((2, 16, 1024), F32), shape((2, 16, 2304), F32), shape((8, width), F32)
    scatters = []
    for groups, columns in ((2, 512), (2, 512), (2, 512), (2, 768), (1, 1024), (1, 512), (1, 512)):
        scatters += scatter_scratch(groups, depth, columns)
    return pl.pallas_call(
        functools.partial(woven_kernel, length, depth),
        out_shape=(shape((length, width), BF16), shape((length, width), BF16), da, dw, total),
        in_specs=[far] * 15,
        out_specs=(far,) * 5,
        scratch_shapes=[vmem(array.shape, array.dtype) for array in inputs]
        + [vmem(array.shape, array.dtype) for array in (da, dw, total)]
        + [
            vmem((1, length), jnp.int32),
            vmem((1, length), jnp.int32),
            dma((26,)),
            vmem((2, 16, 1024), BF16),
            vmem((2, 16, 2304), BF16),
            full(1024),
            full(2304),
            full(1024),
            full(2304),
            vmem((8, width), F32),
            vmem((8, 8, width), F32),
            vmem((depth, 8, width), F32),
            dma((2, Reduce.COPIES)),
        ]
        + [dma((2, Gather.COPIES))] * 6
        + scatters
        + [dma((2, Scatter.COPIES))] * 2
        + layer_scratch(length, width),
        compiler_params=pltpu.CompilerParams(
            collective_id=0, has_side_effects=True, vmem_limit_bytes=63 * 1024 * 1024
        ),
        name="woven",
    )(*inputs)


def per_device(
    direct,
    tokens,
    segment_ids,
    padding,
    mixer_gain,
    query_weight,
    key_weight,
    value_weight,
    slot_weight,
    out_weight,
    feed_gain,
    up_weight,
    up_bias,
    down_weight,
    down_bias,
    cotangent,
):
    gains = (mixer_gain[None], feed_gain[None])
    biases = (up_bias[None], down_bias[None])
    if direct:
        owns = (
            query_weight, key_weight, value_weight, slot_weight, out_weight.T, up_weight,
            down_weight.T,
        )
        depth = lax.axis_size("dp") // 4
        results = write(
            *woven(depth, tokens, cotangent, segment_ids, padding, *gains, *biases, *owns)
        )
        (
            out, grad_out, gain_one, query, key, value, slot, out_t, gain_two, up, bias_one, down_t,
            bias_two,
        ) = results
        return (
            out, grad_out, gain_one[0], query, key, value, slot, out_t.T, gain_two[0], up,
            bias_one[0], down_t.T, bias_two[0],
        )
    own_a = jnp.concatenate([query_weight, key_weight, value_weight, slot_weight], 1)
    own_b = jnp.concatenate([out_weight.T, up_weight, down_weight.T], 1)
    wa, wb = (
        lax.all_gather(lax.all_gather(own.astype(BF16), "dp", axis=0, tiled=True), "tensor")
        for own in (own_a, own_b)
    )
    half = lax.axis_index("tensor")
    pick = lambda rows: lax.dynamic_slice_in_dim(rows, half, 1, 0)
    out, grad_out, ga, gw, small = layer(
        tokens, cotangent, pick(segment_ids), pick(padding), *gains, *biases, wa, wb
    )
    da, dw = (
        lax.psum_scatter(
            lax.psum_scatter(part.astype(F32), "tensor", scatter_dimension=0),
            "dp",
            scatter_dimension=0,
            tiled=True,
        )
        for part in (ga, gw)
    )
    small = lax.psum(small, ("dp", "tensor"))
    return (
        out,
        grad_out,
        small[1],
        da[:, 0:256],
        da[:, 256:512],
        da[:, 512:768],
        da[:, 768:1024],
        dw[:, 0:256].T,
        small[0],
        dw[:, 256:1280],
        small[4:8].reshape(-1),
        dw[:, 1280:2304].T,
        small[2],
    )


def solution(mesh):
    in_specs = (
        P(("dp", "tensor"), None),
        P("dp", None),
        P("dp", None),
        P(),
        P("dp", "tensor"),
        P("dp", "tensor"),
        P("dp", "tensor"),
        P("dp", "tensor"),
        P("tensor", "dp"),
        P(),
        P("dp", "tensor"),
        P(),
        P("tensor", "dp"),
        P(),
        P(("dp", "tensor"), None),
    )
    out_specs = (
        P(("dp", "tensor"), None),
        P(("dp", "tensor"), None),
        P(),
        P("dp", "tensor"),
        P("dp", "tensor"),
        P("dp", "tensor"),
        P("dp", "tensor"),
        P("tensor", "dp"),
        P(),
        P("dp", "tensor"),
        P(),
        P("tensor", "dp"),
        P(),
    )
    direct = mesh.shape["dp"] == 16 and mesh.shape["tensor"] == 2
    return jax.shard_map(
        functools.partial(per_device, direct),
        mesh=mesh,
        in_specs=in_specs,
        out_specs=out_specs,
        check_vma=False,
    )
```

```python
import functools
import math

import jax
import jax.numpy as jnp
from jax import lax
from jax.experimental import pallas as pl
from jax.experimental.pallas import tpu as pltpu
from jax.sharding import PartitionSpec as P

HEAD_DIM = 64
SLOTS = 64
CHUNK = 128
UNROLL = 4
GROUP = 256
TILE = 512
WIDE = 512
LAST = 256

F32 = jnp.float32
BF16 = jnp.bfloat16
MESH = pl.DeviceIdType.MESH


def dot(left, right):
    return lax.dot_general(left, right, (((1,), (0,)), ((), ())), preferred_element_type=F32)


def dot_rt(left, right):
    return lax.dot_general(left, right, (((1,), (1,)), ((), ())), preferred_element_type=F32)


def dot_lt(left, right):
    return lax.dot_general(left, right, (((0,), (0,)), ((), ())), preferred_element_type=F32)


def twice(block):
    return jnp.concatenate([block, block], axis=1)


def standardise(rows):
    centred = rows - jnp.mean(rows, axis=-1, keepdims=True)
    scale = lax.rsqrt(jnp.mean(centred * centred, axis=-1, keepdims=True) + 1e-05)
    return centred * scale, scale


def head_stack(block):
    lane = lax.broadcasted_iota(jnp.int32, block.shape, 1) // HEAD_DIM
    zero = jnp.zeros_like(block)
    return jnp.concatenate([jnp.where(lane == h, block, zero) for h in range(4)], axis=0)


def diagonal(product):
    parts = [product[h * HEAD_DIM : (h + 1) * HEAD_DIM, :] for h in range(4)]
    lane = lax.broadcasted_iota(jnp.int32, parts[0].shape, 1) // HEAD_DIM
    kept = parts[3]
    for h in range(3):
        kept = jnp.where(lane == h, parts[h], kept)
    return kept


def over_heads(block, reduce, rest):
    halves = []
    lane = lax.broadcasted_iota(jnp.int32, (block.shape[0], 128), 1) < HEAD_DIM
    for j in range(block.shape[1] // 128):
        part = block[:, j * 128 : (j + 1) * 128]
        first = reduce(jnp.where(lane, part, rest), axis=1, keepdims=True)
        second = reduce(jnp.where(lane, rest, part), axis=1, keepdims=True)
        halves.append(jnp.where(lane, first, second))
    return jnp.concatenate(halves, axis=1)


def head_max(block):
    return over_heads(block, jnp.max, -jnp.inf)


def head_sum(block):
    return over_heads(block, jnp.sum, 0.0)


def head_pairs(product, allowed):
    parts = [product[h * CHUNK : (h + 1) * CHUNK, :] * allowed for h in range(4)]
    return jnp.concatenate(parts, axis=1).astype(BF16)


def flip_pairs(pairs):
    parts = [pairs[:, h * CHUNK : (h + 1) * CHUNK].T for h in range(4)]
    return jnp.concatenate(parts, axis=1)


def beside(*blocks):
    return jnp.concatenate(blocks, axis=1)


def above(*blocks):
    return jnp.concatenate(blocks, axis=0)


def flat(block):
    return block.reshape(-1, block.shape[-1])


def rows_to_columns(seg_row, pad_row, segc, keepc, length):
    segc[pl.ds(0, 8), :] = jnp.full((8, 128), -1.0, F32)
    segc[pl.ds(8 + length, 8), :] = jnp.full((8, 128), -2.0, F32)
    for c in range(length // CHUNK):
        here = slice(c * CHUNK, (c + 1) * CHUNK)
        seg = jnp.broadcast_to(seg_row[:, here].astype(F32), (CHUNK, CHUNK))
        pad = jnp.broadcast_to(pad_row[:, here].astype(F32), (CHUNK, CHUNK))
        segc[pl.ds(8 + c * CHUNK, CHUNK), :] = seg.T
        keepc[pl.ds(c * CHUNK, CHUNK), :] = 1.0 - pad.T


def normalise(r, tok, cot, gain, n1, small):
    rows = pl.ds(pl.multiple_of(r * TILE, TILE), TILE)
    xhat, _ = standardise(tok[rows, :].astype(F32))
    n1[rows, :] = (xhat * gain[...]).astype(BF16)
    small[2:3, :] += jnp.sum(cot[rows, :].astype(F32), axis=0, keepdims=True)


def project_qk(g, r, wa, n1, q, k):
    rows = pl.ds(pl.multiple_of(r * WIDE, WIDE), WIDE)
    out = dot(n1[rows, :], flat(wa[g, ..., 0:512]))
    q[g, rows, :] = out[:, 0:256].astype(BF16)
    k[g, rows, :] = out[:, 256:512].astype(BF16)


def project_vw(g, r, wa, keepc, n1, v, w):
    rows = pl.ds(pl.multiple_of(r * WIDE, WIDE), WIDE)
    out = dot(n1[rows, :], flat(wa[g, ..., 512:1024]))
    v[g, rows, :] = out[:, 0:256].astype(BF16)
    w[g, rows, :] = (jnp.exp(out[:, 256:512]) * twice(keepc[rows, :])).astype(BF16)


def chunk_masks(c, segc):
    base = pl.multiple_of(c * CHUNK, CHUNK)
    seg = segc[pl.ds(base + 8, CHUNK), :]
    across = seg.T
    row = lax.broadcasted_iota(jnp.int32, (CHUNK, CHUNK), 0)
    column = lax.broadcasted_iota(jnp.int32, (CHUNK, CHUNK), 1)
    same = seg == across
    causal = jnp.where(same & (column <= row), 1.0, 0.0)
    before = segc[pl.ds(base + 7, 1), :]
    first = segc[pl.ds(base + 8, 1), :]
    last = segc[pl.ds(base + 7 + CHUNK, 1), :]
    after = segc[pl.ds(base + 8 + CHUNK, 1), :]
    one = lambda test: jnp.where(test, 1.0, 0.0)
    return causal, dict(
        from_before=one(seg == before),
        to_after=one(seg == last),
        from_after=one(seg == after),
        to_before=one(seg == first),
        carry_on=one(before == last),
        carry_back=one(after == first),
    )


def mix_forward(
    g, i, segc, keepc, q, k, v, w, probs, inv, score, mixed, kw, wv, zsum, kw_all, wv_all, pt_all,
    mt_all,
):
    run = range(UNROLL)
    chunks = [UNROLL * i + n for n in run]
    rows = [pl.ds(pl.multiple_of(c * CHUNK, CHUNK), CHUNK) for c in chunks]
    masks = [chunk_masks(c, segc) for c in chunks]
    keep = [twice(keepc[r, :]) for r in rows]
    qc, kc, vc, wc = ([ref[g, r, :] for r in rows] for ref in (q, k, v, w))
    state_k, state_v, state_z = [kw[...]], [wv[...]], [zsum[0:1, :]]
    causal = [mask for mask, _ in masks]
    edge = [edges for _, edges in masks]
    come = [twice(edge[n]["from_before"]) for n in run]
    come_low = [come[n].astype(BF16) for n in run]
    pairs = [head_pairs(dot_rt(head_stack(qc[n]), kc[n]), causal[n]) for n in run]
    for n in run:
        carry = twice(edge[n]["carry_on"])
        wg = wc[n] * twice(edge[n]["to_after"]).astype(BF16)
        state_k.append(state_k[n] * carry + diagonal(dot_lt(kc[n], wg)))
        state_v.append(state_v[n] * carry + diagonal(dot_lt(wg, vc[n])))
        state_z.append(state_z[n] * carry + jnp.sum(wg.astype(F32), axis=0, keepdims=True))
    kw_low = [head_stack(state_k[n].astype(BF16)) for n in run]
    wv_low = [head_stack(state_v[n].astype(BF16)) for n in run]
    inverse = [
        1.0 / (dot(causal[n].astype(BF16), wc[n]) + come[n] * state_z[n] + (1.0 - keep[n]))
        for n in run
    ]
    scores = [
        dot(beside(pairs[n], qc[n] * come_low[n]), above(head_stack(wc[n]), kw_low[n]))
        * (inverse[n] * (HEAD_DIM**-0.5))
        for n in run
    ]
    powers = [jnp.exp(scores[n] - head_max(scores[n])) for n in run]
    chances = [powers[n] / head_sum(powers[n]) for n in run]
    ratio = [(chances[n] * inverse[n]).astype(BF16) for n in run]
    mixing = [head_pairs(dot_rt(head_stack(ratio[n]), wc[n]), causal[n]) for n in run]
    out = [
        dot(beside(mixing[n], ratio[n] * come_low[n]), above(head_stack(vc[n]), wv_low[n]))
        for n in run
    ]
    for n in run:
        r = rows[n]
        kw_all[g, chunks[n]] = diagonal(kw_low[n].T)
        wv_all[g, chunks[n]] = diagonal(wv_low[n].T)
        pt_all[g, r, :] = flip_pairs(pairs[n])
        mt_all[g, r, :] = flip_pairs(mixing[n])
        inv[g, r, :] = inverse[n]
        score[g, r, :] = scores[n]
        probs[g, r, :] = chances[n]
        mixed[g, r, :] = (out[n] * keep[n]).astype(BF16)
    kw[...] = state_k[-1]
    wv[...] = state_v[-1]
    zsum[...] = jnp.broadcast_to(state_z[-1], zsum.shape)


def mix_backward(
    g, i, segc, keepc, q, k, v, w, probs, inv, score, gm, rg, uq, zgrad, kw_all, wv_all, pt_all,
    mt_all, gy, between,
):
    run = range(UNROLL)
    chunks = [UNROLL * i + UNROLL - 1 - n for n in run]
    rows = [pl.ds(pl.multiple_of(c * CHUNK, CHUNK), CHUNK) for c in chunks]
    masks = [chunk_masks(c, segc) for c in chunks]
    qc, kc, vc, wc, grad, chances, inverse, scores, pairs_t, mixing_t = (
        [ref[g, r, :] for r in rows]
        for ref in (q, k, v, w, gm, probs, inv, score, pt_all, mt_all)
    )
    kw_t, wv_t = ([head_stack(ref[g, c]) for c in chunks] for ref in (kw_all, wv_all))
    state_v, state_k, state_z = [rg[...]], [uq[...]], [zgrad[0:1, :]]
    causal = [mask for mask, _ in masks]
    edge = [edges for _, edges in masks]
    come_low = [twice(edge[n]["from_before"]).astype(BF16) for n in run]
    late = [twice(edge[n]["from_after"]) for n in run]
    late_low = [late[n].astype(BF16) for n in run]
    back = [twice(edge[n]["to_before"]) for n in run]
    back_low = [back[n].astype(BF16) for n in run]
    carry = [twice(edge[n]["carry_back"]) for n in run]
    grads = [head_stack(grad[n]) for n in run]
    d_mixing = [head_pairs(dot_rt(grads[n], vc[n]), causal[n]) for n in run]
    d_chance = [
        dot(beside(d_mixing[n], grad[n] * come_low[n]), above(head_stack(wc[n]), wv_t[n]))
        * inverse[n]
        for n in run
    ]
    ratio = [(chances[n] * inverse[n]).astype(BF16) for n in run]
    ratios = [head_stack(ratio[n]) for n in run]
    for n in run:
        added = diagonal(dot_lt(ratio[n] * back_low[n], grad[n]))
        state_v.append(state_v[n] * carry[n] + added)
    rg_low = [head_stack(state_v[n].astype(BF16)) for n in run]
    w_late = [wc[n] * late_low[n] for n in run]
    gv = [dot(beside(mixing_t[n], w_late[n]), above(grads[n], rg_low[n])) for n in run]
    weighted = [d_chance[n] * chances[n] for n in run]
    d_score = [weighted[n] - chances[n] * head_sum(weighted[n]) for n in run]
    d_pw = [(d_score[n] * inverse[n] * (HEAD_DIM**-0.5)).astype(BF16) for n in run]
    d_total = [(weighted[n] + d_score[n] * scores[n]) * inverse[n] for n in run]
    d_pws = [head_stack(d_pw[n]) for n in run]
    d_pairs = [head_pairs(dot_rt(d_pws[n], wc[n]), causal[n]) for n in run]
    for n in run:
        added = diagonal(dot_lt(d_pw[n] * back_low[n], qc[n]))
        state_k.append(state_k[n] * carry[n] + added)
        added = jnp.sum(d_total[n] * back[n], axis=0, keepdims=True)
        state_z.append(state_z[n] * carry[n] + added)
    uq_low = [head_stack(state_k[n].astype(BF16)) for n in run]
    between()
    dw = []
    for n in run:
        z_high = d_total[n].astype(BF16)
        z_low = (d_total[n] - z_high.astype(F32)).astype(BF16)
        anti = -causal[n].T.astype(BF16)
        left = beside(
            flip_pairs(d_mixing[n]), pairs_t[n], vc[n] * late_low[n], kc[n] * late_low[n], anti, anti
        )
        right = above(ratios[n], d_pws[n], rg_low[n].T, uq_low[n].T, z_high, z_low)
        dw.append(dot(left, right) - late[n] * state_z[n])
    gq = [
        dot(beside(d_pairs[n], d_pw[n] * come_low[n]), above(head_stack(kc[n]), kw_t[n]))
        for n in run
    ]
    gk = [
        dot(beside(flip_pairs(d_pairs[n]), w_late[n]), above(head_stack(qc[n]), uq_low[n]))
        for n in run
    ]
    for n in run:
        gy[g, rows[n], 512:768] = gv[n].astype(BF16)
        gy[g, rows[n], 768:1024] = (dw[n] * wc[n].astype(F32)).astype(BF16)
        gy[g, rows[n], 0:256] = gq[n].astype(BF16)
        gy[g, rows[n], 256:512] = gk[n].astype(BF16)
    rg[...] = state_v[-1]
    uq[...] = state_k[-1]
    zgrad[...] = jnp.broadcast_to(state_z[-1], zgrad.shape)


def units(j):
    return j // 2 % 2, (j // 4 * 2 + j % 2) * 256


def feed_in(r, tok, gain, wb, mixed, n2, gh, scales):
    rows = pl.ds(pl.multiple_of(r * TILE, TILE), TILE)
    hidden = tok[rows, :].astype(F32)
    for g in range(2):
        hidden += dot_rt(mixed[g, rows, :], flat(wb[g, ..., 0:256]))
    hat, scale = standardise(hidden)
    gh[rows, :] = hat
    scales[rows, :] = scale
    n2[rows, :] = (hat * gain[...]).astype(BF16)


def feed_up(part, r, up_bias, wb, n2, act, lin):
    rows = pl.ds(pl.multiple_of(r * TILE, TILE), TILE)
    normed = n2[rows, :]
    k0 = 0.7978845608
    k1 = k0 * 0.044715

    def linear_of(j):
        g, column = units(j)
        up = flat(wb[g, ..., 256 + column : 512 + column])
        bias = up_bias[:, g * 1024 + column : g * 1024 + column + 256]
        return dot(normed, up) + bias

    after = linear_of(4 * part)
    for j in range(4 * part, 4 * part + 4):
        linear = after
        if j < 4 * part + 3:
            after = linear_of(j + 1)
        square = linear * linear
        gate = 0.5 * jnp.tanh(linear * (square * k1 + k0)) + 0.5
        active = linear * gate
        slope = gate + active * (1.0 - gate) * (square * (6.0 * k1) + 2.0 * k0)
        g, column = units(j)
        act[g, rows, column : column + 256] = active.astype(BF16)
        lin[g, rows, column : column + 256] = slope.astype(BF16)


def feed_grad(part, r, cot, wb, lin, small):
    rows = pl.ds(pl.multiple_of(r * TILE, TILE), TILE)
    grad = cot[rows, :]

    def grad_of(j):
        g, column = units(j)
        down = flat(wb[g, ..., 1280 + column : 1536 + column])
        return dot(grad, down) * lin[g, rows, column : column + 256].astype(F32)

    after = grad_of(4 * part)
    for j in range(4 * part, 4 * part + 4):
        grad_low = after.astype(BF16)
        if j < 4 * part + 3:
            after = grad_of(j + 1)
        g, column = units(j)
        lin[g, rows, column : column + 256] = grad_low
        row, here = 4 + 2 * g + column // 512, column % 512
        small[row : row + 1, here : here + 256] += jnp.sum(
            grad_low.astype(F32), axis=0, keepdims=True
        )


def feed_back(r, cot, gain, wb, keepc, lin, gh, scales, gm, small):
    half = TILE // 2
    parts = [pl.ds(pl.multiple_of(r * TILE + n * half, half), half) for n in range(2)]
    backs = [
        dot_rt(lin[0, part, :], flat(wb[0, ..., 256:1280]))
        + dot_rt(lin[1, part, :], flat(wb[1, ..., 256:1280]))
        for part in parts
    ]
    hats = [gh[part, :] for part in parts]
    keeps = [twice(keepc[part, :]) for part in parts]
    hidden = []
    for part, back, hat in zip(parts, backs, hats):
        scaled = back * gain[...]
        inner = scaled - jnp.mean(scaled, axis=-1, keepdims=True)
        inner -= hat * jnp.mean(scaled * hat, axis=-1, keepdims=True)
        hidden.append(cot[part, :].astype(F32) + scales[part, :] * inner)
    mixed_grads = [
        [(dot(rows.astype(BF16), flat(wb[g, ..., 0:256])) * keep).astype(BF16) for g in range(2)]
        for rows, keep in zip(hidden, keeps)
    ]
    for n, part in enumerate(parts):
        gh[part, :] = hidden[n]
        for g in range(2):
            gm[g, part, :] = mixed_grads[n][g]
        small[0:1, :] += jnp.sum(backs[n] * hats[n], axis=0, keepdims=True)


def emit(r, tok, down_bias, wb, mixed, act):
    rows = pl.ds(pl.multiple_of(r * LAST, LAST), LAST)
    total = tok[rows, :].astype(F32)
    for g in range(2):
        total += dot_rt(mixed[g, rows, :], flat(wb[g, ..., 0:256]))
    total += down_bias[...]
    for g in range(2):
        total += dot_rt(act[g, rows, :], flat(wb[g, ..., 1280:2304]))
    tok[rows, :] = total.astype(BF16)


def transpose_into(source, target, length):
    for r in range(length // 256):
        here = slice(r * 256, (r + 1) * 256)
        turned = source[here, :].astype(BF16).T
        target[..., here] = turned.reshape(target.shape[:-1] + (256,))


def weight_grads(left_t, target, jobs):
    shape = target.shape[1:-1]

    def product(job):
        _, right, at, _, columns = job
        return dot(flat(left_t[...]), right[:, at : at + columns]).astype(BF16)

    after = product(jobs[0])
    for n, (g, _, _, to, columns) in enumerate(jobs):
        here = after
        if n + 1 < len(jobs):
            after = product(jobs[n + 1])
        target[g, ..., to : to + columns] = here.reshape(shape + (columns,))


def finish(r, tok, cot, gain, wa, gy, gh, small):
    rows = pl.ds(pl.multiple_of(r * LAST, LAST), LAST)
    hat, scale = standardise(tok[rows, :].astype(F32))
    back = dot_rt(gy[0, rows, :], flat(wa[0])) + dot_rt(gy[1, rows, :], flat(wa[1]))
    scaled = back * gain[...]
    inner = scaled - jnp.mean(scaled, axis=-1, keepdims=True)
    inner -= hat * jnp.mean(scaled * hat, axis=-1, keepdims=True)
    cot[rows, :] = (gh[rows, :] + scale * inner).astype(BF16)
    small[1:2, :] += jnp.sum(back * hat, axis=0, keepdims=True)


class Quiet:
    def nothing(self, *at):
        pass

    before = enter = normalised = weights_a = projected = mixing = nothing
    weights_up = feeding = weights_down = grads_down = feeding_down = grads_up = nothing
    mixing_back = mixed_back = grads_a = finishing = finished = gained = after = nothing


LAYER_INPUTS = 6
UP_PIECES = [(0, 768), (768, 1280)]
DOWN_PIECES = [(1280, 1792), (1792, 2304)]


def layer_body(
    length,
    comm,
    seg_row,
    pad_row,
    gain_one,
    gain_two,
    up_bias,
    down_bias,
    wa,
    wb,
    ga,
    gw,
    small,
    tok,
    cot,
    segc,
    keepc,
    n1,
    q,
    k,
    v,
    w,
    probs,
    inv,
    score,
    mixed,
    state_k,
    state_v,
    state_z,
    kw_all,
    wv_all,
    pt_all,
    mt_all,
    act,
    lin,
    gh,
    scales,
    gm,
    flip,
    n1_flip,
):
    runs, tiles = length // (UNROLL * CHUNK), length // TILE

    def clear():
        state_k[...] = jnp.zeros_like(state_k)
        state_v[...] = jnp.zeros_like(state_v)
        state_z[...] = jnp.zeros_like(state_z)

    comm.before()
    small[...] = jnp.zeros_like(small)
    rows_to_columns(seg_row, pad_row, segc, keepc, length)
    comm.enter()

    @pl.loop(0, tiles)
    def _(r):
        normalise(r, tok, cot, gain_one, n1, small)

    comm.normalised()
    transpose_into(cot, flip, length)
    transpose_into(n1, n1_flip, length)

    @pl.loop(0, 2)
    def _(g):
        comm.weights_a(g, 0)
        clear()

        @pl.loop(0, length // WIDE)
        def _(r):
            project_qk(g, r, wa, n1, q, k)

        comm.weights_a(g, 1)

        @pl.loop(0, length // WIDE)
        def _(r):
            project_vw(g, r, wa, keepc, n1, v, w)

        comm.projected(g)

        @pl.loop(0, runs)
        def _(i):
            comm.mixing(g, i)
            mix_forward(
                g, i, segc, keepc, q, k, v, w, probs, inv, score, mixed, state_k, state_v, state_z,
                kw_all, wv_all, pt_all, mt_all,
            )

    comm.weights_up(0)

    @pl.loop(0, tiles)
    def _(r):
        comm.feeding(0, r)
        feed_in(r, tok, gain_two, wb, mixed, n1, gh, scales)
        feed_up(0, r, up_bias, wb, n1, act, lin)

    transpose_into(n1, ga.at[0], length)
    comm.weights_up(1)

    @pl.loop(0, tiles)
    def _(r):
        comm.feeding(1, r)
        feed_up(1, r, up_bias, wb, n1, act, lin)

    for part in range(2):
        at = part * 512
        weight_grads(flip, gw, [(g, act.at[g], at, 1280 + at, 512) for g in range(2)])
        comm.grads_down(part)

    for part in range(2):
        comm.weights_down(part)

        @pl.loop(0, tiles)
        def _(r):
            feed_grad(part, r, cot, wb, lin, small)

    @pl.loop(0, tiles)
    def _(r):
        comm.feeding_down(r)
        feed_back(r, cot, gain_two, wb, keepc, lin, gh, scales, gm, small)

    weight_grads(ga.at[0], gw, [(g, lin.at[g], 512, 768, 512) for g in range(2)])
    comm.grads_up(0)
    weight_grads(ga.at[0], gw, [(g, lin.at[g], 0, 256, 512) for g in range(2)])
    transpose_into(gh, flip, length)
    weight_grads(flip, gw, [(g, mixed.at[g], 0, 0, GROUP) for g in range(2)])
    comm.grads_up(1)

    @pl.loop(0, 2)
    def _(g):
        clear()

        @pl.loop(0, runs)
        def _(i):
            comm.mixing_back(g, i, 0)
            mix_backward(
                g, runs - 1 - i, segc, keepc, q, k, v, w, probs, inv, score, gm, state_v, state_k,
                state_z, kw_all, wv_all, pt_all, mt_all, lin,
                functools.partial(comm.mixing_back, g, i, 1),
            )

        comm.mixed_back(g)
        for part in range(2):
            weight_grads(n1_flip, ga, [(g, lin.at[g], part * 512, part * 512, 512)])
            comm.grads_a(g, part)

    @pl.loop(0, length // LAST)
    def _(r):
        comm.finishing(0, r)
        finish(r, tok, cot, gain_one, wa, lin, gh, small)
        comm.finished(0, r)

    comm.gained()

    @pl.loop(0, length // LAST)
    def _(r):
        comm.finishing(1, r)
        emit(r, tok, down_bias, wb, mixed, act)
        comm.finished(1, r)

    comm.after()


def layer_scratch(length, width):
    vmem = pltpu.VMEM
    chunks = length // CHUNK
    return [
        vmem((length + 16, 128), F32),
        vmem((length, 128), F32),
        vmem((length, width), BF16),
        vmem((2, length, GROUP), BF16),
        vmem((2, length, GROUP), BF16),
        vmem((2, length, GROUP), BF16),
        vmem((2, length, GROUP), BF16),
        vmem((2, length, GROUP), F32),
        vmem((2, length, GROUP), F32),
        vmem((2, length, GROUP), F32),
        vmem((2, length, GROUP), BF16),
        vmem((HEAD_DIM, GROUP), F32),
        vmem((HEAD_DIM, GROUP), F32),
        vmem((8, GROUP), F32),
        vmem((2, chunks, HEAD_DIM, GROUP), BF16),
        vmem((2, chunks, HEAD_DIM, GROUP), BF16),
        vmem((2, length, 4 * CHUNK), BF16),
        vmem((2, length, 4 * CHUNK), BF16),
        vmem((2, length, 1024), BF16),
        vmem((2, length, 1024), BF16),
        vmem((length, width), F32),
        vmem((length, 1), F32),
        vmem((2, length, GROUP), BF16),
        vmem((width, length), BF16),
        vmem((width, length), BF16),
    ]


def layer_kernel(length, tokens, cotangent, *refs):
    inputs, (out, grad_out), rest = refs[: LAYER_INPUTS + 2], refs[8:10], refs[10:]
    out[...] = tokens[...]
    grad_out[...] = cotangent[...]
    ga, gw, small = rest[:3]
    layer_body(length, Quiet(), *inputs, ga, gw, small, out, grad_out, *rest[3:])


def layer(tokens, cotangent, seg_row, pad_row, gain_one, gain_two, up_bias, down_bias, wa, wb):
    length, width = tokens.shape
    shape = jax.ShapeDtypeStruct
    cut = lambda full: full.reshape(2, -1, 2, 2, 2, 16, full.shape[-1])
    wa, wb = cut(wa), cut(wb)
    space = pl.BlockSpec(memory_space=pltpu.VMEM)
    out, grad_out, ga, gw, small = pl.pallas_call(
        functools.partial(layer_kernel, length),
        out_shape=(
            shape((length, width), BF16),
            shape((length, width), BF16),
            shape(wa.shape, BF16),
            shape(wb.shape, BF16),
            shape((8, width), F32),
        ),
        in_specs=[space] * 10,
        out_specs=tuple([space] * 5),
        scratch_shapes=layer_scratch(length, width),
        compiler_params=pltpu.CompilerParams(vmem_limit_bytes=62 * 1024 * 1024),
        name="layer",
    )(tokens, cotangent, seg_row, pad_row, gain_one, gain_two, up_bias, down_bias, wa, wb)
    whole = lambda full: full.reshape(2, width, full.shape[-1])
    return out, grad_out, whole(ga), whole(gw), small


class Place:
    def __init__(self, depth):
        index = lax.axis_index("dp")
        t = lax.axis_index("tensor")
        x, y, z = lax.rem(index, 2), lax.rem(index // 2, 2), index // 4
        self.depth = depth
        self.x, self.y, self.z, self.t, self.other = x, y, z, t, 1 - t
        self.near = (y + t * (1 - 2 * y), x + (1 - t) * (1 - 2 * x))
        self.next = (y + (1 - t) * (1 - 2 * y), x + t * (1 - 2 * x))
        self.far = (1 - y, 1 - x)
        chip = lambda z, y, x: (z * 2 + y) * 2 + x
        self.levels = [lax.rem(z + s, depth) for s in range(depth)]
        self.chips_z = [chip(level, y, x) for level in self.levels]
        self.to_near = {"dp": chip(z, *self.near)}
        self.to_next = {"dp": chip(z, *self.next)}
        self.to_pair = {"tensor": self.other}
        self.spot = (y * 2 + x) * 2 + t
        flip = lambda value, bit: value + bit * (1 - 2 * value)
        self.level = [
            {
                "dp": chip(z, flip(y, offset // 4), flip(x, offset // 2 % 2)),
                "tensor": flip(t, offset % 2),
            }
            for offset in range(8)
        ]

    def along_z(self, step, core):
        return {"dp": self.chips_z[step], "tensor": core}

    def friends(self):
        along = [self.along_z(s, core) for s in range(1, self.depth) for core in range(2)]
        return self.level[1:] + along

    def knock(self):
        barrier = pltpu.get_barrier_semaphore()
        for friend in self.friends():
            pl.semaphore_signal(barrier, inc=1, device_id=friend, device_id_type=MESH)

    def enter(self):
        pl.semaphore_wait(pltpu.get_barrier_semaphore(), len(self.friends()))


class Copies:
    def __init__(self, sems):
        self.sems = sems

    def build(self, source, target, device, out_sem, in_sem):
        return pltpu.make_async_remote_copy(
            src_ref=source,
            dst_ref=target,
            send_sem=self.sems.at[0, out_sem],
            recv_sem=self.sems.at[1, in_sem],
            device_id=device,
            device_id_type=MESH,
        )

    def start(self, source, target, device, number, in_sem=None, only=None):
        def begin():
            landing = number if in_sem is None else in_sem
            self.build(source(), target, device, number, landing).start()

        begin() if only is None else pl.when(only)(begin)

    def landed(self, target, number, only=None):
        def wait():
            self.build(target, target, {"tensor": 0}, number, number).wait_recv()

        wait() if only is None else pl.when(only)(wait)

    def sent(self, source, numbers, only=None):
        def wait():
            for number in numbers:
                self.build(source, source, {"tensor": 0}, number, number).wait_send()

        wait() if only is None else pl.when(only)(wait)


class Gather(Copies):
    COPIES = 14

    def __init__(self, place, own, full, group, columns, sems):
        super().__init__(sems)
        self.p, self.own, self.full, self.columns = place, own, full, columns
        self.group = group
        self.groups = slice(None) if group is None else slice(group, group + 1)
        self.mine = None if group is None else place.t == group
        self.pairs = None if group is None else place.t != group

    def at(self, g, z, spot, half):
        return self.full.at[g, z, spot[0], spot[1], half, :, self.columns]

    def block(self, spot, half):
        return self.at(self.groups, slice(None), spot, half)

    def forward(self, spot, device, number):
        block = lambda: self.block(spot, self.p.t)
        self.start(block, block(), device, number)

    def first(self):
        p = self.p
        here = (p.y, p.x)
        for s in range(1, p.depth):
            for core in range(2):
                self.start(
                    lambda core=core: self.own.at[core, :, self.columns],
                    self.at(p.t, p.z, here, core),
                    p.along_z(s, core),
                    2 * (s - 1) + core,
                    2 * (s - 1) + p.t,
                    only=self.mine,
                )
        self.start(
            lambda: self.own.at[p.other, :, self.columns],
            self.at(p.t, p.z, here, p.other),
            p.to_pair,
            6,
            only=self.mine,
        )

        def keep():
            self.full[p.t, p.z, p.y, p.x, p.t, :, self.columns] = self.own[p.t, :, self.columns]

        keep() if self.mine is None else pl.when(self.mine)(keep)

    def second(self):
        p = self.p
        here = (p.y, p.x)
        for n in range(6):
            if self.group is None or n % 2 == self.group:
                self.landed(self.at(p.t, p.z, here, p.t), n)
        self.landed(self.at(p.t, p.z, here, p.t), 6, only=self.pairs)
        self.forward(here, p.to_near, 7)
        self.forward(here, p.to_next, 8)
        self.forward(here, p.to_pair, 9)

    def third(self):
        p = self.p
        self.landed(self.block(p.near, p.t), 7)
        self.forward(p.near, p.to_next, 10)
        self.forward(p.near, p.to_pair, 11)
        self.landed(self.block(p.next, p.t), 8)
        self.forward(p.next, p.to_pair, 12)

    def fourth(self):
        p = self.p
        self.landed(self.block(p.far, p.t), 10)
        self.forward(p.far, p.to_pair, 13)

    def last(self):
        p = self.p
        for n in (9, 11, 12, 13):
            self.landed(self.block((p.y, p.x), p.other), n)

    def left(self):
        p = self.p
        self.sent(self.own.at[0, :, self.columns], range(7), self.mine)
        self.sent(self.block((p.y, p.x), p.t), range(7, 14))


class Scatter(Copies):
    COPIES = 11

    def __init__(self, place, part, group, columns, pair_in, near_in, next_in, last_in, sems):
        super().__init__(sems)
        self.p, self.part, self.columns = place, part, columns
        self.pair_in, self.near_in, self.next_in, self.last_in = pair_in, near_in, next_in, last_in
        self.group = group
        self.groups = slice(None) if group is None else slice(group, group + 1)
        self.mine = None if group is None else place.t == group
        self.pairs = None if group is None else place.t != group

    def at(self, g, z, spot, half):
        return self.part.at[g, z, spot[0], spot[1], half, :, self.columns]

    def block(self, spot, half):
        return self.at(self.groups, slice(None), spot, half)

    def add(self, spot, landed):
        p = self.p
        here = (self.groups, slice(None), spot[0], spot[1], p.t, slice(None), self.columns)
        self.part[here] = (self.part[here].astype(F32) + landed.astype(F32)).astype(BF16)

    def first(self):
        p = self.p
        self.start(
            lambda: self.part.at[self.groups, :, :, :, p.other, :, self.columns],
            self.pair_in,
            p.to_pair,
            0,
        )

    def second(self):
        p = self.p
        self.landed(self.pair_in, 0)
        for spot, number in ((p.far, 1), (p.near, 2)):
            self.add(spot, self.pair_in[:, :, spot[0], spot[1]])
            self.start(
                lambda spot=spot: self.block(spot, p.t),
                self.near_in.at[number - 1],
                p.to_near,
                number,
            )
        for spot in (p.next, (p.y, p.x)):
            self.add(spot, self.pair_in[:, :, spot[0], spot[1]])

    def third(self):
        p = self.p
        self.landed(self.near_in.at[0], 1)
        self.add(p.next, self.near_in[0])
        self.start(lambda: self.block(p.next, p.t), self.next_in, p.to_next, 3)
        self.landed(self.near_in.at[1], 2)
        self.add((p.y, p.x), self.near_in[1])

    def fourth(self):
        p = self.p
        here = (p.y, p.x)
        self.landed(self.next_in, 3)
        self.add(here, self.next_in[...])
        for s in range(1, p.depth):
            for core in range(2) if self.group is None else (self.group,):
                self.start(
                    lambda s=s, core=core: self.at(core, p.levels[s], here, p.t),
                    self.last_in.at[2 * (s - 1) + p.t],
                    p.along_z(s, core),
                    4 + 2 * (s - 1) + core,
                    4 + 2 * (s - 1) + p.t,
                )
        self.start(
            lambda: self.at(p.other, p.z, here, p.t),
            self.last_in.at[2 * (p.depth - 1)],
            p.to_pair,
            10,
            only=self.pairs,
        )

    def last(self, target):
        p = self.p

        def write():
            for n in range(7):
                self.landed(self.last_in.at[n], 4 + n)
            mine = self.part[p.t, p.z, p.y, p.x, p.t, :, self.columns].astype(F32)
            rest = self.last_in[2 * (p.depth - 1)].astype(F32)
            for s in range(1, p.depth):
                mine += self.last_in[2 * (s - 1) + p.t].astype(F32)
                rest += self.last_in[2 * (s - 1) + p.other].astype(F32)
            target[p.t] = mine
            target[p.other] = rest

        write() if self.mine is None else pl.when(self.mine)(write)

    def left(self):
        p = self.p
        self.sent(self.pair_in, (0,))
        self.sent(self.next_in, (1, 2, 3))
        for core in range(2) if self.group is None else (self.group,):
            self.sent(self.last_in.at[0], [4 + 2 * s + core for s in range(p.depth - 1)])
        self.sent(self.last_in.at[0], (10,), self.pairs)


def scatter_scratch(groups, depth, columns):
    vmem = pltpu.VMEM
    return [
        vmem((groups, depth, 2, 2, 16, columns), BF16),
        vmem((2, groups, depth, 16, columns), BF16),
        vmem((groups, depth, 16, columns), BF16),
        vmem((2 * depth - 1, 16, columns), BF16),
    ]


class Reduce(Copies):
    COPIES = 12

    def __init__(self, place, own, parts, sums, sems):
        super().__init__(sems)
        self.p, self.own, self.parts, self.sums = place, own, parts, sums

    def first(self):
        p = self.p
        self.parts[p.spot] = self.own[...]
        for offset in range(1, 8):
            self.start(
                lambda: self.own, self.parts.at[p.spot], p.level[offset], offset - 1
            )

    def second(self):
        p = self.p
        for n in range(7):
            self.landed(self.own, n)
        total = self.parts[0]
        for spot in range(1, 8):
            total += self.parts[spot]
        self.sums[p.z] = total
        for s in range(1, p.depth):
            self.start(
                lambda: self.sums.at[p.z], self.sums.at[p.z], {"dp": p.chips_z[s]}, 6 + s
            )

    def last(self):
        p = self.p
        for s in range(1, p.depth):
            self.landed(self.own, 6 + s)
        total = self.sums[0]
        for z in range(1, p.depth):
            total += self.sums[z]
        return total

    def left(self):
        self.sent(self.own, range(6 + self.p.depth))


class Woven:
    def __init__(self, place, far, near, own, full, gathers, scatters, gains):
        self.p, self.far, self.near, self.own = place, far, near, own
        wa, wb, ga, gw = full
        own_a, own_b = own
        ranges = [(own_a, wa, 0, 0, 512), (own_a, wa, 0, 512, 1024), (own_a, wa, 1, 0, 1024)]
        ranges += [(own_b, wb, None, *part) for part in UP_PIECES + DOWN_PIECES]
        gather = [
            Gather(place, part, whole, g, slice(first, last), sems)
            for (part, whole, g, first, last), sems in zip(ranges, gathers)
        ]
        self.a0, self.a1, self.b = gather[:2], gather[2], gather[3:]
        ranges = [(gw, None, *part) for part in DOWN_PIECES + UP_PIECES[::-1]]
        ranges += [(ga, 0, 0, 1024), (ga, 1, 0, 512), (ga, 1, 512, 1024)]
        scatter = [
            Scatter(place, part, g, slice(first, last), *buffers)
            for (part, g, first, last), buffers in zip(ranges, scatters)
        ]
        self.down_grad, self.up_grad = scatter[:2], scatter[2:4]
        self.a0_grad, self.a1_grad = scatter[4], scatter[5:]
        self.gains = gains
        self.everything = scatter + [gains]

    def table(self, at, steps):
        for place, calls in steps.items():
            here = None
            for value, wanted in zip(at, place):
                here = (value == wanted) if here is None else here & (value == wanted)

            @pl.when(here)
            def _(calls=calls):
                for call in calls:
                    call()

    def fetch(self, n):
        return pltpu.make_async_copy(self.far[n], self.near[n], self.near["sems"].at[n])

    def put(self, name, n):
        return pltpu.make_async_copy(self.near[name], self.far[name], self.near["sems"].at[n])

    def put_rows(self, which, r):
        rows = pl.ds(pl.multiple_of(r * LAST, LAST), LAST)
        source, target = ((1, "grad_out"), (0, "out"))[which]
        return pltpu.make_async_copy(
            self.near[source].at[rows],
            self.far[target].at[rows],
            self.near["sems"].at[18 + 4 * which + r],
        )

    def before(self):
        self.p.knock()
        for n in range(14, -1, -1):
            self.fetch(n).start()
        for n in range(2, 15):
            self.fetch(n).wait()
        first = self.p.t == 0
        for rows, row in ((2, "seg_row"), (3, "pad_row")):
            rows = self.near[rows]
            self.near[row][...] = jnp.where(first, rows[0:1, :], rows[1:2, :])
        own_a, own_b = self.own
        halves = lambda n: self.near[n][...].astype(BF16).reshape(2, 16, -1)
        for n in range(4):
            own_a[:, :, 256 * n : 256 * n + 256] = halves(8 + n)
        own_b[:, :, 0:256] = halves(12)
        own_b[:, :, 256:1280] = halves(13)
        own_b[:, :, 1280:2304] = halves(14)

    def enter(self):
        self.p.enter()
        self.a0[0].first()
        self.a0[1].first()
        self.fetch(0).wait()
        self.fetch(1).wait()

    def normalised(self):
        pass

    def weights_a(self, g, part):
        one, two = self.a0
        a1, b = self.a1, self.b
        self.table(
            (g,),
            (
                {
                    (0,): (
                        one.second, a1.first, two.second, b[0].first, one.third, two.third,
                        one.fourth, a1.second, one.last,
                    ),
                    (1,): (a1.fourth, a1.last),
                },
                {
                    (0,): (b[1].first, two.fourth, two.last),
                    (1,): (b[0].third, b[3].first),
                },
            )[part],
        )

    def projected(self, g):
        b = self.b
        self.table((g,), {(0,): (self.a1.third, b[0].second), (1,): (b[2].second,)})

    def mixing(self, g, i):
        b = self.b
        steps = {
            (0, 1): (b[1].second, self.a0[0].left, self.a0[1].left, b[2].first),
            (1, 1): (b[1].third, b[0].fourth),
        }
        self.table((g, i), steps)

    def weights_up(self, part):
        b = self.b
        if part == 0:
            b[3].second()
            b[0].last()
        else:
            b[1].last()

    def feeding(self, part, r):
        b = self.b
        steps = {(0, 1): (b[2].third, b[1].fourth), (1, 1): (b[3].third, b[2].fourth)}
        self.table((part, r), steps)

    def grads_down(self, part):
        if part == 1:
            self.b[3].fourth()
        else:
            self.a1.left()
            self.b[0].left()
            self.b[1].left()
        self.down_grad[part].first()

    def weights_down(self, part):
        self.b[2 + part].last()
        self.b[2 + part].left()
        if part == 1:
            self.down_grad[0].second()

    def feeding_down(self, r):
        one, two = self.down_grad
        self.table((r,), {(0,): (two.second,)})

    def grads_up(self, part):
        self.up_grad[part].first()
        self.down_grad[part].third()

    def mixing_back(self, g, i, part):
        up, rest = self.up_grad
        one, two = self.down_grad
        steps = {
            (0, 0, 1): (up.second, one.fourth),
            (0, 1, 0): (rest.second, two.fourth),
            (1, 1, 0): (self.a0_grad.second, self.down_last),
            (1, 1, 1): (rest.third,),
        }
        self.table((g, i, part), steps)

    def mixed_back(self, g):
        self.table((g,), {(1,): (self.up_grad[0].fourth,)})

    def grads_a(self, g, part):
        one, two = self.a1_grad
        if part == 0:
            self.table((g,), {(1,): (one.first,)})
        else:
            self.table((g,), {(0,): (self.a0_grad.first, self.up_grad[0].third), (1,): (two.first,)})

    def finishing(self, which, r):
        one, two = self.a1_grad
        steps = {
            (0, 1): (one.second,),
            (0, 2): (self.a0_grad.third, two.second),
            (0, 3): (self.up_grad[1].fourth,),
            (1, 1): (one.third,),
            (1, 2): (self.a0_grad.fourth,),
            (1, 3): (two.third,),
        }
        self.table((which, r), steps)

    def down_last(self):
        dw = self.near["dw"]
        self.down_grad[0].last(dw.at[:, :, 1280:1792])
        self.down_grad[1].last(dw.at[:, :, 1792:2304])

    def finished(self, which, r):
        self.put_rows(which, r).start()

    def gained(self):
        self.gains.first()

    def after(self):
        one, two = self.a1_grad
        up, rest = self.up_grad
        da, dw = self.near["da"], self.near["dw"]
        self.gains.second()
        one.fourth()
        two.fourth()
        up.last(dw.at[:, :, 768:1280])
        rest.last(dw.at[:, :, 0:768])
        self.put("dw", 15).start()
        self.near["total"][...] = self.gains.last()
        self.put("total", 16).start()
        self.a0_grad.last(da)
        one.last(da.at[:, :, 0:512])
        two.last(da.at[:, :, 512:1024])
        self.put("da", 17).start()
        self.everything_left()

    def everything_left(self):
        for copies in self.everything:
            copies.left()
        for r in range(4):
            self.put_rows(0, r).wait()
            self.put_rows(1, r).wait()
        self.put("dw", 15).wait()
        self.put("total", 16).wait()
        self.put("da", 17).wait()


def woven_kernel(length, depth, *refs):
    refs = list(refs)
    take = lambda n: [refs.pop(0) for _ in range(n)]
    far = dict(enumerate(take(15)))
    far.update(zip(("out", "grad_out", "da", "dw", "total"), take(5)))
    near = dict(enumerate(take(15)))
    near.update(zip(("da", "dw", "total", "seg_row", "pad_row", "sems"), take(6)))
    own, full = take(2), take(4)
    small, parts, sums, gain_sems = take(4)
    gathers = take(7)
    scatters = [take(4) for _ in range(7)]
    scatters = [buffers + [sems] for buffers, sems in zip(scatters, gathers)]
    place = Place(depth)
    gains = Reduce(place, small, parts, sums, gain_sems)
    comm = Woven(place, far, near, own, full, gathers, scatters, gains)
    layer_body(
        length, comm, near["seg_row"], near["pad_row"], *[near[n] for n in range(4, 8)], *full,
        small, near[0], near[1], *refs,
    )


def write_kernel(out_in, grad_in, da, dw, small, *refs):
    (
        out, grad_out, mixer_gain, query, key, value, slot, out_t, feed_gain, up, up_bias, down_t,
        down_bias,
    ) = refs
    out[...] = out_in[...]
    grad_out[...] = grad_in[...]
    rows = lambda part: part.reshape(-1, part.shape[-1])
    query[...] = rows(da[:, :, 0:256])
    key[...] = rows(da[:, :, 256:512])
    value[...] = rows(da[:, :, 512:768])
    slot[...] = rows(da[:, :, 768:1024])
    out_t[...] = rows(dw[:, :, 0:256])
    up[...] = rows(dw[:, :, 256:1280])
    down_t[...] = rows(dw[:, :, 1280:2304])
    feed_gain[...] = small[0:1, :]
    mixer_gain[...] = small[1:2, :]
    down_bias[...] = small[2:3, :]
    for row in range(4):
        up_bias[:, row * 512 : (row + 1) * 512] = small[4 + row : 5 + row, :]


def write(out, grad_out, da, dw, small):
    shape = jax.ShapeDtypeStruct
    space = pl.BlockSpec(memory_space=pltpu.VMEM)
    width = out.shape[1]
    square, wide = shape((32, 256), F32), shape((32, 1024), F32)
    row = shape((1, width), F32)
    return pl.pallas_call(
        write_kernel,
        out_shape=(
            shape(out.shape, BF16),
            shape(out.shape, BF16),
            row,
            square,
            square,
            square,
            square,
            square,
            row,
            wide,
            shape((1, 4 * width), F32),
            wide,
            row,
        ),
        in_specs=[space] * 5,
        out_specs=(space,) * 13,
        name="write",
    )(out, grad_out, da, dw, small)


def woven(depth, *inputs):
    length, width = inputs[0].shape
    shape = jax.ShapeDtypeStruct
    far = pl.BlockSpec(memory_space=pl.ANY)
    vmem = pltpu.VMEM
    dma = pltpu.SemaphoreType.DMA
    full = lambda columns: vmem((2, depth, 2, 2, 2, 16, columns), BF16)
    da, dw, total = shape((2, 16, 1024), F32), shape((2, 16, 2304), F32), shape((8, width), F32)
    scatters = []
    for groups, columns in ((2, 512), (2, 512), (2, 512), (2, 768), (1, 1024), (1, 512), (1, 512)):
        scatters += scatter_scratch(groups, depth, columns)
    return pl.pallas_call(
        functools.partial(woven_kernel, length, depth),
        out_shape=(shape((length, width), BF16), shape((length, width), BF16), da, dw, total),
        in_specs=[far] * 15,
        out_specs=(far,) * 5,
        scratch_shapes=[vmem(array.shape, array.dtype) for array in inputs]
        + [vmem(array.shape, array.dtype) for array in (da, dw, total)]
        + [
            vmem((1, length), jnp.int32),
            vmem((1, length), jnp.int32),
            dma((26,)),
            vmem((2, 16, 1024), BF16),
            vmem((2, 16, 2304), BF16),
            full(1024),
            full(2304),
            full(1024),
            full(2304),
            vmem((8, width), F32),
            vmem((8, 8, width), F32),
            vmem((depth, 8, width), F32),
            dma((2, Reduce.COPIES)),
        ]
        + [dma((2, Gather.COPIES))] * 7
        + scatters
        + layer_scratch(length, width),
        compiler_params=pltpu.CompilerParams(
            collective_id=0, has_side_effects=True, vmem_limit_bytes=63 * 1024 * 1024
        ),
        name="woven",
    )(*inputs)


def per_device(
    direct,
    tokens,
    segment_ids,
    padding,
    mixer_gain,
    query_weight,
    key_weight,
    value_weight,
    slot_weight,
    out_weight,
    feed_gain,
    up_weight,
    up_bias,
    down_weight,
    down_bias,
    cotangent,
):
    gains = (mixer_gain[None], feed_gain[None])
    biases = (up_bias[None], down_bias[None])
    if direct:
        owns = (
            query_weight, key_weight, value_weight, slot_weight, out_weight.T, up_weight,
            down_weight.T,
        )
        depth = lax.axis_size("dp") // 4
        results = write(
            *woven(depth, tokens, cotangent, segment_ids, padding, *gains, *biases, *owns)
        )
        (
            out, grad_out, gain_one, query, key, value, slot, out_t, gain_two, up, bias_one, down_t,
            bias_two,
        ) = results
        return (
            out, grad_out, gain_one[0], query, key, value, slot, out_t.T, gain_two[0], up,
            bias_one[0], down_t.T, bias_two[0],
        )
    own_a = jnp.concatenate([query_weight, key_weight, value_weight, slot_weight], 1)
    own_b = jnp.concatenate([out_weight.T, up_weight, down_weight.T], 1)
    wa, wb = (
        lax.all_gather(lax.all_gather(own.astype(BF16), "dp", axis=0, tiled=True), "tensor")
        for own in (own_a, own_b)
    )
    half = lax.axis_index("tensor")
    pick = lambda rows: lax.dynamic_slice_in_dim(rows, half, 1, 0)
    out, grad_out, ga, gw, small = layer(
        tokens, cotangent, pick(segment_ids), pick(padding), *gains, *biases, wa, wb
    )
    da, dw = (
        lax.psum_scatter(
            lax.psum_scatter(part.astype(F32), "tensor", scatter_dimension=0),
            "dp",
            scatter_dimension=0,
            tiled=True,
        )
        for part in (ga, gw)
    )
    small = lax.psum(small, ("dp", "tensor"))
    return (
        out,
        grad_out,
        small[1],
        da[:, 0:256],
        da[:, 256:512],
        da[:, 512:768],
        da[:, 768:1024],
        dw[:, 0:256].T,
        small[0],
        dw[:, 256:1280],
        small[4:8].reshape(-1),
        dw[:, 1280:2304].T,
        small[2],
    )


def solution(mesh):
    in_specs = (
        P(("dp", "tensor"), None),
        P("dp", None),
        P("dp", None),
        P(),
        P("dp", "tensor"),
        P("dp", "tensor"),
        P("dp", "tensor"),
        P("dp", "tensor"),
        P("tensor", "dp"),
        P(),
        P("dp", "tensor"),
        P(),
        P("tensor", "dp"),
        P(),
        P(("dp", "tensor"), None),
    )
    out_specs = (
        P(("dp", "tensor"), None),
        P(("dp", "tensor"), None),
        P(),
        P("dp", "tensor"),
        P("dp", "tensor"),
        P("dp", "tensor"),
        P("dp", "tensor"),
        P("tensor", "dp"),
        P(),
        P("dp", "tensor"),
        P(),
        P("tensor", "dp"),
        P(),
    )
    direct = mesh.shape["dp"] == 16 and mesh.shape["tensor"] == 2
    return jax.shard_map(
        functools.partial(per_device, direct),
        mesh=mesh,
        in_specs=in_specs,
        out_specs=out_specs,
        check_vma=False,
    )
```

```python
import functools
import math

import jax
import jax.numpy as jnp
from jax import lax
from jax.experimental import pallas as pl
from jax.experimental.pallas import tpu as pltpu
from jax.sharding import PartitionSpec as P

HEAD_DIM = 64
SLOTS = 64
CHUNK = 128
UNROLL = 4
GROUP = 256
TILE = 512
WIDE = 512
LAST = 256

F32 = jnp.float32
BF16 = jnp.bfloat16
MESH = pl.DeviceIdType.MESH


def dot(left, right):
    return lax.dot_general(left, right, (((1,), (0,)), ((), ())), preferred_element_type=F32)


def dot_rt(left, right):
    return lax.dot_general(left, right, (((1,), (1,)), ((), ())), preferred_element_type=F32)


def dot_lt(left, right):
    return lax.dot_general(left, right, (((0,), (0,)), ((), ())), preferred_element_type=F32)


def twice(block):
    return jnp.concatenate([block, block], axis=1)


def standardise(rows):
    centred = rows - jnp.mean(rows, axis=-1, keepdims=True)
    scale = lax.rsqrt(jnp.mean(centred * centred, axis=-1, keepdims=True) + 1e-05)
    return centred * scale, scale


def head_stack(block):
    lane = lax.broadcasted_iota(jnp.int32, block.shape, 1) // HEAD_DIM
    zero = jnp.zeros_like(block)
    return jnp.concatenate([jnp.where(lane == h, block, zero) for h in range(4)], axis=0)


def diagonal(product):
    parts = [product[h * HEAD_DIM : (h + 1) * HEAD_DIM, :] for h in range(4)]
    lane = lax.broadcasted_iota(jnp.int32, parts[0].shape, 1) // HEAD_DIM
    kept = parts[3]
    for h in range(3):
        kept = jnp.where(lane == h, parts[h], kept)
    return kept


def over_heads(block, reduce, rest):
    halves = []
    lane = lax.broadcasted_iota(jnp.int32, (block.shape[0], 128), 1) < HEAD_DIM
    for j in range(block.shape[1] // 128):
        part = block[:, j * 128 : (j + 1) * 128]
        first = reduce(jnp.where(lane, part, rest), axis=1, keepdims=True)
        second = reduce(jnp.where(lane, rest, part), axis=1, keepdims=True)
        halves.append(jnp.where(lane, first, second))
    return jnp.concatenate(halves, axis=1)


def head_max(block):
    return over_heads(block, jnp.max, -jnp.inf)


def head_sum(block):
    return over_heads(block, jnp.sum, 0.0)


def head_pairs(product, allowed):
    parts = [product[h * CHUNK : (h + 1) * CHUNK, :] * allowed for h in range(4)]
    return jnp.concatenate(parts, axis=1).astype(BF16)


def flip_pairs(pairs):
    parts = [pairs[:, h * CHUNK : (h + 1) * CHUNK].T for h in range(4)]
    return jnp.concatenate(parts, axis=1)


def beside(*blocks):
    return jnp.concatenate(blocks, axis=1)


def above(*blocks):
    return jnp.concatenate(blocks, axis=0)


def flat(block):
    return block.reshape(-1, block.shape[-1])


def rows_to_columns(seg_row, pad_row, segc, keepc, length):
    segc[pl.ds(0, 8), :] = jnp.full((8, 128), -1.0, F32)
    segc[pl.ds(8 + length, 8), :] = jnp.full((8, 128), -2.0, F32)
    for c in range(length // CHUNK):
        here = slice(c * CHUNK, (c + 1) * CHUNK)
        seg = jnp.broadcast_to(seg_row[:, here].astype(F32), (CHUNK, CHUNK))
        pad = jnp.broadcast_to(pad_row[:, here].astype(F32), (CHUNK, CHUNK))
        segc[pl.ds(8 + c * CHUNK, CHUNK), :] = seg.T
        keepc[pl.ds(c * CHUNK, CHUNK), :] = 1.0 - pad.T


def normalise(r, tok, cot, gain, n1, small):
    rows = pl.ds(pl.multiple_of(r * TILE, TILE), TILE)
    xhat, _ = standardise(tok[rows, :].astype(F32))
    n1[rows, :] = (xhat * gain[...]).astype(BF16)
    small[2:3, :] += jnp.sum(cot[rows, :].astype(F32), axis=0, keepdims=True)


def project_qk(g, r, wa, n1, q, k):
    rows = pl.ds(pl.multiple_of(r * WIDE, WIDE), WIDE)
    out = dot(n1[rows, :], flat(wa[g, ..., 0:512]))
    q[g, rows, :] = out[:, 0:256].astype(BF16)
    k[g, rows, :] = out[:, 256:512].astype(BF16)


def project_vw(g, r, wa, keepc, n1, v, w):
    rows = pl.ds(pl.multiple_of(r * WIDE, WIDE), WIDE)
    out = dot(n1[rows, :], flat(wa[g, ..., 512:1024]))
    v[g, rows, :] = out[:, 0:256].astype(BF16)
    w[g, rows, :] = (jnp.exp(out[:, 256:512]) * twice(keepc[rows, :])).astype(BF16)


def chunk_masks(c, segc):
    base = pl.multiple_of(c * CHUNK, CHUNK)
    seg = segc[pl.ds(base + 8, CHUNK), :]
    across = seg.T
    row = lax.broadcasted_iota(jnp.int32, (CHUNK, CHUNK), 0)
    column = lax.broadcasted_iota(jnp.int32, (CHUNK, CHUNK), 1)
    same = seg == across
    causal = jnp.where(same & (column <= row), 1.0, 0.0)
    before = segc[pl.ds(base + 7, 1), :]
    first = segc[pl.ds(base + 8, 1), :]
    last = segc[pl.ds(base + 7 + CHUNK, 1), :]
    after = segc[pl.ds(base + 8 + CHUNK, 1), :]
    one = lambda test: jnp.where(test, 1.0, 0.0)
    return causal, dict(
        from_before=one(seg == before),
        to_after=one(seg == last),
        from_after=one(seg == after),
        to_before=one(seg == first),
        carry_on=one(before == last),
        carry_back=one(after == first),
    )


def mix_forward(
    g, i, segc, keepc, q, k, v, w, probs, inv, score, mixed, kw, wv, zsum, kw_all, wv_all, pt_all,
    mt_all,
):
    run = range(UNROLL)
    chunks = [UNROLL * i + n for n in run]
    rows = [pl.ds(pl.multiple_of(c * CHUNK, CHUNK), CHUNK) for c in chunks]
    masks = [chunk_masks(c, segc) for c in chunks]
    keep = [twice(keepc[r, :]) for r in rows]
    qc, kc, vc, wc = ([ref[g, r, :] for r in rows] for ref in (q, k, v, w))
    state_k, state_v, state_z = [kw[...]], [wv[...]], [zsum[0:1, :]]
    causal = [mask for mask, _ in masks]
    edge = [edges for _, edges in masks]
    come = [twice(edge[n]["from_before"]) for n in run]
    come_low = [come[n].astype(BF16) for n in run]
    pairs = [head_pairs(dot_rt(head_stack(qc[n]), kc[n]), causal[n]) for n in run]
    for n in run:
        carry = twice(edge[n]["carry_on"])
        wg = wc[n] * twice(edge[n]["to_after"]).astype(BF16)
        state_k.append(state_k[n] * carry + diagonal(dot_lt(kc[n], wg)))
        state_v.append(state_v[n] * carry + diagonal(dot_lt(wg, vc[n])))
        state_z.append(state_z[n] * carry + jnp.sum(wg.astype(F32), axis=0, keepdims=True))
    kw_low = [head_stack(state_k[n].astype(BF16)) for n in run]
    wv_low = [head_stack(state_v[n].astype(BF16)) for n in run]
    inverse = [
        1.0 / (dot(causal[n].astype(BF16), wc[n]) + come[n] * state_z[n] + (1.0 - keep[n]))
        for n in run
    ]
    scores = [
        dot(beside(pairs[n], qc[n] * come_low[n]), above(head_stack(wc[n]), kw_low[n]))
        * (inverse[n] * (HEAD_DIM**-0.5))
        for n in run
    ]
    powers = [jnp.exp(scores[n] - head_max(scores[n])) for n in run]
    chances = [powers[n] / head_sum(powers[n]) for n in run]
    ratio = [(chances[n] * inverse[n]).astype(BF16) for n in run]
    mixing = [head_pairs(dot_rt(head_stack(ratio[n]), wc[n]), causal[n]) for n in run]
    out = [
        dot(beside(mixing[n], ratio[n] * come_low[n]), above(head_stack(vc[n]), wv_low[n]))
        for n in run
    ]
    for n in run:
        r = rows[n]
        kw_all[g, chunks[n]] = diagonal(kw_low[n].T)
        wv_all[g, chunks[n]] = diagonal(wv_low[n].T)
        pt_all[g, r, :] = flip_pairs(pairs[n])
        mt_all[g, r, :] = flip_pairs(mixing[n])
        inv[g, r, :] = inverse[n]
        score[g, r, :] = scores[n].astype(BF16)
        probs[g, r, :] = chances[n]
        mixed[g, r, :] = (out[n] * keep[n]).astype(BF16)
    kw[...] = state_k[-1]
    wv[...] = state_v[-1]
    zsum[...] = jnp.broadcast_to(state_z[-1], zsum.shape)


def mix_backward(
    g, i, segc, keepc, q, k, v, w, probs, inv, score, gm, rg, uq, zgrad, kw_all, wv_all, pt_all,
    mt_all, gy, between,
):
    run = range(UNROLL)
    chunks = [UNROLL * i + UNROLL - 1 - n for n in run]
    rows = [pl.ds(pl.multiple_of(c * CHUNK, CHUNK), CHUNK) for c in chunks]
    masks = [chunk_masks(c, segc) for c in chunks]
    qc, kc, vc, wc, grad, chances, inverse, scores, pairs_t, mixing_t = (
        [ref[g, r, :] for r in rows]
        for ref in (q, k, v, w, gm, probs, inv, score, pt_all, mt_all)
    )
    kw_t, wv_t = ([head_stack(ref[g, c]) for c in chunks] for ref in (kw_all, wv_all))
    state_v, state_k, state_z = [rg[...]], [uq[...]], [zgrad[0:1, :]]
    causal = [mask for mask, _ in masks]
    edge = [edges for _, edges in masks]
    come_low = [twice(edge[n]["from_before"]).astype(BF16) for n in run]
    late = [twice(edge[n]["from_after"]) for n in run]
    late_low = [late[n].astype(BF16) for n in run]
    back = [twice(edge[n]["to_before"]) for n in run]
    back_low = [back[n].astype(BF16) for n in run]
    carry = [twice(edge[n]["carry_back"]) for n in run]
    grads = [head_stack(grad[n]) for n in run]
    d_mixing = [head_pairs(dot_rt(grads[n], vc[n]), causal[n]) for n in run]
    d_chance = [
        dot(beside(d_mixing[n], grad[n] * come_low[n]), above(head_stack(wc[n]), wv_t[n]))
        * inverse[n]
        for n in run
    ]
    ratio = [(chances[n] * inverse[n]).astype(BF16) for n in run]
    ratios = [head_stack(ratio[n]) for n in run]
    for n in run:
        added = diagonal(dot_lt(ratio[n] * back_low[n], grad[n]))
        state_v.append(state_v[n] * carry[n] + added)
    rg_low = [head_stack(state_v[n].astype(BF16)) for n in run]
    w_late = [wc[n] * late_low[n] for n in run]
    gv = [dot(beside(mixing_t[n], w_late[n]), above(grads[n], rg_low[n])) for n in run]
    weighted = [d_chance[n] * chances[n] for n in run]
    d_score = [weighted[n] - chances[n] * head_sum(weighted[n]) for n in run]
    d_pw = [(d_score[n] * inverse[n] * (HEAD_DIM**-0.5)).astype(BF16) for n in run]
    d_total = [
        (weighted[n] + d_score[n] * scores[n].astype(F32)) * inverse[n] for n in run
    ]
    d_pws = [head_stack(d_pw[n]) for n in run]
    d_pairs = [head_pairs(dot_rt(d_pws[n], wc[n]), causal[n]) for n in run]
    for n in run:
        added = diagonal(dot_lt(d_pw[n] * back_low[n], qc[n]))
        state_k.append(state_k[n] * carry[n] + added)
        added = jnp.sum(d_total[n] * back[n], axis=0, keepdims=True)
        state_z.append(state_z[n] * carry[n] + added)
    uq_low = [head_stack(state_k[n].astype(BF16)) for n in run]
    between()
    dw = []
    for n in run:
        z_high = d_total[n].astype(BF16)
        z_low = (d_total[n] - z_high.astype(F32)).astype(BF16)
        anti = -causal[n].T.astype(BF16)
        left = beside(
            flip_pairs(d_mixing[n]), pairs_t[n], vc[n] * late_low[n], kc[n] * late_low[n], anti, anti
        )
        right = above(ratios[n], d_pws[n], rg_low[n].T, uq_low[n].T, z_high, z_low)
        dw.append(dot(left, right) - late[n] * state_z[n])
    gq = [
        dot(beside(d_pairs[n], d_pw[n] * come_low[n]), above(head_stack(kc[n]), kw_t[n]))
        for n in run
    ]
    gk = [
        dot(beside(flip_pairs(d_pairs[n]), w_late[n]), above(head_stack(qc[n]), uq_low[n]))
        for n in run
    ]
    for n in run:
        gy[g, rows[n], 512:768] = gv[n].astype(BF16)
        gy[g, rows[n], 768:1024] = (dw[n] * wc[n].astype(F32)).astype(BF16)
        gy[g, rows[n], 0:256] = gq[n].astype(BF16)
        gy[g, rows[n], 256:512] = gk[n].astype(BF16)
    rg[...] = state_v[-1]
    uq[...] = state_k[-1]
    zgrad[...] = jnp.broadcast_to(state_z[-1], zgrad.shape)


def units(j):
    return j // 2 % 2, (j // 4 * 2 + j % 2) * 256


def feed_in(r, tok, gain, wb, mixed, n2, gh, scales):
    rows = pl.ds(pl.multiple_of(r * TILE, TILE), TILE)
    hidden = tok[rows, :].astype(F32)
    for g in range(2):
        hidden += dot_rt(mixed[g, rows, :], flat(wb[g, ..., 0:256]))
    hat, scale = standardise(hidden)
    gh[rows, :] = hat
    scales[rows, :] = scale
    n2[rows, :] = (hat * gain[...]).astype(BF16)


def feed_up(part, r, up_bias, wb, n2, act, lin):
    rows = pl.ds(pl.multiple_of(r * TILE, TILE), TILE)
    normed = n2[rows, :]
    k0 = 0.7978845608
    k1 = k0 * 0.044715

    def linear_of(j):
        g, column = units(j)
        up = flat(wb[g, ..., 256 + column : 512 + column])
        bias = up_bias[:, g * 1024 + column : g * 1024 + column + 256]
        return dot(normed, up) + bias

    after = linear_of(4 * part)
    for j in range(4 * part, 4 * part + 4):
        linear = after
        if j < 4 * part + 3:
            after = linear_of(j + 1)
        square = linear * linear
        gate = 0.5 * jnp.tanh(linear * (square * k1 + k0)) + 0.5
        active = linear * gate
        slope = gate + active * (1.0 - gate) * (square * (6.0 * k1) + 2.0 * k0)
        g, column = units(j)
        act[g, rows, column : column + 256] = active.astype(BF16)
        lin[g, rows, column : column + 256] = slope.astype(BF16)


def feed_grad(part, r, cot, wb, lin, small):
    rows = pl.ds(pl.multiple_of(r * TILE, TILE), TILE)
    grad = cot[rows, :]

    def grad_of(j):
        g, column = units(j)
        down = flat(wb[g, ..., 1280 + column : 1536 + column])
        return dot(grad, down) * lin[g, rows, column : column + 256].astype(F32)

    after = grad_of(4 * part)
    for j in range(4 * part, 4 * part + 4):
        grad_low = after.astype(BF16)
        if j < 4 * part + 3:
            after = grad_of(j + 1)
        g, column = units(j)
        lin[g, rows, column : column + 256] = grad_low
        row, here = 4 + 2 * g + column // 512, column % 512
        small[row : row + 1, here : here + 256] += jnp.sum(
            grad_low.astype(F32), axis=0, keepdims=True
        )


def feed_back(r, cot, gain, wb, keepc, lin, gh, scales, gm, small):
    half = TILE // 2
    parts = [pl.ds(pl.multiple_of(r * TILE + n * half, half), half) for n in range(2)]
    backs = [
        dot_rt(lin[0, part, :], flat(wb[0, ..., 256:1280]))
        + dot_rt(lin[1, part, :], flat(wb[1, ..., 256:1280]))
        for part in parts
    ]
    hats = [gh[part, :] for part in parts]
    keeps = [twice(keepc[part, :]) for part in parts]
    hidden = []
    for part, back, hat in zip(parts, backs, hats):
        scaled = back * gain[...]
        inner = scaled - jnp.mean(scaled, axis=-1, keepdims=True)
        inner -= hat * jnp.mean(scaled * hat, axis=-1, keepdims=True)
        hidden.append(cot[part, :].astype(F32) + scales[part, :] * inner)
    mixed_grads = [
        [(dot(rows.astype(BF16), flat(wb[g, ..., 0:256])) * keep).astype(BF16) for g in range(2)]
        for rows, keep in zip(hidden, keeps)
    ]
    for n, part in enumerate(parts):
        gh[part, :] = hidden[n]
        for g in range(2):
            gm[g, part, :] = mixed_grads[n][g]
        small[0:1, :] += jnp.sum(backs[n] * hats[n], axis=0, keepdims=True)


def emit(r, tok, down_bias, wb, mixed, act):
    rows = pl.ds(pl.multiple_of(r * LAST, LAST), LAST)
    total = tok[rows, :].astype(F32)
    for g in range(2):
        total += dot_rt(mixed[g, rows, :], flat(wb[g, ..., 0:256]))
    total += down_bias[...]
    for g in range(2):
        total += dot_rt(act[g, rows, :], flat(wb[g, ..., 1280:2304]))
    tok[rows, :] = total.astype(BF16)


def transpose_into(source, target, length):
    for r in range(length // 256):
        here = slice(r * 256, (r + 1) * 256)
        turned = source[here, :].astype(BF16).T
        target[..., here] = turned.reshape(target.shape[:-1] + (256,))


def weight_grads(left_t, target, jobs):
    shape = target.shape[1:-1]

    def product(job):
        _, right, at, _, columns = job
        return dot(flat(left_t[...]), right[:, at : at + columns]).astype(BF16)

    after = product(jobs[0])
    for n, (g, _, _, to, columns) in enumerate(jobs):
        here = after
        if n + 1 < len(jobs):
            after = product(jobs[n + 1])
        target[g, ..., to : to + columns] = here.reshape(shape + (columns,))


def finish(r, tok, cot, gain, wa, gy, gh, small):
    rows = pl.ds(pl.multiple_of(r * LAST, LAST), LAST)
    hat, scale = standardise(tok[rows, :].astype(F32))
    back = dot_rt(gy[0, rows, :], flat(wa[0])) + dot_rt(gy[1, rows, :], flat(wa[1]))
    scaled = back * gain[...]
    inner = scaled - jnp.mean(scaled, axis=-1, keepdims=True)
    inner -= hat * jnp.mean(scaled * hat, axis=-1, keepdims=True)
    cot[rows, :] = (gh[rows, :] + scale * inner).astype(BF16)
    small[1:2, :] += jnp.sum(back * hat, axis=0, keepdims=True)


class Quiet:
    def nothing(self, *at):
        pass

    before = enter = normalised = weights_a = projected = mixing = nothing
    weights_up = feeding = fed_up = weights_down = grads_down = fed_grad = feeding_down = grads_up = nothing
    mixing_back = mixed_back = grads_a = finishing = finished = gained = grads_last = after = nothing


LAYER_INPUTS = 6
UP_PIECES = [(0, 768), (768, 1280)]
DOWN_PIECES = [(1280, 1792), (1792, 2304)]
GRAD_PIECES = DOWN_PIECES + [(256, 768), (768, 1280), (0, 256)]


def layer_body(
    length,
    comm,
    seg_row,
    pad_row,
    gain_one,
    gain_two,
    up_bias,
    down_bias,
    wa,
    wb,
    ga,
    gw,
    small,
    tok,
    cot,
    segc,
    keepc,
    n1,
    q,
    k,
    v,
    w,
    probs,
    inv,
    score,
    mixed,
    state_k,
    state_v,
    state_z,
    kw_all,
    wv_all,
    pt_all,
    mt_all,
    act,
    lin,
    gh,
    scales,
    gm,
    flip,
    n1_flip,
):
    runs, tiles = length // (UNROLL * CHUNK), length // TILE

    def clear():
        state_k[...] = jnp.zeros_like(state_k)
        state_v[...] = jnp.zeros_like(state_v)
        state_z[...] = jnp.zeros_like(state_z)

    comm.before()
    small[...] = jnp.zeros_like(small)
    rows_to_columns(seg_row, pad_row, segc, keepc, length)
    comm.enter()

    @pl.loop(0, tiles)
    def _(r):
        normalise(r, tok, cot, gain_one, n1, small)

    comm.normalised()
    transpose_into(cot, flip, length)
    transpose_into(n1, n1_flip, length)

    @pl.loop(0, 2)
    def _(g):
        comm.weights_a(g, 0)
        clear()

        @pl.loop(0, length // WIDE)
        def _(r):
            project_qk(g, r, wa, n1, q, k)

        comm.weights_a(g, 1)

        @pl.loop(0, length // WIDE)
        def _(r):
            project_vw(g, r, wa, keepc, n1, v, w)

        comm.projected(g)

        @pl.loop(0, runs)
        def _(i):
            comm.mixing(g, i)
            mix_forward(
                g, i, segc, keepc, q, k, v, w, probs, inv, score, mixed, state_k, state_v, state_z,
                kw_all, wv_all, pt_all, mt_all,
            )

    comm.weights_up(0)

    @pl.loop(0, tiles)
    def _(r):
        comm.feeding(0, r)
        feed_in(r, tok, gain_two, wb, mixed, n1, gh, scales)
        feed_up(0, r, up_bias, wb, n1, act, lin)

    transpose_into(n1, ga.at[0], length)
    comm.weights_up(1)

    @pl.loop(0, tiles)
    def _(r):
        comm.feeding(1, r)
        feed_up(1, r, up_bias, wb, n1, act, lin)

    comm.fed_up()
    for part in range(2):
        at = part * 512
        weight_grads(flip, gw, [(g, act.at[g], at, 1280 + at, 512) for g in range(2)])
        comm.grads_down(part)

    for part in range(2):
        comm.weights_down(part)

        @pl.loop(0, tiles)
        def _(r):
            feed_grad(part, r, cot, wb, lin, small)

        comm.fed_grad(part)
        at = part * 512
        weight_grads(ga.at[0], gw, [(g, lin.at[g], at, 256 + at, 512) for g in range(2)])
        comm.grads_up(part)

    @pl.loop(0, tiles)
    def _(r):
        comm.feeding_down(r)
        feed_back(r, cot, gain_two, wb, keepc, lin, gh, scales, gm, small)

    transpose_into(gh, flip, length)
    weight_grads(flip, gw, [(g, mixed.at[g], 0, 0, GROUP) for g in range(2)])
    comm.grads_up(2)

    @pl.loop(0, 2)
    def _(g):
        clear()

        @pl.loop(0, runs)
        def _(i):
            comm.mixing_back(g, i, 0)
            mix_backward(
                g, runs - 1 - i, segc, keepc, q, k, v, w, probs, inv, score, gm, state_v, state_k,
                state_z, kw_all, wv_all, pt_all, mt_all, lin,
                functools.partial(comm.mixing_back, g, i, 1),
            )

        comm.mixed_back(g)

        weight_grads(n1_flip, ga, [(g, lin.at[g], 0, 0, 512), (g, lin.at[g], 512, 512, 256)])

        @pl.when(g == 0)
        def _():
            weight_grads(n1_flip, ga, [(0, lin.at[0], 768, 768, 256)])

        comm.grads_a(g)

    @pl.loop(0, length // LAST)
    def _(r):
        comm.finishing(0, r)
        finish(r, tok, cot, gain_one, wa, lin, gh, small)
        comm.finished(0, r)

    comm.gained()
    weight_grads(n1_flip, ga, [(1, lin.at[1], 768, 768, 256)])
    comm.grads_last()

    @pl.loop(0, length // LAST)
    def _(r):
        comm.finishing(1, r)
        emit(r, tok, down_bias, wb, mixed, act)
        comm.finished(1, r)

    comm.after()


def layer_scratch(length, width):
    vmem = pltpu.VMEM
    chunks = length // CHUNK
    return [
        vmem((length + 16, 128), F32),
        vmem((length, 128), F32),
        vmem((length, width), BF16),
        vmem((2, length, GROUP), BF16),
        vmem((2, length, GROUP), BF16),
        vmem((2, length, GROUP), BF16),
        vmem((2, length, GROUP), BF16),
        vmem((2, length, GROUP), F32),
        vmem((2, length, GROUP), F32),
        vmem((2, length, GROUP), BF16),
        vmem((2, length, GROUP), BF16),
        vmem((HEAD_DIM, GROUP), F32),
        vmem((HEAD_DIM, GROUP), F32),
        vmem((8, GROUP), F32),
        vmem((2, chunks, HEAD_DIM, GROUP), BF16),
        vmem((2, chunks, HEAD_DIM, GROUP), BF16),
        vmem((2, length, 4 * CHUNK), BF16),
        vmem((2, length, 4 * CHUNK), BF16),
        vmem((2, length, 1024), BF16),
        vmem((2, length, 1024), BF16),
        vmem((length, width), F32),
        vmem((length, 1), F32),
        vmem((2, length, GROUP), BF16),
        vmem((width, length), BF16),
        vmem((width, length), BF16),
    ]


def layer_kernel(length, tokens, cotangent, *refs):
    inputs, (out, grad_out), rest = refs[: LAYER_INPUTS + 2], refs[8:10], refs[10:]
    out[...] = tokens[...]
    grad_out[...] = cotangent[...]
    ga, gw, small = rest[:3]
    layer_body(length, Quiet(), *inputs, ga, gw, small, out, grad_out, *rest[3:])


def layer(tokens, cotangent, seg_row, pad_row, gain_one, gain_two, up_bias, down_bias, wa, wb):
    length, width = tokens.shape
    shape = jax.ShapeDtypeStruct
    cut = lambda full: full.reshape(2, -1, 2, 2, 2, 16, full.shape[-1])
    wa, wb = cut(wa), cut(wb)
    space = pl.BlockSpec(memory_space=pltpu.VMEM)
    out, grad_out, ga, gw, small = pl.pallas_call(
        functools.partial(layer_kernel, length),
        out_shape=(
            shape((length, width), BF16),
            shape((length, width), BF16),
            shape(wa.shape, BF16),
            shape(wb.shape, BF16),
            shape((8, width), F32),
        ),
        in_specs=[space] * 10,
        out_specs=tuple([space] * 5),
        scratch_shapes=layer_scratch(length, width),
        compiler_params=pltpu.CompilerParams(vmem_limit_bytes=62 * 1024 * 1024),
        name="layer",
    )(tokens, cotangent, seg_row, pad_row, gain_one, gain_two, up_bias, down_bias, wa, wb)
    whole = lambda full: full.reshape(2, width, full.shape[-1])
    return out, grad_out, whole(ga), whole(gw), small


class Place:
    def __init__(self, depth):
        index = lax.axis_index("dp")
        t = lax.axis_index("tensor")
        x, y, z = lax.rem(index, 2), lax.rem(index // 2, 2), index // 4
        self.depth = depth
        self.x, self.y, self.z, self.t, self.other = x, y, z, t, 1 - t
        self.near = (y + t * (1 - 2 * y), x + (1 - t) * (1 - 2 * x))
        self.next = (y + (1 - t) * (1 - 2 * y), x + t * (1 - 2 * x))
        self.far = (1 - y, 1 - x)
        chip = lambda z, y, x: (z * 2 + y) * 2 + x
        self.levels = [lax.rem(z + s, depth) for s in range(depth)]
        self.chips_z = [chip(level, y, x) for level in self.levels]
        self.to_near = {"dp": chip(z, *self.near)}
        self.to_next = {"dp": chip(z, *self.next)}
        self.to_far = {"dp": chip(z, *self.far)}
        self.to_pair = {"tensor": self.other}
        self.spot = (y * 2 + x) * 2 + t
        flip = lambda value, bit: value + bit * (1 - 2 * value)
        self.level = [
            {
                "dp": chip(z, flip(y, offset // 4), flip(x, offset // 2 % 2)),
                "tensor": flip(t, offset % 2),
            }
            for offset in range(8)
        ]

    def along_z(self, step, core):
        return {"dp": self.chips_z[step], "tensor": core}

    def friends(self):
        along = [self.along_z(s, core) for s in range(1, self.depth) for core in range(2)]
        return self.level[1:] + along

    def knock(self):
        barrier = pltpu.get_barrier_semaphore()
        for friend in self.friends():
            pl.semaphore_signal(barrier, inc=1, device_id=friend, device_id_type=MESH)

    def enter(self):
        pl.semaphore_wait(pltpu.get_barrier_semaphore(), len(self.friends()))


class Copies:
    def __init__(self, sems):
        self.sems = sems

    def build(self, source, target, device, out_sem, in_sem):
        return pltpu.make_async_remote_copy(
            src_ref=source,
            dst_ref=target,
            send_sem=self.sems.at[0, out_sem],
            recv_sem=self.sems.at[1, in_sem],
            device_id=device,
            device_id_type=MESH,
        )

    def start(self, source, target, device, number, in_sem=None, only=None):
        def begin():
            landing = number if in_sem is None else in_sem
            self.build(source(), target, device, number, landing).start()

        begin() if only is None else pl.when(only)(begin)

    def landed(self, target, number, only=None):
        def wait():
            self.build(target, target, {"tensor": 0}, number, number).wait_recv()

        wait() if only is None else pl.when(only)(wait)

    def sent(self, source, numbers, only=None):
        def wait():
            for number in numbers:
                self.build(source, source, {"tensor": 0}, number, number).wait_send()

        wait() if only is None else pl.when(only)(wait)


class Gather(Copies):
    COPIES = 14

    def __init__(self, place, own, full, group, columns, sems):
        super().__init__(sems)
        self.p, self.own, self.full, self.columns = place, own, full, columns
        self.group = group
        self.groups = slice(None) if group is None else slice(group, group + 1)
        self.mine = None if group is None else place.t == group
        self.pairs = None if group is None else place.t != group

    def at(self, g, z, spot, half):
        return self.full.at[g, z, spot[0], spot[1], half, :, self.columns]

    def block(self, spot, half):
        return self.at(self.groups, slice(None), spot, half)

    def forward(self, spot, device, number):
        block = lambda: self.block(spot, self.p.t)
        self.start(block, block(), device, number)

    def first(self):
        p = self.p
        here = (p.y, p.x)
        for s in range(1, p.depth):
            for core in range(2):
                self.start(
                    lambda core=core: self.own.at[core, :, self.columns],
                    self.at(p.t, p.z, here, core),
                    p.along_z(s, core),
                    2 * (s - 1) + core,
                    2 * (s - 1) + p.t,
                    only=self.mine,
                )
        self.start(
            lambda: self.own.at[p.other, :, self.columns],
            self.at(p.t, p.z, here, p.other),
            p.to_pair,
            6,
            only=self.mine,
        )

        def keep():
            self.full[p.t, p.z, p.y, p.x, p.t, :, self.columns] = self.own[p.t, :, self.columns]

        keep() if self.mine is None else pl.when(self.mine)(keep)

    def second(self):
        p = self.p
        here = (p.y, p.x)
        for n in range(6):
            if self.group is None or n % 2 == self.group:
                self.landed(self.at(p.t, p.z, here, p.t), n)
        self.landed(self.at(p.t, p.z, here, p.t), 6, only=self.pairs)
        self.forward(here, p.to_near, 7)
        self.forward(here, p.to_next, 8)
        self.forward(here, p.to_pair, 9)

    def third(self):
        p = self.p
        self.landed(self.block(p.near, p.t), 7)
        self.forward(p.near, p.to_next, 10)
        self.forward(p.near, p.to_pair, 11)
        self.landed(self.block(p.next, p.t), 8)
        self.forward(p.next, p.to_pair, 12)

    def fourth(self):
        p = self.p
        self.landed(self.block(p.far, p.t), 10)
        self.forward(p.far, p.to_pair, 13)

    def last(self):
        p = self.p
        for n in (9, 11, 12, 13):
            self.landed(self.block((p.y, p.x), p.other), n)

    def left(self):
        p = self.p
        self.sent(self.own.at[0, :, self.columns], range(7), self.mine)
        self.sent(self.block((p.y, p.x), p.t), range(7, 14))


class Scatter(Copies):
    COPIES = 11

    def __init__(self, place, part, group, columns, pair_in, near_in, next_in, last_in, sems):
        super().__init__(sems)
        self.p, self.part, self.columns = place, part, columns
        self.pair_in, self.near_in, self.next_in, self.last_in = pair_in, near_in, next_in, last_in
        self.group = group
        self.groups = slice(None) if group is None else slice(group, group + 1)
        self.mine = None if group is None else place.t == group
        self.pairs = None if group is None else place.t != group

    def at(self, g, z, spot, half):
        return self.part.at[g, z, spot[0], spot[1], half, :, self.columns]

    def block(self, spot, half):
        return self.at(self.groups, slice(None), spot, half)

    def add(self, spot, landed):
        p = self.p
        here = (self.groups, slice(None), spot[0], spot[1], p.t, slice(None), self.columns)
        self.part[here] = (self.part[here].astype(F32) + landed.astype(F32)).astype(BF16)

    def first(self):
        p = self.p
        self.start(
            lambda: self.part.at[self.groups, :, :, :, p.other, :, self.columns],
            self.pair_in,
            p.to_pair,
            0,
        )

    def second(self):
        p = self.p
        self.landed(self.pair_in, 0)
        for spot, number in ((p.far, 1), (p.near, 2)):
            self.add(spot, self.pair_in[:, :, spot[0], spot[1]])
            self.start(
                lambda spot=spot: self.block(spot, p.t),
                self.near_in.at[number - 1],
                p.to_near,
                number,
            )
        for spot in (p.next, (p.y, p.x)):
            self.add(spot, self.pair_in[:, :, spot[0], spot[1]])

    def third(self):
        p = self.p
        self.landed(self.near_in.at[0], 1)
        self.add(p.next, self.near_in[0])
        self.start(lambda: self.block(p.next, p.t), self.next_in, p.to_next, 3)
        self.landed(self.near_in.at[1], 2)
        self.add((p.y, p.x), self.near_in[1])

    def fourth(self):
        p = self.p
        self.landed(self.next_in, 3)
        self.add((p.y, p.x), self.next_in[...])
        self.up_the_levels()

    def up_the_levels(self):
        p = self.p
        here = (p.y, p.x)
        for s in range(1, p.depth):
            for core in range(2) if self.group is None else (self.group,):
                self.start(
                    lambda s=s, core=core: self.at(core, p.levels[s], here, p.t),
                    self.last_in.at[2 * (s - 1) + p.t],
                    p.along_z(s, core),
                    4 + 2 * (s - 1) + core,
                    4 + 2 * (s - 1) + p.t,
                )
        self.start(
            lambda: self.at(p.other, p.z, here, p.t),
            self.last_in.at[2 * (p.depth - 1)],
            p.to_pair,
            10,
            only=self.pairs,
        )

    def last(self, target):
        p = self.p

        def write():
            for n in range(7):
                self.landed(self.last_in.at[n], 4 + n)
            mine = self.part[p.t, p.z, p.y, p.x, p.t, :, self.columns].astype(F32)
            rest = self.last_in[2 * (p.depth - 1)].astype(F32)
            for s in range(1, p.depth):
                mine += self.last_in[2 * (s - 1) + p.t].astype(F32)
                rest += self.last_in[2 * (s - 1) + p.other].astype(F32)
            target[p.t] = mine
            target[p.other] = rest

        write() if self.mine is None else pl.when(self.mine)(write)

    def left(self):
        p = self.p
        self.sent(self.pair_in, (0,))
        self.sent(self.next_in, (1, 2, 3))
        for core in range(2) if self.group is None else (self.group,):
            self.sent(self.last_in.at[0], [4 + 2 * s + core for s in range(p.depth - 1)])
        self.sent(self.last_in.at[0], (10,), self.pairs)


class ShortScatter(Scatter):
    def second(self):
        p = self.p
        self.landed(self.pair_in, 0)
        for spot, target, device, number in (
            (p.far, self.near_in.at[0], p.to_far, 1),
            (p.near, self.near_in.at[1], p.to_near, 2),
            (p.next, self.next_in, p.to_next, 3),
        ):
            self.add(spot, self.pair_in[:, :, spot[0], spot[1]])
            self.start(lambda spot=spot: self.block(spot, p.t), target, device, number)
        self.add((p.y, p.x), self.pair_in[:, :, p.y, p.x])

    def fourth(self):
        p = self.p
        for part, number in ((self.next_in, 3), (self.near_in.at[1], 2), (self.near_in.at[0], 1)):
            self.landed(part, number)
            self.add((p.y, p.x), part[...])
        self.up_the_levels()


def scatter_scratch(groups, depth, columns):
    vmem = pltpu.VMEM
    return [
        vmem((groups, depth, 2, 2, 16, columns), BF16),
        vmem((2, groups, depth, 16, columns), BF16),
        vmem((groups, depth, 16, columns), BF16),
        vmem((2 * depth - 1, 16, columns), BF16),
    ]


class Reduce(Copies):
    COPIES = 12

    def __init__(self, place, own, parts, sums, sems):
        super().__init__(sems)
        self.p, self.own, self.parts, self.sums = place, own, parts, sums

    def first(self):
        p = self.p
        self.parts[p.spot] = self.own[...]
        for offset in range(1, 8):
            self.start(
                lambda: self.own, self.parts.at[p.spot], p.level[offset], offset - 1
            )

    def second(self):
        p = self.p
        for n in range(7):
            self.landed(self.own, n)
        total = self.parts[0]
        for spot in range(1, 8):
            total += self.parts[spot]
        self.sums[p.z] = total
        for s in range(1, p.depth):
            self.start(
                lambda: self.sums.at[p.z], self.sums.at[p.z], {"dp": p.chips_z[s]}, 6 + s
            )

    def last(self):
        p = self.p
        for s in range(1, p.depth):
            self.landed(self.own, 6 + s)
        total = self.sums[0]
        for z in range(1, p.depth):
            total += self.sums[z]
        return total

    def left(self):
        self.sent(self.own, range(6 + self.p.depth))


class Woven:
    def __init__(self, place, far, near, own, full, gathers, scatters, gains):
        self.p, self.far, self.near, self.own = place, far, near, own
        wa, wb, ga, gw = full
        own_a, own_b = own
        ranges = [(own_a, wa, 0, 0, 512), (own_a, wa, 0, 512, 1024), (own_a, wa, 1, 0, 1024)]
        ranges += [(own_b, wb, None, *part) for part in UP_PIECES + DOWN_PIECES]
        gather = [
            Gather(place, part, whole, g, slice(first, last), sems)
            for (part, whole, g, first, last), sems in zip(ranges, gathers)
        ]
        self.a0, self.a1, self.b = gather[:2], gather[2], gather[3:]
        ranges = [(gw, None, *part) for part in GRAD_PIECES]
        ranges += [(ga, 0, 0, 1024), (ga, 1, 0, 768), (ga, 1, 768, 1024)]
        kinds = [Scatter] * 5 + [ShortScatter] * 3
        scatter = [
            kind(place, part, g, slice(first, last), *buffers)
            for kind, (part, g, first, last), buffers in zip(kinds, ranges, scatters)
        ]
        self.down_grad, self.up_grad, self.out_grad = scatter[:2], scatter[2:4], scatter[4]
        self.a0_grad, self.a1_grad = scatter[5], scatter[6:]
        self.gains = gains
        self.everything = scatter + [gains]

    def table(self, at, steps):
        for place, calls in steps.items():
            here = None
            for value, wanted in zip(at, place):
                here = (value == wanted) if here is None else here & (value == wanted)

            @pl.when(here)
            def _(calls=calls):
                for call in calls:
                    call()

    def fetch(self, n):
        return pltpu.make_async_copy(self.far[n], self.near[n], self.near["sems"].at[n])

    def put(self, name, n):
        return pltpu.make_async_copy(self.near[name], self.far[name], self.near["sems"].at[n])

    def put_rows(self, which, r):
        rows = pl.ds(pl.multiple_of(r * LAST, LAST), LAST)
        source, target = ((1, "grad_out"), (0, "out"))[which]
        return pltpu.make_async_copy(
            self.near[source].at[rows],
            self.far[target].at[rows],
            self.near["sems"].at[18 + 4 * which + r],
        )

    def before(self):
        self.p.knock()
        for n in range(14, -1, -1):
            self.fetch(n).start()
        for n in range(2, 15):
            self.fetch(n).wait()
        first = self.p.t == 0
        for rows, row in ((2, "seg_row"), (3, "pad_row")):
            rows = self.near[rows]
            self.near[row][...] = jnp.where(first, rows[0:1, :], rows[1:2, :])
        own_a, own_b = self.own
        halves = lambda n: self.near[n][...].astype(BF16).reshape(2, 16, -1)
        for n in range(4):
            own_a[:, :, 256 * n : 256 * n + 256] = halves(8 + n)
        own_b[:, :, 0:256] = halves(12)
        own_b[:, :, 256:1280] = halves(13)
        own_b[:, :, 1280:2304] = halves(14)

    def enter(self):
        self.p.enter()
        self.a0[0].first()
        self.a0[1].first()
        self.fetch(0).wait()
        self.fetch(1).wait()

    def normalised(self):
        pass

    def weights_a(self, g, part):
        one, two = self.a0
        a1, b = self.a1, self.b
        self.table(
            (g,),
            (
                {
                    (0,): (
                        one.second, a1.first, two.second, b[0].first, one.third, two.third,
                        one.fourth, a1.second, one.last,
                    ),
                    (1,): (a1.fourth, a1.last),
                },
                {
                    (0,): (b[1].first, two.fourth, two.last),
                    (1,): (b[0].third, b[3].first),
                },
            )[part],
        )

    def projected(self, g):
        b = self.b
        self.table((g,), {(0,): (self.a1.third, b[0].second), (1,): (b[2].second,)})

    def mixing(self, g, i):
        b = self.b
        steps = {
            (0, 1): (b[1].second, self.a0[0].left, self.a0[1].left, b[2].first),
            (1, 1): (b[1].third, b[0].fourth),
        }
        self.table((g, i), steps)

    def weights_up(self, part):
        b = self.b
        if part == 0:
            b[3].second()
            b[0].last()
        else:
            b[1].last()

    def feeding(self, part, r):
        b = self.b
        steps = {(0, 1): (b[2].third, b[1].fourth), (1, 1): (b[3].third,)}
        self.table((part, r), steps)

    def fed_up(self):
        self.b[2].fourth()

    def grads_down(self, part):
        if part == 0:
            self.a1.left()
            self.b[0].left()
            self.b[1].left()
        self.down_grad[part].first()

    def weights_down(self, part):
        self.b[2 + part].last()
        self.b[2 + part].left()
        if part == 1:
            self.down_grad[1].second()

    def fed_grad(self, part):
        if part == 0:
            self.b[3].fourth()
            self.down_grad[0].second()

    def grads_up(self, part):
        if part < 2:
            self.up_grad[part].first()
        if part == 1:
            self.up_grad[0].second()
        if part == 2:
            self.out_grad.first()
            self.down_grad[1].third()
            self.up_grad[1].second()

    def feeding_down(self, r):
        self.table((r,), {(1,): (self.down_grad[0].third,)})

    def mixing_back(self, g, i, part):
        one, two = self.down_grad
        up, rest = self.up_grad
        steps = {
            (0, 1, 0): (one.fourth, self.out_grad.second),
            (0, 1, 1): (up.third,),
            (1, 0, 1): (self.a0_grad.second, self.down_last, up.fourth),
            (1, 1, 0): (self.out_grad.third,),
        }
        self.table((g, i, part), steps)

    def mixed_back(self, g):
        self.table((g,), {(0,): (self.down_grad[1].fourth,)})

    def grads_a(self, g):
        one, two = self.a1_grad
        self.table((g,), {(0,): (self.a0_grad.first, self.up_grad[1].third), (1,): (one.first,)})

    def grads_last(self):
        self.a1_grad[1].first()

    def finishing(self, which, r):
        one, two = self.a1_grad
        steps = {
            (0, 1): (one.second,),
            (0, 2): (self.up_grad[1].fourth,),
            (1, 0): (self.out_grad.fourth, self.a0_grad.fourth),
            (1, 1): (two.second,),
            (1, 3): (one.fourth,),
        }
        self.table((which, r), steps)

    def down_last(self):
        self.down_grad[0].last(self.near["dw"].at[:, :, 1280:1792])

    def finished(self, which, r):
        self.put_rows(which, r).start()

    def gained(self):
        self.gains.first()

    def after(self):
        one, two = self.a1_grad
        da, dw = self.near["da"], self.near["dw"]
        self.gains.second()
        two.fourth()
        self.down_grad[1].last(dw.at[:, :, 1792:2304])
        self.up_grad[0].last(dw.at[:, :, 256:768])
        self.up_grad[1].last(dw.at[:, :, 768:1280])
        self.out_grad.last(dw.at[:, :, 0:256])
        self.put("dw", 15).start()
        self.near["total"][...] = self.gains.last()
        self.put("total", 16).start()
        self.a0_grad.last(da)
        one.last(da.at[:, :, 0:768])
        two.last(da.at[:, :, 768:1024])
        self.put("da", 17).start()
        self.everything_left()

    def everything_left(self):
        for copies in self.everything:
            copies.left()
        for r in range(4):
            self.put_rows(0, r).wait()
            self.put_rows(1, r).wait()
        self.put("dw", 15).wait()
        self.put("total", 16).wait()
        self.put("da", 17).wait()


def woven_kernel(length, depth, *refs):
    refs = list(refs)
    take = lambda n: [refs.pop(0) for _ in range(n)]
    far = dict(enumerate(take(15)))
    far.update(zip(("out", "grad_out", "da", "dw", "total"), take(5)))
    near = dict(enumerate(take(15)))
    near.update(zip(("da", "dw", "total", "seg_row", "pad_row", "sems"), take(6)))
    own, full = take(2), take(4)
    small, parts, sums, gain_sems = take(4)
    gathers = take(7)
    scatters = [take(4) for _ in range(8)]
    scatters = [buffers + [sems] for buffers, sems in zip(scatters, gathers + take(1))]
    place = Place(depth)
    gains = Reduce(place, small, parts, sums, gain_sems)
    comm = Woven(place, far, near, own, full, gathers, scatters, gains)
    layer_body(
        length, comm, near["seg_row"], near["pad_row"], *[near[n] for n in range(4, 8)], *full,
        small, near[0], near[1], *refs,
    )


def write_kernel(out_in, grad_in, da, dw, small, *refs):
    (
        out, grad_out, mixer_gain, query, key, value, slot, out_t, feed_gain, up, up_bias, down_t,
        down_bias,
    ) = refs
    out[...] = out_in[...]
    grad_out[...] = grad_in[...]
    rows = lambda part: part.reshape(-1, part.shape[-1])
    query[...] = rows(da[:, :, 0:256])
    key[...] = rows(da[:, :, 256:512])
    value[...] = rows(da[:, :, 512:768])
    slot[...] = rows(da[:, :, 768:1024])
    out_t[...] = rows(dw[:, :, 0:256])
    up[...] = rows(dw[:, :, 256:1280])
    down_t[...] = rows(dw[:, :, 1280:2304])
    feed_gain[...] = small[0:1, :]
    mixer_gain[...] = small[1:2, :]
    down_bias[...] = small[2:3, :]
    for row in range(4):
        up_bias[:, row * 512 : (row + 1) * 512] = small[4 + row : 5 + row, :]


def write(out, grad_out, da, dw, small):
    shape = jax.ShapeDtypeStruct
    space = pl.BlockSpec(memory_space=pltpu.VMEM)
    width = out.shape[1]
    square, wide = shape((32, 256), F32), shape((32, 1024), F32)
    row = shape((1, width), F32)
    return pl.pallas_call(
        write_kernel,
        out_shape=(
            shape(out.shape, BF16),
            shape(out.shape, BF16),
            row,
            square,
            square,
            square,
            square,
            square,
            row,
            wide,
            shape((1, 4 * width), F32),
            wide,
            row,
        ),
        in_specs=[space] * 5,
        out_specs=(space,) * 13,
        name="write",
    )(out, grad_out, da, dw, small)


def woven(depth, *inputs):
    length, width = inputs[0].shape
    shape = jax.ShapeDtypeStruct
    far = pl.BlockSpec(memory_space=pl.ANY)
    vmem = pltpu.VMEM
    dma = pltpu.SemaphoreType.DMA
    full = lambda columns: vmem((2, depth, 2, 2, 2, 16, columns), BF16)
    da, dw, total = shape((2, 16, 1024), F32), shape((2, 16, 2304), F32), shape((8, width), F32)
    scatters = []
    for groups, columns in [(2, 512)] * 4 + [(2, 256), (1, 1024), (1, 768), (1, 256)]:
        scatters += scatter_scratch(groups, depth, columns)
    return pl.pallas_call(
        functools.partial(woven_kernel, length, depth),
        out_shape=(shape((length, width), BF16), shape((length, width), BF16), da, dw, total),
        in_specs=[far] * 15,
        out_specs=(far,) * 5,
        scratch_shapes=[vmem(array.shape, array.dtype) for array in inputs]
        + [vmem(array.shape, array.dtype) for array in (da, dw, total)]
        + [
            vmem((1, length), jnp.int32),
            vmem((1, length), jnp.int32),
            dma((26,)),
            vmem((2, 16, 1024), BF16),
            vmem((2, 16, 2304), BF16),
            full(1024),
            full(2304),
            full(1024),
            full(2304),
            vmem((8, width), F32),
            vmem((8, 8, width), F32),
            vmem((depth, 8, width), F32),
            dma((2, Reduce.COPIES)),
        ]
        + [dma((2, Gather.COPIES))] * 7
        + scatters
        + [dma((2, Scatter.COPIES))]
        + layer_scratch(length, width),
        compiler_params=pltpu.CompilerParams(
            collective_id=0, has_side_effects=True, vmem_limit_bytes=63 * 1024 * 1024
        ),
        name="woven",
    )(*inputs)


def per_device(
    direct,
    tokens,
    segment_ids,
    padding,
    mixer_gain,
    query_weight,
    key_weight,
    value_weight,
    slot_weight,
    out_weight,
    feed_gain,
    up_weight,
    up_bias,
    down_weight,
    down_bias,
    cotangent,
):
    gains = (mixer_gain[None], feed_gain[None])
    biases = (up_bias[None], down_bias[None])
    if direct:
        owns = (
            query_weight, key_weight, value_weight, slot_weight, out_weight.T, up_weight,
            down_weight.T,
        )
        depth = lax.axis_size("dp") // 4
        results = write(
            *woven(depth, tokens, cotangent, segment_ids, padding, *gains, *biases, *owns)
        )
        (
            out, grad_out, gain_one, query, key, value, slot, out_t, gain_two, up, bias_one, down_t,
            bias_two,
        ) = results
        return (
            out, grad_out, gain_one[0], query, key, value, slot, out_t.T, gain_two[0], up,
            bias_one[0], down_t.T, bias_two[0],
        )
    own_a = jnp.concatenate([query_weight, key_weight, value_weight, slot_weight], 1)
    own_b = jnp.concatenate([out_weight.T, up_weight, down_weight.T], 1)
    wa, wb = (
        lax.all_gather(lax.all_gather(own.astype(BF16), "dp", axis=0, tiled=True), "tensor")
        for own in (own_a, own_b)
    )
    half = lax.axis_index("tensor")
    pick = lambda rows: lax.dynamic_slice_in_dim(rows, half, 1, 0)
    out, grad_out, ga, gw, small = layer(
        tokens, cotangent, pick(segment_ids), pick(padding), *gains, *biases, wa, wb
    )
    da, dw = (
        lax.psum_scatter(
            lax.psum_scatter(part.astype(F32), "tensor", scatter_dimension=0),
            "dp",
            scatter_dimension=0,
            tiled=True,
        )
        for part in (ga, gw)
    )
    small = lax.psum(small, ("dp", "tensor"))
    return (
        out,
        grad_out,
        small[1],
        da[:, 0:256],
        da[:, 256:512],
        da[:, 512:768],
        da[:, 768:1024],
        dw[:, 0:256].T,
        small[0],
        dw[:, 256:1280],
        small[4:8].reshape(-1),
        dw[:, 1280:2304].T,
        small[2],
    )


def solution(mesh):
    in_specs = (
        P(("dp", "tensor"), None),
        P("dp", None),
        P("dp", None),
        P(),
        P("dp", "tensor"),
        P("dp", "tensor"),
        P("dp", "tensor"),
        P("dp", "tensor"),
        P("tensor", "dp"),
        P(),
        P("dp", "tensor"),
        P(),
        P("tensor", "dp"),
        P(),
        P(("dp", "tensor"), None),
    )
    out_specs = (
        P(("dp", "tensor"), None),
        P(("dp", "tensor"), None),
        P(),
        P("dp", "tensor"),
        P("dp", "tensor"),
        P("dp", "tensor"),
        P("dp", "tensor"),
        P("tensor", "dp"),
        P(),
        P("dp", "tensor"),
        P(),
        P("tensor", "dp"),
        P(),
    )
    direct = mesh.shape["dp"] == 16 and mesh.shape["tensor"] == 2
    return jax.shard_map(
        functools.partial(per_device, direct),
        mesh=mesh,
        in_specs=in_specs,
        out_specs=out_specs,
        check_vma=False,
    )
```

```python
import functools
import math

import jax
import jax.numpy as jnp
from jax import lax
from jax.experimental import pallas as pl
from jax.experimental.pallas import tpu as pltpu
from jax.sharding import PartitionSpec as P

HEAD_DIM = 64
SLOTS = 64
CHUNK = 128
UNROLL = 4
GROUP = 256
TILE = 512
WIDE = 512
LAST = 256

F32 = jnp.float32
BF16 = jnp.bfloat16
MESH = pl.DeviceIdType.MESH


def dot(left, right):
    return lax.dot_general(left, right, (((1,), (0,)), ((), ())), preferred_element_type=F32)


def dot_rt(left, right):
    return lax.dot_general(left, right, (((1,), (1,)), ((), ())), preferred_element_type=F32)


def dot_lt(left, right):
    return lax.dot_general(left, right, (((0,), (0,)), ((), ())), preferred_element_type=F32)


def twice(block):
    return jnp.concatenate([block, block], axis=1)


def standardise(rows):
    centred = rows - jnp.mean(rows, axis=-1, keepdims=True)
    scale = lax.rsqrt(jnp.mean(centred * centred, axis=-1, keepdims=True) + 1e-05)
    return centred * scale, scale


def head_stack(block):
    lane = lax.broadcasted_iota(jnp.int32, block.shape, 1) // HEAD_DIM
    zero = jnp.zeros_like(block)
    return jnp.concatenate([jnp.where(lane == h, block, zero) for h in range(4)], axis=0)


def diagonal(product):
    parts = [product[h * HEAD_DIM : (h + 1) * HEAD_DIM, :] for h in range(4)]
    lane = lax.broadcasted_iota(jnp.int32, parts[0].shape, 1) // HEAD_DIM
    kept = parts[3]
    for h in range(3):
        kept = jnp.where(lane == h, parts[h], kept)
    return kept


def over_heads(block, reduce, rest):
    halves = []
    lane = lax.broadcasted_iota(jnp.int32, (block.shape[0], 128), 1) < HEAD_DIM
    for j in range(block.shape[1] // 128):
        part = block[:, j * 128 : (j + 1) * 128]
        first = reduce(jnp.where(lane, part, rest), axis=1, keepdims=True)
        second = reduce(jnp.where(lane, rest, part), axis=1, keepdims=True)
        halves.append(jnp.where(lane, first, second))
    return jnp.concatenate(halves, axis=1)


def head_max(block):
    return over_heads(block, jnp.max, -jnp.inf)


def head_sum(block):
    return over_heads(block, jnp.sum, 0.0)


def head_pairs(product, allowed):
    parts = [product[h * CHUNK : (h + 1) * CHUNK, :] * allowed for h in range(4)]
    return jnp.concatenate(parts, axis=1).astype(BF16)


def flip_pairs(pairs):
    parts = [pairs[:, h * CHUNK : (h + 1) * CHUNK].T for h in range(4)]
    return jnp.concatenate(parts, axis=1)


def beside(*blocks):
    return jnp.concatenate(blocks, axis=1)


def above(*blocks):
    return jnp.concatenate(blocks, axis=0)


def flat(block):
    return block.reshape(-1, block.shape[-1])


def rows_to_columns(seg_row, pad_row, segc, keepc, length):
    segc[pl.ds(0, 8), :] = jnp.full((8, 128), -1.0, F32)
    segc[pl.ds(8 + length, 8), :] = jnp.full((8, 128), -2.0, F32)
    for c in range(length // CHUNK):
        here = slice(c * CHUNK, (c + 1) * CHUNK)
        seg = jnp.broadcast_to(seg_row[:, here].astype(F32), (CHUNK, CHUNK))
        pad = jnp.broadcast_to(pad_row[:, here].astype(F32), (CHUNK, CHUNK))
        segc[pl.ds(8 + c * CHUNK, CHUNK), :] = seg.T
        keepc[pl.ds(c * CHUNK, CHUNK), :] = 1.0 - pad.T


def normalise(r, tok, cot, gain, n1, small):
    rows = pl.ds(pl.multiple_of(r * TILE, TILE), TILE)
    xhat, _ = standardise(tok[rows, :].astype(F32))
    n1[rows, :] = (xhat * gain[...]).astype(BF16)
    small[2:3, :] += jnp.sum(cot[rows, :].astype(F32), axis=0, keepdims=True)


def project_qk(g, r, wa, n1, q, k):
    rows = pl.ds(pl.multiple_of(r * WIDE, WIDE), WIDE)
    out = dot(n1[rows, :], flat(wa[g, ..., 0:512]))
    q[g, rows, :] = out[:, 0:256].astype(BF16)
    k[g, rows, :] = out[:, 256:512].astype(BF16)


def project_vw(g, r, wa, keepc, n1, v, w):
    rows = pl.ds(pl.multiple_of(r * WIDE, WIDE), WIDE)
    out = dot(n1[rows, :], flat(wa[g, ..., 512:1024]))
    v[g, rows, :] = out[:, 0:256].astype(BF16)
    w[g, rows, :] = (jnp.exp(out[:, 256:512]) * twice(keepc[rows, :])).astype(BF16)


def chunk_masks(c, segc):
    base = pl.multiple_of(c * CHUNK, CHUNK)
    seg = segc[pl.ds(base + 8, CHUNK), :]
    across = seg.T
    row = lax.broadcasted_iota(jnp.int32, (CHUNK, CHUNK), 0)
    column = lax.broadcasted_iota(jnp.int32, (CHUNK, CHUNK), 1)
    same = seg == across
    causal = jnp.where(same & (column <= row), 1.0, 0.0)
    before = segc[pl.ds(base + 7, 1), :]
    first = segc[pl.ds(base + 8, 1), :]
    last = segc[pl.ds(base + 7 + CHUNK, 1), :]
    after = segc[pl.ds(base + 8 + CHUNK, 1), :]
    one = lambda test: jnp.where(test, 1.0, 0.0)
    return causal, dict(
        from_before=one(seg == before),
        to_after=one(seg == last),
        from_after=one(seg == after),
        to_before=one(seg == first),
        carry_on=one(before == last),
        carry_back=one(after == first),
    )


def mix_forward(
    g, i, segc, keepc, q, k, v, w, probs, inv, score, mixed, kw, wv, zsum, kw_all, wv_all, pt_all,
    mt_all,
):
    run = range(UNROLL)
    chunks = [UNROLL * i + n for n in run]
    rows = [pl.ds(pl.multiple_of(c * CHUNK, CHUNK), CHUNK) for c in chunks]
    masks = [chunk_masks(c, segc) for c in chunks]
    keep = [twice(keepc[r, :]) for r in rows]
    qc, kc, vc, wc = ([ref[g, r, :] for r in rows] for ref in (q, k, v, w))
    state_k, state_v, state_z = [kw[...]], [wv[...]], [zsum[0:1, :]]
    causal = [mask for mask, _ in masks]
    edge = [edges for _, edges in masks]
    come = [twice(edge[n]["from_before"]) for n in run]
    come_low = [come[n].astype(BF16) for n in run]
    pairs = [head_pairs(dot_rt(head_stack(qc[n]), kc[n]), causal[n]) for n in run]
    for n in run:
        carry = twice(edge[n]["carry_on"])
        wg = wc[n] * twice(edge[n]["to_after"]).astype(BF16)
        state_k.append(state_k[n] * carry + diagonal(dot_lt(kc[n], wg)))
        state_v.append(state_v[n] * carry + diagonal(dot_lt(wg, vc[n])))
        state_z.append(state_z[n] * carry + jnp.sum(wg.astype(F32), axis=0, keepdims=True))
    kw_low = [head_stack(state_k[n].astype(BF16)) for n in run]
    wv_low = [head_stack(state_v[n].astype(BF16)) for n in run]
    inverse = [
        1.0 / (dot(causal[n].astype(BF16), wc[n]) + come[n] * state_z[n] + (1.0 - keep[n]))
        for n in run
    ]
    scores = [
        dot(beside(pairs[n], qc[n] * come_low[n]), above(head_stack(wc[n]), kw_low[n]))
        * (inverse[n] * (HEAD_DIM**-0.5))
        for n in run
    ]
    powers = [jnp.exp(scores[n] - head_max(scores[n])) for n in run]
    chances = [powers[n] / head_sum(powers[n]) for n in run]
    ratio = [(chances[n] * inverse[n]).astype(BF16) for n in run]
    mixing = [head_pairs(dot_rt(head_stack(ratio[n]), wc[n]), causal[n]) for n in run]
    out = [
        dot(beside(mixing[n], ratio[n] * come_low[n]), above(head_stack(vc[n]), wv_low[n]))
        for n in run
    ]
    for n in run:
        r = rows[n]
        kw_all[g, chunks[n]] = diagonal(kw_low[n].T)
        wv_all[g, chunks[n]] = diagonal(wv_low[n].T)
        pt_all[g, r, :] = flip_pairs(pairs[n])
        mt_all[g, r, :] = flip_pairs(mixing[n])
        inv[g, r, :] = inverse[n]
        score[g, r, :] = scores[n].astype(BF16)
        probs[g, r, :] = chances[n]
        mixed[g, r, :] = (out[n] * keep[n]).astype(BF16)
    kw[...] = state_k[-1]
    wv[...] = state_v[-1]
    zsum[...] = jnp.broadcast_to(state_z[-1], zsum.shape)


def mix_backward(
    g, i, segc, keepc, q, k, v, w, probs, inv, score, gm, rg, uq, zgrad, kw_all, wv_all, pt_all,
    mt_all, gy,
):
    run = range(UNROLL)
    chunks = [UNROLL * i + UNROLL - 1 - n for n in run]
    rows = [pl.ds(pl.multiple_of(c * CHUNK, CHUNK), CHUNK) for c in chunks]
    masks = [chunk_masks(c, segc) for c in chunks]
    qc, kc, vc, wc, grad, chances, inverse, scores, pairs_t, mixing_t = (
        [ref[g, r, :] for r in rows]
        for ref in (q, k, v, w, gm, probs, inv, score, pt_all, mt_all)
    )
    kw_t, wv_t = ([head_stack(ref[g, c]) for c in chunks] for ref in (kw_all, wv_all))
    state_v, state_k, state_z = [rg[...]], [uq[...]], [zgrad[0:1, :]]
    causal = [mask for mask, _ in masks]
    edge = [edges for _, edges in masks]
    come_low = [twice(edge[n]["from_before"]).astype(BF16) for n in run]
    late = [twice(edge[n]["from_after"]) for n in run]
    late_low = [late[n].astype(BF16) for n in run]
    back = [twice(edge[n]["to_before"]) for n in run]
    back_low = [back[n].astype(BF16) for n in run]
    carry = [twice(edge[n]["carry_back"]) for n in run]
    grads = [head_stack(grad[n]) for n in run]
    d_mixing = [head_pairs(dot_rt(grads[n], vc[n]), causal[n]) for n in run]
    d_chance = [
        dot(beside(d_mixing[n], grad[n] * come_low[n]), above(head_stack(wc[n]), wv_t[n]))
        * inverse[n]
        for n in run
    ]
    ratio = [(chances[n] * inverse[n]).astype(BF16) for n in run]
    ratios = [head_stack(ratio[n]) for n in run]
    for n in run:
        added = diagonal(dot_lt(ratio[n] * back_low[n], grad[n]))
        state_v.append(state_v[n] * carry[n] + added)
    rg_low = [head_stack(state_v[n].astype(BF16)) for n in run]
    w_late = [wc[n] * late_low[n] for n in run]
    gv = [dot(beside(mixing_t[n], w_late[n]), above(grads[n], rg_low[n])) for n in run]
    weighted = [d_chance[n] * chances[n] for n in run]
    d_score = [weighted[n] - chances[n] * head_sum(weighted[n]) for n in run]
    d_pw = [(d_score[n] * inverse[n] * (HEAD_DIM**-0.5)).astype(BF16) for n in run]
    d_total = [
        (weighted[n] + d_score[n] * scores[n].astype(F32)) * inverse[n] for n in run
    ]
    d_pws = [head_stack(d_pw[n]) for n in run]
    d_pairs = [head_pairs(dot_rt(d_pws[n], wc[n]), causal[n]) for n in run]
    for n in run:
        added = diagonal(dot_lt(d_pw[n] * back_low[n], qc[n]))
        state_k.append(state_k[n] * carry[n] + added)
        added = jnp.sum(d_total[n] * back[n], axis=0, keepdims=True)
        state_z.append(state_z[n] * carry[n] + added)
    uq_low = [head_stack(state_k[n].astype(BF16)) for n in run]
    dw = []
    for n in run:
        z_high = d_total[n].astype(BF16)
        z_low = (d_total[n] - z_high.astype(F32)).astype(BF16)
        anti = -causal[n].T.astype(BF16)
        left = beside(
            flip_pairs(d_mixing[n]), pairs_t[n], vc[n] * late_low[n], kc[n] * late_low[n], anti, anti
        )
        right = above(ratios[n], d_pws[n], rg_low[n].T, uq_low[n].T, z_high, z_low)
        dw.append(dot(left, right) - late[n] * state_z[n])
    gq = [
        dot(beside(d_pairs[n], d_pw[n] * come_low[n]), above(head_stack(kc[n]), kw_t[n]))
        for n in run
    ]
    gk = [
        dot(beside(flip_pairs(d_pairs[n]), w_late[n]), above(head_stack(qc[n]), uq_low[n]))
        for n in run
    ]
    for n in run:
        gy[g, rows[n], 512:768] = gv[n].astype(BF16)
        gy[g, rows[n], 768:1024] = (dw[n] * wc[n].astype(F32)).astype(BF16)
        gy[g, rows[n], 0:256] = gq[n].astype(BF16)
        gy[g, rows[n], 256:512] = gk[n].astype(BF16)
    rg[...] = state_v[-1]
    uq[...] = state_k[-1]
    zgrad[...] = jnp.broadcast_to(state_z[-1], zgrad.shape)


def units(j):
    return j // 2 % 2, (j // 4 * 2 + j % 2) * 256


def feed_in(r, tok, gain, wb, mixed, n2, gh, scales):
    rows = pl.ds(pl.multiple_of(r * TILE, TILE), TILE)
    hidden = tok[rows, :].astype(F32)
    for g in range(2):
        hidden += dot_rt(mixed[g, rows, :], flat(wb[g, ..., 0:256]))
    hat, scale = standardise(hidden)
    gh[rows, :] = hat
    scales[rows, :] = scale
    n2[rows, :] = (hat * gain[...]).astype(BF16)


def feed_up(part, r, up_bias, wb, n2, act, lin):
    rows = pl.ds(pl.multiple_of(r * TILE, TILE), TILE)
    normed = n2[rows, :]
    k0 = 0.7978845608
    k1 = k0 * 0.044715

    def linear_of(j):
        g, column = units(j)
        up = flat(wb[g, ..., 256 + column : 512 + column])
        bias = up_bias[:, g * 1024 + column : g * 1024 + column + 256]
        return dot(normed, up) + bias

    after = linear_of(4 * part)
    for j in range(4 * part, 4 * part + 4):
        linear = after
        if j < 4 * part + 3:
            after = linear_of(j + 1)
        square = linear * linear
        gate = 0.5 * jnp.tanh(linear * (square * k1 + k0)) + 0.5
        active = linear * gate
        slope = gate + active * (1.0 - gate) * (square * (6.0 * k1) + 2.0 * k0)
        g, column = units(j)
        act[g, rows, column : column + 256] = active.astype(BF16)
        lin[g, rows, column : column + 256] = slope.astype(BF16)


def feed_grad(part, r, cot, wb, lin, small):
    rows = pl.ds(pl.multiple_of(r * TILE, TILE), TILE)
    grad = cot[rows, :]

    def grad_of(j):
        g, column = units(j)
        down = flat(wb[g, ..., 1280 + column : 1536 + column])
        return dot(grad, down) * lin[g, rows, column : column + 256].astype(F32)

    after = grad_of(4 * part)
    for j in range(4 * part, 4 * part + 4):
        grad_low = after.astype(BF16)
        if j < 4 * part + 3:
            after = grad_of(j + 1)
        g, column = units(j)
        lin[g, rows, column : column + 256] = grad_low
        row, here = 4 + 2 * g + column // 512, column % 512
        small[row : row + 1, here : here + 256] += jnp.sum(
            grad_low.astype(F32), axis=0, keepdims=True
        )


def feed_back(r, cot, gain, wb, keepc, lin, gh, scales, gm, small):
    half = TILE // 2
    parts = [pl.ds(pl.multiple_of(r * TILE + n * half, half), half) for n in range(2)]
    backs = [
        dot_rt(lin[0, part, :], flat(wb[0, ..., 256:1280]))
        + dot_rt(lin[1, part, :], flat(wb[1, ..., 256:1280]))
        for part in parts
    ]
    hats = [gh[part, :] for part in parts]
    keeps = [twice(keepc[part, :]) for part in parts]
    hidden = []
    for part, back, hat in zip(parts, backs, hats):
        scaled = back * gain[...]
        inner = scaled - jnp.mean(scaled, axis=-1, keepdims=True)
        inner -= hat * jnp.mean(scaled * hat, axis=-1, keepdims=True)
        hidden.append(cot[part, :].astype(F32) + scales[part, :] * inner)
    mixed_grads = [
        [(dot(rows.astype(BF16), flat(wb[g, ..., 0:256])) * keep).astype(BF16) for g in range(2)]
        for rows, keep in zip(hidden, keeps)
    ]
    for n, part in enumerate(parts):
        gh[part, :] = hidden[n]
        for g in range(2):
            gm[g, part, :] = mixed_grads[n][g]
        small[0:1, :] += jnp.sum(backs[n] * hats[n], axis=0, keepdims=True)


def emit(r, tok, down_bias, wb, mixed, act):
    rows = pl.ds(pl.multiple_of(r * LAST, LAST), LAST)
    total = tok[rows, :].astype(F32)
    for g in range(2):
        total += dot_rt(mixed[g, rows, :], flat(wb[g, ..., 0:256]))
    total += down_bias[...]
    for g in range(2):
        total += dot_rt(act[g, rows, :], flat(wb[g, ..., 1280:2304]))
    tok[rows, :] = total.astype(BF16)


def transpose_into(source, target, length):
    for r in range(length // 256):
        here = slice(r * 256, (r + 1) * 256)
        turned = source[here, :].astype(BF16).T
        target[..., here] = turned.reshape(target.shape[:-1] + (256,))


def weight_grads(left_t, target, jobs):
    shape = target.shape[1:-1]

    def product(job):
        _, right, at, _, columns = job
        return dot(flat(left_t[...]), right[:, at : at + columns]).astype(BF16)

    after = product(jobs[0])
    for n, (g, _, _, to, columns) in enumerate(jobs):
        here = after
        if n + 1 < len(jobs):
            after = product(jobs[n + 1])
        target[g, ..., to : to + columns] = here.reshape(shape + (columns,))


def finish(r, tok, cot, gain, wa, gy, gh, small):
    rows = pl.ds(pl.multiple_of(r * LAST, LAST), LAST)
    hat, scale = standardise(tok[rows, :].astype(F32))
    back = dot_rt(gy[0, rows, :], flat(wa[0])) + dot_rt(gy[1, rows, :], flat(wa[1]))
    scaled = back * gain[...]
    inner = scaled - jnp.mean(scaled, axis=-1, keepdims=True)
    inner -= hat * jnp.mean(scaled * hat, axis=-1, keepdims=True)
    cot[rows, :] = (gh[rows, :] + scale * inner).astype(BF16)
    small[1:2, :] += jnp.sum(back * hat, axis=0, keepdims=True)


class Quiet:
    def nothing(self, *at):
        pass

    before = enter = normalised = weights_a = projected = mixing = nothing
    weights_up = feeding = fed_up = weights_down = grads_down = fed_grad = feeding_down = grads_up = nothing
    mixing_back = mixed_back = grads_a = finishing = finished = gained = grads_last = after = nothing


LAYER_INPUTS = 6
UP_PIECES = [(0, 768), (768, 1280)]
DOWN_PIECES = [(1280, 1792), (1792, 2304)]
GRAD_PIECES = DOWN_PIECES + [(256, 768), (768, 1280), (0, 256)]


def layer_body(
    length,
    comm,
    seg_row,
    pad_row,
    gain_one,
    gain_two,
    up_bias,
    down_bias,
    wa,
    wb,
    ga,
    gw,
    small,
    tok,
    cot,
    segc,
    keepc,
    n1,
    q,
    k,
    v,
    w,
    probs,
    inv,
    score,
    mixed,
    state_k,
    state_v,
    state_z,
    kw_all,
    wv_all,
    pt_all,
    mt_all,
    act,
    lin,
    gh,
    scales,
    gm,
    flip,
    n1_flip,
):
    runs, tiles = length // (UNROLL * CHUNK), length // TILE

    def clear():
        state_k[...] = jnp.zeros_like(state_k)
        state_v[...] = jnp.zeros_like(state_v)
        state_z[...] = jnp.zeros_like(state_z)

    comm.before()
    small[...] = jnp.zeros_like(small)
    rows_to_columns(seg_row, pad_row, segc, keepc, length)
    comm.enter()

    @pl.loop(0, tiles)
    def _(r):
        normalise(r, tok, cot, gain_one, n1, small)

    comm.normalised()
    transpose_into(cot, flip, length)
    transpose_into(n1, n1_flip, length)

    @pl.loop(0, 2)
    def _(g):
        comm.weights_a(g, 0)
        clear()

        @pl.loop(0, length // WIDE)
        def _(r):
            project_qk(g, r, wa, n1, q, k)

        comm.weights_a(g, 1)

        @pl.loop(0, length // WIDE)
        def _(r):
            project_vw(g, r, wa, keepc, n1, v, w)

        comm.projected(g)

        @pl.loop(0, runs)
        def _(i):
            comm.mixing(g, i)
            mix_forward(
                g, i, segc, keepc, q, k, v, w, probs, inv, score, mixed, state_k, state_v, state_z,
                kw_all, wv_all, pt_all, mt_all,
            )

    comm.weights_up(0)

    @pl.loop(0, tiles)
    def _(r):
        comm.feeding(0, r)
        feed_in(r, tok, gain_two, wb, mixed, n1, gh, scales)
        feed_up(0, r, up_bias, wb, n1, act, lin)

    transpose_into(n1, ga.at[0], length)
    comm.weights_up(1)

    @pl.loop(0, tiles)
    def _(r):
        comm.feeding(1, r)
        feed_up(1, r, up_bias, wb, n1, act, lin)

    comm.fed_up()
    for part in range(2):
        at = part * 512
        weight_grads(flip, gw, [(g, act.at[g], at, 1280 + at, 512) for g in range(2)])
        comm.grads_down(part)

    for part in range(2):
        comm.weights_down(part)

        @pl.loop(0, tiles)
        def _(r):
            feed_grad(part, r, cot, wb, lin, small)

        comm.fed_grad(part)
        at = part * 512
        weight_grads(ga.at[0], gw, [(g, lin.at[g], at, 256 + at, 512) for g in range(2)])
        comm.grads_up(part)

    @pl.loop(0, tiles)
    def _(r):
        comm.feeding_down(r)
        feed_back(r, cot, gain_two, wb, keepc, lin, gh, scales, gm, small)

    transpose_into(gh, flip, length)
    weight_grads(flip, gw, [(g, mixed.at[g], 0, 0, GROUP) for g in range(2)])
    comm.grads_up(2)

    @pl.loop(0, 2)
    def _(g):
        clear()

        @pl.loop(0, runs)
        def _(i):
            comm.mixing_back(g, i)
            mix_backward(
                g, runs - 1 - i, segc, keepc, q, k, v, w, probs, inv, score, gm, state_v, state_k,
                state_z, kw_all, wv_all, pt_all, mt_all, lin,
            )

        comm.mixed_back(g)

        weight_grads(n1_flip, ga, [(g, lin.at[g], 0, 0, 512), (g, lin.at[g], 512, 512, 256)])

        @pl.when(g == 0)
        def _():
            weight_grads(n1_flip, ga, [(0, lin.at[0], 768, 768, 256)])

        comm.grads_a(g)

    @pl.loop(0, length // LAST)
    def _(r):
        comm.finishing(0, r)
        finish(r, tok, cot, gain_one, wa, lin, gh, small)
        comm.finished(0, r)

    comm.gained()
    weight_grads(n1_flip, ga, [(1, lin.at[1], 768, 768, 256)])
    comm.grads_last()

    @pl.loop(0, length // LAST)
    def _(r):
        comm.finishing(1, r)
        emit(r, tok, down_bias, wb, mixed, act)
        comm.finished(1, r)

    comm.after()


def layer_scratch(length, width):
    vmem = pltpu.VMEM
    chunks = length // CHUNK
    return [
        vmem((length + 16, 128), F32),
        vmem((length, 128), F32),
        vmem((length, width), BF16),
        vmem((2, length, GROUP), BF16),
        vmem((2, length, GROUP), BF16),
        vmem((2, length, GROUP), BF16),
        vmem((2, length, GROUP), BF16),
        vmem((2, length, GROUP), F32),
        vmem((2, length, GROUP), F32),
        vmem((2, length, GROUP), BF16),
        vmem((2, length, GROUP), BF16),
        vmem((HEAD_DIM, GROUP), F32),
        vmem((HEAD_DIM, GROUP), F32),
        vmem((8, GROUP), F32),
        vmem((2, chunks, HEAD_DIM, GROUP), BF16),
        vmem((2, chunks, HEAD_DIM, GROUP), BF16),
        vmem((2, length, 4 * CHUNK), BF16),
        vmem((2, length, 4 * CHUNK), BF16),
        vmem((2, length, 1024), BF16),
        vmem((2, length, 1024), BF16),
        vmem((length, width), F32),
        vmem((length, 1), F32),
        vmem((2, length, GROUP), BF16),
        vmem((width, length), BF16),
        vmem((width, length), BF16),
    ]


def layer_kernel(length, tokens, cotangent, *refs):
    inputs, (out, grad_out), rest = refs[: LAYER_INPUTS + 2], refs[8:10], refs[10:]
    out[...] = tokens[...]
    grad_out[...] = cotangent[...]
    ga, gw, small = rest[:3]
    layer_body(length, Quiet(), *inputs, ga, gw, small, out, grad_out, *rest[3:])


def layer(tokens, cotangent, seg_row, pad_row, gain_one, gain_two, up_bias, down_bias, wa, wb):
    length, width = tokens.shape
    shape = jax.ShapeDtypeStruct
    cut = lambda full: full.reshape(2, -1, 2, 2, 2, 16, full.shape[-1])
    wa, wb = cut(wa), cut(wb)
    space = pl.BlockSpec(memory_space=pltpu.VMEM)
    out, grad_out, ga, gw, small = pl.pallas_call(
        functools.partial(layer_kernel, length),
        out_shape=(
            shape((length, width), BF16),
            shape((length, width), BF16),
            shape(wa.shape, BF16),
            shape(wb.shape, BF16),
            shape((8, width), F32),
        ),
        in_specs=[space] * 10,
        out_specs=tuple([space] * 5),
        scratch_shapes=layer_scratch(length, width),
        compiler_params=pltpu.CompilerParams(vmem_limit_bytes=62 * 1024 * 1024),
        name="layer",
    )(tokens, cotangent, seg_row, pad_row, gain_one, gain_two, up_bias, down_bias, wa, wb)
    whole = lambda full: full.reshape(2, width, full.shape[-1])
    return out, grad_out, whole(ga), whole(gw), small


class Place:
    def __init__(self, depth):
        index = lax.axis_index("dp")
        t = lax.axis_index("tensor")
        x, y, z = lax.rem(index, 2), lax.rem(index // 2, 2), index // 4
        self.depth = depth
        self.x, self.y, self.z, self.t, self.other = x, y, z, t, 1 - t
        self.near = (y + t * (1 - 2 * y), x + (1 - t) * (1 - 2 * x))
        self.next = (y + (1 - t) * (1 - 2 * y), x + t * (1 - 2 * x))
        self.far = (1 - y, 1 - x)
        chip = lambda z, y, x: (z * 2 + y) * 2 + x
        self.levels = [lax.rem(z + s, depth) for s in range(depth)]
        self.chips_z = [chip(level, y, x) for level in self.levels]
        self.to_near = {"dp": chip(z, *self.near)}
        self.to_next = {"dp": chip(z, *self.next)}
        self.to_far = {"dp": chip(z, *self.far)}
        self.to_pair = {"tensor": self.other}
        self.spot = (y * 2 + x) * 2 + t
        flip = lambda value, bit: value + bit * (1 - 2 * value)
        self.level = [
            {
                "dp": chip(z, flip(y, offset // 4), flip(x, offset // 2 % 2)),
                "tensor": flip(t, offset % 2),
            }
            for offset in range(8)
        ]

    def along_z(self, step, core):
        return {"dp": self.chips_z[step], "tensor": core}

    def friends(self):
        along = [self.along_z(s, core) for s in range(1, self.depth) for core in range(2)]
        return self.level[1:] + along

    def knock(self):
        barrier = pltpu.get_barrier_semaphore()
        for friend in self.friends():
            pl.semaphore_signal(barrier, inc=1, device_id=friend, device_id_type=MESH)

    def enter(self):
        pl.semaphore_wait(pltpu.get_barrier_semaphore(), len(self.friends()))


class Copies:
    def __init__(self, sems):
        self.sems = sems

    def build(self, source, target, device, out_sem, in_sem):
        return pltpu.make_async_remote_copy(
            src_ref=source,
            dst_ref=target,
            send_sem=self.sems[0].at[out_sem],
            recv_sem=self.sems[1].at[in_sem],
            device_id=device,
            device_id_type=MESH,
        )

    def start(self, source, target, device, number, in_sem=None, only=None):
        def begin():
            landing = number if in_sem is None else in_sem
            self.build(source(), target, device, number, landing).start()

        begin() if only is None else pl.when(only)(begin)

    def landed(self, target, number, only=None):
        def wait():
            self.build(target, target, {"tensor": 0}, number, number).wait_recv()

        wait() if only is None else pl.when(only)(wait)

    def sent(self, source, numbers, only=None):
        def wait():
            for number in numbers:
                self.build(source, source, {"tensor": 0}, number, number).wait_send()

        wait() if only is None else pl.when(only)(wait)


class Gather(Copies):
    SENDS, COPIES = 11, 14

    def __init__(self, place, own, full, group, columns, sems):
        super().__init__(sems)
        self.p, self.own, self.full, self.columns = place, own, full, columns
        self.group = group
        self.groups = slice(None) if group is None else slice(group, group + 1)
        self.mine = None if group is None else place.t == group
        self.pairs = None if group is None else place.t != group

    def at(self, g, z, spot, half):
        return self.full.at[g, z, spot[0], spot[1], half, :, self.columns]

    def block(self, spot, half):
        return self.at(self.groups, slice(None), spot, half)

    def forward(self, spot, device, number, in_sem=None):
        block = lambda: self.block(spot, self.p.t)
        self.start(block, block(), device, number, in_sem)

    def first(self):
        p = self.p
        here = (p.y, p.x)
        for s in range(1, p.depth):
            for core in range(2):
                self.start(
                    lambda core=core: self.own.at[core, :, self.columns],
                    self.at(p.t, p.z, here, core),
                    p.along_z(s, core),
                    2 * (s - 1) + core,
                    2 * (s - 1) + p.t,
                    only=self.mine,
                )
        self.start(
            lambda: self.own.at[p.other, :, self.columns],
            self.at(p.t, p.z, here, p.other),
            p.to_pair,
            6,
            only=self.mine,
        )

        def keep():
            self.full[p.t, p.z, p.y, p.x, p.t, :, self.columns] = self.own[p.t, :, self.columns]

        keep() if self.mine is None else pl.when(self.mine)(keep)

    def second(self):
        p = self.p
        here = (p.y, p.x)
        for n in range(6):
            if self.group is None or n % 2 == self.group:
                self.landed(self.at(p.t, p.z, here, p.t), n)
        self.landed(self.at(p.t, p.z, here, p.t), 6, only=self.pairs)
        self.forward(here, p.to_near, 7)
        self.forward(here, p.to_next, 8)
        self.forward(here, p.to_pair, 9)

    def third(self):
        p = self.p
        self.sent(self.own.at[0, :, self.columns], range(7), self.mine)
        self.landed(self.block(p.near, p.t), 7)
        self.forward(p.near, p.to_next, 0, 10)
        self.forward(p.near, p.to_pair, 1, 11)
        self.landed(self.block(p.next, p.t), 8)
        self.forward(p.next, p.to_pair, 2, 12)

    def fourth(self):
        p = self.p
        self.landed(self.block(p.far, p.t), 10)
        self.forward(p.far, p.to_pair, 3, 13)

    def last(self):
        p = self.p
        for n in (9, 11, 12, 13):
            self.landed(self.block((p.y, p.x), p.other), n)

    def left(self):
        p = self.p
        self.sent(self.block((p.y, p.x), p.t), (0, 1, 2, 3, 7, 8, 9))


class Scatter(Copies):
    COPIES = 11

    def __init__(self, place, part, group, columns, pair_in, near_in, next_in, last_in, sems):
        super().__init__(sems)
        self.p, self.part, self.columns = place, part, columns
        self.pair_in, self.near_in, self.next_in, self.last_in = pair_in, near_in, next_in, last_in
        self.group = group
        self.groups = slice(None) if group is None else slice(group, group + 1)
        self.mine = None if group is None else place.t == group
        self.pairs = None if group is None else place.t != group

    def at(self, g, z, spot, half):
        return self.part.at[g, z, spot[0], spot[1], half, :, self.columns]

    def block(self, spot, half):
        return self.at(self.groups, slice(None), spot, half)

    def add(self, spot, landed):
        p = self.p
        here = (self.groups, slice(None), spot[0], spot[1], p.t, slice(None), self.columns)
        self.part[here] = (self.part[here].astype(F32) + landed.astype(F32)).astype(BF16)

    def first(self):
        p = self.p
        self.start(
            lambda: self.part.at[self.groups, :, :, :, p.other, :, self.columns],
            self.pair_in,
            p.to_pair,
            0,
        )

    def second(self):
        p = self.p
        self.landed(self.pair_in, 0)
        for spot, number in ((p.far, 1), (p.near, 2)):
            self.add(spot, self.pair_in[:, :, spot[0], spot[1]])
            self.start(
                lambda spot=spot: self.block(spot, p.t),
                self.near_in.at[number - 1],
                p.to_near,
                number,
            )
        for spot in (p.next, (p.y, p.x)):
            self.add(spot, self.pair_in[:, :, spot[0], spot[1]])

    def third(self):
        p = self.p
        self.landed(self.near_in.at[0], 1)
        self.add(p.next, self.near_in[0])
        self.start(lambda: self.block(p.next, p.t), self.next_in, p.to_next, 3)
        self.landed(self.near_in.at[1], 2)
        self.add((p.y, p.x), self.near_in[1])

    def fourth(self):
        p = self.p
        self.landed(self.next_in, 3)
        self.add((p.y, p.x), self.next_in[...])
        self.up_the_levels()

    def up_the_levels(self):
        p = self.p
        here = (p.y, p.x)
        for s in range(1, p.depth):
            for core in range(2) if self.group is None else (self.group,):
                self.start(
                    lambda s=s, core=core: self.at(core, p.levels[s], here, p.t),
                    self.last_in.at[2 * (s - 1) + p.t],
                    p.along_z(s, core),
                    4 + 2 * (s - 1) + core,
                    4 + 2 * (s - 1) + p.t,
                )
        self.start(
            lambda: self.at(p.other, p.z, here, p.t),
            self.last_in.at[2 * (p.depth - 1)],
            p.to_pair,
            10,
            only=self.pairs,
        )

    def last(self, target):
        p = self.p

        def write():
            for n in range(7):
                self.landed(self.last_in.at[n], 4 + n)
            mine = self.part[p.t, p.z, p.y, p.x, p.t, :, self.columns].astype(F32)
            rest = self.last_in[2 * (p.depth - 1)].astype(F32)
            for s in range(1, p.depth):
                mine += self.last_in[2 * (s - 1) + p.t].astype(F32)
                rest += self.last_in[2 * (s - 1) + p.other].astype(F32)
            target[p.t] = mine
            target[p.other] = rest

        write() if self.mine is None else pl.when(self.mine)(write)

    def left(self):
        p = self.p
        self.sent(self.pair_in, (0,))
        self.sent(self.next_in, (1, 2, 3))
        for core in range(2) if self.group is None else (self.group,):
            self.sent(self.last_in.at[0], [4 + 2 * s + core for s in range(p.depth - 1)])
        self.sent(self.last_in.at[0], (10,), self.pairs)


class ShortScatter(Scatter):
    def second(self):
        p = self.p
        self.landed(self.pair_in, 0)
        for spot, target, device, number in (
            (p.far, self.near_in.at[0], p.to_far, 1),
            (p.near, self.near_in.at[1], p.to_near, 2),
            (p.next, self.next_in, p.to_next, 3),
        ):
            self.add(spot, self.pair_in[:, :, spot[0], spot[1]])
            self.start(lambda spot=spot: self.block(spot, p.t), target, device, number)
        self.add((p.y, p.x), self.pair_in[:, :, p.y, p.x])

    def fourth(self):
        p = self.p
        for part, number in ((self.next_in, 3), (self.near_in.at[1], 2), (self.near_in.at[0], 1)):
            self.landed(part, number)
            self.add((p.y, p.x), part[...])
        self.up_the_levels()


def scatter_scratch(groups, depth, columns):
    vmem = pltpu.VMEM
    return [
        vmem((groups, depth, 2, 2, 16, columns), BF16),
        vmem((2, groups, depth, 16, columns), BF16),
        vmem((groups, depth, 16, columns), BF16),
        vmem((2 * depth - 1, 16, columns), BF16),
    ]


class Reduce(Copies):
    COPIES = 10

    def __init__(self, place, own, parts, sums, sems):
        super().__init__(sems)
        self.p, self.own, self.parts, self.sums = place, own, parts, sums

    def first(self):
        p = self.p
        self.parts[p.spot] = self.own[...]
        for offset in range(1, 8):
            self.start(
                lambda: self.own, self.parts.at[p.spot], p.level[offset], offset - 1
            )

    def second(self):
        p = self.p
        for n in range(7):
            self.landed(self.own, n)
        total = self.parts[0]
        for spot in range(1, 8):
            total += self.parts[spot]
        self.sums[p.z] = total
        for s in range(1, p.depth):
            self.start(
                lambda: self.sums.at[p.z], self.sums.at[p.z], {"dp": p.chips_z[s]}, 6 + s
            )

    def last(self):
        p = self.p
        for s in range(1, p.depth):
            self.landed(self.own, 6 + s)
        total = self.sums[0]
        for z in range(1, p.depth):
            total += self.sums[z]
        return total

    def left(self):
        self.sent(self.own, range(6 + self.p.depth))


class Woven:
    def __init__(self, place, far, near, own, full, gathers, scatters, gains):
        self.p, self.far, self.near, self.own = place, far, near, own
        wa, wb, ga, gw = full
        own_a, own_b = own
        ranges = [(own_a, wa, 0, 0, 512), (own_a, wa, 0, 512, 1024), (own_a, wa, 1, 0, 1024)]
        ranges += [(own_b, wb, None, *part) for part in UP_PIECES + DOWN_PIECES]
        gather = [
            Gather(place, part, whole, g, slice(first, last), sems)
            for (part, whole, g, first, last), sems in zip(ranges, gathers)
        ]
        self.a0, self.a1, self.b = gather[:2], gather[2], gather[3:]
        ranges = [(gw, None, *part) for part in GRAD_PIECES]
        ranges += [(ga, 0, 0, 1024), (ga, 1, 0, 768), (ga, 1, 768, 1024)]
        kinds = [Scatter] * 5 + [ShortScatter] * 3
        scatter = [
            kind(place, part, g, slice(first, last), *buffers)
            for kind, (part, g, first, last), buffers in zip(kinds, ranges, scatters)
        ]
        self.down_grad, self.up_grad, self.out_grad = scatter[:2], scatter[2:4], scatter[4]
        self.a0_grad, self.a1_grad = scatter[5], scatter[6:]
        self.gains = gains
        self.everything = scatter + [gains]

    def table(self, at, steps):
        for place, calls in steps.items():
            here = None
            for value, wanted in zip(at, place):
                here = (value == wanted) if here is None else here & (value == wanted)

            @pl.when(here)
            def _(calls=calls):
                for call in calls:
                    call()

    def fetch(self, n):
        return pltpu.make_async_copy(self.far[n], self.near[n], self.near["sems"].at[n])

    def put(self, name, n):
        return pltpu.make_async_copy(self.near[name], self.far[name], self.near["sems"].at[n])

    def put_rows(self, which, r):
        rows = pl.ds(pl.multiple_of(r * LAST, LAST), LAST)
        source, target = ((1, "grad_out"), (0, "out"))[which]
        return pltpu.make_async_copy(
            self.near[source].at[rows],
            self.far[target].at[rows],
            self.near["sems"].at[18 + 4 * which + r],
        )

    def before(self):
        self.p.knock()
        for n in range(14, -1, -1):
            self.fetch(n).start()
        for n in range(2, 15):
            self.fetch(n).wait()
        first = self.p.t == 0
        for rows, row in ((2, "seg_row"), (3, "pad_row")):
            rows = self.near[rows]
            self.near[row][...] = jnp.where(first, rows[0:1, :], rows[1:2, :])
        own_a, own_b = self.own
        halves = lambda n: self.near[n][...].astype(BF16).reshape(2, 16, -1)
        for n in range(4):
            own_a[:, :, 256 * n : 256 * n + 256] = halves(8 + n)
        own_b[:, :, 0:256] = halves(12)
        own_b[:, :, 256:1280] = halves(13)
        own_b[:, :, 1280:2304] = halves(14)

    def enter(self):
        self.p.enter()
        self.a0[0].first()
        self.a0[1].first()
        self.fetch(0).wait()
        self.fetch(1).wait()

    def normalised(self):
        pass

    def weights_a(self, g, part):
        one, two = self.a0
        a1, b = self.a1, self.b
        self.table(
            (g,),
            (
                {
                    (0,): (
                        one.second, a1.first, two.second, b[0].first, one.third, two.third,
                        one.fourth, a1.second, one.last,
                    ),
                    (1,): (a1.fourth, a1.last),
                },
                {
                    (0,): (b[1].first, two.fourth, two.last),
                    (1,): (b[0].third, b[3].first),
                },
            )[part],
        )

    def projected(self, g):
        b = self.b
        self.table((g,), {(0,): (self.a1.third, b[0].second), (1,): (b[2].second,)})

    def mixing(self, g, i):
        b = self.b
        steps = {
            (0, 1): (b[1].second, self.a0[0].left, self.a0[1].left, b[2].first),
            (1, 1): (b[1].third, b[0].fourth),
        }
        self.table((g, i), steps)

    def weights_up(self, part):
        b = self.b
        if part == 0:
            b[3].second()
            b[0].last()
        else:
            b[1].last()

    def feeding(self, part, r):
        b = self.b
        steps = {(0, 1): (b[2].third, b[1].fourth), (1, 1): (b[3].third,)}
        self.table((part, r), steps)

    def fed_up(self):
        self.b[2].fourth()

    def grads_down(self, part):
        if part == 0:
            self.a1.left()
            self.b[0].left()
            self.b[1].left()
        self.down_grad[part].first()

    def weights_down(self, part):
        self.b[2 + part].last()
        self.b[2 + part].left()
        if part == 1:
            self.down_grad[1].second()

    def fed_grad(self, part):
        if part == 0:
            self.b[3].fourth()
            self.down_grad[0].second()

    def grads_up(self, part):
        if part < 2:
            self.up_grad[part].first()
        if part == 1:
            self.up_grad[0].second()
        if part == 2:
            self.out_grad.first()
            self.down_grad[1].third()
            self.up_grad[1].second()

    def feeding_down(self, r):
        self.table((r,), {(1,): (self.down_grad[0].third,)})

    def mixing_back(self, g, i):
        one, two = self.down_grad
        up, rest = self.up_grad
        steps = {
            (0, 1): (one.fourth, self.out_grad.second),
            (1, 1): (self.a0_grad.second, self.out_grad.third, self.down_last, up.fourth),
        }
        self.table((g, i), steps)

    def mixed_back(self, g):
        self.table((g,), {(0,): (self.up_grad[0].third, self.down_grad[1].fourth)})

    def grads_a(self, g):
        one, two = self.a1_grad
        self.table((g,), {(0,): (self.a0_grad.first, self.up_grad[1].third), (1,): (one.first,)})

    def grads_last(self):
        self.a1_grad[1].first()

    def finishing(self, which, r):
        one, two = self.a1_grad
        steps = {
            (0, 1): (one.second,),
            (0, 2): (self.up_grad[1].fourth,),
            (1, 0): (self.out_grad.fourth, self.a0_grad.fourth),
            (1, 1): (two.second,),
            (1, 3): (one.fourth,),
        }
        self.table((which, r), steps)

    def down_last(self):
        self.down_grad[0].last(self.near["dw"].at[:, :, 1280:1792])

    def finished(self, which, r):
        self.put_rows(which, r).start()

    def gained(self):
        self.gains.first()

    def after(self):
        one, two = self.a1_grad
        da, dw = self.near["da"], self.near["dw"]
        self.gains.second()
        two.fourth()
        self.down_grad[1].last(dw.at[:, :, 1792:2304])
        self.up_grad[0].last(dw.at[:, :, 256:768])
        self.up_grad[1].last(dw.at[:, :, 768:1280])
        self.out_grad.last(dw.at[:, :, 0:256])
        self.put("dw", 15).start()
        self.near["total"][...] = self.gains.last()
        self.put("total", 16).start()
        self.a0_grad.last(da)
        one.last(da.at[:, :, 0:768])
        two.last(da.at[:, :, 768:1024])
        self.put("da", 17).start()
        self.everything_left()

    def everything_left(self):
        for copies in self.everything:
            copies.left()
        for r in range(4):
            self.put_rows(0, r).wait()
            self.put_rows(1, r).wait()
        self.put("dw", 15).wait()
        self.put("total", 16).wait()
        self.put("da", 17).wait()


def woven_kernel(length, depth, *refs):
    refs = list(refs)
    take = lambda n: [refs.pop(0) for _ in range(n)]
    far = dict(enumerate(take(15)))
    far.update(zip(("out", "grad_out", "da", "dw", "total"), take(5)))
    near = dict(enumerate(take(15)))
    near.update(zip(("da", "dw", "total", "seg_row", "pad_row", "sems"), take(6)))
    own, full = take(2), take(4)
    small, parts, sums = take(3)
    gain_sems = take(2)
    gathers = [take(2) for _ in range(7)]
    scatters = [take(4) for _ in range(8)]
    scatters = [buffers + [sems] for buffers, sems in zip(scatters, gathers + [take(2)])]
    place = Place(depth)
    gains = Reduce(place, small, parts, sums, gain_sems)
    comm = Woven(place, far, near, own, full, gathers, scatters, gains)
    layer_body(
        length, comm, near["seg_row"], near["pad_row"], *[near[n] for n in range(4, 8)], *full,
        small, near[0], near[1], *refs,
    )


def write_kernel(out_in, grad_in, da, dw, small, *refs):
    (
        out, grad_out, mixer_gain, query, key, value, slot, out_t, feed_gain, up, up_bias, down_t,
        down_bias,
    ) = refs
    out[...] = out_in[...]
    grad_out[...] = grad_in[...]

    @pl.when(pl.program_id(0) == 0)
    def _():
        rows = lambda part: part.reshape(-1, part.shape[-1])
        query[...] = rows(da[:, :, 0:256])
        key[...] = rows(da[:, :, 256:512])
        value[...] = rows(da[:, :, 512:768])
        slot[...] = rows(da[:, :, 768:1024])
        out_t[...] = rows(dw[:, :, 0:256])
        up[...] = rows(dw[:, :, 256:1280])
        down_t[...] = rows(dw[:, :, 1280:2304])
        feed_gain[...] = small[0:1, :]
        mixer_gain[...] = small[1:2, :]
        down_bias[...] = small[2:3, :]
        for row in range(4):
            up_bias[:, row * 512 : (row + 1) * 512] = small[4 + row : 5 + row, :]


def write(out, grad_out, da, dw, small):
    shape = jax.ShapeDtypeStruct
    length, width = out.shape
    square, wide = shape((32, 256), F32), shape((32, 1024), F32)
    row, big = shape((1, width), F32), shape(out.shape, BF16)
    outputs = (big, big, row) + (square,) * 5 + (row, wide, shape((1, 4 * width), F32), wide, row)
    half = pl.BlockSpec((length // 2, width), lambda i: (i, 0))
    whole = lambda array: pl.BlockSpec(array.shape, lambda i: (0,) * len(array.shape))
    return pl.pallas_call(
        write_kernel,
        grid=(2,),
        out_shape=outputs,
        in_specs=[half, half, whole(da), whole(dw), whole(small)],
        out_specs=(half, half) + tuple(whole(array) for array in outputs[2:]),
        name="write",
    )(out, grad_out, da, dw, small)


def woven(depth, *inputs):
    length, width = inputs[0].shape
    shape = jax.ShapeDtypeStruct
    far = pl.BlockSpec(memory_space=pl.ANY)
    vmem = pltpu.VMEM
    dma = pltpu.SemaphoreType.DMA
    full = lambda columns: vmem((2, depth, 2, 2, 2, 16, columns), BF16)
    da, dw, total = shape((2, 16, 1024), F32), shape((2, 16, 2304), F32), shape((8, width), F32)
    scatters = []
    for groups, columns in [(2, 512)] * 4 + [(2, 256), (1, 1024), (1, 768), (1, 256)]:
        scatters += scatter_scratch(groups, depth, columns)
    return pl.pallas_call(
        functools.partial(woven_kernel, length, depth),
        out_shape=(shape((length, width), BF16), shape((length, width), BF16), da, dw, total),
        in_specs=[far] * 15,
        out_specs=(far,) * 5,
        scratch_shapes=[vmem(array.shape, array.dtype) for array in inputs]
        + [vmem(array.shape, array.dtype) for array in (da, dw, total)]
        + [
            vmem((1, length), jnp.int32),
            vmem((1, length), jnp.int32),
            dma((26,)),
            vmem((2, 16, 1024), BF16),
            vmem((2, 16, 2304), BF16),
            full(1024),
            full(2304),
            full(1024),
            full(2304),
            vmem((8, width), F32),
            vmem((8, 8, width), F32),
            vmem((depth, 8, width), F32),
            dma((Reduce.COPIES,)),
            dma((Reduce.COPIES,)),
        ]
        + [dma((Gather.SENDS,)), dma((Gather.COPIES,))] * 7
        + scatters
        + [dma((Scatter.COPIES,))] * 2
        + layer_scratch(length, width),
        compiler_params=pltpu.CompilerParams(
            collective_id=0, has_side_effects=True, vmem_limit_bytes=63 * 1024 * 1024
        ),
        name="woven",
    )(*inputs)


def per_device(
    direct,
    tokens,
    segment_ids,
    padding,
    mixer_gain,
    query_weight,
    key_weight,
    value_weight,
    slot_weight,
    out_weight,
    feed_gain,
    up_weight,
    up_bias,
    down_weight,
    down_bias,
    cotangent,
):
    gains = (mixer_gain[None], feed_gain[None])
    biases = (up_bias[None], down_bias[None])
    if direct:
        owns = (
            query_weight, key_weight, value_weight, slot_weight, out_weight.T, up_weight,
            down_weight.T,
        )
        depth = lax.axis_size("dp") // 4
        results = write(
            *woven(depth, tokens, cotangent, segment_ids, padding, *gains, *biases, *owns)
        )
        (
            out, grad_out, gain_one, query, key, value, slot, out_t, gain_two, up, bias_one, down_t,
            bias_two,
        ) = results
        return (
            out, grad_out, gain_one[0], query, key, value, slot, out_t.T, gain_two[0], up,
            bias_one[0], down_t.T, bias_two[0],
        )
    own_a = jnp.concatenate([query_weight, key_weight, value_weight, slot_weight], 1)
    own_b = jnp.concatenate([out_weight.T, up_weight, down_weight.T], 1)
    wa, wb = (
        lax.all_gather(lax.all_gather(own.astype(BF16), "dp", axis=0, tiled=True), "tensor")
        for own in (own_a, own_b)
    )
    half = lax.axis_index("tensor")
    pick = lambda rows: lax.dynamic_slice_in_dim(rows, half, 1, 0)
    out, grad_out, ga, gw, small = layer(
        tokens, cotangent, pick(segment_ids), pick(padding), *gains, *biases, wa, wb
    )
    da, dw = (
        lax.psum_scatter(
            lax.psum_scatter(part.astype(F32), "tensor", scatter_dimension=0),
            "dp",
            scatter_dimension=0,
            tiled=True,
        )
        for part in (ga, gw)
    )
    small = lax.psum(small, ("dp", "tensor"))
    return (
        out,
        grad_out,
        small[1],
        da[:, 0:256],
        da[:, 256:512],
        da[:, 512:768],
        da[:, 768:1024],
        dw[:, 0:256].T,
        small[0],
        dw[:, 256:1280],
        small[4:8].reshape(-1),
        dw[:, 1280:2304].T,
        small[2],
    )


def solution(mesh):
    in_specs = (
        P(("dp", "tensor"), None),
        P("dp", None),
        P("dp", None),
        P(),
        P("dp", "tensor"),
        P("dp", "tensor"),
        P("dp", "tensor"),
        P("dp", "tensor"),
        P("tensor", "dp"),
        P(),
        P("dp", "tensor"),
        P(),
        P("tensor", "dp"),
        P(),
        P(("dp", "tensor"), None),
    )
    out_specs = (
        P(("dp", "tensor"), None),
        P(("dp", "tensor"), None),
        P(),
        P("dp", "tensor"),
        P("dp", "tensor"),
        P("dp", "tensor"),
        P("dp", "tensor"),
        P("tensor", "dp"),
        P(),
        P("dp", "tensor"),
        P(),
        P("tensor", "dp"),
        P(),
    )
    direct = mesh.shape["dp"] == 16 and mesh.shape["tensor"] == 2
    return jax.shard_map(
        functools.partial(per_device, direct),
        mesh=mesh,
        in_specs=in_specs,
        out_specs=out_specs,
        check_vma=False,
    )
```

```python
import functools
import math

import jax
import jax.numpy as jnp
from jax import lax
from jax.experimental import pallas as pl
from jax.experimental.pallas import tpu as pltpu
from jax.sharding import PartitionSpec as P

HEAD_DIM = 64
SLOTS = 64
CHUNK = 128
UNROLL = 4
GROUP = 256
TILE = 512
WIDE = 512
LAST = 512

F32 = jnp.float32
BF16 = jnp.bfloat16
MESH = pl.DeviceIdType.MESH


def dot(left, right):
    return lax.dot_general(left, right, (((1,), (0,)), ((), ())), preferred_element_type=F32)


def dot_rt(left, right):
    return lax.dot_general(left, right, (((1,), (1,)), ((), ())), preferred_element_type=F32)


def dot_lt(left, right):
    return lax.dot_general(left, right, (((0,), (0,)), ((), ())), preferred_element_type=F32)


def twice(block):
    return jnp.concatenate([block, block], axis=1)


def standardise(rows):
    centred = rows - jnp.mean(rows, axis=-1, keepdims=True)
    scale = lax.rsqrt(jnp.mean(centred * centred, axis=-1, keepdims=True) + 1e-05)
    return centred * scale, scale


def head_stack(block):
    lane = lax.broadcasted_iota(jnp.int32, block.shape, 1) // HEAD_DIM
    zero = jnp.zeros_like(block)
    return jnp.concatenate([jnp.where(lane == h, block, zero) for h in range(4)], axis=0)


def diagonal(product):
    parts = [product[h * HEAD_DIM : (h + 1) * HEAD_DIM, :] for h in range(4)]
    lane = lax.broadcasted_iota(jnp.int32, parts[0].shape, 1) // HEAD_DIM
    kept = parts[3]
    for h in range(3):
        kept = jnp.where(lane == h, parts[h], kept)
    return kept


def over_heads(block, reduce, rest):
    halves = []
    lane = lax.broadcasted_iota(jnp.int32, (block.shape[0], 128), 1) < HEAD_DIM
    for j in range(block.shape[1] // 128):
        part = block[:, j * 128 : (j + 1) * 128]
        first = reduce(jnp.where(lane, part, rest), axis=1, keepdims=True)
        second = reduce(jnp.where(lane, rest, part), axis=1, keepdims=True)
        halves.append(jnp.where(lane, first, second))
    return jnp.concatenate(halves, axis=1)


def head_max(block):
    return over_heads(block, jnp.max, -jnp.inf)


def head_sum(block):
    return over_heads(block, jnp.sum, 0.0)


def head_pairs(product, allowed):
    parts = [product[h * CHUNK : (h + 1) * CHUNK, :] * allowed for h in range(4)]
    return jnp.concatenate(parts, axis=1).astype(BF16)


def flip_pairs(pairs):
    parts = [pairs[:, h * CHUNK : (h + 1) * CHUNK].T for h in range(4)]
    return jnp.concatenate(parts, axis=1)


def beside(*blocks):
    return jnp.concatenate(blocks, axis=1)


def above(*blocks):
    return jnp.concatenate(blocks, axis=0)


def flat(block):
    return block.reshape(-1, block.shape[-1])


def rows_to_columns(seg_row, pad_row, segc, keepc, length):
    segc[pl.ds(0, 8), :] = jnp.full((8, 128), -1.0, F32)
    segc[pl.ds(8 + length, 8), :] = jnp.full((8, 128), -2.0, F32)
    for c in range(length // CHUNK):
        here = slice(c * CHUNK, (c + 1) * CHUNK)
        seg = jnp.broadcast_to(seg_row[:, here].astype(F32), (CHUNK, CHUNK))
        pad = jnp.broadcast_to(pad_row[:, here].astype(F32), (CHUNK, CHUNK))
        segc[pl.ds(8 + c * CHUNK, CHUNK), :] = seg.T
        keepc[pl.ds(c * CHUNK, CHUNK), :] = 1.0 - pad.T


def normalise(r, tok, cot, gain, n1, small):
    rows = pl.ds(pl.multiple_of(r * TILE, TILE), TILE)
    xhat, _ = standardise(tok[rows, :].astype(F32))
    n1[rows, :] = (xhat * gain[...]).astype(BF16)
    small[2:3, :] += jnp.sum(cot[rows, :].astype(F32), axis=0, keepdims=True)


def project_qk(g, r, wa, n1, q, k):
    rows = pl.ds(pl.multiple_of(r * WIDE, WIDE), WIDE)
    out = dot(n1[rows, :], flat(wa[g, ..., 0:512]))
    q[g, rows, :] = out[:, 0:256].astype(BF16)
    k[g, rows, :] = out[:, 256:512].astype(BF16)


def project_vw(g, r, wa, keepc, n1, v, w):
    rows = pl.ds(pl.multiple_of(r * WIDE, WIDE), WIDE)
    out = dot(n1[rows, :], flat(wa[g, ..., 512:1024]))
    v[g, rows, :] = out[:, 0:256].astype(BF16)
    w[g, rows, :] = (jnp.exp(out[:, 256:512]) * twice(keepc[rows, :])).astype(BF16)


def chunk_masks(c, segc):
    base = pl.multiple_of(c * CHUNK, CHUNK)
    seg = segc[pl.ds(base + 8, CHUNK), :]
    across = seg.T
    row = lax.broadcasted_iota(jnp.int32, (CHUNK, CHUNK), 0)
    column = lax.broadcasted_iota(jnp.int32, (CHUNK, CHUNK), 1)
    same = seg == across
    causal = jnp.where(same & (column <= row), 1.0, 0.0)
    before = segc[pl.ds(base + 7, 1), :]
    first = segc[pl.ds(base + 8, 1), :]
    last = segc[pl.ds(base + 7 + CHUNK, 1), :]
    after = segc[pl.ds(base + 8 + CHUNK, 1), :]
    one = lambda test: jnp.where(test, 1.0, 0.0)
    return causal, dict(
        from_before=one(seg == before),
        to_after=one(seg == last),
        from_after=one(seg == after),
        to_before=one(seg == first),
        carry_on=one(before == last),
        carry_back=one(after == first),
    )


def mix_forward(
    g, i, segc, keepc, q, k, v, w, probs, inv, score, mixed, kw, wv, zsum, kw_all, wv_all, pt_all,
    mt_all,
):
    run = range(UNROLL)
    chunks = [UNROLL * i + n for n in run]
    rows = [pl.ds(pl.multiple_of(c * CHUNK, CHUNK), CHUNK) for c in chunks]
    masks = [chunk_masks(c, segc) for c in chunks]
    keep = [twice(keepc[r, :]) for r in rows]
    qc, kc, vc, wc = ([ref[g, r, :] for r in rows] for ref in (q, k, v, w))
    state_k, state_v, state_z = [kw[...]], [wv[...]], [zsum[0:1, :]]
    causal = [mask for mask, _ in masks]
    edge = [edges for _, edges in masks]
    come = [twice(edge[n]["from_before"]) for n in run]
    come_low = [come[n].astype(BF16) for n in run]
    pairs = [head_pairs(dot_rt(head_stack(qc[n]), kc[n]), causal[n]) for n in run]
    for n in run:
        carry = twice(edge[n]["carry_on"])
        wg = wc[n] * twice(edge[n]["to_after"]).astype(BF16)
        state_k.append(state_k[n] * carry + diagonal(dot_lt(kc[n], wg)))
        state_v.append(state_v[n] * carry + diagonal(dot_lt(wg, vc[n])))
        state_z.append(state_z[n] * carry + jnp.sum(wg.astype(F32), axis=0, keepdims=True))
    kw_low = [head_stack(state_k[n].astype(BF16)) for n in run]
    wv_low = [head_stack(state_v[n].astype(BF16)) for n in run]
    inverse = [
        1.0 / (dot(causal[n].astype(BF16), wc[n]) + come[n] * state_z[n] + (1.0 - keep[n]))
        for n in run
    ]
    scores = [
        dot(beside(pairs[n], qc[n] * come_low[n]), above(head_stack(wc[n]), kw_low[n]))
        * (inverse[n] * (HEAD_DIM**-0.5))
        for n in run
    ]
    powers = [jnp.exp(scores[n] - head_max(scores[n])) for n in run]
    chances = [powers[n] / head_sum(powers[n]) for n in run]
    ratio = [(chances[n] * inverse[n]).astype(BF16) for n in run]
    mixing = [head_pairs(dot_rt(head_stack(ratio[n]), wc[n]), causal[n]) for n in run]
    out = [
        dot(beside(mixing[n], ratio[n] * come_low[n]), above(head_stack(vc[n]), wv_low[n]))
        for n in run
    ]
    for n in run:
        r = rows[n]
        kw_all[g, chunks[n]] = diagonal(kw_low[n].T)
        wv_all[g, chunks[n]] = diagonal(wv_low[n].T)
        pt_all[g, r, :] = flip_pairs(pairs[n])
        mt_all[g, r, :] = flip_pairs(mixing[n])
        inv[g, r, :] = inverse[n]
        score[g, r, :] = scores[n].astype(BF16)
        probs[g, r, :] = chances[n]
        mixed[g, r, :] = (out[n] * keep[n]).astype(BF16)
    kw[...] = state_k[-1]
    wv[...] = state_v[-1]
    zsum[...] = jnp.broadcast_to(state_z[-1], zsum.shape)


def mix_backward(
    g, i, segc, keepc, q, k, v, w, probs, inv, score, gm, rg, uq, zgrad, kw_all, wv_all, pt_all,
    mt_all, gy,
):
    run = range(UNROLL)
    chunks = [UNROLL * i + UNROLL - 1 - n for n in run]
    rows = [pl.ds(pl.multiple_of(c * CHUNK, CHUNK), CHUNK) for c in chunks]
    masks = [chunk_masks(c, segc) for c in chunks]
    qc, kc, vc, wc, grad, chances, inverse, scores, pairs_t, mixing_t = (
        [ref[g, r, :] for r in rows]
        for ref in (q, k, v, w, gm, probs, inv, score, pt_all, mt_all)
    )
    kw_t, wv_t = ([head_stack(ref[g, c]) for c in chunks] for ref in (kw_all, wv_all))
    state_v, state_k, state_z = [rg[...]], [uq[...]], [zgrad[0:1, :]]
    causal = [mask for mask, _ in masks]
    edge = [edges for _, edges in masks]
    come_low = [twice(edge[n]["from_before"]).astype(BF16) for n in run]
    late = [twice(edge[n]["from_after"]) for n in run]
    late_low = [late[n].astype(BF16) for n in run]
    back = [twice(edge[n]["to_before"]) for n in run]
    back_low = [back[n].astype(BF16) for n in run]
    carry = [twice(edge[n]["carry_back"]) for n in run]
    grads = [head_stack(grad[n]) for n in run]
    d_mixing = [head_pairs(dot_rt(grads[n], vc[n]), causal[n]) for n in run]
    d_chance = [
        dot(beside(d_mixing[n], grad[n] * come_low[n]), above(head_stack(wc[n]), wv_t[n]))
        * inverse[n]
        for n in run
    ]
    ratio = [(chances[n] * inverse[n]).astype(BF16) for n in run]
    ratios = [head_stack(ratio[n]) for n in run]
    for n in run:
        added = diagonal(dot_lt(ratio[n] * back_low[n], grad[n]))
        state_v.append(state_v[n] * carry[n] + added)
    rg_low = [head_stack(state_v[n].astype(BF16)) for n in run]
    w_late = [wc[n] * late_low[n] for n in run]
    gv = [dot(beside(mixing_t[n], w_late[n]), above(grads[n], rg_low[n])) for n in run]
    weighted = [d_chance[n] * chances[n] for n in run]
    d_score = [weighted[n] - chances[n] * head_sum(weighted[n]) for n in run]
    d_pw = [(d_score[n] * inverse[n] * (HEAD_DIM**-0.5)).astype(BF16) for n in run]
    d_total = [
        (weighted[n] + d_score[n] * scores[n].astype(F32)) * inverse[n] for n in run
    ]
    d_pws = [head_stack(d_pw[n]) for n in run]
    d_pairs = [head_pairs(dot_rt(d_pws[n], wc[n]), causal[n]) for n in run]
    for n in run:
        added = diagonal(dot_lt(d_pw[n] * back_low[n], qc[n]))
        state_k.append(state_k[n] * carry[n] + added)
        added = jnp.sum(d_total[n] * back[n], axis=0, keepdims=True)
        state_z.append(state_z[n] * carry[n] + added)
    uq_low = [head_stack(state_k[n].astype(BF16)) for n in run]
    dw = []
    for n in run:
        z_high = d_total[n].astype(BF16)
        z_low = (d_total[n] - z_high.astype(F32)).astype(BF16)
        anti = -causal[n].T.astype(BF16)
        left = beside(
            flip_pairs(d_mixing[n]), pairs_t[n], vc[n] * late_low[n], kc[n] * late_low[n], anti, anti
        )
        right = above(ratios[n], d_pws[n], rg_low[n].T, uq_low[n].T, z_high, z_low)
        dw.append(dot(left, right) - late[n] * state_z[n])
    gq = [
        dot(beside(d_pairs[n], d_pw[n] * come_low[n]), above(head_stack(kc[n]), kw_t[n]))
        for n in run
    ]
    gk = [
        dot(beside(flip_pairs(d_pairs[n]), w_late[n]), above(head_stack(qc[n]), uq_low[n]))
        for n in run
    ]
    for n in run:
        gy[g, rows[n], 512:768] = gv[n].astype(BF16)
        gy[g, rows[n], 768:1024] = (dw[n] * wc[n].astype(F32)).astype(BF16)
        gy[g, rows[n], 0:256] = gq[n].astype(BF16)
        gy[g, rows[n], 256:512] = gk[n].astype(BF16)
    rg[...] = state_v[-1]
    uq[...] = state_k[-1]
    zgrad[...] = jnp.broadcast_to(state_z[-1], zgrad.shape)


def units(j):
    return j // 2 % 2, (j // 4 * 2 + j % 2) * 256


def feed_in(r, tok, gain, wb, mixed, n2, gh, scales):
    rows = pl.ds(pl.multiple_of(r * TILE, TILE), TILE)
    hidden = tok[rows, :].astype(F32)
    for g in range(2):
        hidden += dot_rt(mixed[g, rows, :], flat(wb[g, ..., 0:256]))
    hat, scale = standardise(hidden)
    gh[rows, :] = hat
    scales[rows, :] = scale
    n2[rows, :] = (hat * gain[...]).astype(BF16)


def feed_up(part, r, up_bias, wb, n2, act, lin):
    rows = pl.ds(pl.multiple_of(r * TILE, TILE), TILE)
    normed = n2[rows, :]
    k0 = 0.7978845608
    k1 = k0 * 0.044715

    def linear_of(j):
        g, column = units(j)
        up = flat(wb[g, ..., 256 + column : 512 + column])
        bias = up_bias[:, g * 1024 + column : g * 1024 + column + 256]
        return dot(normed, up) + bias

    after = linear_of(4 * part)
    for j in range(4 * part, 4 * part + 4):
        linear = after
        if j < 4 * part + 3:
            after = linear_of(j + 1)
        square = linear * linear
        gate = 0.5 * jnp.tanh(linear * (square * k1 + k0)) + 0.5
        active = linear * gate
        slope = gate + active * (1.0 - gate) * (square * (6.0 * k1) + 2.0 * k0)
        g, column = units(j)
        act[g, rows, column : column + 256] = active.astype(BF16)
        lin[g, rows, column : column + 256] = slope.astype(BF16)


def feed_grad(part, r, cot, wb, lin, small):
    rows = pl.ds(pl.multiple_of(r * TILE, TILE), TILE)
    grad = cot[rows, :]

    def grad_of(j):
        g, column = units(j)
        down = flat(wb[g, ..., 1280 + column : 1536 + column])
        return dot(grad, down) * lin[g, rows, column : column + 256].astype(F32)

    after = grad_of(4 * part)
    for j in range(4 * part, 4 * part + 4):
        grad_low = after.astype(BF16)
        if j < 4 * part + 3:
            after = grad_of(j + 1)
        g, column = units(j)
        lin[g, rows, column : column + 256] = grad_low
        row, here = 4 + 2 * g + column // 512, column % 512
        small[row : row + 1, here : here + 256] += jnp.sum(
            grad_low.astype(F32), axis=0, keepdims=True
        )


def feed_back(r, cot, gain, wb, keepc, lin, gh, scales, gm, small):
    half = TILE // 2
    parts = [pl.ds(pl.multiple_of(r * TILE + n * half, half), half) for n in range(2)]
    backs = [
        dot_rt(lin[0, part, :], flat(wb[0, ..., 256:1280]))
        + dot_rt(lin[1, part, :], flat(wb[1, ..., 256:1280]))
        for part in parts
    ]
    hats = [gh[part, :] for part in parts]
    keeps = [twice(keepc[part, :]) for part in parts]
    hidden = []
    for part, back, hat in zip(parts, backs, hats):
        scaled = back * gain[...]
        inner = scaled - jnp.mean(scaled, axis=-1, keepdims=True)
        inner -= hat * jnp.mean(scaled * hat, axis=-1, keepdims=True)
        hidden.append(cot[part, :].astype(F32) + scales[part, :] * inner)
    mixed_grads = [
        [(dot(rows.astype(BF16), flat(wb[g, ..., 0:256])) * keep).astype(BF16) for g in range(2)]
        for rows, keep in zip(hidden, keeps)
    ]
    for n, part in enumerate(parts):
        gh[part, :] = hidden[n]
        for g in range(2):
            gm[g, part, :] = mixed_grads[n][g]
        small[0:1, :] += jnp.sum(backs[n] * hats[n], axis=0, keepdims=True)


def emit(r, tok, down_bias, wb, mixed, act):
    rows = pl.ds(pl.multiple_of(r * LAST, LAST), LAST)
    total = tok[rows, :].astype(F32)
    for g in range(2):
        total += dot_rt(mixed[g, rows, :], flat(wb[g, ..., 0:256]))
    total += down_bias[...]
    for g in range(2):
        total += dot_rt(act[g, rows, :], flat(wb[g, ..., 1280:2304]))
    tok[rows, :] = total.astype(BF16)


def transpose_into(source, target, length):
    for r in range(length // 256):
        here = slice(r * 256, (r + 1) * 256)
        turned = source[here, :].astype(BF16).T
        target[..., here] = turned.reshape(target.shape[:-1] + (256,))


def weight_grads(left_t, target, jobs):
    shape = target.shape[1:-1]

    def product(job):
        _, right, at, _, columns = job
        return dot(flat(left_t[...]), right[:, at : at + columns]).astype(BF16)

    after = product(jobs[0])
    for n, (g, _, _, to, columns) in enumerate(jobs):
        here = after
        if n + 1 < len(jobs):
            after = product(jobs[n + 1])
        target[g, ..., to : to + columns] = here.reshape(shape + (columns,))


def finish(r, tok, cot, gain, wa, gy, gh, small):
    rows = pl.ds(pl.multiple_of(r * LAST, LAST), LAST)
    hat, scale = standardise(tok[rows, :].astype(F32))
    back = dot_rt(gy[0, rows, :], flat(wa[0])) + dot_rt(gy[1, rows, :], flat(wa[1]))
    scaled = back * gain[...]
    inner = scaled - jnp.mean(scaled, axis=-1, keepdims=True)
    inner -= hat * jnp.mean(scaled * hat, axis=-1, keepdims=True)
    cot[rows, :] = (gh[rows, :] + scale * inner).astype(BF16)
    small[1:2, :] += jnp.sum(back * hat, axis=0, keepdims=True)


class Quiet:
    def nothing(self, *at):
        pass

    before = enter = normalised = weights_a = projected = mixing = nothing
    weights_up = feeding = fed_up = weights_down = grads_down = fed_grad = feeding_down = grads_up = nothing
    mixing_back = mixed_back = grads_a = finishing = finished = gained = grads_last = after = nothing


LAYER_INPUTS = 6
UP_PIECES = [(0, 768), (768, 1280)]
DOWN_PIECES = [(1280, 1792), (1792, 2304)]
GRAD_PIECES = DOWN_PIECES + [(256, 768), (768, 1280), (0, 256)]


def layer_body(
    length,
    comm,
    seg_row,
    pad_row,
    gain_one,
    gain_two,
    up_bias,
    down_bias,
    wa,
    wb,
    ga,
    gw,
    small,
    tok,
    cot,
    segc,
    keepc,
    n1,
    q,
    k,
    v,
    w,
    probs,
    inv,
    score,
    mixed,
    state_k,
    state_v,
    state_z,
    kw_all,
    wv_all,
    pt_all,
    mt_all,
    act,
    lin,
    gh,
    scales,
    gm,
    flip,
    n1_flip,
):
    runs, tiles = length // (UNROLL * CHUNK), length // TILE

    def clear():
        state_k[...] = jnp.zeros_like(state_k)
        state_v[...] = jnp.zeros_like(state_v)
        state_z[...] = jnp.zeros_like(state_z)

    comm.before()
    small[...] = jnp.zeros_like(small)
    rows_to_columns(seg_row, pad_row, segc, keepc, length)
    comm.enter()

    @pl.loop(0, tiles)
    def _(r):
        normalise(r, tok, cot, gain_one, n1, small)

    comm.normalised()
    transpose_into(cot, flip, length)
    transpose_into(n1, n1_flip, length)

    @pl.loop(0, 2)
    def _(g):
        comm.weights_a(g, 0)
        clear()

        @pl.loop(0, length // WIDE)
        def _(r):
            project_qk(g, r, wa, n1, q, k)

        comm.weights_a(g, 1)

        @pl.loop(0, length // WIDE)
        def _(r):
            project_vw(g, r, wa, keepc, n1, v, w)

        comm.projected(g)

        @pl.loop(0, runs)
        def _(i):
            comm.mixing(g, i)
            mix_forward(
                g, i, segc, keepc, q, k, v, w, probs, inv, score, mixed, state_k, state_v, state_z,
                kw_all, wv_all, pt_all, mt_all,
            )

    comm.weights_up(0)

    @pl.loop(0, tiles)
    def _(r):
        comm.feeding(0, r)
        feed_in(r, tok, gain_two, wb, mixed, n1, gh, scales)
        feed_up(0, r, up_bias, wb, n1, act, lin)

    transpose_into(n1, ga.at[0], length)
    comm.weights_up(1)

    @pl.loop(0, tiles)
    def _(r):
        comm.feeding(1, r)
        feed_up(1, r, up_bias, wb, n1, act, lin)

    comm.fed_up()
    for part in range(2):
        at = part * 512
        weight_grads(flip, gw, [(g, act.at[g], at, 1280 + at, 512) for g in range(2)])
        comm.grads_down(part)

    for part in range(2):
        comm.weights_down(part)

        @pl.loop(0, tiles)
        def _(r):
            feed_grad(part, r, cot, wb, lin, small)

        comm.fed_grad(part)
        at = part * 512
        weight_grads(ga.at[0], gw, [(g, lin.at[g], at, 256 + at, 512) for g in range(2)])
        comm.grads_up(part)

    @pl.loop(0, tiles)
    def _(r):
        comm.feeding_down(r)
        feed_back(r, cot, gain_two, wb, keepc, lin, gh, scales, gm, small)

    transpose_into(gh, flip, length)
    weight_grads(flip, gw, [(g, mixed.at[g], 0, 0, GROUP) for g in range(2)])
    comm.grads_up(2)

    @pl.loop(0, 2)
    def _(g):
        clear()

        @pl.loop(0, runs)
        def _(i):
            comm.mixing_back(g, i)
            mix_backward(
                g, runs - 1 - i, segc, keepc, q, k, v, w, probs, inv, score, gm, state_v, state_k,
                state_z, kw_all, wv_all, pt_all, mt_all, lin,
            )

        comm.mixed_back(g)

        weight_grads(n1_flip, ga, [(g, lin.at[g], 0, 0, 512), (g, lin.at[g], 512, 512, 256)])

        @pl.when(g == 0)
        def _():
            weight_grads(n1_flip, ga, [(0, lin.at[0], 768, 768, 256)])

        comm.grads_a(g)

    @pl.loop(0, length // LAST)
    def _(r):
        comm.finishing(0, r)
        finish(r, tok, cot, gain_one, wa, lin, gh, small)
        comm.finished(0, r)

    comm.gained()
    weight_grads(n1_flip, ga, [(1, lin.at[1], 768, 768, 256)])
    comm.grads_last()

    @pl.loop(0, length // LAST)
    def _(r):
        comm.finishing(1, r)
        emit(r, tok, down_bias, wb, mixed, act)
        comm.finished(1, r)

    comm.after()


def layer_scratch(length, width):
    vmem = pltpu.VMEM
    chunks = length // CHUNK
    return [
        vmem((length + 16, 128), F32),
        vmem((length, 128), F32),
        vmem((length, width), BF16),
        vmem((2, length, GROUP), BF16),
        vmem((2, length, GROUP), BF16),
        vmem((2, length, GROUP), BF16),
        vmem((2, length, GROUP), BF16),
        vmem((2, length, GROUP), F32),
        vmem((2, length, GROUP), F32),
        vmem((2, length, GROUP), BF16),
        vmem((2, length, GROUP), BF16),
        vmem((HEAD_DIM, GROUP), F32),
        vmem((HEAD_DIM, GROUP), F32),
        vmem((8, GROUP), F32),
        vmem((2, chunks, HEAD_DIM, GROUP), BF16),
        vmem((2, chunks, HEAD_DIM, GROUP), BF16),
        vmem((2, length, 4 * CHUNK), BF16),
        vmem((2, length, 4 * CHUNK), BF16),
        vmem((2, length, 1024), BF16),
        vmem((2, length, 1024), BF16),
        vmem((length, width), F32),
        vmem((length, 1), F32),
        vmem((2, length, GROUP), BF16),
        vmem((width, length), BF16),
        vmem((width, length), BF16),
    ]


def layer_kernel(length, tokens, cotangent, *refs):
    inputs, (out, grad_out), rest = refs[: LAYER_INPUTS + 2], refs[8:10], refs[10:]
    out[...] = tokens[...]
    grad_out[...] = cotangent[...]
    ga, gw, small = rest[:3]
    layer_body(length, Quiet(), *inputs, ga, gw, small, out, grad_out, *rest[3:])


def layer(tokens, cotangent, seg_row, pad_row, gain_one, gain_two, up_bias, down_bias, wa, wb):
    length, width = tokens.shape
    shape = jax.ShapeDtypeStruct
    cut = lambda full: full.reshape(2, -1, 2, 2, 2, 16, full.shape[-1])
    wa, wb = cut(wa), cut(wb)
    space = pl.BlockSpec(memory_space=pltpu.VMEM)
    out, grad_out, ga, gw, small = pl.pallas_call(
        functools.partial(layer_kernel, length),
        out_shape=(
            shape((length, width), BF16),
            shape((length, width), BF16),
            shape(wa.shape, BF16),
            shape(wb.shape, BF16),
            shape((8, width), F32),
        ),
        in_specs=[space] * 10,
        out_specs=tuple([space] * 5),
        scratch_shapes=layer_scratch(length, width),
        compiler_params=pltpu.CompilerParams(vmem_limit_bytes=62 * 1024 * 1024),
        name="layer",
    )(tokens, cotangent, seg_row, pad_row, gain_one, gain_two, up_bias, down_bias, wa, wb)
    whole = lambda full: full.reshape(2, width, full.shape[-1])
    return out, grad_out, whole(ga), whole(gw), small


class Place:
    def __init__(self, depth):
        index = lax.axis_index("dp")
        t = lax.axis_index("tensor")
        x, y, z = lax.rem(index, 2), lax.rem(index // 2, 2), index // 4
        self.depth = depth
        self.x, self.y, self.z, self.t, self.other = x, y, z, t, 1 - t
        self.near = (y + t * (1 - 2 * y), x + (1 - t) * (1 - 2 * x))
        self.next = (y + (1 - t) * (1 - 2 * y), x + t * (1 - 2 * x))
        self.far = (1 - y, 1 - x)
        chip = lambda z, y, x: (z * 2 + y) * 2 + x
        self.levels = [lax.rem(z + s, depth) for s in range(depth)]
        self.chips_z = [chip(level, y, x) for level in self.levels]
        self.to_near = {"dp": chip(z, *self.near)}
        self.to_next = {"dp": chip(z, *self.next)}
        self.to_far = {"dp": chip(z, *self.far)}
        self.to_pair = {"tensor": self.other}
        self.spot = (y * 2 + x) * 2 + t
        flip = lambda value, bit: value + bit * (1 - 2 * value)
        self.level = [
            {
                "dp": chip(z, flip(y, offset // 4), flip(x, offset // 2 % 2)),
                "tensor": flip(t, offset % 2),
            }
            for offset in range(8)
        ]

    def along_z(self, step, core):
        return {"dp": self.chips_z[step], "tensor": core}

    def friends(self):
        along = [self.along_z(s, core) for s in range(1, self.depth) for core in range(2)]
        return self.level[1:] + along

    def knock(self):
        barrier = pltpu.get_barrier_semaphore()
        for friend in self.friends():
            pl.semaphore_signal(barrier, inc=1, device_id=friend, device_id_type=MESH)

    def enter(self):
        pl.semaphore_wait(pltpu.get_barrier_semaphore(), len(self.friends()))


class Copies:
    def __init__(self, sems):
        self.sems = sems

    def build(self, source, target, device, out_sem, in_sem):
        return pltpu.make_async_remote_copy(
            src_ref=source,
            dst_ref=target,
            send_sem=self.sems[0].at[out_sem],
            recv_sem=self.sems[1].at[in_sem],
            device_id=device,
            device_id_type=MESH,
        )

    def start(self, source, target, device, number, in_sem=None, only=None):
        def begin():
            landing = number if in_sem is None else in_sem
            self.build(source(), target, device, number, landing).start()

        begin() if only is None else pl.when(only)(begin)

    def landed(self, target, number, only=None):
        def wait():
            self.build(target, target, {"tensor": 0}, number, number).wait_recv()

        wait() if only is None else pl.when(only)(wait)

    def sent(self, source, numbers, only=None):
        def wait():
            for number in numbers:
                self.build(source, source, {"tensor": 0}, number, number).wait_send()

        wait() if only is None else pl.when(only)(wait)


class Gather(Copies):
    SENDS, COPIES = 11, 14

    def __init__(self, place, own, full, group, columns, sems):
        super().__init__(sems)
        self.p, self.own, self.full, self.columns = place, own, full, columns
        self.group = group
        self.groups = slice(None) if group is None else slice(group, group + 1)
        self.mine = None if group is None else place.t == group
        self.pairs = None if group is None else place.t != group

    def at(self, g, z, spot, half):
        return self.full.at[g, z, spot[0], spot[1], half, :, self.columns]

    def block(self, spot, half):
        return self.at(self.groups, slice(None), spot, half)

    def forward(self, spot, device, number, in_sem=None):
        block = lambda: self.block(spot, self.p.t)
        self.start(block, block(), device, number, in_sem)

    def first(self):
        p = self.p
        here = (p.y, p.x)
        for s in range(1, p.depth):
            for core in range(2):
                self.start(
                    lambda core=core: self.own.at[core, :, self.columns],
                    self.at(p.t, p.z, here, core),
                    p.along_z(s, core),
                    2 * (s - 1) + core,
                    2 * (s - 1) + p.t,
                    only=self.mine,
                )
        self.start(
            lambda: self.own.at[p.other, :, self.columns],
            self.at(p.t, p.z, here, p.other),
            p.to_pair,
            6,
            only=self.mine,
        )

        def keep():
            self.full[p.t, p.z, p.y, p.x, p.t, :, self.columns] = self.own[p.t, :, self.columns]

        keep() if self.mine is None else pl.when(self.mine)(keep)

    def second(self):
        p = self.p
        here = (p.y, p.x)
        for n in range(6):
            if self.group is None or n % 2 == self.group:
                self.landed(self.at(p.t, p.z, here, p.t), n)
        self.landed(self.at(p.t, p.z, here, p.t), 6, only=self.pairs)
        self.forward(here, p.to_near, 7)
        self.forward(here, p.to_next, 8)
        self.forward(here, p.to_pair, 9)

    def third(self):
        p = self.p
        self.sent(self.own.at[0, :, self.columns], range(7), self.mine)
        self.landed(self.block(p.near, p.t), 7)
        self.forward(p.near, p.to_next, 0, 10)
        self.forward(p.near, p.to_pair, 1, 11)
        self.landed(self.block(p.next, p.t), 8)
        self.forward(p.next, p.to_pair, 2, 12)

    def fourth(self):
        p = self.p
        self.landed(self.block(p.far, p.t), 10)
        self.forward(p.far, p.to_pair, 3, 13)

    def last(self):
        p = self.p
        for n in (9, 11, 12, 13):
            self.landed(self.block((p.y, p.x), p.other), n)

    def left(self):
        p = self.p
        self.sent(self.block((p.y, p.x), p.t), (0, 1, 2, 3, 7, 8, 9))


class Scatter(Copies):
    COPIES = 11

    def __init__(self, place, part, group, columns, pair_in, near_in, next_in, last_in, sems):
        super().__init__(sems)
        self.p, self.part, self.columns = place, part, columns
        self.pair_in, self.near_in, self.next_in, self.last_in = pair_in, near_in, next_in, last_in
        self.group = group
        self.groups = slice(None) if group is None else slice(group, group + 1)
        self.mine = None if group is None else place.t == group
        self.pairs = None if group is None else place.t != group

    def at(self, g, z, spot, half):
        return self.part.at[g, z, spot[0], spot[1], half, :, self.columns]

    def block(self, spot, half):
        return self.at(self.groups, slice(None), spot, half)

    def add(self, spot, landed):
        p = self.p
        here = (self.groups, slice(None), spot[0], spot[1], p.t, slice(None), self.columns)
        self.part[here] = (self.part[here].astype(F32) + landed.astype(F32)).astype(BF16)

    def first(self):
        p = self.p
        self.start(
            lambda: self.part.at[self.groups, :, :, :, p.other, :, self.columns],
            self.pair_in,
            p.to_pair,
            0,
        )

    def second(self):
        p = self.p
        self.landed(self.pair_in, 0)
        for spot, number in ((p.far, 1), (p.near, 2)):
            self.add(spot, self.pair_in[:, :, spot[0], spot[1]])
            self.start(
                lambda spot=spot: self.block(spot, p.t),
                self.near_in.at[number - 1],
                p.to_near,
                number,
            )
        for spot in (p.next, (p.y, p.x)):
            self.add(spot, self.pair_in[:, :, spot[0], spot[1]])

    def third(self):
        p = self.p
        self.landed(self.near_in.at[0], 1)
        self.add(p.next, self.near_in[0])
        self.start(lambda: self.block(p.next, p.t), self.next_in, p.to_next, 3)
        self.landed(self.near_in.at[1], 2)
        self.add((p.y, p.x), self.near_in[1])

    def fourth(self):
        p = self.p
        self.landed(self.next_in, 3)
        self.add((p.y, p.x), self.next_in[...])
        self.up_the_levels()

    def up_the_levels(self):
        p = self.p
        here = (p.y, p.x)
        for s in range(1, p.depth):
            for core in range(2) if self.group is None else (self.group,):
                self.start(
                    lambda s=s, core=core: self.at(core, p.levels[s], here, p.t),
                    self.last_in.at[2 * (s - 1) + p.t],
                    p.along_z(s, core),
                    4 + 2 * (s - 1) + core,
                    4 + 2 * (s - 1) + p.t,
                )
        self.start(
            lambda: self.at(p.other, p.z, here, p.t),
            self.last_in.at[2 * (p.depth - 1)],
            p.to_pair,
            10,
            only=self.pairs,
        )

    def last(self, target):
        p = self.p

        def write():
            for n in range(7):
                self.landed(self.last_in.at[n], 4 + n)
            mine = self.part[p.t, p.z, p.y, p.x, p.t, :, self.columns].astype(F32)
            rest = self.last_in[2 * (p.depth - 1)].astype(F32)
            for s in range(1, p.depth):
                mine += self.last_in[2 * (s - 1) + p.t].astype(F32)
                rest += self.last_in[2 * (s - 1) + p.other].astype(F32)
            target[p.t] = mine
            target[p.other] = rest

        write() if self.mine is None else pl.when(self.mine)(write)

    def left(self):
        p = self.p
        self.sent(self.pair_in, (0,))
        self.sent(self.next_in, (1, 2, 3))
        for core in range(2) if self.group is None else (self.group,):
            self.sent(self.last_in.at[0], [4 + 2 * s + core for s in range(p.depth - 1)])
        self.sent(self.last_in.at[0], (10,), self.pairs)


class ShortScatter(Scatter):
    def second(self):
        p = self.p
        self.landed(self.pair_in, 0)
        for spot, target, device, number in (
            (p.far, self.near_in.at[0], p.to_far, 1),
            (p.near, self.near_in.at[1], p.to_near, 2),
            (p.next, self.next_in, p.to_next, 3),
        ):
            self.add(spot, self.pair_in[:, :, spot[0], spot[1]])
            self.start(lambda spot=spot: self.block(spot, p.t), target, device, number)
        self.add((p.y, p.x), self.pair_in[:, :, p.y, p.x])

    def fourth(self):
        p = self.p
        for part, number in ((self.next_in, 3), (self.near_in.at[1], 2), (self.near_in.at[0], 1)):
            self.landed(part, number)
            self.add((p.y, p.x), part[...])
        self.up_the_levels()


def scatter_scratch(groups, depth, columns):
    vmem = pltpu.VMEM
    return [
        vmem((groups, depth, 2, 2, 16, columns), BF16),
        vmem((2, groups, depth, 16, columns), BF16),
        vmem((groups, depth, 16, columns), BF16),
        vmem((2 * depth - 1, 16, columns), BF16),
    ]


class Reduce(Copies):
    COPIES = 10

    def __init__(self, place, own, parts, sums, sems):
        super().__init__(sems)
        self.p, self.own, self.parts, self.sums = place, own, parts, sums

    def first(self):
        p = self.p
        self.parts[p.spot] = self.own[...]
        for offset in range(1, 8):
            self.start(
                lambda: self.own, self.parts.at[p.spot], p.level[offset], offset - 1
            )

    def second(self):
        p = self.p
        for n in range(7):
            self.landed(self.own, n)
        total = self.parts[0]
        for spot in range(1, 8):
            total += self.parts[spot]
        self.sums[p.z] = total
        for s in range(1, p.depth):
            self.start(
                lambda: self.sums.at[p.z], self.sums.at[p.z], {"dp": p.chips_z[s]}, 6 + s
            )

    def last(self):
        p = self.p
        for s in range(1, p.depth):
            self.landed(self.own, 6 + s)
        total = self.sums[0]
        for z in range(1, p.depth):
            total += self.sums[z]
        return total

    def left(self):
        self.sent(self.own, range(6 + self.p.depth))


class Woven:
    def __init__(self, place, far, near, own, full, gathers, scatters, gains):
        self.p, self.far, self.near, self.own = place, far, near, own
        wa, wb, ga, gw = full
        own_a, own_b = own
        ranges = [(own_a, wa, 0, 0, 512), (own_a, wa, 0, 512, 1024), (own_a, wa, 1, 0, 1024)]
        ranges += [(own_b, wb, None, *part) for part in UP_PIECES + DOWN_PIECES]
        gather = [
            Gather(place, part, whole, g, slice(first, last), sems)
            for (part, whole, g, first, last), sems in zip(ranges, gathers)
        ]
        self.a0, self.a1, self.b = gather[:2], gather[2], gather[3:]
        ranges = [(gw, None, *part) for part in GRAD_PIECES]
        ranges += [(ga, 0, 0, 1024), (ga, 1, 0, 768), (ga, 1, 768, 1024)]
        kinds = [Scatter] * 4 + [ShortScatter] * 4
        scatter = [
            kind(place, part, g, slice(first, last), *buffers)
            for kind, (part, g, first, last), buffers in zip(kinds, ranges, scatters)
        ]
        self.down_grad, self.up_grad, self.out_grad = scatter[:2], scatter[2:4], scatter[4]
        self.a0_grad, self.a1_grad = scatter[5], scatter[6:]
        self.gains = gains
        self.everything = scatter + [gains]

    def table(self, at, steps):
        for place, calls in steps.items():
            here = None
            for value, wanted in zip(at, place):
                here = (value == wanted) if here is None else here & (value == wanted)

            @pl.when(here)
            def _(calls=calls):
                for call in calls:
                    call()

    def fetch(self, n):
        return pltpu.make_async_copy(self.far[n], self.near[n], self.near["sems"].at[n])

    def put(self, name, n):
        return pltpu.make_async_copy(self.near[name], self.far[name], self.near["sems"].at[n])

    def put_rows(self, which, r):
        rows = pl.ds(pl.multiple_of(r * LAST, LAST), LAST)
        source, target = ((1, "grad_out"), (0, "out"))[which]
        return pltpu.make_async_copy(
            self.near[source].at[rows],
            self.far[target].at[rows],
            self.near["sems"].at[18 + 2 * which + r],
        )

    def before(self):
        self.p.knock()
        for n in range(14, -1, -1):
            self.fetch(n).start()
        for n in range(2, 15):
            self.fetch(n).wait()
        first = self.p.t == 0
        for rows, row in ((2, "seg_row"), (3, "pad_row")):
            rows = self.near[rows]
            self.near[row][...] = jnp.where(first, rows[0:1, :], rows[1:2, :])
        own_a, own_b = self.own
        halves = lambda n: self.near[n][...].astype(BF16).reshape(2, 16, -1)
        for n in range(4):
            own_a[:, :, 256 * n : 256 * n + 256] = halves(8 + n)
        own_b[:, :, 0:256] = halves(12)
        own_b[:, :, 256:1280] = halves(13)
        own_b[:, :, 1280:2304] = halves(14)

    def enter(self):
        self.p.enter()
        self.a0[0].first()
        self.a0[1].first()
        self.fetch(0).wait()
        self.fetch(1).wait()

    def normalised(self):
        pass

    def weights_a(self, g, part):
        one, two = self.a0
        a1, b = self.a1, self.b
        self.table(
            (g,),
            (
                {
                    (0,): (
                        one.second, a1.first, two.second, b[0].first, one.third, two.third,
                        one.fourth, a1.second, one.last,
                    ),
                    (1,): (a1.fourth, a1.last),
                },
                {
                    (0,): (b[1].first, two.fourth, two.last),
                    (1,): (b[3].first,),
                },
            )[part],
        )

    def projected(self, g):
        b = self.b
        self.table((g,), {(0,): (self.a1.third, b[0].second), (1,): (b[0].third,)})

    def mixing(self, g, i):
        b = self.b
        steps = {
            (0, 1): (b[1].second, self.a0[0].left, self.a0[1].left, b[2].first),
            (1, 1): (b[2].second, b[1].third, b[0].fourth),
        }
        self.table((g, i), steps)

    def weights_up(self, part):
        b = self.b
        if part == 0:
            b[3].second()
            b[0].last()
        else:
            b[1].last()

    def feeding(self, part, r):
        b = self.b
        steps = {(0, 1): (b[2].third, b[1].fourth), (1, 1): (b[3].third,)}
        self.table((part, r), steps)

    def fed_up(self):
        self.b[2].fourth()

    def grads_down(self, part):
        if part == 0:
            self.a1.left()
            self.b[0].left()
            self.b[1].left()
        self.down_grad[part].first()

    def weights_down(self, part):
        self.b[2 + part].last()
        self.b[2 + part].left()
        if part == 1:
            self.down_grad[1].second()

    def fed_grad(self, part):
        if part == 0:
            self.b[3].fourth()
            self.down_grad[0].second()

    def grads_up(self, part):
        if part < 2:
            self.up_grad[part].first()
        if part == 1:
            self.up_grad[0].second()
        if part == 2:
            self.out_grad.first()
            self.down_grad[1].third()
            self.up_grad[1].second()

    def feeding_down(self, r):
        self.table((r,), {(1,): (self.down_grad[0].third,)})

    def mixing_back(self, g, i):
        one, two = self.down_grad
        up, rest = self.up_grad
        steps = {
            (0, 1): (one.fourth, self.out_grad.second),
            (1, 1): (self.a0_grad.second, self.down_last, up.fourth, self.out_grad.fourth),
        }
        self.table((g, i), steps)

    def mixed_back(self, g):
        self.table((g,), {(0,): (self.up_grad[0].third, self.down_grad[1].fourth)})

    def grads_a(self, g):
        one, two = self.a1_grad
        self.table((g,), {(0,): (self.a0_grad.first, self.up_grad[1].third), (1,): (one.first,)})

    def grads_last(self):
        self.a1_grad[1].first()

    def finishing(self, which, r):
        one, two = self.a1_grad
        steps = {
            (0, 1): (one.second, self.up_grad[1].fourth),
            (1, 0): (self.a0_grad.fourth,),
            (1, 1): (two.second,),
        }
        self.table((which, r), steps)

    def down_last(self):
        self.down_grad[0].last(self.near["dw"].at[:, :, 1280:1792])

    def finished(self, which, r):
        self.put_rows(which, r).start()

    def gained(self):
        self.gains.first()

    def after(self):
        one, two = self.a1_grad
        da, dw = self.near["da"], self.near["dw"]
        one.fourth()
        self.gains.second()
        two.fourth()
        self.down_grad[1].last(dw.at[:, :, 1792:2304])
        self.up_grad[0].last(dw.at[:, :, 256:768])
        self.up_grad[1].last(dw.at[:, :, 768:1280])
        self.out_grad.last(dw.at[:, :, 0:256])
        self.put("dw", 15).start()
        self.near["total"][...] = self.gains.last()
        self.put("total", 16).start()
        self.a0_grad.last(da)
        one.last(da.at[:, :, 0:768])
        two.last(da.at[:, :, 768:1024])
        self.put("da", 17).start()
        self.everything_left()

    def everything_left(self):
        for copies in self.everything:
            copies.left()
        for r in range(2):
            self.put_rows(0, r).wait()
            self.put_rows(1, r).wait()
        self.put("dw", 15).wait()
        self.put("total", 16).wait()
        self.put("da", 17).wait()


def woven_kernel(length, depth, *refs):
    refs = list(refs)
    take = lambda n: [refs.pop(0) for _ in range(n)]
    far = dict(enumerate(take(15)))
    far.update(zip(("out", "grad_out", "da", "dw", "total"), take(5)))
    near = dict(enumerate(take(15)))
    near.update(zip(("da", "dw", "total", "seg_row", "pad_row", "sems"), take(6)))
    own, full = take(2), take(4)
    small, parts, sums = take(3)
    gain_sems = take(2)
    gathers = [take(2) for _ in range(7)]
    scatters = [take(4) for _ in range(8)]
    scatters = [buffers + [sems] for buffers, sems in zip(scatters, gathers + [take(2)])]
    place = Place(depth)
    gains = Reduce(place, small, parts, sums, gain_sems)
    comm = Woven(place, far, near, own, full, gathers, scatters, gains)
    layer_body(
        length, comm, near["seg_row"], near["pad_row"], *[near[n] for n in range(4, 8)], *full,
        small, near[0], near[1], *refs,
    )


def write_kernel(out_in, grad_in, da, dw, small, *refs):
    (
        out, grad_out, mixer_gain, query, key, value, slot, out_t, feed_gain, up, up_bias, down_t,
        down_bias,
    ) = refs
    out[...] = out_in[...]
    grad_out[...] = grad_in[...]

    @pl.when(pl.program_id(0) == 0)
    def _():
        rows = lambda part: part.reshape(-1, part.shape[-1])
        query[...] = rows(da[:, :, 0:256])
        key[...] = rows(da[:, :, 256:512])
        value[...] = rows(da[:, :, 512:768])
        slot[...] = rows(da[:, :, 768:1024])
        out_t[...] = rows(dw[:, :, 0:256])
        up[...] = rows(dw[:, :, 256:1280])
        down_t[...] = rows(dw[:, :, 1280:2304])
        feed_gain[...] = small[0:1, :]
        mixer_gain[...] = small[1:2, :]
        down_bias[...] = small[2:3, :]
        for row in range(4):
            up_bias[:, row * 512 : (row + 1) * 512] = small[4 + row : 5 + row, :]


def write(out, grad_out, da, dw, small):
    shape = jax.ShapeDtypeStruct
    length, width = out.shape
    square, wide = shape((32, 256), F32), shape((32, 1024), F32)
    row, big = shape((1, width), F32), shape(out.shape, BF16)
    outputs = (big, big, row) + (square,) * 5 + (row, wide, shape((1, 4 * width), F32), wide, row)
    half = pl.BlockSpec((length // 2, width), lambda i: (i, 0))
    whole = lambda array: pl.BlockSpec(array.shape, lambda i: (0,) * len(array.shape))
    return pl.pallas_call(
        write_kernel,
        grid=(2,),
        out_shape=outputs,
        in_specs=[half, half, whole(da), whole(dw), whole(small)],
        out_specs=(half, half) + tuple(whole(array) for array in outputs[2:]),
        name="write",
    )(out, grad_out, da, dw, small)


def woven(depth, *inputs):
    length, width = inputs[0].shape
    shape = jax.ShapeDtypeStruct
    far = pl.BlockSpec(memory_space=pl.ANY)
    vmem = pltpu.VMEM
    dma = pltpu.SemaphoreType.DMA
    full = lambda columns: vmem((2, depth, 2, 2, 2, 16, columns), BF16)
    da, dw, total = shape((2, 16, 1024), F32), shape((2, 16, 2304), F32), shape((8, width), F32)
    scatters = []
    for groups, columns in [(2, 512)] * 4 + [(2, 256), (1, 1024), (1, 768), (1, 256)]:
        scatters += scatter_scratch(groups, depth, columns)
    return pl.pallas_call(
        functools.partial(woven_kernel, length, depth),
        out_shape=(shape((length, width), BF16), shape((length, width), BF16), da, dw, total),
        in_specs=[far] * 15,
        out_specs=(far,) * 5,
        scratch_shapes=[vmem(array.shape, array.dtype) for array in inputs]
        + [vmem(array.shape, array.dtype) for array in (da, dw, total)]
        + [
            vmem((1, length), jnp.int32),
            vmem((1, length), jnp.int32),
            dma((22,)),
            vmem((2, 16, 1024), BF16),
            vmem((2, 16, 2304), BF16),
            full(1024),
            full(2304),
            full(1024),
            full(2304),
            vmem((8, width), F32),
            vmem((8, 8, width), F32),
            vmem((depth, 8, width), F32),
            dma((Reduce.COPIES,)),
            dma((Reduce.COPIES,)),
        ]
        + [dma((Gather.SENDS,)), dma((Gather.COPIES,))] * 7
        + scatters
        + [dma((Scatter.COPIES,))] * 2
        + layer_scratch(length, width),
        compiler_params=pltpu.CompilerParams(
            collective_id=0, has_side_effects=True, vmem_limit_bytes=63 * 1024 * 1024
        ),
        name="woven",
    )(*inputs)


def per_device(
    direct,
    tokens,
    segment_ids,
    padding,
    mixer_gain,
    query_weight,
    key_weight,
    value_weight,
    slot_weight,
    out_weight,
    feed_gain,
    up_weight,
    up_bias,
    down_weight,
    down_bias,
    cotangent,
):
    gains = (mixer_gain[None], feed_gain[None])
    biases = (up_bias[None], down_bias[None])
    if direct:
        owns = (
            query_weight, key_weight, value_weight, slot_weight, out_weight.T, up_weight,
            down_weight.T,
        )
        depth = lax.axis_size("dp") // 4
        results = write(
            *woven(depth, tokens, cotangent, segment_ids, padding, *gains, *biases, *owns)
        )
        (
            out, grad_out, gain_one, query, key, value, slot, out_t, gain_two, up, bias_one, down_t,
            bias_two,
        ) = results
        return (
            out, grad_out, gain_one[0], query, key, value, slot, out_t.T, gain_two[0], up,
            bias_one[0], down_t.T, bias_two[0],
        )
    own_a = jnp.concatenate([query_weight, key_weight, value_weight, slot_weight], 1)
    own_b = jnp.concatenate([out_weight.T, up_weight, down_weight.T], 1)
    wa, wb = (
        lax.all_gather(lax.all_gather(own.astype(BF16), "dp", axis=0, tiled=True), "tensor")
        for own in (own_a, own_b)
    )
    half = lax.axis_index("tensor")
    pick = lambda rows: lax.dynamic_slice_in_dim(rows, half, 1, 0)
    out, grad_out, ga, gw, small = layer(
        tokens, cotangent, pick(segment_ids), pick(padding), *gains, *biases, wa, wb
    )
    da, dw = (
        lax.psum_scatter(
            lax.psum_scatter(part.astype(F32), "tensor", scatter_dimension=0),
            "dp",
            scatter_dimension=0,
            tiled=True,
        )
        for part in (ga, gw)
    )
    small = lax.psum(small, ("dp", "tensor"))
    return (
        out,
        grad_out,
        small[1],
        da[:, 0:256],
        da[:, 256:512],
        da[:, 512:768],
        da[:, 768:1024],
        dw[:, 0:256].T,
        small[0],
        dw[:, 256:1280],
        small[4:8].reshape(-1),
        dw[:, 1280:2304].T,
        small[2],
    )


def solution(mesh):
    in_specs = (
        P(("dp", "tensor"), None),
        P("dp", None),
        P("dp", None),
        P(),
        P("dp", "tensor"),
        P("dp", "tensor"),
        P("dp", "tensor"),
        P("dp", "tensor"),
        P("tensor", "dp"),
        P(),
        P("dp", "tensor"),
        P(),
        P("tensor", "dp"),
        P(),
        P(("dp", "tensor"), None),
    )
    out_specs = (
        P(("dp", "tensor"), None),
        P(("dp", "tensor"), None),
        P(),
        P("dp", "tensor"),
        P("dp", "tensor"),
        P("dp", "tensor"),
        P("dp", "tensor"),
        P("tensor", "dp"),
        P(),
        P("dp", "tensor"),
        P(),
        P("tensor", "dp"),
        P(),
    )
    direct = mesh.shape["dp"] == 16 and mesh.shape["tensor"] == 2
    return jax.shard_map(
        functools.partial(per_device, direct),
        mesh=mesh,
        in_specs=in_specs,
        out_specs=out_specs,
        check_vma=False,
    )
```

```python
import functools
import math

import jax
import jax.numpy as jnp
from jax import lax
from jax.experimental import pallas as pl
from jax.experimental.pallas import tpu as pltpu
from jax.sharding import PartitionSpec as P

HEAD_DIM = 64
SLOTS = 64
CHUNK = 128
UNROLL = 4
GROUP = 256
TILE = 512
WIDE = 512
LAST = 512

F32 = jnp.float32
BF16 = jnp.bfloat16
MESH = pl.DeviceIdType.MESH


def dot(left, right):
    return lax.dot_general(left, right, (((1,), (0,)), ((), ())), preferred_element_type=F32)


def dot_rt(left, right):
    return lax.dot_general(left, right, (((1,), (1,)), ((), ())), preferred_element_type=F32)


def dot_lt(left, right):
    return lax.dot_general(left, right, (((0,), (0,)), ((), ())), preferred_element_type=F32)


def twice(block):
    return jnp.concatenate([block, block], axis=1)


def standardise(rows):
    centred = rows - jnp.mean(rows, axis=-1, keepdims=True)
    scale = lax.rsqrt(jnp.mean(centred * centred, axis=-1, keepdims=True) + 1e-05)
    return centred * scale, scale


def head_stack(block):
    lane = lax.broadcasted_iota(jnp.int32, block.shape, 1) // HEAD_DIM
    zero = jnp.zeros_like(block)
    return jnp.concatenate([jnp.where(lane == h, block, zero) for h in range(4)], axis=0)


def diagonal(product):
    parts = [product[h * HEAD_DIM : (h + 1) * HEAD_DIM, :] for h in range(4)]
    lane = lax.broadcasted_iota(jnp.int32, parts[0].shape, 1) // HEAD_DIM
    kept = parts[3]
    for h in range(3):
        kept = jnp.where(lane == h, parts[h], kept)
    return kept


def over_heads(block, reduce, rest):
    halves = []
    lane = lax.broadcasted_iota(jnp.int32, (block.shape[0], 128), 1) < HEAD_DIM
    for j in range(block.shape[1] // 128):
        part = block[:, j * 128 : (j + 1) * 128]
        first = reduce(jnp.where(lane, part, rest), axis=1, keepdims=True)
        second = reduce(jnp.where(lane, rest, part), axis=1, keepdims=True)
        halves.append(jnp.where(lane, first, second))
    return jnp.concatenate(halves, axis=1)


def head_max(block):
    return over_heads(block, jnp.max, -jnp.inf)


def head_sum(block):
    return over_heads(block, jnp.sum, 0.0)


def head_pairs(product, allowed):
    parts = [product[h * CHUNK : (h + 1) * CHUNK, :] * allowed for h in range(4)]
    return jnp.concatenate(parts, axis=1).astype(BF16)


def flip_pairs(pairs):
    parts = [pairs[:, h * CHUNK : (h + 1) * CHUNK].T for h in range(4)]
    return jnp.concatenate(parts, axis=1)


def beside(*blocks):
    return jnp.concatenate(blocks, axis=1)


def above(*blocks):
    return jnp.concatenate(blocks, axis=0)


def flat(block):
    return block.reshape(-1, block.shape[-1])


def rows_to_columns(seg_row, pad_row, segc, keepc, length):
    segc[pl.ds(0, 8), :] = jnp.full((8, 128), -1.0, F32)
    segc[pl.ds(8 + length, 8), :] = jnp.full((8, 128), -2.0, F32)
    for c in range(length // CHUNK):
        here = slice(c * CHUNK, (c + 1) * CHUNK)
        seg = jnp.broadcast_to(seg_row[:, here].astype(F32), (CHUNK, CHUNK))
        pad = jnp.broadcast_to(pad_row[:, here].astype(F32), (CHUNK, CHUNK))
        segc[pl.ds(8 + c * CHUNK, CHUNK), :] = seg.T
        keepc[pl.ds(c * CHUNK, CHUNK), :] = 1.0 - pad.T


def normalise(r, tok, cot, gain, n1, small):
    rows = pl.ds(pl.multiple_of(r * TILE, TILE), TILE)
    xhat, _ = standardise(tok[rows, :].astype(F32))
    n1[rows, :] = (xhat * gain[...]).astype(BF16)
    small[2:3, :] += jnp.sum(cot[rows, :].astype(F32), axis=0, keepdims=True)


def project_qk(g, r, wa, n1, q, k):
    rows = pl.ds(pl.multiple_of(r * WIDE, WIDE), WIDE)
    out = dot(n1[rows, :], flat(wa[g, ..., 0:512]))
    q[g, rows, :] = out[:, 0:256].astype(BF16)
    k[g, rows, :] = out[:, 256:512].astype(BF16)


def project_vw(g, r, wa, keepc, n1, v, w):
    rows = pl.ds(pl.multiple_of(r * WIDE, WIDE), WIDE)
    out = dot(n1[rows, :], flat(wa[g, ..., 512:1024]))
    v[g, rows, :] = out[:, 0:256].astype(BF16)
    w[g, rows, :] = (jnp.exp(out[:, 256:512]) * twice(keepc[rows, :])).astype(BF16)


def chunk_masks(c, segc):
    base = pl.multiple_of(c * CHUNK, CHUNK)
    seg = segc[pl.ds(base + 8, CHUNK), :]
    across = seg.T
    row = lax.broadcasted_iota(jnp.int32, (CHUNK, CHUNK), 0)
    column = lax.broadcasted_iota(jnp.int32, (CHUNK, CHUNK), 1)
    same = seg == across
    causal = jnp.where(same & (column <= row), 1.0, 0.0)
    before = segc[pl.ds(base + 7, 1), :]
    first = segc[pl.ds(base + 8, 1), :]
    last = segc[pl.ds(base + 7 + CHUNK, 1), :]
    after = segc[pl.ds(base + 8 + CHUNK, 1), :]
    one = lambda test: jnp.where(test, 1.0, 0.0)
    return causal, dict(
        from_before=one(seg == before),
        to_after=one(seg == last),
        from_after=one(seg == after),
        to_before=one(seg == first),
        carry_on=one(before == last),
        carry_back=one(after == first),
    )


def mix_forward(
    g, i, segc, keepc, q, k, v, w, probs, inv, score, mixed, kw, wv, zsum, kw_all, wv_all, pt_all,
    mt_all,
):
    run = range(UNROLL)
    chunks = [UNROLL * i + n for n in run]
    rows = [pl.ds(pl.multiple_of(c * CHUNK, CHUNK), CHUNK) for c in chunks]
    masks = [chunk_masks(c, segc) for c in chunks]
    keep = [twice(keepc[r, :]) for r in rows]
    qc, kc, vc, wc = ([ref[g, r, :] for r in rows] for ref in (q, k, v, w))
    state_k, state_v, state_z = [kw[...]], [wv[...]], [zsum[0:1, :]]
    causal = [mask for mask, _ in masks]
    edge = [edges for _, edges in masks]
    come = [twice(edge[n]["from_before"]) for n in run]
    come_low = [come[n].astype(BF16) for n in run]
    pairs = [head_pairs(dot_rt(head_stack(qc[n]), kc[n]), causal[n]) for n in run]
    for n in run:
        carry = twice(edge[n]["carry_on"])
        wg = wc[n] * twice(edge[n]["to_after"]).astype(BF16)
        state_k.append(state_k[n] * carry + diagonal(dot_lt(kc[n], wg)))
        state_v.append(state_v[n] * carry + diagonal(dot_lt(wg, vc[n])))
        state_z.append(state_z[n] * carry + jnp.sum(wg.astype(F32), axis=0, keepdims=True))
    kw_low = [head_stack(state_k[n].astype(BF16)) for n in run]
    wv_low = [head_stack(state_v[n].astype(BF16)) for n in run]
    inverse = [
        1.0 / (dot(causal[n].astype(BF16), wc[n]) + come[n] * state_z[n] + (1.0 - keep[n]))
        for n in run
    ]
    scores = [
        dot(beside(pairs[n], qc[n] * come_low[n]), above(head_stack(wc[n]), kw_low[n]))
        * (inverse[n] * (HEAD_DIM**-0.5))
        for n in run
    ]
    powers = [jnp.exp(scores[n] - head_max(scores[n])) for n in run]
    chances = [powers[n] / head_sum(powers[n]) for n in run]
    ratio = [(chances[n] * inverse[n]).astype(BF16) for n in run]
    mixing = [head_pairs(dot_rt(head_stack(ratio[n]), wc[n]), causal[n]) for n in run]
    out = [
        dot(beside(mixing[n], ratio[n] * come_low[n]), above(head_stack(vc[n]), wv_low[n]))
        for n in run
    ]
    for n in run:
        r = rows[n]
        kw_all[g, chunks[n]] = diagonal(kw_low[n].T)
        wv_all[g, chunks[n]] = diagonal(wv_low[n].T)
        pt_all[g, r, :] = flip_pairs(pairs[n])
        mt_all[g, r, :] = flip_pairs(mixing[n])
        inv[g, r, :] = inverse[n]
        score[g, r, :] = scores[n].astype(BF16)
        probs[g, r, :] = chances[n]
        mixed[g, r, :] = (out[n] * keep[n]).astype(BF16)
    kw[...] = state_k[-1]
    wv[...] = state_v[-1]
    zsum[...] = jnp.broadcast_to(state_z[-1], zsum.shape)


def mix_backward(
    g, i, segc, keepc, q, k, v, w, probs, inv, score, gm, rg, uq, zgrad, kw_all, wv_all, pt_all,
    mt_all, gy,
):
    run = range(UNROLL)
    chunks = [UNROLL * i + UNROLL - 1 - n for n in run]
    rows = [pl.ds(pl.multiple_of(c * CHUNK, CHUNK), CHUNK) for c in chunks]
    masks = [chunk_masks(c, segc) for c in chunks]
    qc, kc, vc, wc, grad, chances, inverse, scores, pairs_t, mixing_t = (
        [ref[g, r, :] for r in rows]
        for ref in (q, k, v, w, gm, probs, inv, score, pt_all, mt_all)
    )
    kw_t, wv_t = ([head_stack(ref[g, c]) for c in chunks] for ref in (kw_all, wv_all))
    state_v, state_k, state_z = [rg[...]], [uq[...]], [zgrad[0:1, :]]
    causal = [mask for mask, _ in masks]
    edge = [edges for _, edges in masks]
    come_low = [twice(edge[n]["from_before"]).astype(BF16) for n in run]
    late = [twice(edge[n]["from_after"]) for n in run]
    late_low = [late[n].astype(BF16) for n in run]
    back = [twice(edge[n]["to_before"]) for n in run]
    back_low = [back[n].astype(BF16) for n in run]
    carry = [twice(edge[n]["carry_back"]) for n in run]
    grads = [head_stack(grad[n]) for n in run]
    d_mixing = [head_pairs(dot_rt(grads[n], vc[n]), causal[n]) for n in run]
    d_chance = [
        dot(beside(d_mixing[n], grad[n] * come_low[n]), above(head_stack(wc[n]), wv_t[n]))
        * inverse[n]
        for n in run
    ]
    ratio = [(chances[n] * inverse[n]).astype(BF16) for n in run]
    ratios = [head_stack(ratio[n]) for n in run]
    for n in run:
        added = diagonal(dot_lt(ratio[n] * back_low[n], grad[n]))
        state_v.append(state_v[n] * carry[n] + added)
    rg_low = [head_stack(state_v[n].astype(BF16)) for n in run]
    w_late = [wc[n] * late_low[n] for n in run]
    gv = [dot(beside(mixing_t[n], w_late[n]), above(grads[n], rg_low[n])) for n in run]
    weighted = [d_chance[n] * chances[n] for n in run]
    d_score = [weighted[n] - chances[n] * head_sum(weighted[n]) for n in run]
    d_pw = [(d_score[n] * inverse[n] * (HEAD_DIM**-0.5)).astype(BF16) for n in run]
    d_total = [
        (weighted[n] + d_score[n] * scores[n].astype(F32)) * inverse[n] for n in run
    ]
    d_pws = [head_stack(d_pw[n]) for n in run]
    d_pairs = [head_pairs(dot_rt(d_pws[n], wc[n]), causal[n]) for n in run]
    for n in run:
        added = diagonal(dot_lt(d_pw[n] * back_low[n], qc[n]))
        state_k.append(state_k[n] * carry[n] + added)
        added = jnp.sum(d_total[n] * back[n], axis=0, keepdims=True)
        state_z.append(state_z[n] * carry[n] + added)
    uq_low = [head_stack(state_k[n].astype(BF16)) for n in run]
    dw = []
    for n in run:
        z_high = d_total[n].astype(BF16)
        z_low = (d_total[n] - z_high.astype(F32)).astype(BF16)
        anti = -causal[n].T.astype(BF16)
        left = beside(
            flip_pairs(d_mixing[n]), pairs_t[n], vc[n] * late_low[n], kc[n] * late_low[n], anti, anti
        )
        right = above(ratios[n], d_pws[n], rg_low[n].T, uq_low[n].T, z_high, z_low)
        dw.append(dot(left, right) - late[n] * state_z[n])
    gq = [
        dot(beside(d_pairs[n], d_pw[n] * come_low[n]), above(head_stack(kc[n]), kw_t[n]))
        for n in run
    ]
    gk = [
        dot(beside(flip_pairs(d_pairs[n]), w_late[n]), above(head_stack(qc[n]), uq_low[n]))
        for n in run
    ]
    for n in run:
        gy[g, rows[n], 512:768] = gv[n].astype(BF16)
        gy[g, rows[n], 768:1024] = (dw[n] * wc[n].astype(F32)).astype(BF16)
        gy[g, rows[n], 0:256] = gq[n].astype(BF16)
        gy[g, rows[n], 256:512] = gk[n].astype(BF16)
    rg[...] = state_v[-1]
    uq[...] = state_k[-1]
    zgrad[...] = jnp.broadcast_to(state_z[-1], zgrad.shape)


def units(j):
    return j // 2 % 2, (j // 4 * 2 + j % 2) * 256


def feed_in(r, tok, gain, wb, mixed, n2, gh, scales):
    rows = pl.ds(pl.multiple_of(r * TILE, TILE), TILE)
    hidden = tok[rows, :].astype(F32)
    for g in range(2):
        hidden += dot_rt(mixed[g, rows, :], flat(wb[g, ..., 0:256]))
    hat, scale = standardise(hidden)
    gh[rows, :] = hat
    scales[rows, :] = scale
    n2[rows, :] = (hat * gain[...]).astype(BF16)


def feed_up(part, r, up_bias, wb, n2, act, lin):
    rows = pl.ds(pl.multiple_of(r * TILE, TILE), TILE)
    normed = n2[rows, :]
    k0 = 0.7978845608
    k1 = k0 * 0.044715

    def linear_of(j):
        g, column = units(j)
        up = flat(wb[g, ..., 256 + column : 512 + column])
        bias = up_bias[:, g * 1024 + column : g * 1024 + column + 256]
        return dot(normed, up) + bias

    after = linear_of(4 * part)
    for j in range(4 * part, 4 * part + 4):
        linear = after
        if j < 4 * part + 3:
            after = linear_of(j + 1)
        square = linear * linear
        gate = 0.5 * jnp.tanh(linear * (square * k1 + k0)) + 0.5
        active = linear * gate
        slope = gate + active * (1.0 - gate) * (square * (6.0 * k1) + 2.0 * k0)
        g, column = units(j)
        act[g, rows, column : column + 256] = active.astype(BF16)
        lin[g, rows, column : column + 256] = slope.astype(BF16)


def feed_grad(part, r, cot, wb, lin, small):
    rows = pl.ds(pl.multiple_of(r * TILE, TILE), TILE)
    grad = cot[rows, :]

    def grad_of(j):
        g, column = units(j)
        down = flat(wb[g, ..., 1280 + column : 1536 + column])
        return dot(grad, down) * lin[g, rows, column : column + 256].astype(F32)

    after = grad_of(4 * part)
    for j in range(4 * part, 4 * part + 4):
        grad_low = after.astype(BF16)
        if j < 4 * part + 3:
            after = grad_of(j + 1)
        g, column = units(j)
        lin[g, rows, column : column + 256] = grad_low
        row, here = 4 + 2 * g + column // 512, column % 512
        small[row : row + 1, here : here + 256] += jnp.sum(
            grad_low.astype(F32), axis=0, keepdims=True
        )


def feed_back(r, cot, gain, wb, keepc, lin, gh, scales, gm, small):
    half = TILE // 2
    parts = [pl.ds(pl.multiple_of(r * TILE + n * half, half), half) for n in range(2)]
    backs = [
        dot_rt(lin[0, part, :], flat(wb[0, ..., 256:1280]))
        + dot_rt(lin[1, part, :], flat(wb[1, ..., 256:1280]))
        for part in parts
    ]
    hats = [gh[part, :] for part in parts]
    keeps = [twice(keepc[part, :]) for part in parts]
    hidden = []
    for part, back, hat in zip(parts, backs, hats):
        scaled = back * gain[...]
        inner = scaled - jnp.mean(scaled, axis=-1, keepdims=True)
        inner -= hat * jnp.mean(scaled * hat, axis=-1, keepdims=True)
        hidden.append(cot[part, :].astype(F32) + scales[part, :] * inner)
    mixed_grads = [
        [(dot(rows.astype(BF16), flat(wb[g, ..., 0:256])) * keep).astype(BF16) for g in range(2)]
        for rows, keep in zip(hidden, keeps)
    ]
    for n, part in enumerate(parts):
        gh[part, :] = hidden[n]
        for g in range(2):
            gm[g, part, :] = mixed_grads[n][g]
        small[0:1, :] += jnp.sum(backs[n] * hats[n], axis=0, keepdims=True)


def emit(r, tok, down_bias, wb, mixed, act):
    rows = pl.ds(pl.multiple_of(r * LAST, LAST), LAST)
    total = tok[rows, :].astype(F32)
    for g in range(2):
        total += dot_rt(mixed[g, rows, :], flat(wb[g, ..., 0:256]))
    total += down_bias[...]
    for g in range(2):
        total += dot_rt(act[g, rows, :], flat(wb[g, ..., 1280:2304]))
    tok[rows, :] = total.astype(BF16)


def transpose_into(source, target, length):
    for r in range(length // 256):
        here = slice(r * 256, (r + 1) * 256)
        turned = source[here, :].astype(BF16).T
        target[..., here] = turned.reshape(target.shape[:-1] + (256,))


def weight_grads(left_t, target, jobs):
    shape = target.shape[1:-1]

    def product(job):
        _, right, at, _, columns = job
        return dot(flat(left_t[...]), right[:, at : at + columns]).astype(BF16)

    after = product(jobs[0])
    for n, (g, _, _, to, columns) in enumerate(jobs):
        here = after
        if n + 1 < len(jobs):
            after = product(jobs[n + 1])
        target[g, ..., to : to + columns] = here.reshape(shape + (columns,))


def finish(r, tok, cot, gain, wa, gy, gh, small):
    rows = pl.ds(pl.multiple_of(r * LAST, LAST), LAST)
    hat, scale = standardise(tok[rows, :].astype(F32))
    back = dot_rt(gy[0, rows, :], flat(wa[0])) + dot_rt(gy[1, rows, :], flat(wa[1]))
    scaled = back * gain[...]
    inner = scaled - jnp.mean(scaled, axis=-1, keepdims=True)
    inner -= hat * jnp.mean(scaled * hat, axis=-1, keepdims=True)
    cot[rows, :] = (gh[rows, :] + scale * inner).astype(BF16)
    small[1:2, :] += jnp.sum(back * hat, axis=0, keepdims=True)


class Quiet:
    def nothing(self, *at):
        pass

    before = enter = normalised = weights_a = projected = mixing = nothing
    weights_up = feeding = fed_up = weights_down = grads_down = fed_grad = feeding_down = grads_up = nothing
    mixing_back = mixed_back = grads_a = finishing = finished = gained = grads_last = after = nothing


LAYER_INPUTS = 6
UP_PIECES = [(0, 768), (768, 1280)]
DOWN_PIECES = [(1280, 1792), (1792, 2304)]
GRAD_PIECES = DOWN_PIECES + [(256, 768), (768, 1280), (0, 256)]


def layer_body(
    length,
    comm,
    seg_row,
    pad_row,
    gain_one,
    gain_two,
    up_bias,
    down_bias,
    wa,
    wb,
    ga,
    gw,
    small,
    tok,
    cot,
    segc,
    keepc,
    n1,
    q,
    k,
    v,
    w,
    probs,
    inv,
    score,
    mixed,
    state_k,
    state_v,
    state_z,
    kw_all,
    wv_all,
    pt_all,
    mt_all,
    act,
    lin,
    gh,
    scales,
    gm,
    flip,
    n1_flip,
):
    runs, tiles = length // (UNROLL * CHUNK), length // TILE

    def clear():
        state_k[...] = jnp.zeros_like(state_k)
        state_v[...] = jnp.zeros_like(state_v)
        state_z[...] = jnp.zeros_like(state_z)

    comm.before()
    small[...] = jnp.zeros_like(small)
    rows_to_columns(seg_row, pad_row, segc, keepc, length)
    comm.enter()

    @pl.loop(0, tiles)
    def _(r):
        normalise(r, tok, cot, gain_one, n1, small)

    comm.normalised()
    transpose_into(cot, flip, length)
    transpose_into(n1, n1_flip, length)

    @pl.loop(0, 2)
    def _(g):
        comm.weights_a(g, 0)
        clear()

        @pl.loop(0, length // WIDE)
        def _(r):
            project_qk(g, r, wa, n1, q, k)

        comm.weights_a(g, 1)

        @pl.loop(0, length // WIDE)
        def _(r):
            project_vw(g, r, wa, keepc, n1, v, w)

        comm.projected(g)

        @pl.loop(0, runs)
        def _(i):
            comm.mixing(g, i)
            mix_forward(
                g, i, segc, keepc, q, k, v, w, probs, inv, score, mixed, state_k, state_v, state_z,
                kw_all, wv_all, pt_all, mt_all,
            )

    comm.weights_up(0)

    @pl.loop(0, tiles)
    def _(r):
        comm.feeding(0, r)
        feed_in(r, tok, gain_two, wb, mixed, n1, gh, scales)
        feed_up(0, r, up_bias, wb, n1, act, lin)

    transpose_into(n1, ga.at[0], length)
    comm.weights_up(1)

    @pl.loop(0, tiles)
    def _(r):
        comm.feeding(1, r)
        feed_up(1, r, up_bias, wb, n1, act, lin)

    comm.fed_up()
    for part in range(2):
        at = part * 512
        weight_grads(flip, gw, [(g, act.at[g], at, 1280 + at, 512) for g in range(2)])
        comm.grads_down(part)

    for part in range(2):
        comm.weights_down(part)

        @pl.loop(0, tiles)
        def _(r):
            feed_grad(part, r, cot, wb, lin, small)

        comm.fed_grad(part)
        at = part * 512
        weight_grads(ga.at[0], gw, [(g, lin.at[g], at, 256 + at, 512) for g in range(2)])
        comm.grads_up(part)

    @pl.loop(0, tiles)
    def _(r):
        comm.feeding_down(r)
        feed_back(r, cot, gain_two, wb, keepc, lin, gh, scales, gm, small)

    transpose_into(gh, flip, length)
    weight_grads(flip, gw, [(g, mixed.at[g], 0, 0, GROUP) for g in range(2)])
    comm.grads_up(2)

    @pl.loop(0, 2)
    def _(g):
        clear()

        @pl.loop(0, runs)
        def _(i):
            comm.mixing_back(g, i)
            mix_backward(
                g, runs - 1 - i, segc, keepc, q, k, v, w, probs, inv, score, gm, state_v, state_k,
                state_z, kw_all, wv_all, pt_all, mt_all, lin,
            )

        comm.mixed_back(g)

        weight_grads(n1_flip, ga, [(g, lin.at[g], 0, 0, 512), (g, lin.at[g], 512, 512, 256)])

        @pl.when(g == 0)
        def _():
            weight_grads(n1_flip, ga, [(0, lin.at[0], 768, 768, 256)])

        comm.grads_a(g)

    @pl.loop(0, length // LAST)
    def _(r):
        comm.finishing(0, r)
        finish(r, tok, cot, gain_one, wa, lin, gh, small)
        comm.finished(0, r)

    comm.gained()
    weight_grads(n1_flip, ga, [(1, lin.at[1], 768, 768, 256)])
    comm.grads_last()

    @pl.loop(0, length // LAST)
    def _(r):
        comm.finishing(1, r)
        emit(r, tok, down_bias, wb, mixed, act)
        comm.finished(1, r)

    comm.after()


def layer_scratch(length, width):
    vmem = pltpu.VMEM
    chunks = length // CHUNK
    return [
        vmem((length + 16, 128), F32),
        vmem((length, 128), F32),
        vmem((length, width), BF16),
        vmem((2, length, GROUP), BF16),
        vmem((2, length, GROUP), BF16),
        vmem((2, length, GROUP), BF16),
        vmem((2, length, GROUP), BF16),
        vmem((2, length, GROUP), F32),
        vmem((2, length, GROUP), F32),
        vmem((2, length, GROUP), BF16),
        vmem((2, length, GROUP), BF16),
        vmem((HEAD_DIM, GROUP), F32),
        vmem((HEAD_DIM, GROUP), F32),
        vmem((8, GROUP), F32),
        vmem((2, chunks, HEAD_DIM, GROUP), BF16),
        vmem((2, chunks, HEAD_DIM, GROUP), BF16),
        vmem((2, length, 4 * CHUNK), BF16),
        vmem((2, length, 4 * CHUNK), BF16),
        vmem((2, length, 1024), BF16),
        vmem((2, length, 1024), BF16),
        vmem((length, width), F32),
        vmem((length, 1), F32),
        vmem((2, length, GROUP), BF16),
        vmem((width, length), BF16),
        vmem((width, length), BF16),
    ]


def layer_kernel(length, tokens, cotangent, *refs):
    inputs, (out, grad_out), rest = refs[: LAYER_INPUTS + 2], refs[8:10], refs[10:]
    out[...] = tokens[...]
    grad_out[...] = cotangent[...]
    ga, gw, small = rest[:3]
    layer_body(length, Quiet(), *inputs, ga, gw, small, out, grad_out, *rest[3:])


def layer(tokens, cotangent, seg_row, pad_row, gain_one, gain_two, up_bias, down_bias, wa, wb):
    length, width = tokens.shape
    shape = jax.ShapeDtypeStruct
    cut = lambda full: full.reshape(2, -1, 2, 2, 2, 16, full.shape[-1])
    wa, wb = cut(wa), cut(wb)
    space = pl.BlockSpec(memory_space=pltpu.VMEM)
    out, grad_out, ga, gw, small = pl.pallas_call(
        functools.partial(layer_kernel, length),
        out_shape=(
            shape((length, width), BF16),
            shape((length, width), BF16),
            shape(wa.shape, BF16),
            shape(wb.shape, BF16),
            shape((8, width), F32),
        ),
        in_specs=[space] * 10,
        out_specs=tuple([space] * 5),
        scratch_shapes=layer_scratch(length, width),
        compiler_params=pltpu.CompilerParams(vmem_limit_bytes=62 * 1024 * 1024),
        name="layer",
    )(tokens, cotangent, seg_row, pad_row, gain_one, gain_two, up_bias, down_bias, wa, wb)
    whole = lambda full: full.reshape(2, width, full.shape[-1])
    return out, grad_out, whole(ga), whole(gw), small


class Place:
    def __init__(self, depth):
        index = lax.axis_index("dp")
        t = lax.axis_index("tensor")
        x, y, z = lax.rem(index, 2), lax.rem(index // 2, 2), index // 4
        self.depth = depth
        self.x, self.y, self.z, self.t, self.other = x, y, z, t, 1 - t
        self.near = (y + t * (1 - 2 * y), x + (1 - t) * (1 - 2 * x))
        self.next = (y + (1 - t) * (1 - 2 * y), x + t * (1 - 2 * x))
        self.far = (1 - y, 1 - x)
        chip = lambda z, y, x: (z * 2 + y) * 2 + x
        self.levels = [lax.rem(z + s, depth) for s in range(depth)]
        self.chips_z = [chip(level, y, x) for level in self.levels]
        self.to_near = {"dp": chip(z, *self.near)}
        self.to_next = {"dp": chip(z, *self.next)}
        self.to_far = {"dp": chip(z, *self.far)}
        self.to_pair = {"tensor": self.other}
        self.spot = (y * 2 + x) * 2 + t
        flip = lambda value, bit: value + bit * (1 - 2 * value)
        self.level = [
            {
                "dp": chip(z, flip(y, offset // 4), flip(x, offset // 2 % 2)),
                "tensor": flip(t, offset % 2),
            }
            for offset in range(8)
        ]

    def along_z(self, step, core):
        return {"dp": self.chips_z[step], "tensor": core}

    def friends(self):
        along = [self.along_z(s, core) for s in range(1, self.depth) for core in range(2)]
        return self.level[1:] + along

    def knock(self):
        barrier = pltpu.get_barrier_semaphore()
        for friend in self.friends():
            pl.semaphore_signal(barrier, inc=1, device_id=friend, device_id_type=MESH)

    def enter(self):
        pl.semaphore_wait(pltpu.get_barrier_semaphore(), len(self.friends()))


class Copies:
    def __init__(self, sems):
        self.sems = sems

    def build(self, source, target, device, out_sem, in_sem):
        return pltpu.make_async_remote_copy(
            src_ref=source,
            dst_ref=target,
            send_sem=self.sems[0].at[out_sem],
            recv_sem=self.sems[1].at[in_sem],
            device_id=device,
            device_id_type=MESH,
        )

    def start(self, source, target, device, number, in_sem=None, only=None):
        def begin():
            landing = number if in_sem is None else in_sem
            self.build(source(), target, device, number, landing).start()

        begin() if only is None else pl.when(only)(begin)

    def landed(self, target, number, only=None):
        def wait():
            self.build(target, target, {"tensor": 0}, number, number).wait_recv()

        wait() if only is None else pl.when(only)(wait)

    def sent(self, source, numbers, only=None):
        def wait():
            for number in numbers:
                self.build(source, source, {"tensor": 0}, number, number).wait_send()

        wait() if only is None else pl.when(only)(wait)


class Gather(Copies):
    SENDS, COPIES = 11, 14

    def __init__(self, place, own, full, group, columns, sems):
        super().__init__(sems)
        self.p, self.own, self.full, self.columns = place, own, full, columns
        self.group = group
        self.groups = slice(None) if group is None else slice(group, group + 1)
        self.mine = None if group is None else place.t == group
        self.pairs = None if group is None else place.t != group

    def at(self, g, z, spot, half):
        return self.full.at[g, z, spot[0], spot[1], half, :, self.columns]

    def block(self, spot, half):
        return self.at(self.groups, slice(None), spot, half)

    def forward(self, spot, device, number, in_sem=None):
        block = lambda: self.block(spot, self.p.t)
        self.start(block, block(), device, number, in_sem)

    def first(self):
        p = self.p
        here = (p.y, p.x)
        for s in range(1, p.depth):
            for core in range(2):
                self.start(
                    lambda core=core: self.own.at[core, :, self.columns],
                    self.at(p.t, p.z, here, core),
                    p.along_z(s, core),
                    2 * (s - 1) + core,
                    2 * (s - 1) + p.t,
                    only=self.mine,
                )
        self.start(
            lambda: self.own.at[p.other, :, self.columns],
            self.at(p.t, p.z, here, p.other),
            p.to_pair,
            6,
            only=self.mine,
        )

        def keep():
            self.full[p.t, p.z, p.y, p.x, p.t, :, self.columns] = self.own[p.t, :, self.columns]

        keep() if self.mine is None else pl.when(self.mine)(keep)

    def second(self):
        p = self.p
        here = (p.y, p.x)
        for n in range(6):
            if self.group is None or n % 2 == self.group:
                self.landed(self.at(p.t, p.z, here, p.t), n)
        self.landed(self.at(p.t, p.z, here, p.t), 6, only=self.pairs)
        self.forward(here, p.to_near, 7)
        self.forward(here, p.to_next, 8)
        self.forward(here, p.to_pair, 9)

    def third(self):
        p = self.p
        self.sent(self.own.at[0, :, self.columns], range(7), self.mine)
        self.landed(self.block(p.near, p.t), 7)
        self.forward(p.near, p.to_next, 0, 10)
        self.forward(p.near, p.to_pair, 1, 11)
        self.landed(self.block(p.next, p.t), 8)
        self.forward(p.next, p.to_pair, 2, 12)

    def fourth(self):
        p = self.p
        self.landed(self.block(p.far, p.t), 10)
        self.forward(p.far, p.to_pair, 3, 13)

    def last(self):
        p = self.p
        for n in (9, 11, 12, 13):
            self.landed(self.block((p.y, p.x), p.other), n)

    def left(self):
        p = self.p
        self.sent(self.block((p.y, p.x), p.t), (0, 1, 2, 3, 7, 8, 9))


class Scatter(Copies):
    COPIES = 11

    def __init__(self, place, part, group, columns, pair_in, near_in, next_in, last_in, sems):
        super().__init__(sems)
        self.p, self.part, self.columns = place, part, columns
        self.pair_in, self.near_in, self.next_in, self.last_in = pair_in, near_in, next_in, last_in
        self.group = group
        self.groups = slice(None) if group is None else slice(group, group + 1)
        self.mine = None if group is None else place.t == group
        self.pairs = None if group is None else place.t != group

    def at(self, g, z, spot, half):
        return self.part.at[g, z, spot[0], spot[1], half, :, self.columns]

    def block(self, spot, half):
        return self.at(self.groups, slice(None), spot, half)

    def add(self, spot, landed):
        p = self.p
        here = (self.groups, slice(None), spot[0], spot[1], p.t, slice(None), self.columns)
        self.part[here] = (self.part[here].astype(F32) + landed.astype(F32)).astype(BF16)

    def first(self):
        p = self.p
        self.start(
            lambda: self.part.at[self.groups, :, :, :, p.other, :, self.columns],
            self.pair_in,
            p.to_pair,
            0,
        )

    def second(self):
        p = self.p
        self.landed(self.pair_in, 0)
        for spot, number in ((p.far, 1), (p.near, 2)):
            self.add(spot, self.pair_in[:, :, spot[0], spot[1]])
            self.start(
                lambda spot=spot: self.block(spot, p.t),
                self.near_in.at[number - 1],
                p.to_near,
                number,
            )
        for spot in (p.next, (p.y, p.x)):
            self.add(spot, self.pair_in[:, :, spot[0], spot[1]])

    def third(self):
        p = self.p
        self.landed(self.near_in.at[0], 1)
        self.add(p.next, self.near_in[0])
        self.start(lambda: self.block(p.next, p.t), self.next_in, p.to_next, 3)
        self.landed(self.near_in.at[1], 2)
        self.add((p.y, p.x), self.near_in[1])

    def fourth(self):
        p = self.p
        self.landed(self.next_in, 3)
        self.add((p.y, p.x), self.next_in[...])
        self.up_the_levels()

    def up_the_levels(self):
        p = self.p
        here = (p.y, p.x)
        for s in range(1, p.depth):
            for core in range(2) if self.group is None else (self.group,):
                self.start(
                    lambda s=s, core=core: self.at(core, p.levels[s], here, p.t),
                    self.last_in.at[2 * (s - 1) + p.t],
                    p.along_z(s, core),
                    4 + 2 * (s - 1) + core,
                    4 + 2 * (s - 1) + p.t,
                )
        self.start(
            lambda: self.at(p.other, p.z, here, p.t),
            self.last_in.at[2 * (p.depth - 1)],
            p.to_pair,
            10,
            only=self.pairs,
        )

    def last(self, target):
        p = self.p

        def write():
            for n in range(7):
                self.landed(self.last_in.at[n], 4 + n)
            mine = self.part[p.t, p.z, p.y, p.x, p.t, :, self.columns].astype(F32)
            rest = self.last_in[2 * (p.depth - 1)].astype(F32)
            for s in range(1, p.depth):
                mine += self.last_in[2 * (s - 1) + p.t].astype(F32)
                rest += self.last_in[2 * (s - 1) + p.other].astype(F32)
            target[p.t] = mine
            target[p.other] = rest

        write() if self.mine is None else pl.when(self.mine)(write)

    def left(self):
        p = self.p
        self.sent(self.pair_in, (0,))
        self.sent(self.next_in, (1, 2, 3))
        for core in range(2) if self.group is None else (self.group,):
            self.sent(self.last_in.at[0], [4 + 2 * s + core for s in range(p.depth - 1)])
        self.sent(self.last_in.at[0], (10,), self.pairs)


class ShortScatter(Scatter):
    def second(self):
        p = self.p
        self.landed(self.pair_in, 0)
        for spot, target, device, number in (
            (p.far, self.near_in.at[0], p.to_far, 1),
            (p.near, self.near_in.at[1], p.to_near, 2),
            (p.next, self.next_in, p.to_next, 3),
        ):
            self.add(spot, self.pair_in[:, :, spot[0], spot[1]])
            self.start(lambda spot=spot: self.block(spot, p.t), target, device, number)
        self.add((p.y, p.x), self.pair_in[:, :, p.y, p.x])

    def fourth(self):
        p = self.p
        for part, number in ((self.next_in, 3), (self.near_in.at[1], 2), (self.near_in.at[0], 1)):
            self.landed(part, number)
            self.add((p.y, p.x), part[...])
        self.up_the_levels()


def scatter_scratch(groups, depth, columns):
    vmem = pltpu.VMEM
    return [
        vmem((groups, depth, 2, 2, 16, columns), BF16),
        vmem((2, groups, depth, 16, columns), BF16),
        vmem((groups, depth, 16, columns), BF16),
        vmem((2 * depth - 1, 16, columns), BF16),
    ]


class Reduce(Copies):
    COPIES = 10

    def __init__(self, place, own, parts, sums, sems):
        super().__init__(sems)
        self.p, self.own, self.parts, self.sums = place, own, parts, sums

    def first(self):
        p = self.p
        self.parts[p.spot] = self.own[...]
        for offset in range(1, 8):
            self.start(
                lambda: self.own, self.parts.at[p.spot], p.level[offset], offset - 1
            )

    def second(self):
        p = self.p
        for n in range(7):
            self.landed(self.own, n)
        total = self.parts[0]
        for spot in range(1, 8):
            total += self.parts[spot]
        self.sums[p.z] = total
        for s in range(1, p.depth):
            self.start(
                lambda: self.sums.at[p.z], self.sums.at[p.z], {"dp": p.chips_z[s]}, 6 + s
            )

    def last(self):
        p = self.p
        for s in range(1, p.depth):
            self.landed(self.own, 6 + s)
        total = self.sums[0]
        for z in range(1, p.depth):
            total += self.sums[z]
        return total

    def left(self):
        self.sent(self.own, range(6 + self.p.depth))


class Woven:
    def __init__(self, place, far, near, own, full, gathers, scatters, gains):
        self.p, self.far, self.near, self.own = place, far, near, own
        wa, wb, ga, gw = full
        own_a, own_b = own
        ranges = [(own_a, wa, 0, 0, 512), (own_a, wa, 0, 512, 1024), (own_a, wa, 1, 0, 1024)]
        ranges += [(own_b, wb, None, *part) for part in UP_PIECES + DOWN_PIECES]
        gather = [
            Gather(place, part, whole, g, slice(first, last), sems)
            for (part, whole, g, first, last), sems in zip(ranges, gathers)
        ]
        self.a0, self.a1, self.b = gather[:2], gather[2], gather[3:]
        ranges = [(gw, None, *part) for part in GRAD_PIECES]
        ranges += [(ga, 0, 0, 1024), (ga, 1, 0, 768), (ga, 1, 768, 1024)]
        kinds = [Scatter] * 5 + [ShortScatter] * 3
        scatter = [
            kind(place, part, g, slice(first, last), *buffers)
            for kind, (part, g, first, last), buffers in zip(kinds, ranges, scatters)
        ]
        self.down_grad, self.up_grad, self.out_grad = scatter[:2], scatter[2:4], scatter[4]
        self.a0_grad, self.a1_grad = scatter[5], scatter[6:]
        self.gains = gains
        self.everything = scatter + [gains]

    def table(self, at, steps):
        for place, calls in steps.items():
            here = None
            for value, wanted in zip(at, place):
                here = (value == wanted) if here is None else here & (value == wanted)

            @pl.when(here)
            def _(calls=calls):
                for call in calls:
                    call()

    def fetch(self, n):
        return pltpu.make_async_copy(self.far[n], self.near[n], self.near["sems"].at[n])

    def put(self, name, n):
        return pltpu.make_async_copy(self.near[name], self.far[name], self.near["sems"].at[n])

    def put_rows(self, which, r):
        rows = pl.ds(pl.multiple_of(r * LAST, LAST), LAST)
        source, target = ((1, "grad_out"), (0, "out"))[which]
        return pltpu.make_async_copy(
            self.near[source].at[rows],
            self.far[target].at[rows],
            self.near["sems"].at[18 + 2 * which + r],
        )

    def before(self):
        self.p.knock()
        for n in range(14, -1, -1):
            self.fetch(n).start()
        for n in range(2, 15):
            self.fetch(n).wait()
        first = self.p.t == 0
        for rows, row in ((2, "seg_row"), (3, "pad_row")):
            rows = self.near[rows]
            self.near[row][...] = jnp.where(first, rows[0:1, :], rows[1:2, :])
        own_a, own_b = self.own
        halves = lambda n: self.near[n][...].astype(BF16).reshape(2, 16, -1)
        for n in range(4):
            own_a[:, :, 256 * n : 256 * n + 256] = halves(8 + n)
        own_b[:, :, 0:256] = halves(12)
        own_b[:, :, 256:1280] = halves(13)
        own_b[:, :, 1280:2304] = halves(14)

    def enter(self):
        self.p.enter()
        self.a0[0].first()
        self.a0[1].first()
        self.fetch(0).wait()
        self.fetch(1).wait()

    def normalised(self):
        pass

    def weights_a(self, g, part):
        one, two = self.a0
        a1, b = self.a1, self.b
        self.table(
            (g,),
            (
                {
                    (0,): (
                        one.second, a1.first, two.second, b[0].first, one.third, two.third,
                        one.fourth, a1.second, one.last,
                    ),
                    (1,): (a1.fourth, a1.last),
                },
                {
                    (0,): (b[1].first, two.fourth, two.last),
                    (1,): (b[0].third, b[3].first),
                },
            )[part],
        )

    def projected(self, g):
        b = self.b
        self.table((g,), {(0,): (self.a1.third, b[0].second), (1,): (b[2].second,)})

    def mixing(self, g, i):
        b = self.b
        steps = {
            (0, 1): (b[1].second, self.a0[0].left, self.a0[1].left, b[2].first),
            (1, 1): (b[1].third, b[0].fourth),
        }
        self.table((g, i), steps)

    def weights_up(self, part):
        b = self.b
        if part == 0:
            b[3].second()
            b[0].last()
        else:
            b[1].last()

    def feeding(self, part, r):
        b = self.b
        steps = {(0, 1): (b[2].third, b[1].fourth), (1, 1): (b[3].third,)}
        self.table((part, r), steps)

    def fed_up(self):
        self.b[2].fourth()

    def grads_down(self, part):
        if part == 0:
            self.a1.left()
            self.b[0].left()
            self.b[1].left()
        self.down_grad[part].first()

    def weights_down(self, part):
        self.b[2 + part].last()
        self.b[2 + part].left()
        if part == 1:
            self.down_grad[1].second()

    def fed_grad(self, part):
        if part == 0:
            self.b[3].fourth()
            self.down_grad[0].second()

    def grads_up(self, part):
        if part < 2:
            self.up_grad[part].first()
        if part == 1:
            self.up_grad[0].second()
        if part == 2:
            self.out_grad.first()
            self.down_grad[1].third()
            self.up_grad[1].second()

    def feeding_down(self, r):
        self.table((r,), {(1,): (self.down_grad[0].third,)})

    def mixing_back(self, g, i):
        one, two = self.down_grad
        up, rest = self.up_grad
        steps = {
            (0, 1): (one.fourth, self.out_grad.second),
            (1, 1): (self.a0_grad.second, self.out_grad.third, self.down_last, up.fourth),
        }
        self.table((g, i), steps)

    def mixed_back(self, g):
        self.table((g,), {(0,): (self.up_grad[0].third, self.down_grad[1].fourth)})

    def grads_a(self, g):
        one, two = self.a1_grad
        self.table((g,), {(0,): (self.a0_grad.first, self.up_grad[1].third), (1,): (one.first,)})

    def grads_last(self):
        self.a1_grad[1].first()

    def finishing(self, which, r):
        one, two = self.a1_grad
        steps = {
            (0, 1): (one.second, self.up_grad[1].fourth),
            (1, 0): (self.out_grad.fourth, self.a0_grad.fourth),
            (1, 1): (two.second,),
        }
        self.table((which, r), steps)

    def down_last(self):
        self.down_grad[0].last(self.near["dw"].at[:, :, 1280:1792])

    def finished(self, which, r):
        self.put_rows(which, r).start()

    def gained(self):
        self.gains.first()

    def after(self):
        one, two = self.a1_grad
        da, dw = self.near["da"], self.near["dw"]
        one.fourth()
        self.gains.second()
        two.fourth()
        self.down_grad[1].last(dw.at[:, :, 1792:2304])
        self.up_grad[0].last(dw.at[:, :, 256:768])
        self.up_grad[1].last(dw.at[:, :, 768:1280])
        self.out_grad.last(dw.at[:, :, 0:256])
        self.put("dw", 15).start()
        self.near["total"][...] = self.gains.last()
        self.put("total", 16).start()
        self.a0_grad.last(da)
        one.last(da.at[:, :, 0:768])
        two.last(da.at[:, :, 768:1024])
        self.put("da", 17).start()
        self.everything_left()

    def everything_left(self):
        for copies in self.everything:
            copies.left()
        for r in range(2):
            self.put_rows(0, r).wait()
            self.put_rows(1, r).wait()
        self.put("dw", 15).wait()
        self.put("total", 16).wait()
        self.put("da", 17).wait()


def woven_kernel(length, depth, *refs):
    refs = list(refs)
    take = lambda n: [refs.pop(0) for _ in range(n)]
    far = dict(enumerate(take(15)))
    far.update(zip(("out", "grad_out", "da", "dw", "total"), take(5)))
    near = dict(enumerate(take(15)))
    near.update(zip(("da", "dw", "total", "seg_row", "pad_row", "sems"), take(6)))
    own, full = take(2), take(4)
    small, parts, sums = take(3)
    gain_sems = take(2)
    gathers = [take(2) for _ in range(7)]
    scatters = [take(4) for _ in range(8)]
    scatters = [buffers + [sems] for buffers, sems in zip(scatters, gathers + [take(2)])]
    place = Place(depth)
    gains = Reduce(place, small, parts, sums, gain_sems)
    comm = Woven(place, far, near, own, full, gathers, scatters, gains)
    layer_body(
        length, comm, near["seg_row"], near["pad_row"], *[near[n] for n in range(4, 8)], *full,
        small, near[0], near[1], *refs,
    )


def write_kernel(out_in, grad_in, da, dw, small, *refs):
    (
        out, grad_out, mixer_gain, query, key, value, slot, out_t, feed_gain, up, up_bias, down_t,
        down_bias,
    ) = refs
    out[...] = out_in[...]
    grad_out[...] = grad_in[...]

    @pl.when(pl.program_id(0) == 0)
    def _():
        rows = lambda part: part.reshape(-1, part.shape[-1])
        query[...] = rows(da[:, :, 0:256])
        key[...] = rows(da[:, :, 256:512])
        value[...] = rows(da[:, :, 512:768])
        slot[...] = rows(da[:, :, 768:1024])
        out_t[...] = rows(dw[:, :, 0:256])
        up[...] = rows(dw[:, :, 256:1280])
        down_t[...] = rows(dw[:, :, 1280:2304])
        feed_gain[...] = small[0:1, :]
        mixer_gain[...] = small[1:2, :]
        down_bias[...] = small[2:3, :]
        for row in range(4):
            up_bias[:, row * 512 : (row + 1) * 512] = small[4 + row : 5 + row, :]


def write(out, grad_out, da, dw, small):
    shape = jax.ShapeDtypeStruct
    length, width = out.shape
    square, wide = shape((32, 256), F32), shape((32, 1024), F32)
    row, big = shape((1, width), F32), shape(out.shape, BF16)
    outputs = (big, big, row) + (square,) * 5 + (row, wide, shape((1, 4 * width), F32), wide, row)
    half = pl.BlockSpec((length // 2, width), lambda i: (i, 0))
    whole = lambda array: pl.BlockSpec(array.shape, lambda i: (0,) * len(array.shape))
    return pl.pallas_call(
        write_kernel,
        grid=(2,),
        out_shape=outputs,
        in_specs=[half, half, whole(da), whole(dw), whole(small)],
        out_specs=(half, half) + tuple(whole(array) for array in outputs[2:]),
        name="write",
    )(out, grad_out, da, dw, small)


def woven(depth, *inputs):
    length, width = inputs[0].shape
    shape = jax.ShapeDtypeStruct
    far = pl.BlockSpec(memory_space=pl.ANY)
    vmem = pltpu.VMEM
    dma = pltpu.SemaphoreType.DMA
    full = lambda columns: vmem((2, depth, 2, 2, 2, 16, columns), BF16)
    da, dw, total = shape((2, 16, 1024), F32), shape((2, 16, 2304), F32), shape((8, width), F32)
    scatters = []
    for groups, columns in [(2, 512)] * 4 + [(2, 256), (1, 1024), (1, 768), (1, 256)]:
        scatters += scatter_scratch(groups, depth, columns)
    return pl.pallas_call(
        functools.partial(woven_kernel, length, depth),
        out_shape=(shape((length, width), BF16), shape((length, width), BF16), da, dw, total),
        in_specs=[far] * 15,
        out_specs=(far,) * 5,
        scratch_shapes=[vmem(array.shape, array.dtype) for array in inputs]
        + [vmem(array.shape, array.dtype) for array in (da, dw, total)]
        + [
            vmem((1, length), jnp.int32),
            vmem((1, length), jnp.int32),
            dma((22,)),
            vmem((2, 16, 1024), BF16),
            vmem((2, 16, 2304), BF16),
            full(1024),
            full(2304),
            full(1024),
            full(2304),
            vmem((8, width), F32),
            vmem((8, 8, width), F32),
            vmem((depth, 8, width), F32),
            dma((Reduce.COPIES,)),
            dma((Reduce.COPIES,)),
        ]
        + [dma((Gather.SENDS,)), dma((Gather.COPIES,))] * 7
        + scatters
        + [dma((Scatter.COPIES,))] * 2
        + layer_scratch(length, width),
        compiler_params=pltpu.CompilerParams(
            collective_id=0, has_side_effects=True, vmem_limit_bytes=63 * 1024 * 1024
        ),
        name="woven",
    )(*inputs)


def per_device(
    direct,
    tokens,
    segment_ids,
    padding,
    mixer_gain,
    query_weight,
    key_weight,
    value_weight,
    slot_weight,
    out_weight,
    feed_gain,
    up_weight,
    up_bias,
    down_weight,
    down_bias,
    cotangent,
):
    gains = (mixer_gain[None], feed_gain[None])
    biases = (up_bias[None], down_bias[None])
    if direct:
        owns = (
            query_weight, key_weight, value_weight, slot_weight, out_weight.T, up_weight,
            down_weight.T,
        )
        depth = lax.axis_size("dp") // 4
        results = write(
            *woven(depth, tokens, cotangent, segment_ids, padding, *gains, *biases, *owns)
        )
        (
            out, grad_out, gain_one, query, key, value, slot, out_t, gain_two, up, bias_one, down_t,
            bias_two,
        ) = results
        return (
            out, grad_out, gain_one[0], query, key, value, slot, out_t.T, gain_two[0], up,
            bias_one[0], down_t.T, bias_two[0],
        )
    own_a = jnp.concatenate([query_weight, key_weight, value_weight, slot_weight], 1)
    own_b = jnp.concatenate([out_weight.T, up_weight, down_weight.T], 1)
    wa, wb = (
        lax.all_gather(lax.all_gather(own.astype(BF16), "dp", axis=0, tiled=True), "tensor")
        for own in (own_a, own_b)
    )
    half = lax.axis_index("tensor")
    pick = lambda rows: lax.dynamic_slice_in_dim(rows, half, 1, 0)
    out, grad_out, ga, gw, small = layer(
        tokens, cotangent, pick(segment_ids), pick(padding), *gains, *biases, wa, wb
    )
    da, dw = (
        lax.psum_scatter(
            lax.psum_scatter(part.astype(F32), "tensor", scatter_dimension=0),
            "dp",
            scatter_dimension=0,
            tiled=True,
        )
        for part in (ga, gw)
    )
    small = lax.psum(small, ("dp", "tensor"))
    return (
        out,
        grad_out,
        small[1],
        da[:, 0:256],
        da[:, 256:512],
        da[:, 512:768],
        da[:, 768:1024],
        dw[:, 0:256].T,
        small[0],
        dw[:, 256:1280],
        small[4:8].reshape(-1),
        dw[:, 1280:2304].T,
        small[2],
    )


def solution(mesh):
    in_specs = (
        P(("dp", "tensor"), None),
        P("dp", None),
        P("dp", None),
        P(),
        P("dp", "tensor"),
        P("dp", "tensor"),
        P("dp", "tensor"),
        P("dp", "tensor"),
        P("tensor", "dp"),
        P(),
        P("dp", "tensor"),
        P(),
        P("tensor", "dp"),
        P(),
        P(("dp", "tensor"), None),
    )
    out_specs = (
        P(("dp", "tensor"), None),
        P(("dp", "tensor"), None),
        P(),
        P("dp", "tensor"),
        P("dp", "tensor"),
        P("dp", "tensor"),
        P("dp", "tensor"),
        P("tensor", "dp"),
        P(),
        P("dp", "tensor"),
        P(),
        P("tensor", "dp"),
        P(),
    )
    direct = mesh.shape["dp"] == 16 and mesh.shape["tensor"] == 2
    return jax.shard_map(
        functools.partial(per_device, direct),
        mesh=mesh,
        in_specs=in_specs,
        out_specs=out_specs,
        check_vma=False,
    )
```
